32 devices in a mesh: ctx: 8 (over y, x, core), dp: 4 (over z).
Axes of the slice: x: 2, y: 2, z: 4, core: 2. Of those that a mesh axis runs over, the one named last changes fastest.
Arguments:
- tokens: bfloat16 [4, 3072, 4096], P('dp', 'ctx'), may hold values from -6 to 6
- key_input: bfloat16 [4, 3072, 2048], P('dp', 'ctx'), may hold values from -6 to 6
- values: bfloat16 [4, 3072, 2048], P('dp', 'ctx'), may hold values from -6 to 6
- q_weight: bfloat16 [4096, 2048], P(('ctx', 'dp')), may hold values from -0.09375 to 0.09375
- q_spikes: int32 [4, 3072, 2048], P('dp', 'ctx'), may hold values 0 or 1
- k_spikes: int32 [4, 3072, 2048], P('dp', 'ctx'), may hold values 0 or 1
- cotangent: bfloat16 [4, 3072, 2048], P('dp', 'ctx'), may hold values from -6 to 6
Outputs:
- attended: bfloat16 [4, 3072, 2048], P('dp', 'ctx')
- grad_tokens: bfloat16 [4, 3072, 4096], P('dp', 'ctx')
- grad_keys: bfloat16 [4, 3072, 2048], P('dp', 'ctx')
- grad_values: bfloat16 [4, 3072, 2048], P('dp', 'ctx')
The draws below stay inside these ranges and needn't reach their ends.
All inputs are finite; a program needn't handle non-finite values. No bound on the sum of `q_spikes` or of `k_spikes` on one device may be relied on, other than what follows from the above.
Results may differ from the reference program's by a relative error of at most 0.005.
Values may be sent and summed in bfloat16 or wider, within the bound.
No kernel may reach another device: no remote copies, remote signals or barrier semaphores. Data moves between devices by JAX's collectives and lax.ppermute only.
A program may use at most 256 MiB of HBM per device.

```python
import math
import jax
import jax.numpy as jnp
from jax import lax

D = 4096
HEADS = 16
HEAD = 128
TOK_DEV = 384
HD = 2048
SEQ = 3072
BATCH = 4
N_CTX = 8


def with_ends(drawn, rng, low, high):
    longest = drawn.shape.index(max(drawn.shape))
    spots = []
    for shift in (0, 1):
        where = [jax.random.randint(jax.random.fold_in(rng, axis), (), 0, length) for axis, length in enumerate(drawn.shape)]
        where[longest] = (where[longest] + shift) % drawn.shape[longest]
        spots.append(tuple(where))
    return drawn.at[spots[0]].set(low).at[spots[1]].set(high)


def level_of(rng, dims, split, low, high):
    level = 1.0
    for axis_at, shards_of in split:
        draws = jax.random.uniform(jax.random.fold_in(jax.random.fold_in(rng, 6), axis_at), (shards_of,), jnp.float32, low / len(split), high / len(split))
        level = level * jnp.repeat(jnp.exp(draws), dims[axis_at] // shards_of).reshape((-1,) + (1,) * (len(dims) - 1 - axis_at))
    return level


def gaussian(stream_key, shape, scale, limit, split=(), dtype=jnp.bfloat16):
    values = jax.random.normal(stream_key, shape, jnp.float32) * scale
    if len(split) > 0:
        values = level_of(stream_key, shape, split, -0.22, 0.18) * values
    return jnp.clip(values, min=-limit, max=limit).astype(dtype)


def setup_inputs(seed: int = 0) -> dict:
    seeds = jax.random.split(jax.random.key(seed), 8)
    tokens = gaussian(seeds[0], (BATCH, SEQ, D), 1.0, 6.0, ((0, 4), (1, 8)))
    key_input = gaussian(seeds[1], (BATCH, SEQ, HD), 1.0, 6.0, ((0, 4), (1, 8)))
    values = gaussian(seeds[2], (BATCH, SEQ, HD), 1.0, 6.0, ((0, 4), (1, 8)))
    q_weight = gaussian(seeds[3], (D, HD), D ** -0.5, 0.09375, ((0, 32),))
    q_spikes = with_ends((jax.random.randint(seeds[4], (BATCH, SEQ, HD), 0, 3) < 1).astype(jnp.int32), jax.random.fold_in(seeds[4], 1), 0, 1)
    k_spikes = with_ends((jax.random.randint(seeds[5], (BATCH, SEQ, HD), 0, 3) < 1).astype(jnp.int32), jax.random.fold_in(seeds[5], 1), 0, 1)
    cotangent = gaussian(seeds[6], (BATCH, SEQ, HD), 1.0, 6.0, ((0, 4), (1, 8)))
    return {"tokens": tokens, "key_input": key_input, "values": values, "q_weight": q_weight, "q_spikes": q_spikes, "k_spikes": k_spikes, "cotangent": cotangent}


exact_mode = lax.Precision.HIGHEST

def to_blocks(array):
    shaped = array.astype(jnp.float32).reshape(BATCH, N_CTX, TOK_DEV, HEADS, HEAD)
    return jnp.transpose(shaped, (1, 0, 2, 3, 4))

def from_blocks(array):
    return jnp.transpose(array, (1, 0, 2, 3, 4)).reshape(BATCH, SEQ, HEADS * HEAD)

def rounded(array):
    narrow = lax.optimization_barrier(array.astype(jnp.bfloat16))
    return narrow.astype(jnp.float32)

def reference(tokens, key_input, values, q_weight, q_spikes, k_spikes, cotangent):
    factor = 3.0 / math.sqrt(HEAD * SEQ)
    token_rows = tokens.reshape(BATCH * SEQ, D)
    projected = jnp.dot(token_rows, q_weight, preferred_element_type=jnp.float32).reshape(BATCH, SEQ, HD)
    queries = (projected * q_spikes.astype(jnp.float32)).astype(jnp.bfloat16)
    keys = key_input * k_spikes.astype(jnp.bfloat16)
    block_data = (to_blocks(queries), to_blocks(keys), to_blocks(values), to_blocks(cotangent))
    causal = jnp.tril(jnp.ones((TOK_DEV, TOK_DEV), jnp.float32))

    def both_scores(query_wide, key_wide, value_wide, grad_wide):
        scores = jnp.einsum('blhe,bmhe->bhlm', query_wide, key_wide, precision=exact_mode) * causal
        grad_scores = jnp.einsum('blhf,bmhf->bhlm', grad_wide, value_wide, precision=exact_mode) * causal
        return (rounded(scores), rounded(grad_scores))

    def forward_step(memory, inputs_now):
        query_wide, key_wide, value_wide, grad_wide = inputs_now
        scores, grad_scores = both_scores(query_wide, key_wide, value_wide, grad_wide)
        output = jnp.einsum('bhlm,bmhf->blhf', scores, value_wide, precision=exact_mode)
        output = output + jnp.einsum('blhe,bhef->blhf', query_wide, memory, precision=exact_mode)
        query_grad = jnp.einsum('bhlm,bmhe->blhe', grad_scores, key_wide, precision=exact_mode)
        query_grad = query_grad + jnp.einsum('blhf,bhef->blhe', grad_wide, memory, precision=exact_mode)
        memory = memory + jnp.einsum('blhe,blhf->bhef', key_wide, value_wide, precision=exact_mode)
        return (memory, (output, query_grad))

    def backward_step(memory, inputs_now):
        query_wide, key_wide, value_wide, grad_wide = inputs_now
        scores, grad_scores = both_scores(query_wide, key_wide, value_wide, grad_wide)
        key_grad = jnp.einsum('bhlm,blhe->bmhe', grad_scores, query_wide, precision=exact_mode)
        key_grad = key_grad + jnp.einsum('bmhf,bhef->bmhe', value_wide, memory, precision=exact_mode)
        value_grad = jnp.einsum('bhlm,blhf->bmhf', scores, grad_wide, precision=exact_mode)
        value_grad = value_grad + jnp.einsum('bmhe,bhef->bmhf', key_wide, memory, precision=exact_mode)
        memory = memory + jnp.einsum('blhe,blhf->bhef', query_wide, grad_wide, precision=exact_mode)
        return (memory, (key_grad, value_grad))
    zeroes = jnp.zeros((BATCH, HEADS, HEAD, HEAD), jnp.float32)
    _, (output, query_grad) = lax.scan(forward_step, zeroes, block_data)
    _, (key_grad, value_grad) = lax.scan(backward_step, zeroes, block_data, reverse=True)
    attended = (factor * from_blocks(output)).astype(jnp.bfloat16)
    masked_grad = (factor * from_blocks(query_grad) * q_spikes.astype(jnp.float32)).astype(jnp.bfloat16)
    grad_tokens = jnp.dot(masked_grad.reshape(BATCH * SEQ, HD), q_weight.T, preferred_element_type=jnp.float32)
    grad_tokens = grad_tokens.reshape(BATCH, SEQ, D).astype(jnp.bfloat16)
    grad_keys = (factor * from_blocks(key_grad) * k_spikes.astype(jnp.float32)).astype(jnp.bfloat16)
    grad_values = (factor * from_blocks(value_grad)).astype(jnp.bfloat16)
    return (attended, grad_tokens, grad_keys, grad_values)
```

```python
import math

import jax
import jax.numpy as jnp
from jax import lax
from jax.sharding import Mesh, PartitionSpec as P

HEADS = 16
HEAD = 128
CHUNKS = 4
CTX = ("chip", "core")


def scan_sum(part, count, reverse):
    place = lax.axis_index(CTX)
    total = part
    state = jnp.zeros_like(part)
    bits = count.bit_length() - 1
    for bit in range(bits):
        step = 1 << bit
        last = bit == bits - 1
        pairs = []
        for source in range(count):
            high = bool(source & step)
            if not last or high == reverse:
                pairs.append((source, source ^ step))
        got = lax.ppermute(total.astype(jnp.bfloat16), CTX, pairs).astype(jnp.float32)
        if last:
            state = state + got
        else:
            mine = ((place // step) % 2) == (0 if reverse else 1)
            state = state + jnp.where(mine, got, 0.0)
            total = total + got
    return state


def per_device(tokens, key_input, values, q_weight, q_spikes, k_spikes, cotangent):
    batches, length, model_width = tokens.shape
    head_total = q_weight.shape[1]
    chips = lax.axis_size("chip")
    count = chips * 2
    sequence = length * count
    factor = 3.0 / math.sqrt(HEAD * sequence)
    core = lax.axis_index("core")
    token_rows = tokens.reshape(batches * length, chips, 2, model_width // (2 * chips))
    mine = lax.dynamic_index_in_dim(token_rows, core, 2, False).reshape(batches * length, -1)
    theirs = lax.dynamic_index_in_dim(token_rows, 1 - core, 2, False).reshape(
        batches * length, -1
    )
    wide = head_total // CHUNKS
    weights = []
    for chunk in range(CHUNKS):
        part = q_weight[:, chunk * wide : (chunk + 1) * wide]
        half = lax.all_gather(part, ("chip", "dp"), axis=0, tiled=True)
        weights.append((half, lax.ppermute(half, "core", [(0, 1), (1, 0)])))
    f32 = jnp.float32
    projected = jnp.concatenate(
        [
            jnp.dot(mine, half, preferred_element_type=f32)
            + jnp.dot(theirs, other, preferred_element_type=f32)
            for half, other in weights
        ],
        axis=1,
    )
    queries = (
        projected.reshape(batches, length, head_total) * q_spikes.astype(jnp.float32)
    ).astype(jnp.bfloat16)
    spiked_keys = key_input * k_spikes.astype(jnp.bfloat16)

    def by_heads(array):
        return array.reshape(batches, length, HEADS, HEAD)

    query_wide = by_heads(queries)
    key_wide = by_heads(spiked_keys)
    value_wide = by_heads(values)
    grad_wide = by_heads(cotangent)
    causal = jnp.tril(jnp.ones((length, length), jnp.float32))

    def prod(form, a, b):
        return jnp.einsum(form, a, b, preferred_element_type=f32)

    own_memory = prod("blhe,blhf->bhef", key_wide, value_wide)
    before = scan_sum(own_memory, count, False).astype(jnp.bfloat16)
    grad_scores = prod("blhf,bmhf->bhlm", grad_wide, value_wide)
    grad_scores = (grad_scores * causal).astype(jnp.bfloat16)
    query_grad = prod("bhlm,bmhe->blhe", grad_scores, key_wide)
    query_grad = query_grad + prod("blhf,bhef->blhe", grad_wide, before)
    shape_out = (batches, length, head_total)
    masked_grad = (factor * query_grad.reshape(shape_out) * q_spikes.astype(f32)).astype(
        jnp.bfloat16
    )
    masked_rows = masked_grad.reshape(batches * length, head_total)

    own_adjoint = prod("blhe,blhf->bhef", query_wide, grad_wide)
    later_adjoint = scan_sum(own_adjoint, count, True).astype(jnp.bfloat16)
    scores = prod("blhe,bmhe->bhlm", query_wide, key_wide)
    scores = (scores * causal).astype(jnp.bfloat16)
    output = prod("bhlm,bmhf->blhf", scores, value_wide)
    output = output + prod("blhe,bhef->blhf", query_wide, before)
    attended = (factor * output.reshape(shape_out)).astype(jnp.bfloat16)

    contract = (((1,), (1,)), ((), ()))
    halves = []
    for side in range(2):
        total = 0.0
        for chunk in range(CHUNKS):
            total = total + lax.dot_general(
                masked_rows[:, chunk * wide : (chunk + 1) * wide],
                weights[chunk][side],
                contract,
                preferred_element_type=f32,
            )
        halves.append(total.astype(jnp.bfloat16).reshape(batches * length, chips, -1))
    first = jnp.where(core == 0, halves[0], halves[1])
    second = jnp.where(core == 0, halves[1], halves[0])
    grad_tokens = jnp.stack([first, second], axis=2).reshape(batches, length, model_width)

    key_grad = prod("bhlm,blhe->bmhe", grad_scores, query_wide)
    key_grad = key_grad + prod("bmhf,bhef->bmhe", value_wide, later_adjoint)
    value_grad = prod("bhlm,blhf->bmhf", scores, grad_wide)
    value_grad = value_grad + prod("bmhe,bhef->bmhf", key_wide, later_adjoint)
    grad_keys = (factor * key_grad.reshape(shape_out) * k_spikes.astype(f32)).astype(jnp.bfloat16)
    grad_values = (factor * value_grad.reshape(shape_out)).astype(jnp.bfloat16)
    return (attended, grad_tokens, grad_keys, grad_values)


def solution(mesh):
    count, spread = mesh.shape["ctx"], mesh.shape["dp"]
    fine = Mesh(mesh.devices.reshape(count // 2, 2, spread), ("chip", "core", "dp"))
    block = P("dp", CTX, None)
    rows = P(("chip", "core", "dp"), None)
    in_specs = (block, block, block, rows, block, block, block)
    return jax.shard_map(
        per_device, mesh=fine, in_specs=in_specs, out_specs=(block,) * 4, check_vma=False
    )
```

```python
import functools
import math

import jax
import jax.numpy as jnp
from jax import lax
from jax.experimental import pallas as pl
from jax.experimental.pallas import tpu as pltpu
from jax.sharding import Mesh, PartitionSpec as P

HEAD = 128
ROWS = 128
GROUP = 8
WIDE = 512
PAIR = 256
CTX = ("chip", "core")
SWAP = [(0, 1), (1, 0)]
f32, bf16 = jnp.float32, jnp.bfloat16
VMEM_LIMIT = 40 * 1024 * 1024


def nn(a, b):
    return lax.dot_general(a, b, (((1,), (0,)), ((), ())), preferred_element_type=f32)


def nt(a, b):
    return lax.dot_general(a, b, (((1,), (1,)), ((), ())), preferred_element_type=f32)


def tn(a, b):
    return lax.dot_general(a, b, (((0,), (0,)), ((), ())), preferred_element_type=f32)


def params(flops, moved):
    return dict(
        compiler_params=pltpu.CompilerParams(vmem_limit_bytes=VMEM_LIMIT),
        cost_estimate=pl.CostEstimate(flops=flops, bytes_accessed=moved, transcendentals=0),
    )


def columns(length, wide):
    return pl.BlockSpec((length, wide), lambda j: (0, j))


def states(wide):
    return pl.BlockSpec((wide, HEAD), lambda j: (j, 0))


def memory_kernel(key_ref, spike_ref, value_ref, keys_ref, own_ref, sent_ref):
    keys = key_ref[...] * spike_ref[...].astype(f32).astype(bf16)
    keys_ref[...] = keys
    for at in range(0, PAIR, HEAD):
        own = tn(keys[:, at : at + HEAD], value_ref[:, at : at + HEAD])
        own_ref[at : at + HEAD, :] = own
        sent_ref[at : at + HEAD, :] = own.astype(bf16)


def memory_call(key_input, k_spikes, values):
    length, total = values.shape
    return pl.pallas_call(
        memory_kernel,
        grid=(total // PAIR,),
        in_specs=[columns(length, PAIR)] * 3,
        out_specs=[columns(length, PAIR), states(PAIR), states(PAIR)],
        out_shape=[
            jax.ShapeDtypeStruct((length, total), bf16),
            jax.ShapeDtypeStruct((total, HEAD), f32),
            jax.ShapeDtypeStruct((total, HEAD), bf16),
        ],
        name="own_memory",
        **params(2 * length * total * HEAD, 12 * length * total),
    )(key_input, k_spikes, values)


def lower(square, flipped=False):
    row = lax.broadcasted_iota(jnp.int32, square.shape, 0)
    col = lax.broadcasted_iota(jnp.int32, square.shape, 1)
    keep = (col >= row) if flipped else (col <= row)
    return jnp.where(keep, square, 0.0)


def causal_row(a, b, at):
    end = at + HEAD
    last = lower(nt(a[at:end], b[at:end])).astype(bf16)
    if at == 0:
        return last
    return jnp.concatenate([nt(a[at:end], b[:at]).astype(bf16), last], axis=1)


def causal_column(a, b, at):
    end = at + HEAD
    first = lower(nt(a[at:end], b[at:end]), True).astype(bf16)
    if end == a.shape[0]:
        return first
    return jnp.concatenate([first, nt(a[at:end], b[end:]).astype(bf16)], axis=1)


def masked_kernel(factor, grad_ref, value_ref, keys_ref, spike_ref, high_ref, low_ref, out_ref):
    length = grad_ref.shape[0]
    for head in range(0, PAIR, HEAD):
        part = slice(head, head + HEAD)
        grad, value, keys = grad_ref[:, part], value_ref[:, part], keys_ref[:, part]
        high, low = high_ref[part, :], low_ref[part, :]
        for at in range(0, length, HEAD):
            rows = slice(at, at + HEAD)
            made = nn(causal_row(grad, value, at), keys[: at + HEAD])
            made = made + (nt(grad[rows], high) + nt(grad[rows], low))
            out_ref[rows, part] = (factor * made * spike_ref[rows, part].astype(f32)).astype(bf16)


def masked_call(factor, cotangent, values, keys, q_spikes, high, low):
    length, total = values.shape
    return pl.pallas_call(
        functools.partial(masked_kernel, factor),
        grid=(total // PAIR,),
        in_specs=[columns(length, PAIR)] * 4 + [states(PAIR)] * 2,
        out_specs=columns(length, PAIR),
        out_shape=jax.ShapeDtypeStruct((length, total), bf16),
        name="masked_grad",
        **params(8 * length * total * length, 12 * length * total),
    )(cotangent, values, keys, q_spikes, high, low)


def project_kernel(has_sum, *refs):
    _, *refs = refs
    tokens, pieces = refs[:GROUP], refs[GROUP : 2 * GROUP]
    rest = refs[2 * GROUP :]
    made = nn(
        jnp.concatenate([ref[...] for ref in tokens], axis=1),
        jnp.concatenate([ref[...] for ref in pieces], axis=0),
    )
    if has_sum:
        made = made + rest[0][...]
    rest[-1][...] = made


def token_specs(group, length):
    def one(piece):
        return pl.BlockSpec((length, ROWS), lambda j, places: (0, places[group * GROUP + piece]))

    return [one(piece) for piece in range(GROUP)]


def wide_spec(rows):
    return pl.BlockSpec((rows, WIDE), lambda j, places: (0, j))


def project_call(group, places, tokens, pieces, total_before):
    length = tokens.shape[0]
    total = pieces[0].shape[1]
    has_sum = total_before is not None
    extra = [total_before] if has_sum else []
    return pl.pallas_call(
        functools.partial(project_kernel, has_sum),
        grid_spec=pltpu.PrefetchScalarGridSpec(
            num_scalar_prefetch=1,
            grid=(total // WIDE,),
            in_specs=token_specs(group, length)
            + [wide_spec(ROWS)] * GROUP
            + [wide_spec(length)] * len(extra),
            out_specs=wide_spec(length),
        ),
        out_shape=jax.ShapeDtypeStruct((length, total), f32),
        input_output_aliases={1 + 2 * GROUP: 0} if has_sum else {},
        name="project",
        **params(2 * length * ROWS * GROUP * total, ROWS * GROUP * total * 2 + 8 * length * total),
    )(places, *[tokens] * GROUP, *pieces, *extra)


def query_kernel(*refs):
    _, *refs = refs
    tokens, pieces = refs[:GROUP], refs[GROUP : 2 * GROUP]
    sum_ref, spike_ref, grad_ref, query_ref, own_ref, sent_ref = refs[2 * GROUP :]
    made = nn(
        jnp.concatenate([ref[...] for ref in tokens], axis=1),
        jnp.concatenate([ref[...] for ref in pieces], axis=0),
    )
    made = made + sum_ref[...]
    queries = (made * spike_ref[...].astype(f32)).astype(bf16)
    query_ref[...] = queries
    for at in range(0, WIDE, HEAD):
        own = tn(queries[:, at : at + HEAD], grad_ref[:, at : at + HEAD])
        own_ref[at : at + HEAD, :] = own
        sent_ref[at : at + HEAD, :] = own.astype(bf16)


def query_call(group, places, tokens, pieces, total_before, q_spikes, cotangent):
    length = tokens.shape[0]
    total = pieces[0].shape[1]
    state_spec = pl.BlockSpec((WIDE, HEAD), lambda j, places: (j, 0))
    return pl.pallas_call(
        query_kernel,
        grid_spec=pltpu.PrefetchScalarGridSpec(
            num_scalar_prefetch=1,
            grid=(total // WIDE,),
            in_specs=token_specs(group, length)
            + [wide_spec(ROWS)] * GROUP
            + [wide_spec(length)] * 3,
            out_specs=[wide_spec(length), state_spec, state_spec],
        ),
        out_shape=[
            jax.ShapeDtypeStruct((length, total), bf16),
            jax.ShapeDtypeStruct((total, HEAD), f32),
            jax.ShapeDtypeStruct((total, HEAD), bf16),
        ],
        name="queries",
        **params(2 * length * ROWS * GROUP * total, ROWS * GROUP * total * 2 + 8 * length * total),
    )(places, *[tokens] * GROUP, *pieces, total_before, q_spikes, cotangent)


def back_kernel(group, has_before, places_ref, *refs):
    pieces, masked_ref = refs[:GROUP], refs[GROUP]
    out_ref, sum_ref, round_ref, sems = refs[GROUP + (2 if has_before else 1) :]
    step = pl.program_id(0)
    made = nt(masked_ref[...], jnp.concatenate([ref[...] for ref in pieces], axis=0))

    @pl.when(step == 0)
    def _():
        sum_ref[...] = made

    @pl.when(step > 0)
    def _():
        sum_ref[...] += made

    @pl.when(step == pl.num_programs(0) - 1)
    def _():
        round_ref[...] = sum_ref[...].astype(bf16)
        copies = []
        for piece in range(GROUP):
            place = pl.multiple_of(places_ref[group * GROUP + piece] * ROWS, ROWS)
            copy = pltpu.make_async_copy(
                round_ref.at[:, pl.ds(piece * ROWS, ROWS)],
                out_ref.at[:, pl.ds(place, ROWS)],
                sems.at[piece],
            )
            copy.start()
            copies.append(copy)
        for copy in copies:
            copy.wait()


def back_call(group, places, pieces, masked, before, width):
    length, total = masked.shape
    extra = [] if before is None else [before]
    return pl.pallas_call(
        functools.partial(back_kernel, group, before is not None),
        grid_spec=pltpu.PrefetchScalarGridSpec(
            num_scalar_prefetch=1,
            grid=(total // WIDE,),
            in_specs=[wide_spec(ROWS)] * GROUP
            + [wide_spec(length)]
            + [pl.BlockSpec(memory_space=pl.ANY)] * len(extra),
            out_specs=pl.BlockSpec(memory_space=pl.ANY),
            scratch_shapes=[
                pltpu.VMEM((length, ROWS * GROUP), f32),
                pltpu.VMEM((length, ROWS * GROUP), bf16),
                pltpu.SemaphoreType.DMA((GROUP,)),
            ],
        ),
        out_shape=jax.ShapeDtypeStruct((length, width), bf16),
        input_output_aliases={} if before is None else {2 + GROUP: 0},
        name="grad_tokens",
        **params(2 * length * ROWS * GROUP * total, ROWS * GROUP * total * 2 + 4 * length * total),
    )(places, *pieces, masked, *extra)


def inner_kernel(
    factor, query_ref, keys_ref, value_ref, grad_ref, high_ref, low_ref, out_ref, key_ref, val_ref
):
    length = query_ref.shape[0]
    for head in range(0, PAIR, HEAD):
        part = slice(head, head + HEAD)
        query, keys = query_ref[:, part], keys_ref[:, part]
        value, grad = value_ref[:, part], grad_ref[:, part]
        high, low = high_ref[part, :], low_ref[part, :]
        for at in range(0, length, HEAD):
            rows = slice(at, at + HEAD)
            made = nn(causal_row(query, keys, at), value[: at + HEAD])
            made = made + (nn(query[rows], high) + nn(query[rows], low))
            out_ref[rows, part] = (factor * made).astype(bf16)
            key_ref[rows, part] = nn(causal_column(value, grad, at), query[at:])
            val_ref[rows, part] = nn(causal_column(keys, query, at), grad[at:])


def inner_call(factor, queries, keys, values, cotangent, high, low):
    length, total = values.shape
    return pl.pallas_call(
        functools.partial(inner_kernel, factor),
        grid=(total // PAIR,),
        in_specs=[columns(length, PAIR)] * 4 + [states(PAIR)] * 2,
        out_specs=[columns(length, PAIR)] * 3,
        out_shape=[
            jax.ShapeDtypeStruct((length, total), bf16),
            jax.ShapeDtypeStruct((length, total), f32),
            jax.ShapeDtypeStruct((length, total), f32),
        ],
        name="inner",
        **params(16 * length * total * length, 18 * length * total),
    )(queries, keys, values, cotangent, high, low)


def outer_kernel(
    factor, key_ref, val_ref, keys_ref, value_ref, spike_ref, high_ref, low_ref, gk_ref, gv_ref
):
    for head in range(0, PAIR, HEAD):
        part = slice(head, head + HEAD)
        keys, value = keys_ref[:, part], value_ref[:, part]
        high, low = high_ref[part, :], low_ref[part, :]
        key_grad = key_ref[:, part] + (nt(value, high) + nt(value, low))
        gk_ref[:, part] = (factor * key_grad * spike_ref[:, part].astype(f32)).astype(bf16)
        value_grad = val_ref[:, part] + (nn(keys, high) + nn(keys, low))
        gv_ref[:, part] = (factor * value_grad).astype(bf16)


def outer_call(factor, key_part, value_part, keys, values, k_spikes, high, low):
    length, total = values.shape
    return pl.pallas_call(
        functools.partial(outer_kernel, factor),
        grid=(total // PAIR,),
        in_specs=[columns(length, PAIR)] * 5 + [states(PAIR)] * 2,
        out_specs=[columns(length, PAIR)] * 2,
        out_shape=[jax.ShapeDtypeStruct((length, total), bf16)] * 2,
        name="outer",
        **params(8 * length * total * HEAD, 20 * length * total),
    )(key_part, value_part, keys, values, k_spikes, high, low)


def halves(state):
    high = state.astype(bf16)
    return high, (state - high.astype(f32)).astype(bf16)


def scan_any(own, sent, count, reverse):
    place = lax.axis_index(CTX)
    total = own
    state = jnp.zeros_like(own)
    bits = count.bit_length() - 1
    for bit in range(bits):
        step = 1 << bit
        last = bit == bits - 1
        pairs = []
        for source in range(count):
            high = bool(source & step)
            if not last or high == reverse:
                pairs.append((source, source ^ step))
        got = lax.ppermute(sent, CTX, pairs).astype(f32)
        if last:
            state = state + got
        else:
            mine = ((place // step) % 2) == (0 if reverse else 1)
            state = state + jnp.where(mine, got, 0.0)
            total = total + got
            sent = total.astype(bf16)
    return state


def links(first, keep=lambda source, target: True):
    pairs = []
    for chip in range(4):
        for core in range(2):
            other = chip ^ (first if core == 0 else 3 - first)
            if keep((chip, core), other):
                pairs.append((chip * 2 + core, other * 2 + core))
    return pairs


def scan_four(own, sent, reverse):
    chip, core = lax.axis_index("chip"), lax.axis_index("core")
    low_bit = 1 - chip % 2 if reverse else chip % 2
    flip = 3 if reverse else 0
    half = own.shape[0] // 2
    sibling = lax.ppermute(sent, "core", SWAP)
    both = own + sibling.astype(f32)
    both = jnp.where(core == 0, both[:half], both[half:])

    def upward(source, target):
        at = source[0] ^ flip
        crossing = source[0] ^ target
        return crossing == 1 or not at & 2

    got = lax.ppermute(both.astype(bf16), CTX, links(1, upward)).astype(f32)
    first = jnp.where((core == 1) | (low_bit == 1), got, 0.0)
    message = got + jnp.where((core == 0) | (low_bit == 0), both, 0.0)
    more = lax.ppermute(message.astype(bf16), CTX, links(2, upward)).astype(f32)
    state = first + more
    other = lax.ppermute(state, "core", SWAP)
    whole = jnp.concatenate(
        [jnp.where(core == 0, state, other), jnp.where(core == 0, other, state)], axis=0
    )
    return whole + jnp.where(core == (0 if reverse else 1), sibling.astype(f32), 0.0)


def scan_sum(own, sent, chips, reverse):
    if chips == 4:
        return halves(scan_four(own, sent, reverse))
    return halves(scan_any(own, sent, chips * 2, reverse))


def gather_any(q_weight, chips, spread):
    whole = lax.all_gather(q_weight, ("chip", "core", "dp"), axis=0, tiled=True)
    number = whole.shape[0] // ROWS
    pieces = [whole[at * ROWS : (at + 1) * ROWS] for at in range(number)]
    return pieces, jnp.arange(number, dtype=jnp.int32)


def gather_four(q_weight):
    chip, core, layer = (lax.axis_index(name) for name in ("chip", "core", "dp"))
    inner = (layer == 1) | (layer == 2)
    ends = [(0, 1), (1, 0), (2, 3), (3, 2)]
    middle = [(1, 2), (2, 1)]
    outward = [(1, 0), (2, 3)]
    own = [q_weight]
    near = lax.ppermute(q_weight, "dp", ends)
    mid = lax.ppermute(q_weight, "dp", middle)
    own.append(near)
    own.append(jnp.where(inner, mid, lax.ppermute(mid, "dp", outward)))
    far = lax.ppermute(near, "dp", middle)
    own.append(jnp.where(inner, far, lax.ppermute(far, "dp", outward)))
    layers = [
        layer,
        layer ^ 1,
        jnp.where(layer < 2, 2, 1),
        jnp.where(layer < 2, 3, 0),
    ]
    pieces, places = [], []
    for piece, level in zip(own, layers):
        first = lax.ppermute(piece, CTX, links(1))
        second = lax.ppermute(piece, CTX, links(2))
        third = lax.ppermute(first, CTX, links(2))
        mine = [piece, first, second, third]
        pieces += mine + [lax.ppermute(one, "core", SWAP) for one in mine]
        for side in (core, 1 - core):
            for flip in (0, 1 + side, 2 - side, 3):
                places.append(((chip ^ flip) * 2 + side) * 4 + level)
    return pieces, jnp.stack(places).astype(jnp.int32)


def per_device(tokens, key_input, values, q_weight, q_spikes, k_spikes, cotangent):
    batches, length, width = tokens.shape
    assert batches == 1
    total = q_weight.shape[1]
    chips, spread = lax.axis_size("chip"), lax.axis_size("dp")
    factor = 3.0 / math.sqrt(HEAD * length * chips * 2)
    tokens, key_input, values, q_spikes, k_spikes, cotangent = (
        array.reshape(length, array.shape[2])
        for array in (tokens, key_input, values, q_spikes, k_spikes, cotangent)
    )
    if chips == 4 and spread == 4:
        pieces, places = gather_four(q_weight)
    else:
        pieces, places = gather_any(q_weight, chips, spread)
    keys, own, sent = memory_call(key_input, k_spikes, values)
    high, low = scan_sum(own, sent, chips, False)
    masked = masked_call(factor, cotangent, values, keys, q_spikes, high, low)
    groups = [pieces[at : at + GROUP] for at in range(0, len(pieces), GROUP)]
    partial = grad_tokens = None
    for group, some in enumerate(groups[:-1]):
        partial = project_call(group, places, tokens, some, partial)
        grad_tokens = back_call(group, places, some, masked, grad_tokens, width)
    last = len(groups) - 1
    queries, own, sent = query_call(
        last, places, tokens, groups[last], partial, q_spikes, cotangent
    )
    adjoint = scan_sum(own, sent, chips, True)
    attended, key_part, value_part = inner_call(
        factor, queries, keys, values, cotangent, high, low
    )
    grad_tokens = back_call(last, places, groups[last], masked, grad_tokens, width)
    grad_keys, grad_values = outer_call(
        factor, key_part, value_part, keys, values, k_spikes, *adjoint
    )
    return tuple(
        array.reshape(1, length, array.shape[1])
        for array in (attended, grad_tokens, grad_keys, grad_values)
    )


def solution(mesh):
    count, spread = mesh.shape["ctx"], mesh.shape["dp"]
    fine = Mesh(mesh.devices.reshape(count // 2, 2, spread), ("chip", "core", "dp"))
    block = P("dp", CTX, None)
    rows = P(("chip", "core", "dp"), None)
    in_specs = (block, block, block, rows, block, block, block)
    return jax.shard_map(
        per_device, mesh=fine, in_specs=in_specs, out_specs=(block,) * 4, check_vma=False
    )
```

```python
import functools
import math

import jax
import jax.numpy as jnp
from jax import lax
from jax.experimental import pallas as pl
from jax.experimental.pallas import tpu as pltpu
from jax.sharding import Mesh, PartitionSpec as P

HEAD = 128
PIECE = 128
WIDE = 512
CTX = ("chip", "core")
SWAP = [(0, 1), (1, 0)]
f32, bf16 = jnp.float32, jnp.bfloat16
VMEM_LIMIT = 60 * 1024 * 1024


def nn(a, b):
    return lax.dot_general(a, b, (((1,), (0,)), ((), ())), preferred_element_type=f32)


def nt(a, b):
    return lax.dot_general(a, b, (((1,), (1,)), ((), ())), preferred_element_type=f32)


def tn(a, b):
    return lax.dot_general(a, b, (((0,), (0,)), ((), ())), preferred_element_type=f32)


def params(flops, moved):
    return dict(
        compiler_params=pltpu.CompilerParams(vmem_limit_bytes=VMEM_LIMIT),
        cost_estimate=pl.CostEstimate(flops=flops, bytes_accessed=moved, transcendentals=0),
    )


def columns(length):
    return pl.BlockSpec((length, WIDE), lambda j: (0, j))


def states():
    return pl.BlockSpec((WIDE, HEAD), lambda j: (j, 0))


def anywhere():
    return pl.BlockSpec(memory_space=pl.ANY)


def memory_kernel(key_ref, spike_ref, value_ref, after_ref, keys_ref, own_ref, sent_ref):
    del after_ref
    keys = key_ref[...] * spike_ref[...].astype(f32).astype(bf16)
    keys_ref[...] = keys
    for at in range(0, WIDE, HEAD):
        own = tn(keys[:, at : at + HEAD], value_ref[:, at : at + HEAD])
        own_ref[at : at + HEAD, :] = own
        sent_ref[at : at + HEAD, :] = own.astype(bf16)


def memory_call(key_input, k_spikes, values, after):
    length, total = values.shape
    return pl.pallas_call(
        memory_kernel,
        grid=(total // WIDE,),
        in_specs=[columns(length)] * 3 + [anywhere()],
        out_specs=[columns(length), states(), states()],
        out_shape=[
            jax.ShapeDtypeStruct((length, total), bf16),
            jax.ShapeDtypeStruct((total, HEAD), f32),
            jax.ShapeDtypeStruct((total, HEAD), bf16),
        ],
        name="own_memory",
        **params(2 * length * total * HEAD, 12 * length * total),
    )(key_input, k_spikes, values, after)


def tie_kernel(*refs):
    del refs


def tie(array, *others):
    return pl.pallas_call(
        tie_kernel,
        in_specs=[anywhere()] * (1 + len(others)),
        out_specs=anywhere(),
        out_shape=jax.ShapeDtypeStruct(array.shape, array.dtype),
        input_output_aliases={0: 0},
        name="tie",
        **params(0, 0),
    )(array, *others)


def keep_lower(square, flipped=False):
    row = lax.broadcasted_iota(jnp.int32, square.shape, 0)
    col = lax.broadcasted_iota(jnp.int32, square.shape, 1)
    return jnp.where((col >= row) if flipped else (col <= row), square, 0.0).astype(bf16)


def causal(a, b):
    length = a.shape[0]
    cut = length - HEAD
    top = keep_lower(nt(a[:cut], b[:cut]))
    whole = nt(a[cut:], b)
    bottom = jnp.concatenate([whole[:, :cut].astype(bf16), keep_lower(whole[:, cut:])], axis=1)
    return [(slice(0, cut), slice(0, cut), top), (slice(cut, length), slice(0, length), bottom)]


def causal_turned(a, b):
    length = a.shape[0]
    whole = nt(a[:HEAD], b)
    top = jnp.concatenate(
        [keep_lower(whole[:, :HEAD], True), whole[:, HEAD:].astype(bf16)], axis=1
    )
    bottom = keep_lower(nt(a[HEAD:], b[HEAD:]), True)
    return [
        (slice(0, HEAD), slice(0, length), top),
        (slice(HEAD, length), slice(HEAD, length), bottom),
    ]


def twice(array):
    return jnp.concatenate([array, array], axis=1)


def masked_kernel(factor, grad_ref, value_ref, keys_ref, spike_ref, high_ref, low_ref, out_ref):
    for head in range(0, WIDE, HEAD):
        part = slice(head, head + HEAD)
        grad, value, keys = grad_ref[:, part], value_ref[:, part], keys_ref[:, part]
        state = jnp.concatenate([high_ref[part, :], low_ref[part, :]], axis=1)
        for rows, cols, scores in causal(grad, value):
            made = nn(scores, keys[cols]) + nt(twice(grad[rows]), state)
            out_ref[rows, part] = (factor * made * spike_ref[rows, part].astype(f32)).astype(bf16)


def masked_call(factor, cotangent, values, keys, q_spikes, high, low):
    length, total = values.shape
    return pl.pallas_call(
        functools.partial(masked_kernel, factor),
        grid=(total // WIDE,),
        in_specs=[columns(length)] * 4 + [states()] * 2,
        out_specs=columns(length),
        out_shape=jax.ShapeDtypeStruct((length, total), bf16),
        name="masked_grad",
        **params(8 * length * total * length, 12 * length * total),
    )(cotangent, values, keys, q_spikes, high, low)


def rows_of(blocks):
    return sum(block.shape[0] for block in blocks)


def product(tokens, blocks):
    return nn(
        jnp.concatenate([ref[...] for ref in tokens], axis=1),
        jnp.concatenate([ref[...] for ref in blocks], axis=0),
    )


def project_kernel(number, size, has_sum, *refs):
    _, *refs = refs
    tokens, blocks = refs[:number], refs[number : number + size]
    rest = refs[number + size :]
    made = product(tokens, blocks)
    if has_sum:
        made = made + rest[0][...]
    rest[-1][...] = made


def token_specs(number, length):
    def one(piece):
        return pl.BlockSpec((length, PIECE), lambda j, places: (0, places[piece]))

    return [one(piece) for piece in range(number)]


def wide_spec(rows):
    return pl.BlockSpec((rows, WIDE), lambda j, places: (0, j))


def project_call(places, tokens, blocks, before):
    length = tokens.shape[0]
    total = blocks[0].shape[1]
    depth = rows_of(blocks)
    number = depth // PIECE
    extra = [] if before is None else [before]
    return pl.pallas_call(
        functools.partial(project_kernel, number, len(blocks), before is not None),
        grid_spec=pltpu.PrefetchScalarGridSpec(
            num_scalar_prefetch=1,
            grid=(total // WIDE,),
            in_specs=token_specs(number, length)
            + [wide_spec(block.shape[0]) for block in blocks]
            + [wide_spec(length)] * len(extra),
            out_specs=wide_spec(length),
        ),
        out_shape=jax.ShapeDtypeStruct((length, total), f32),
        input_output_aliases={} if before is None else {1 + number + len(blocks): 0},
        name="project",
        **params(2 * length * depth * total, depth * total * 2 + 8 * length * total),
    )(places, *[tokens] * number, *blocks, *extra)


def query_kernel(number, size, *refs):
    _, *refs = refs
    tokens, blocks = refs[:number], refs[number : number + size]
    sum_ref, spike_ref, grad_ref, query_ref, own_ref, sent_ref = refs[number + size :]
    made = product(tokens, blocks) + sum_ref[...]
    queries = (made * spike_ref[...].astype(f32)).astype(bf16)
    query_ref[...] = queries
    for at in range(0, WIDE, HEAD):
        own = tn(queries[:, at : at + HEAD], grad_ref[:, at : at + HEAD])
        own_ref[at : at + HEAD, :] = own
        sent_ref[at : at + HEAD, :] = own.astype(bf16)


def query_call(places, tokens, blocks, before, q_spikes, cotangent):
    length = tokens.shape[0]
    total = blocks[0].shape[1]
    depth = rows_of(blocks)
    number = depth // PIECE
    state_spec = pl.BlockSpec((WIDE, HEAD), lambda j, places: (j, 0))
    return pl.pallas_call(
        functools.partial(query_kernel, number, len(blocks)),
        grid_spec=pltpu.PrefetchScalarGridSpec(
            num_scalar_prefetch=1,
            grid=(total // WIDE,),
            in_specs=token_specs(number, length)
            + [wide_spec(block.shape[0]) for block in blocks]
            + [wide_spec(length)] * 3,
            out_specs=[wide_spec(length), state_spec, state_spec],
        ),
        out_shape=[
            jax.ShapeDtypeStruct((length, total), bf16),
            jax.ShapeDtypeStruct((total, HEAD), f32),
            jax.ShapeDtypeStruct((total, HEAD), bf16),
        ],
        name="queries",
        **params(2 * length * depth * total, depth * total * 2 + 12 * length * total),
    )(places, *[tokens] * number, *blocks, before, q_spikes, cotangent)


def back_kernel(number, size, has_before, places_ref, *refs):
    blocks, masked_ref = refs[:size], refs[size]
    out_ref, sum_ref, round_ref, sems = refs[size + (2 if has_before else 1) :]
    step = pl.program_id(0)
    made = nt(masked_ref[...], jnp.concatenate([ref[...] for ref in blocks], axis=0))

    @pl.when(step == 0)
    def _():
        sum_ref[...] = made

    @pl.when(step > 0)
    def _():
        sum_ref[...] += made

    @pl.when(step == pl.num_programs(0) - 1)
    def _():
        round_ref[...] = sum_ref[...].astype(bf16)
        copies = []
        for piece in range(number):
            place = pl.multiple_of(places_ref[piece] * PIECE, PIECE)
            copy = pltpu.make_async_copy(
                round_ref.at[:, pl.ds(piece * PIECE, PIECE)],
                out_ref.at[:, pl.ds(place, PIECE)],
                sems.at[piece],
            )
            copy.start()
            copies.append(copy)
        for copy in copies:
            copy.wait()


def back_call(places, blocks, masked, before, width):
    length, total = masked.shape
    depth = rows_of(blocks)
    number = depth // PIECE
    extra = [] if before is None else [before]
    return pl.pallas_call(
        functools.partial(back_kernel, number, len(blocks), before is not None),
        grid_spec=pltpu.PrefetchScalarGridSpec(
            num_scalar_prefetch=1,
            grid=(total // WIDE,),
            in_specs=[wide_spec(block.shape[0]) for block in blocks]
            + [wide_spec(length)]
            + [anywhere()] * len(extra),
            out_specs=anywhere(),
            scratch_shapes=[
                pltpu.VMEM((length, depth), f32),
                pltpu.VMEM((length, depth), bf16),
                pltpu.SemaphoreType.DMA((number,)),
            ],
        ),
        out_shape=jax.ShapeDtypeStruct((length, width), bf16),
        input_output_aliases={} if before is None else {2 + len(blocks): 0},
        name="grad_tokens",
        **params(2 * length * depth * total, depth * total * 2 + 4 * length * total),
    )(places, *blocks, masked, *extra)


def inner_kernel(
    factor, query_ref, keys_ref, value_ref, grad_ref, high_ref, low_ref, out_ref, key_ref, val_ref
):
    for head in range(0, WIDE, HEAD):
        part = slice(head, head + HEAD)
        query, keys = query_ref[:, part], keys_ref[:, part]
        value, grad = value_ref[:, part], grad_ref[:, part]
        state = [high_ref[part, :], low_ref[part, :]]
        for rows, cols, scores in causal(query, keys):
            made = nn(
                jnp.concatenate([scores, twice(query[rows])], axis=1),
                jnp.concatenate([value[cols], *state], axis=0),
            )
            out_ref[rows, part] = (factor * made).astype(bf16)
        for rows, cols, scores in causal_turned(keys, query):
            val_ref[rows, part] = nn(scores, grad[cols])
        for rows, cols, scores in causal_turned(value, grad):
            key_ref[rows, part] = nn(scores, query[cols])


def inner_call(factor, queries, keys, values, cotangent, high, low):
    length, total = values.shape
    return pl.pallas_call(
        functools.partial(inner_kernel, factor),
        grid=(total // WIDE,),
        in_specs=[columns(length)] * 4 + [states()] * 2,
        out_specs=[columns(length)] * 3,
        out_shape=[
            jax.ShapeDtypeStruct((length, total), bf16),
            jax.ShapeDtypeStruct((length, total), f32),
            jax.ShapeDtypeStruct((length, total), f32),
        ],
        name="inner",
        **params(16 * length * total * length, 18 * length * total),
    )(queries, keys, values, cotangent, high, low)


def outer_kernel(
    factor, key_ref, val_ref, keys_ref, value_ref, spike_ref, high_ref, low_ref, gk_ref, gv_ref
):
    for head in range(0, WIDE, HEAD):
        part = slice(head, head + HEAD)
        keys, value = keys_ref[:, part], value_ref[:, part]
        state = [high_ref[part, :], low_ref[part, :]]
        key_grad = key_ref[:, part] + nt(twice(value), jnp.concatenate(state, axis=1))
        gk_ref[:, part] = (factor * key_grad * spike_ref[:, part].astype(f32)).astype(bf16)
        value_grad = val_ref[:, part] + nn(twice(keys), jnp.concatenate(state, axis=0))
        gv_ref[:, part] = (factor * value_grad).astype(bf16)


def outer_call(factor, key_part, value_part, keys, values, k_spikes, high, low):
    length, total = values.shape
    return pl.pallas_call(
        functools.partial(outer_kernel, factor),
        grid=(total // WIDE,),
        in_specs=[columns(length)] * 5 + [states()] * 2,
        out_specs=[columns(length)] * 2,
        out_shape=[jax.ShapeDtypeStruct((length, total), bf16)] * 2,
        name="outer",
        **params(8 * length * total * HEAD, 20 * length * total),
    )(key_part, value_part, keys, values, k_spikes, high, low)


def halves(state):
    high = state.astype(bf16)
    return high, (state - high.astype(f32)).astype(bf16)


def scan_any(own, sent, count, reverse):
    place = lax.axis_index(CTX)
    total = own
    state = jnp.zeros_like(own)
    bits = count.bit_length() - 1
    for bit in range(bits):
        step = 1 << bit
        last = bit == bits - 1
        pairs = []
        for source in range(count):
            high = bool(source & step)
            if not last or high == reverse:
                pairs.append((source, source ^ step))
        got = lax.ppermute(sent, CTX, pairs).astype(f32)
        if last:
            state = state + got
        else:
            mine = ((place // step) % 2) == (0 if reverse else 1)
            state = state + jnp.where(mine, got, 0.0)
            total = total + got
            sent = total.astype(bf16)
    return state


def links(first, keep=lambda source, target: True):
    pairs = []
    for chip in range(4):
        for core in range(2):
            other = chip ^ (first if core == 0 else 3 - first)
            if keep((chip, core), other):
                pairs.append((chip * 2 + core, other * 2 + core))
    return pairs


def scan_four(own, sent, reverse):
    chip, core = lax.axis_index("chip"), lax.axis_index("core")
    low_bit = 1 - chip % 2 if reverse else chip % 2
    flip = 3 if reverse else 0
    half = own.shape[0] // 2
    sibling = lax.ppermute(sent, "core", SWAP)
    both = own + sibling.astype(f32)
    both = jnp.where(core == 0, both[:half], both[half:])

    def upward(source, target):
        at = source[0] ^ flip
        crossing = source[0] ^ target
        return crossing == 1 or not at & 2

    got = lax.ppermute(both.astype(bf16), CTX, links(1, upward)).astype(f32)
    first = jnp.where((core == 1) | (low_bit == 1), got, 0.0)
    message = got + jnp.where((core == 0) | (low_bit == 0), both, 0.0)
    more = lax.ppermute(message.astype(bf16), CTX, links(2, upward)).astype(f32)
    state = first + more
    other = lax.ppermute(state, "core", SWAP)
    whole = jnp.concatenate(
        [jnp.where(core == 0, state, other), jnp.where(core == 0, other, state)], axis=0
    )
    return whole + jnp.where(core == (0 if reverse else 1), sibling.astype(f32), 0.0)


def scan_sum(own, sent, chips, reverse):
    if chips == 4:
        return halves(scan_four(own, sent, reverse))
    return halves(scan_any(own, sent, chips * 2, reverse))


def gather_any(q_weight):
    whole = lax.all_gather(q_weight, ("chip", "core", "dp"), axis=0, tiled=True)
    cut = whole.shape[0] // (2 * PIECE) * PIECE
    number = whole.shape[0] // PIECE
    return [whole[:cut], whole[cut:]], jnp.arange(number, dtype=jnp.int32)


def place_of(chip, side, layer):
    return [(chip * 2 + side) * 4 + one for one in layer]


def crossed(side):
    return (0, 1 + side, 2 - side, 3)


def per_device(tokens, key_input, values, q_weight, q_spikes, k_spikes, cotangent):
    batches, length, width = tokens.shape
    assert batches == 1
    total = q_weight.shape[1]
    chips, spread = lax.axis_size("chip"), lax.axis_size("dp")
    factor = 3.0 / math.sqrt(HEAD * length * chips * 2)
    tokens, key_input, values, q_spikes, k_spikes, cotangent = (
        array.reshape(length, array.shape[2])
        for array in (tokens, key_input, values, q_spikes, k_spikes, cotangent)
    )
    special = chips == 4 and spread == 4

    def sibling(array):
        return lax.ppermute(array, "core", SWAP)

    if special:
        chip, core, layer = (lax.axis_index(name) for name in ("chip", "core", "dp"))
        layered = lax.all_gather(q_weight, "dp", axis=0)
        first = lax.ppermute(q_weight, CTX, links(1))
        second = lax.ppermute(q_weight, CTX, links(2))
        other = sibling(q_weight)
        after = other
    else:
        arrived, places = gather_any(q_weight)
        after = q_weight
    keys, own, sent = memory_call(key_input, k_spikes, values, after)
    high, low = scan_sum(own, sent, chips, False)
    masked = masked_call(factor, cotangent, values, keys, q_spikes, high, low)

    def products(places, blocks, partial, grad_tokens):
        return (
            project_call(places, tokens, blocks, partial),
            back_call(places, blocks, masked, grad_tokens, width),
        )

    if special:
        third = lax.ppermute(first, CTX, links(2))
        around = [(layer + turn) % 4 for turn in range(1, 4)]
        rest = jnp.concatenate(
            [lax.dynamic_index_in_dim(layered, one, 0, False) for one in around], axis=0
        )
        rest_first = lax.ppermute(rest, CTX, links(1))
        rest_second = lax.ppermute(rest, CTX, links(2))
        mine = [q_weight, first, second, third]
        early = mine + [other] + [sibling(one) for one in mine[1:]] + [rest, sibling(rest)]
        sides = (core, 1 - core)
        places = [
            place
            for side in sides
            for flip in crossed(side)
            for place in place_of(chip ^ flip, side, [layer])
        ]
        places += [place for side in sides for place in place_of(chip, side, around)]
        middle_places = [
            place
            for side in sides
            for flip in crossed(side)[1:3]
            for place in place_of(chip ^ flip, side, around)
        ]
        late_places = [place for side in sides for place in place_of(chip ^ 3, side, around)]
        places, middle_places, late_places = (
            jnp.stack(some).astype(jnp.int32) for some in (places, middle_places, late_places)
        )
        partial, grad_tokens = products(places, early, None, None)
        rest_first = tie(rest_first, partial, grad_tokens)
        rest_third = lax.ppermute(rest_first, CTX, links(2))
        mine = [rest_first, rest_second]
        partial, grad_tokens = products(
            middle_places, mine + [sibling(one) for one in mine], partial, grad_tokens
        )
        rest_third = tie(rest_third, partial, grad_tokens)
        late = [rest_third, sibling(rest_third)]
    else:
        half = places.shape[0] // 2
        partial, grad_tokens = products(places[:half], arrived[:1], None, None)
        late, late_places = arrived[1:], places[half:]
    queries, own, sent = query_call(late_places, tokens, late, partial, q_spikes, cotangent)
    adjoint = scan_sum(own, sent, chips, True)
    attended, key_part, value_part = inner_call(
        factor, queries, keys, values, cotangent, high, low
    )
    grad_tokens = back_call(late_places, late, masked, grad_tokens, width)
    grad_keys, grad_values = outer_call(
        factor, key_part, value_part, keys, values, k_spikes, *adjoint
    )
    return tuple(
        array.reshape(1, length, array.shape[1])
        for array in (attended, grad_tokens, grad_keys, grad_values)
    )


def solution(mesh):
    count, spread = mesh.shape["ctx"], mesh.shape["dp"]
    fine = Mesh(mesh.devices.reshape(count // 2, 2, spread), ("chip", "core", "dp"))
    block = P("dp", CTX, None)
    rows = P(("chip", "core", "dp"), None)
    in_specs = (block, block, block, rows, block, block, block)
    return jax.shard_map(
        per_device, mesh=fine, in_specs=in_specs, out_specs=(block,) * 4, check_vma=False
    )
```

```python
import functools
import math

import jax
import jax.numpy as jnp
from jax import lax
from jax.experimental import pallas as pl
from jax.experimental.pallas import tpu as pltpu
from jax.sharding import Mesh, PartitionSpec as P

HEAD = 128
PIECE = 128
WIDE = 512
CTX = ("chip", "core")
SWAP = [(0, 1), (1, 0)]
f32, bf16 = jnp.float32, jnp.bfloat16
VMEM_LIMIT = 26 * 1024 * 1024


def nn(a, b):
    return lax.dot_general(a, b, (((1,), (0,)), ((), ())), preferred_element_type=f32)


def nt(a, b):
    return lax.dot_general(a, b, (((1,), (1,)), ((), ())), preferred_element_type=f32)


def tn(a, b):
    return lax.dot_general(a, b, (((0,), (0,)), ((), ())), preferred_element_type=f32)


def params(flops, moved):
    return dict(
        compiler_params=pltpu.CompilerParams(vmem_limit_bytes=VMEM_LIMIT),
        cost_estimate=pl.CostEstimate(flops=flops, bytes_accessed=moved, transcendentals=0),
    )


def columns(length):
    return pl.BlockSpec((length, WIDE), lambda j: (0, j))


def states():
    return pl.BlockSpec((WIDE, HEAD), lambda j: (j, 0))


def anywhere():
    return pl.BlockSpec(memory_space=pl.ANY)


def memory_kernel(key_ref, spike_ref, value_ref, after_ref, keys_ref, own_ref, sent_ref):
    del after_ref
    keys = key_ref[...] * spike_ref[...].astype(f32).astype(bf16)
    keys_ref[...] = keys
    for at in range(0, WIDE, HEAD):
        own = tn(keys[:, at : at + HEAD], value_ref[:, at : at + HEAD])
        own_ref[at : at + HEAD, :] = own
        sent_ref[at : at + HEAD, :] = own.astype(bf16)


def memory_call(key_input, k_spikes, values, after):
    length, total = values.shape
    return pl.pallas_call(
        memory_kernel,
        grid=(total // WIDE,),
        in_specs=[columns(length)] * 3 + [anywhere()],
        out_specs=[columns(length), states(), states()],
        out_shape=[
            jax.ShapeDtypeStruct((length, total), bf16),
            jax.ShapeDtypeStruct((total, HEAD), f32),
            jax.ShapeDtypeStruct((total, HEAD), bf16),
        ],
        name="own_memory",
        **params(2 * length * total * HEAD, 12 * length * total),
    )(key_input, k_spikes, values, after)


def tie_kernel(*refs):
    del refs


def tie(array, *others):
    return pl.pallas_call(
        tie_kernel,
        in_specs=[anywhere()] * (1 + len(others)),
        out_specs=anywhere(),
        out_shape=jax.ShapeDtypeStruct(array.shape, array.dtype),
        input_output_aliases={0: 0},
        name="tie",
        **params(0, 0),
    )(array, *others)


def keep_lower(square, flipped=False):
    row = lax.broadcasted_iota(jnp.int32, square.shape, 0)
    col = lax.broadcasted_iota(jnp.int32, square.shape, 1)
    return jnp.where((col >= row) if flipped else (col <= row), square, 0.0).astype(bf16)


def causal(a, b):
    length = a.shape[0]
    cut = length - HEAD
    top = keep_lower(nt(a[:cut], b[:cut]))
    whole = nt(a[cut:], b)
    bottom = jnp.concatenate([whole[:, :cut].astype(bf16), keep_lower(whole[:, cut:])], axis=1)
    return [(slice(0, cut), slice(0, cut), top), (slice(cut, length), slice(0, length), bottom)]


def causal_turned(a, b):
    length = a.shape[0]
    whole = nt(a[:HEAD], b)
    top = jnp.concatenate(
        [keep_lower(whole[:, :HEAD], True), whole[:, HEAD:].astype(bf16)], axis=1
    )
    bottom = keep_lower(nt(a[HEAD:], b[HEAD:]), True)
    return [
        (slice(0, HEAD), slice(0, length), top),
        (slice(HEAD, length), slice(HEAD, length), bottom),
    ]


def twice(array):
    return jnp.concatenate([array, array], axis=1)


def masked_kernel(factor, grad_ref, value_ref, keys_ref, spike_ref, high_ref, low_ref, out_ref):
    for head in range(0, WIDE, HEAD):
        part = slice(head, head + HEAD)
        grad, value, keys = grad_ref[:, part], value_ref[:, part], keys_ref[:, part]
        state = jnp.concatenate([high_ref[part, :], low_ref[part, :]], axis=1)
        for rows, cols, scores in causal(grad, value):
            made = nn(scores, keys[cols]) + nt(twice(grad[rows]), state)
            out_ref[rows, part] = (factor * made * spike_ref[rows, part].astype(f32)).astype(bf16)


def masked_call(factor, cotangent, values, keys, q_spikes, high, low):
    length, total = values.shape
    return pl.pallas_call(
        functools.partial(masked_kernel, factor),
        grid=(total // WIDE,),
        in_specs=[columns(length)] * 4 + [states()] * 2,
        out_specs=columns(length),
        out_shape=jax.ShapeDtypeStruct((length, total), bf16),
        name="masked_grad",
        **params(8 * length * total * length, 12 * length * total),
    )(cotangent, values, keys, q_spikes, high, low)


class Copies:
    def __init__(self, sems):
        self.sems = sems
        self.used = 0

    def start(self, source, target):
        copy = pltpu.make_async_copy(source, target, self.sems.at[self.used])
        self.used += 1
        copy.start()
        return copy


def rows_of(blocks):
    return sum(block.shape[0] for block in blocks)


def spans(blocks):
    at = 0
    for block in blocks:
        yield block, at, block.shape[0]
        at += block.shape[0]


def load_rows(copies, blocks, w_ref):
    bring = []
    for block, at, rows in spans(blocks):
        copy = copies.start(block, w_ref.at[pl.ds(at, rows), :])
        bring += [copy] * (rows // PIECE)
    return bring


def load_tokens(copies, places_ref, tokens_ref, some_ref):
    bring = []
    for piece in range(some_ref.shape[1] // PIECE):
        place = pl.multiple_of(places_ref[piece] * PIECE, PIECE)
        bring.append(
            copies.start(
                tokens_ref.at[:, pl.ds(place, PIECE)], some_ref.at[:, pl.ds(piece * PIECE, PIECE)]
            )
        )
    return bring


def wait_once(copies, done):
    for copy in copies:
        if not any(copy is one for one in done):
            copy.wait()
            done.append(copy)


def back_part(copies, places_ref, masked, w_ref, bring, done, out_ref, round_ref):
    going = []
    for at in range(0, w_ref.shape[0], 2 * PIECE):
        wait_once(bring[at // PIECE : at // PIECE + 2], done)
        both = slice(at, at + 2 * PIECE)
        round_ref[:, both] = nt(masked[...], w_ref[both, :]).astype(bf16)
        for piece in (at // PIECE, at // PIECE + 1):
            place = pl.multiple_of(places_ref[piece] * PIECE, PIECE)
            going.append(
                copies.start(
                    round_ref.at[:, pl.ds(piece * PIECE, PIECE)],
                    out_ref.at[:, pl.ds(place, PIECE)],
                )
            )
    return going


def products_kernel(size, has_before, places_ref, tokens_ref, masked_ref, *refs):
    blocks = refs[:size]
    refs = refs[size:]
    if has_before:
        before_ref, _, *refs = refs
    sum_out, back_out, w_ref, some_ref, masked, sum_ref, round_ref, sems = refs
    copies = Copies(sems)
    mask_copy = copies.start(masked_ref, masked)
    bring = load_rows(copies, blocks, w_ref)
    token_copies = load_tokens(copies, places_ref, tokens_ref, some_ref)
    if has_before:
        token_copies.append(copies.start(before_ref, sum_ref))
    mask_copy.wait()
    done = []
    going = back_part(copies, places_ref, masked, w_ref, bring, done, back_out, round_ref)
    wait_once(token_copies, done)
    for at in range(0, w_ref.shape[1], WIDE):
        part = slice(at, at + WIDE)
        made = nn(some_ref[...], w_ref[:, part])
        if has_before:
            made = made + sum_ref[:, part]
        sum_ref[:, part] = made
        here = pl.ds(at, WIDE)
        going.append(copies.start(sum_ref.at[:, here], sum_out.at[:, here]))
    for copy in going:
        copy.wait()


def smem():
    return pl.BlockSpec(memory_space=pltpu.SMEM)


def products_call(places, tokens, blocks, masked, before):
    length, width = tokens.shape
    total = masked.shape[1]
    depth = rows_of(blocks)
    number = depth // PIECE
    extra = [] if before is None else list(before)
    return pl.pallas_call(
        functools.partial(products_kernel, len(blocks), before is not None),
        in_specs=[smem()] + [anywhere()] * (2 + len(blocks) + len(extra)),
        out_specs=[anywhere()] * 2,
        out_shape=[
            jax.ShapeDtypeStruct((length, total), f32),
            jax.ShapeDtypeStruct((length, width), bf16),
        ],
        scratch_shapes=[
            pltpu.VMEM((depth, total), bf16),
            pltpu.VMEM((length, depth), bf16),
            pltpu.VMEM((length, total), bf16),
            pltpu.VMEM((length, total), f32),
            pltpu.VMEM((length, depth), bf16),
            pltpu.SemaphoreType.DMA((len(blocks) + 2 * number + total // WIDE + 2,)),
        ],
        input_output_aliases={3 + len(blocks) + at: at for at in range(len(extra))},
        name="products",
        **params(4 * length * depth * total, depth * total * 2 + 8 * length * total),
    )(places, tokens, masked, *blocks, *extra)


def back_kernel(size, places_ref, masked_ref, *refs):
    blocks = refs[:size]
    _, back_out, w_ref, masked, round_ref, sems = refs[size:]
    copies = Copies(sems)
    mask_copy = copies.start(masked_ref, masked)
    bring = load_rows(copies, blocks, w_ref)
    mask_copy.wait()
    for copy in back_part(copies, places_ref, masked, w_ref, bring, [], back_out, round_ref):
        copy.wait()


def back_call(places, blocks, masked, before):
    length, total = masked.shape
    depth = rows_of(blocks)
    number = depth // PIECE
    return pl.pallas_call(
        functools.partial(back_kernel, len(blocks)),
        in_specs=[smem()] + [anywhere()] * (2 + len(blocks)),
        out_specs=anywhere(),
        out_shape=jax.ShapeDtypeStruct(before.shape, bf16),
        scratch_shapes=[
            pltpu.VMEM((depth, total), bf16),
            pltpu.VMEM((length, total), bf16),
            pltpu.VMEM((length, depth), bf16),
            pltpu.SemaphoreType.DMA((len(blocks) + number + 1,)),
        ],
        input_output_aliases={2 + len(blocks): 0},
        name="grad_tokens",
        **params(2 * length * depth * total, depth * total * 2 + 4 * length * total),
    )(places, masked, *blocks, before)


def query_kernel(size, places_ref, tokens_ref, before_ref, spike_ref, grad_ref, *refs):
    blocks = refs[:size]
    refs = refs[size:]
    query_out, own_out, sent_out, w_ref, some_ref, sum_ref, spikes, grads, *refs = refs
    queries, own_ref, sent_ref, sems = refs
    copies = Copies(sems)
    wide = range(0, w_ref.shape[1], WIDE)
    bring = load_tokens(copies, places_ref, tokens_ref, some_ref)
    bring += load_rows(copies, blocks, w_ref)
    inputs = ((before_ref, sum_ref), (spike_ref, spikes), (grad_ref, grads))
    parts = [
        [copies.start(here.at[:, pl.ds(at, WIDE)], there.at[:, pl.ds(at, WIDE)])
         for here, there in inputs]
        for at in wide
    ]
    wait_once(bring, [])
    going = []
    for at, part_copies in zip(wide, parts):
        part = slice(at, at + WIDE)
        made = nn(some_ref[...], w_ref[:, part])
        for copy in part_copies:
            copy.wait()
        made = ((made + sum_ref[:, part]) * spikes[:, part].astype(f32)).astype(bf16)
        queries[:, part] = made
        going.append(
            copies.start(queries.at[:, pl.ds(at, WIDE)], query_out.at[:, pl.ds(at, WIDE)])
        )
        for head in range(0, WIDE, HEAD):
            own = tn(made[:, head : head + HEAD], grads[:, at + head : at + head + HEAD])
            own_ref[at + head : at + head + HEAD, :] = own
            sent_ref[at + head : at + head + HEAD, :] = own.astype(bf16)
    going.append(copies.start(sent_ref, sent_out))
    going.append(copies.start(own_ref, own_out))
    for copy in going:
        copy.wait()


def query_call(places, tokens, blocks, before, q_spikes, cotangent):
    length = tokens.shape[0]
    total = blocks[0].shape[1]
    depth = rows_of(blocks)
    number = depth // PIECE
    steps = total // WIDE
    return pl.pallas_call(
        functools.partial(query_kernel, len(blocks)),
        in_specs=[smem()] + [anywhere()] * (4 + len(blocks)),
        out_specs=[anywhere()] * 3,
        out_shape=[
            jax.ShapeDtypeStruct((length, total), bf16),
            jax.ShapeDtypeStruct((total, HEAD), f32),
            jax.ShapeDtypeStruct((total, HEAD), bf16),
        ],
        scratch_shapes=[
            pltpu.VMEM((depth, total), bf16),
            pltpu.VMEM((length, depth), bf16),
            pltpu.VMEM((length, total), f32),
            pltpu.VMEM((length, total), jnp.int32),
            pltpu.VMEM((length, total), bf16),
            pltpu.VMEM((length, total), bf16),
            pltpu.VMEM((total, HEAD), f32),
            pltpu.VMEM((total, HEAD), bf16),
            pltpu.SemaphoreType.DMA((len(blocks) + number + 4 * steps + 2,)),
        ],
        name="queries",
        **params(2 * length * depth * total, depth * total * 2 + 12 * length * total),
    )(places, tokens, before, q_spikes, cotangent, *blocks)


def attend_kernel(factor, query_ref, keys_ref, value_ref, high_ref, low_ref, out_ref):
    for head in range(0, WIDE, HEAD):
        part = slice(head, head + HEAD)
        query, keys, value = query_ref[:, part], keys_ref[:, part], value_ref[:, part]
        state = [high_ref[part, :], low_ref[part, :]]
        for rows, cols, scores in causal(query, keys):
            made = nn(
                jnp.concatenate([scores, twice(query[rows])], axis=1),
                jnp.concatenate([value[cols], *state], axis=0),
            )
            out_ref[rows, part] = (factor * made).astype(bf16)


def attend_call(factor, queries, keys, values, high, low):
    length, total = values.shape
    return pl.pallas_call(
        functools.partial(attend_kernel, factor),
        grid=(total // WIDE,),
        in_specs=[columns(length)] * 3 + [states()] * 2,
        out_specs=columns(length),
        out_shape=jax.ShapeDtypeStruct((length, total), bf16),
        name="attended",
        **params(8 * length * total * length, 8 * length * total),
    )(queries, keys, values, high, low)


def inner_kernel(query_ref, keys_ref, value_ref, grad_ref, key_ref, val_ref):
    for head in range(0, WIDE, HEAD):
        part = slice(head, head + HEAD)
        query, keys = query_ref[:, part], keys_ref[:, part]
        value, grad = value_ref[:, part], grad_ref[:, part]
        for rows, cols, scores in causal_turned(keys, query):
            val_ref[rows, part] = nn(scores, grad[cols])
        for rows, cols, scores in causal_turned(value, grad):
            key_ref[rows, part] = nn(scores, query[cols])


def inner_call(queries, keys, values, cotangent):
    length, total = values.shape
    return pl.pallas_call(
        inner_kernel,
        grid=(total // WIDE,),
        in_specs=[columns(length)] * 4,
        out_specs=[columns(length)] * 2,
        out_shape=[jax.ShapeDtypeStruct((length, total), f32)] * 2,
        name="inner",
        **params(12 * length * total * length, 16 * length * total),
    )(queries, keys, values, cotangent)


def outer_kernel(
    factor, key_ref, val_ref, keys_ref, value_ref, spike_ref, high_ref, low_ref, gk_ref, gv_ref
):
    for head in range(0, WIDE, HEAD):
        part = slice(head, head + HEAD)
        keys, value = keys_ref[:, part], value_ref[:, part]
        state = [high_ref[part, :], low_ref[part, :]]
        key_grad = key_ref[:, part] + nt(twice(value), jnp.concatenate(state, axis=1))
        gk_ref[:, part] = (factor * key_grad * spike_ref[:, part].astype(f32)).astype(bf16)
        value_grad = val_ref[:, part] + nn(twice(keys), jnp.concatenate(state, axis=0))
        gv_ref[:, part] = (factor * value_grad).astype(bf16)


def outer_call(factor, key_part, value_part, keys, values, k_spikes, high, low):
    length, total = values.shape
    return pl.pallas_call(
        functools.partial(outer_kernel, factor),
        grid=(total // WIDE,),
        in_specs=[columns(length)] * 5 + [states()] * 2,
        out_specs=[columns(length)] * 2,
        out_shape=[jax.ShapeDtypeStruct((length, total), bf16)] * 2,
        name="outer",
        **params(8 * length * total * HEAD, 20 * length * total),
    )(key_part, value_part, keys, values, k_spikes, high, low)


def halves(state):
    high = state.astype(bf16)
    return high, (state - high.astype(f32)).astype(bf16)


def scan_any(own, sent, count, reverse):
    place = lax.axis_index(CTX)
    total = own
    state = jnp.zeros_like(own)
    bits = count.bit_length() - 1
    for bit in range(bits):
        step = 1 << bit
        last = bit == bits - 1
        pairs = []
        for source in range(count):
            high = bool(source & step)
            if not last or high == reverse:
                pairs.append((source, source ^ step))
        got = lax.ppermute(sent, CTX, pairs).astype(f32)
        if last:
            state = state + got
        else:
            mine = ((place // step) % 2) == (0 if reverse else 1)
            state = state + jnp.where(mine, got, 0.0)
            total = total + got
            sent = total.astype(bf16)
    return state


def links(first, keep=lambda source, target: True):
    pairs = []
    for chip in range(4):
        for core in range(2):
            other = chip ^ (first if core == 0 else 3 - first)
            if keep((chip, core), other):
                pairs.append((chip * 2 + core, other * 2 + core))
    return pairs


def scan_four(own, sent, reverse, beside=()):
    chip, core = lax.axis_index("chip"), lax.axis_index("core")
    low_bit = 1 - chip % 2 if reverse else chip % 2
    flip = 3 if reverse else 0
    half = own.shape[0] // 2
    sibling = lax.ppermute(sent, "core", SWAP)
    both = own + sibling.astype(f32)
    both = jnp.where(core == 0, both[:half], both[half:])

    def upward(source, target):
        at = source[0] ^ flip
        crossing = source[0] ^ target
        return crossing == 1 or not at & 2

    got = lax.ppermute(both.astype(bf16), CTX, links(1, upward)).astype(f32)
    first = jnp.where((core == 1) | (low_bit == 1), got, 0.0)
    message = (got + jnp.where((core == 0) | (low_bit == 0), both, 0.0)).astype(bf16)
    if beside:
        message = tie(message, beside[0])
    more = lax.ppermute(message, CTX, links(2, upward)).astype(f32)
    state = first + more
    if beside:
        state = tie(state, beside[1])
    other = lax.ppermute(state, "core", SWAP)
    whole = jnp.concatenate(
        [jnp.where(core == 0, state, other), jnp.where(core == 0, other, state)], axis=0
    )
    return whole + jnp.where(core == (0 if reverse else 1), sibling.astype(f32), 0.0)


def scan_sum(own, sent, chips, reverse, beside=()):
    if chips == 4:
        return halves(scan_four(own, sent, reverse, beside))
    return halves(scan_any(own, sent, chips * 2, reverse))


def gather_any(q_weight):
    whole = lax.all_gather(q_weight, ("chip", "core", "dp"), axis=0, tiled=True)
    cut = whole.shape[0] // (2 * PIECE) * PIECE
    number = whole.shape[0] // PIECE
    return [whole[:cut], whole[cut:]], jnp.arange(number, dtype=jnp.int32)


def crossed(side):
    return (0, 1 + side, 2 - side, 3)


def per_device(tokens, key_input, values, q_weight, q_spikes, k_spikes, cotangent):
    batches, length, width = tokens.shape
    assert batches == 1
    total = q_weight.shape[1]
    chips, spread = lax.axis_size("chip"), lax.axis_size("dp")
    factor = 3.0 / math.sqrt(HEAD * length * chips * 2)
    tokens, key_input, values, q_spikes, k_spikes, cotangent = (
        array.reshape(length, array.shape[2])
        for array in (tokens, key_input, values, q_spikes, k_spikes, cotangent)
    )
    special = chips == 4 and spread == 4

    def sibling(array):
        return lax.ppermute(array, "core", SWAP)

    def along(array, pairs):
        return lax.ppermute(array, "dp", pairs)

    def cross(array):
        return lax.ppermute(array, CTX, links(1)), lax.ppermute(array, CTX, links(2))

    def onward(array):
        return lax.ppermute(array, CTX, links(2))

    if special:
        chip, core, layer = (lax.axis_index(name) for name in ("chip", "core", "dp"))
        within = (layer == 1) | (layer == 2)
        ends = [(0, 1), (1, 0), (2, 3), (3, 2)]
        middle = [(1, 2), (2, 1)]
        outward = [(1, 0), (2, 3)]
        near = along(q_weight, ends)
        mid = along(q_weight, middle)
        first, second = cross(q_weight)
        after = sibling(q_weight)
    else:
        arrived, places = gather_any(q_weight)
        after = q_weight
    keys, own, sent = memory_call(key_input, k_spikes, values, after)
    high, low = scan_sum(own, sent, chips, False)
    masked = masked_call(factor, cotangent, values, keys, q_spikes, high, low)

    if special:

        def numbers(sides, flips, layers):
            return jnp.stack(
                [
                    ((chip ^ crossed(side)[flip]) * 2 + side) * spread + one
                    for side in sides
                    for flip in flips
                    for one in layers
                ]
            ).astype(jnp.int32)

        sides = (core, 1 - core)
        two = jnp.where(layer < 2, 2, 1)
        three = jnp.where(layer < 2, 3, 0)
        far = along(near, middle)
        near_first, near_second = cross(near)
        mid_out = along(mid, outward)
        third = onward(first)
        far_out = along(far, outward)
        rest = jnp.concatenate(
            [jnp.where(within, mid, mid_out), jnp.where(within, far, far_out)], axis=0
        )
        near_third = onward(near_first)
        mine = [q_weight, first, second, third]
        early = mine + [after] + [sibling(one) for one in mine[1:]]
        mine = [near, near_first, near_second, near_third]
        early += mine + [sibling(one) for one in mine]
        early_places = jnp.concatenate(
            [numbers(sides, range(4), [layer]), numbers(sides, range(4), [layer ^ 1])]
        )
        rest_first, rest_second = cross(rest)
        done = products_call(early_places, tokens, early, masked, None)
        rest_first = tie(rest_first, *done)
        rest_third = onward(rest_first)
        mine = [rest, rest_first, rest_second]
        done = products_call(
            numbers(sides, range(3), [two, three]),
            tokens,
            mine + [sibling(one) for one in mine],
            masked,
            done,
        )
        rest_third = tie(rest_third, *done)
        late = [rest_third, sibling(rest_third)]
        late_places = numbers(sides, [3], [two, three])
    else:
        half = places.shape[0] // 2
        done = products_call(places[:half], tokens, arrived[:1], masked, None)
        late, late_places = arrived[1:], places[half:]
    partial, grad_tokens = done
    queries, own, sent = query_call(late_places, tokens, late, partial, q_spikes, cotangent)
    attended = attend_call(factor, queries, keys, values, high, low)
    key_part, value_part = inner_call(queries, keys, values, cotangent)
    adjoint = scan_sum(own, sent, chips, True, (attended, key_part))
    grad_tokens = back_call(late_places, late, masked, grad_tokens)
    grad_keys, grad_values = outer_call(
        factor, key_part, value_part, keys, values, k_spikes, *adjoint
    )
    return tuple(
        array.reshape(1, length, array.shape[1])
        for array in (attended, grad_tokens, grad_keys, grad_values)
    )


def solution(mesh):
    count, spread = mesh.shape["ctx"], mesh.shape["dp"]
    fine = Mesh(mesh.devices.reshape(count // 2, 2, spread), ("chip", "core", "dp"))
    block = P("dp", CTX, None)
    rows = P(("chip", "core", "dp"), None)
    in_specs = (block, block, block, rows, block, block, block)
    return jax.shard_map(
        per_device, mesh=fine, in_specs=in_specs, out_specs=(block,) * 4, check_vma=False
    )
```

```python
import functools
import math

import jax
import jax.numpy as jnp
from jax import lax
from jax.experimental import pallas as pl
from jax.experimental.pallas import tpu as pltpu
from jax.sharding import Mesh, PartitionSpec as P

HEAD = 128
PIECE = 128
WIDE = 512
PAIR = 256
CTX = ("chip", "core")
SWAP = [(0, 1), (1, 0)]
f32, bf16 = jnp.float32, jnp.bfloat16
VMEM_LIMIT = 60 * 1024 * 1024


def nn(a, b):
    return lax.dot_general(a, b, (((1,), (0,)), ((), ())), preferred_element_type=f32)


def nt(a, b):
    return lax.dot_general(a, b, (((1,), (1,)), ((), ())), preferred_element_type=f32)


def tn(a, b):
    return lax.dot_general(a, b, (((0,), (0,)), ((), ())), preferred_element_type=f32)


def params(flops, moved):
    return dict(
        compiler_params=pltpu.CompilerParams(vmem_limit_bytes=VMEM_LIMIT),
        cost_estimate=pl.CostEstimate(flops=flops, bytes_accessed=moved, transcendentals=0),
    )


def columns(length, wide=WIDE):
    return pl.BlockSpec((length, wide), lambda j: (0, j))


def states(wide=WIDE):
    return pl.BlockSpec((wide, HEAD), lambda j: (j, 0))


MARK = jax.ShapeDtypeStruct((8, HEAD), f32)


def mark_spec():
    return pl.BlockSpec((8, HEAD), lambda *at: (0, 0))


def set_mark(mark_ref):
    mark_ref[...] = jnp.zeros_like(mark_ref)


def anywhere():
    return pl.BlockSpec(memory_space=pl.ANY)


def memory_kernel(key_ref, spike_ref, value_ref, after_ref, keys_ref, mask_ref, own_ref, sent_ref):
    del after_ref
    mask = spike_ref[...].astype(f32).astype(bf16)
    keys = key_ref[...] * mask
    keys_ref[...] = keys
    mask_ref[...] = mask
    for at in range(0, PAIR, HEAD):
        own = tn(keys[:, at : at + HEAD], value_ref[:, at : at + HEAD])
        own_ref[at : at + HEAD, :] = own
        sent_ref[at : at + HEAD, :] = own.astype(bf16)


def memory_call(key_input, k_spikes, values, after):
    length, total = values.shape
    return pl.pallas_call(
        memory_kernel,
        grid=(total // PAIR,),
        in_specs=[columns(length, PAIR)] * 3 + [anywhere()],
        out_specs=[columns(length, PAIR)] * 2 + [states(PAIR)] * 2,
        out_shape=[
            jax.ShapeDtypeStruct((length, total), bf16),
            jax.ShapeDtypeStruct((length, total), bf16),
            jax.ShapeDtypeStruct((total, HEAD), f32),
            jax.ShapeDtypeStruct((total, HEAD), bf16),
        ],
        name="own_memory",
        **params(0, 0),
    )(key_input, k_spikes, values, after)


def join_kernel(*refs):
    del refs


def join(arrays, others=()):
    number = len(arrays)
    return pl.pallas_call(
        join_kernel,
        in_specs=[anywhere()] * (number + len(others)),
        out_specs=[anywhere()] * number,
        out_shape=[jax.ShapeDtypeStruct(one.shape, one.dtype) for one in arrays],
        input_output_aliases={at: at for at in range(number)},
        name="join",
        **params(0, 0),
    )(*arrays, *others)


def keep_lower(square, flipped=False):
    row = lax.broadcasted_iota(jnp.int32, square.shape, 0)
    col = lax.broadcasted_iota(jnp.int32, square.shape, 1)
    return jnp.where((col >= row) if flipped else (col <= row), square, 0.0).astype(bf16)


def causal(a, b):
    length = a.shape[0]
    cut = length - HEAD
    top = keep_lower(nt(a[:cut], b[:cut]))
    whole = nt(a[cut:], b)
    bottom = jnp.concatenate([whole[:, :cut].astype(bf16), keep_lower(whole[:, cut:])], axis=1)
    return [(slice(0, cut), slice(0, cut), top), (slice(cut, length), slice(0, length), bottom)]


def causal_turned(a, b):
    length = a.shape[0]
    whole = nt(a[:HEAD], b)
    top = jnp.concatenate(
        [keep_lower(whole[:, :HEAD], True), whole[:, HEAD:].astype(bf16)], axis=1
    )
    bottom = keep_lower(nt(a[HEAD:], b[HEAD:]), True)
    return [
        (slice(0, HEAD), slice(0, length), top),
        (slice(HEAD, length), slice(HEAD, length), bottom),
    ]


def twice(array):
    return jnp.concatenate([array, array], axis=1)


def masked_kernel(
    factor, grad_ref, value_ref, keys_ref, spike_ref, high_ref, low_ref, out_ref, mask_ref, mark_ref
):
    set_mark(mark_ref)
    mask_ref[...] = spike_ref[...].astype(f32).astype(bf16)
    for head in range(0, WIDE, HEAD):
        part = slice(head, head + HEAD)
        grad, value, keys = grad_ref[:, part], value_ref[:, part], keys_ref[:, part]
        state = jnp.concatenate([high_ref[part, :], low_ref[part, :]], axis=1)
        for rows, cols, scores in causal(grad, value):
            made = nn(scores, keys[cols]) + nt(twice(grad[rows]), state)
            out_ref[rows, part] = (factor * made * spike_ref[rows, part].astype(f32)).astype(bf16)


def masked_call(factor, cotangent, values, keys, q_spikes, high, low):
    length, total = values.shape
    return pl.pallas_call(
        functools.partial(masked_kernel, factor),
        grid=(total // WIDE,),
        in_specs=[columns(length)] * 4 + [states()] * 2,
        out_specs=[columns(length)] * 2 + [mark_spec()],
        out_shape=[jax.ShapeDtypeStruct((length, total), bf16)] * 2 + [MARK],
        name="masked_grad",
        **params(8 * length * total * length, 12 * length * total),
    )(cotangent, values, keys, q_spikes, high, low)


class Copies:
    def __init__(self, sems):
        self.sems = sems
        self.used = 0

    def start(self, source, target):
        copy = pltpu.make_async_copy(source, target, self.sems.at[self.used])
        self.used += 1
        copy.start()
        return copy


def rows_of(blocks):
    return sum(block.shape[0] for block in blocks)


def spans(blocks):
    at = 0
    for block in blocks:
        yield block, at, block.shape[0]
        at += block.shape[0]


def load_rows(copies, blocks, w_ref):
    bring = []
    for block, at, rows in spans(blocks):
        copy = copies.start(block, w_ref.at[pl.ds(at, rows), :])
        bring += [copy] * (rows // PIECE)
    return bring


def load_tokens(copies, places_ref, tokens_ref, some_ref):
    bring = []
    for piece in range(some_ref.shape[1] // PIECE):
        place = pl.multiple_of(places_ref[piece] * PIECE, PIECE)
        bring.append(
            copies.start(
                tokens_ref.at[:, pl.ds(place, PIECE)], some_ref.at[:, pl.ds(piece * PIECE, PIECE)]
            )
        )
    return bring


def wait_once(copies, done):
    for copy in copies:
        if not any(copy is one for one in done):
            copy.wait()
            done.append(copy)


def back_part(copies, places_ref, masked, w_ref, bring, done, out_ref, round_ref):
    going = []
    for at in range(0, w_ref.shape[0], 2 * PIECE):
        wait_once(bring[at // PIECE : at // PIECE + 2], done)
        both = slice(at, at + 2 * PIECE)
        round_ref[:, both] = nt(masked[...], w_ref[both, :]).astype(bf16)
        for piece in (at // PIECE, at // PIECE + 1):
            place = pl.multiple_of(places_ref[piece] * PIECE, PIECE)
            going.append(
                copies.start(
                    round_ref.at[:, pl.ds(piece * PIECE, PIECE)],
                    out_ref.at[:, pl.ds(place, PIECE)],
                )
            )
    return going


def products_kernel(size, has_before, places_ref, tokens_ref, masked_ref, *refs):
    blocks = refs[:size]
    refs = refs[size:]
    if has_before:
        before_ref, _, *refs = refs
    sum_out, back_out, mark_ref, w_ref, some_ref, masked, sum_ref, round_ref, sems = refs
    set_mark(mark_ref)
    copies = Copies(sems)
    mask_copy = copies.start(masked_ref, masked)
    bring = load_rows(copies, blocks, w_ref)
    token_copies = load_tokens(copies, places_ref, tokens_ref, some_ref)
    if has_before:
        token_copies.append(copies.start(before_ref, sum_ref))
    mask_copy.wait()
    done = []
    going = back_part(copies, places_ref, masked, w_ref, bring, done, back_out, round_ref)
    wait_once(token_copies, done)
    for at in range(0, w_ref.shape[1], WIDE):
        part = slice(at, at + WIDE)
        made = nn(some_ref[...], w_ref[:, part])
        if has_before:
            made = made + sum_ref[:, part]
        sum_ref[:, part] = made
        here = pl.ds(at, WIDE)
        going.append(copies.start(sum_ref.at[:, here], sum_out.at[:, here]))
    for copy in going:
        copy.wait()


def smem():
    return pl.BlockSpec(memory_space=pltpu.SMEM)


def products_call(places, tokens, blocks, masked, before):
    length, width = tokens.shape
    total = masked.shape[1]
    depth = rows_of(blocks)
    number = depth // PIECE
    extra = [] if before is None else list(before)
    return pl.pallas_call(
        functools.partial(products_kernel, len(blocks), before is not None),
        in_specs=[smem()] + [anywhere()] * (2 + len(blocks) + len(extra)),
        out_specs=[anywhere()] * 2 + [pl.BlockSpec(memory_space=pltpu.VMEM)],
        out_shape=[
            jax.ShapeDtypeStruct((length, total), f32),
            jax.ShapeDtypeStruct((length, width), bf16),
            MARK,
        ],
        scratch_shapes=[
            pltpu.VMEM((depth, total), bf16),
            pltpu.VMEM((length, depth), bf16),
            pltpu.VMEM((length, total), bf16),
            pltpu.VMEM((length, total), f32),
            pltpu.VMEM((length, depth), bf16),
            pltpu.SemaphoreType.DMA((len(blocks) + 2 * number + total // WIDE + 2,)),
        ],
        input_output_aliases={3 + len(blocks) + at: at for at in range(len(extra))},
        name="products",
        **params(4 * length * depth * total, depth * total * 2 + 8 * length * total),
    )(places, tokens, masked, *blocks, *extra)


def back_kernel(size, places_ref, masked_ref, *refs):
    blocks = refs[:size]
    _, back_out, w_ref, masked, round_ref, sems = refs[size:]
    copies = Copies(sems)
    mask_copy = copies.start(masked_ref, masked)
    bring = load_rows(copies, blocks, w_ref)
    mask_copy.wait()
    for copy in back_part(copies, places_ref, masked, w_ref, bring, [], back_out, round_ref):
        copy.wait()


def back_call(places, blocks, masked, before):
    length, total = masked.shape
    depth = rows_of(blocks)
    number = depth // PIECE
    return pl.pallas_call(
        functools.partial(back_kernel, len(blocks)),
        in_specs=[smem()] + [anywhere()] * (2 + len(blocks)),
        out_specs=anywhere(),
        out_shape=jax.ShapeDtypeStruct(before.shape, bf16),
        scratch_shapes=[
            pltpu.VMEM((depth, total), bf16),
            pltpu.VMEM((length, total), bf16),
            pltpu.VMEM((length, depth), bf16),
            pltpu.SemaphoreType.DMA((len(blocks) + number + 1,)),
        ],
        input_output_aliases={2 + len(blocks): 0},
        name="grad_tokens",
        **params(2 * length * depth * total, depth * total * 2 + 4 * length * total),
    )(places, masked, *blocks, before)


def query_kernel(size, places_ref, tokens_ref, before_ref, spike_ref, grad_ref, *refs):
    blocks = refs[:size]
    refs = refs[size:]
    query_out, own_out, sent_out, w_ref, some_ref, sum_ref, spikes, grads, *refs = refs
    queries, own_ref, sent_ref, sems = refs
    copies = Copies(sems)
    wide = range(0, w_ref.shape[1], WIDE)
    bring = load_tokens(copies, places_ref, tokens_ref, some_ref)
    bring += load_rows(copies, blocks, w_ref)
    inputs = ((before_ref, sum_ref), (spike_ref, spikes), (grad_ref, grads))
    parts = [
        [copies.start(here.at[:, pl.ds(at, WIDE)], there.at[:, pl.ds(at, WIDE)])
         for here, there in inputs]
        for at in wide
    ]
    wait_once(bring, [])
    going = []
    for at, part_copies in zip(wide, parts):
        part = slice(at, at + WIDE)
        made = nn(some_ref[...], w_ref[:, part])
        for copy in part_copies:
            copy.wait()
        made = ((made + sum_ref[:, part]) * spikes[:, part].astype(f32)).astype(bf16)
        queries[:, part] = made
        going.append(
            copies.start(queries.at[:, pl.ds(at, WIDE)], query_out.at[:, pl.ds(at, WIDE)])
        )
        for head in range(0, WIDE, HEAD):
            own = tn(made[:, head : head + HEAD], grads[:, at + head : at + head + HEAD])
            own_ref[at + head : at + head + HEAD, :] = own
            sent_ref[at + head : at + head + HEAD, :] = own.astype(bf16)
    going.append(copies.start(sent_ref, sent_out))
    going.append(copies.start(own_ref, own_out))
    for copy in going:
        copy.wait()


def query_call(places, tokens, blocks, before, q_spikes, cotangent):
    length = tokens.shape[0]
    total = blocks[0].shape[1]
    depth = rows_of(blocks)
    number = depth // PIECE
    steps = total // WIDE
    return pl.pallas_call(
        functools.partial(query_kernel, len(blocks)),
        in_specs=[smem()] + [anywhere()] * (4 + len(blocks)),
        out_specs=[anywhere()] * 3,
        out_shape=[
            jax.ShapeDtypeStruct((length, total), bf16),
            jax.ShapeDtypeStruct((total, HEAD), f32),
            jax.ShapeDtypeStruct((total, HEAD), bf16),
        ],
        scratch_shapes=[
            pltpu.VMEM((depth, total), bf16),
            pltpu.VMEM((length, depth), bf16),
            pltpu.VMEM((length, total), f32),
            pltpu.VMEM((length, total), bf16),
            pltpu.VMEM((length, total), bf16),
            pltpu.VMEM((length, total), bf16),
            pltpu.VMEM((total, HEAD), f32),
            pltpu.VMEM((total, HEAD), bf16),
            pltpu.SemaphoreType.DMA((len(blocks) + number + 4 * steps + 2,)),
        ],
        name="queries",
        **params(2 * length * depth * total, depth * total * 2 + 12 * length * total),
    )(places, tokens, before, q_spikes, cotangent, *blocks)


def attend_kernel(factor, query_ref, keys_ref, value_ref, high_ref, low_ref, out_ref, mark_ref):
    set_mark(mark_ref)
    for head in range(0, WIDE, HEAD):
        part = slice(head, head + HEAD)
        query, keys, value = query_ref[:, part], keys_ref[:, part], value_ref[:, part]
        state = [high_ref[part, :], low_ref[part, :]]
        for rows, cols, scores in causal(query, keys):
            made = nn(
                jnp.concatenate([scores, twice(query[rows])], axis=1),
                jnp.concatenate([value[cols], *state], axis=0),
            )
            out_ref[rows, part] = (factor * made).astype(bf16)


def attend_call(factor, queries, keys, values, high, low):
    length, total = values.shape
    return pl.pallas_call(
        functools.partial(attend_kernel, factor),
        grid=(total // WIDE,),
        in_specs=[columns(length)] * 3 + [states()] * 2,
        out_specs=[columns(length), mark_spec()],
        out_shape=[jax.ShapeDtypeStruct((length, total), bf16), MARK],
        name="attended",
        **params(8 * length * total * length, 8 * length * total),
    )(queries, keys, values, high, low)


def inner_kernel(query_ref, keys_ref, value_ref, grad_ref, key_ref, val_ref, mark_ref):
    set_mark(mark_ref)
    for head in range(0, WIDE, HEAD):
        part = slice(head, head + HEAD)
        query, keys = query_ref[:, part], keys_ref[:, part]
        value, grad = value_ref[:, part], grad_ref[:, part]
        for rows, cols, scores in causal_turned(keys, query):
            val_ref[rows, part] = nn(scores, grad[cols])
        for rows, cols, scores in causal_turned(value, grad):
            key_ref[rows, part] = nn(scores, query[cols])


def inner_call(queries, keys, values, cotangent):
    length, total = values.shape
    return pl.pallas_call(
        inner_kernel,
        grid=(total // WIDE,),
        in_specs=[columns(length)] * 4,
        out_specs=[columns(length)] * 2 + [mark_spec()],
        out_shape=[jax.ShapeDtypeStruct((length, total), f32)] * 2 + [MARK],
        name="inner",
        **params(12 * length * total * length, 16 * length * total),
    )(queries, keys, values, cotangent)


def outer_kernel(
    factor, key_ref, val_ref, keys_ref, value_ref, mask_ref, high_ref, low_ref, gk_ref, gv_ref
):
    for head in range(0, PAIR, HEAD):
        part = slice(head, head + HEAD)
        keys, value = keys_ref[:, part], value_ref[:, part]
        state = [high_ref[part, :], low_ref[part, :]]
        key_grad = key_ref[:, part] + nt(twice(value), jnp.concatenate(state, axis=1))
        gk_ref[:, part] = (factor * key_grad * mask_ref[:, part].astype(f32)).astype(bf16)
        value_grad = val_ref[:, part] + nn(twice(keys), jnp.concatenate(state, axis=0))
        gv_ref[:, part] = (factor * value_grad).astype(bf16)


def outer_call(factor, key_part, value_part, keys, values, k_mask, high, low):
    length, total = values.shape
    return pl.pallas_call(
        functools.partial(outer_kernel, factor),
        grid=(total // PAIR,),
        in_specs=[columns(length, PAIR)] * 5 + [states(PAIR)] * 2,
        out_specs=[columns(length, PAIR)] * 2,
        out_shape=[jax.ShapeDtypeStruct((length, total), bf16)] * 2,
        name="outer",
        **params(8 * length * total * HEAD, 20 * length * total),
    )(key_part, value_part, keys, values, k_mask, high, low)


def halves(state):
    high = state.astype(bf16)
    return high, (state - high.astype(f32)).astype(bf16)


def scan_any(own, sent, count, reverse):
    place = lax.axis_index(CTX)
    total = own
    state = jnp.zeros_like(own)
    bits = count.bit_length() - 1
    for bit in range(bits):
        step = 1 << bit
        last = bit == bits - 1
        pairs = []
        for source in range(count):
            high = bool(source & step)
            if not last or high == reverse:
                pairs.append((source, source ^ step))
        got = lax.ppermute(sent, CTX, pairs).astype(f32)
        if last:
            state = state + got
        else:
            mine = ((place // step) % 2) == (0 if reverse else 1)
            state = state + jnp.where(mine, got, 0.0)
            total = total + got
            sent = total.astype(bf16)
    return state


def links(first, keep=lambda source, target: True):
    pairs = []
    for chip in range(4):
        for core in range(2):
            other = chip ^ (first if core == 0 else 3 - first)
            if keep((chip, core), other):
                pairs.append((chip * 2 + core, other * 2 + core))
    return pairs


def scan_four(own, sent, reverse, beside=()):
    chip, core = lax.axis_index("chip"), lax.axis_index("core")
    low_bit = 1 - chip % 2 if reverse else chip % 2
    flip = 3 if reverse else 0
    half = own.shape[0] // 2
    sibling = lax.ppermute(sent, "core", SWAP)
    both = own + sibling.astype(f32)
    both = jnp.where(core == 0, both[:half], both[half:])

    def upward(source, target):
        at = source[0] ^ flip
        crossing = source[0] ^ target
        return crossing == 1 or not at & 2

    got = lax.ppermute(both.astype(bf16), CTX, links(1, upward)).astype(f32)
    first = jnp.where((core == 1) | (low_bit == 1), got, 0.0)
    message = (got + jnp.where((core == 0) | (low_bit == 0), both, 0.0)).astype(bf16)
    if beside:
        message, = join([message], beside[:1])
    more = lax.ppermute(message, CTX, links(2, upward)).astype(f32)
    state = first + more
    if beside:
        state, = join([state], beside[1:])
    other = lax.ppermute(state, "core", SWAP)
    whole = jnp.concatenate(
        [jnp.where(core == 0, state, other), jnp.where(core == 0, other, state)], axis=0
    )
    return whole + jnp.where(core == (0 if reverse else 1), sibling.astype(f32), 0.0)


def scan_sum(own, sent, chips, reverse, beside=()):
    if chips == 4:
        return halves(scan_four(own, sent, reverse, beside))
    return halves(scan_any(own, sent, chips * 2, reverse))


def gather_any(q_weight):
    whole = lax.all_gather(q_weight, ("chip", "core", "dp"), axis=0, tiled=True)
    cut = whole.shape[0] // (2 * PIECE) * PIECE
    number = whole.shape[0] // PIECE
    return [whole[:cut], whole[cut:]], jnp.arange(number, dtype=jnp.int32)


def crossed(side):
    return (0, 1 + side, 2 - side, 3)


def per_device(tokens, key_input, values, q_weight, q_spikes, k_spikes, cotangent):
    batches, length, width = tokens.shape
    assert batches == 1
    total = q_weight.shape[1]
    chips, spread = lax.axis_size("chip"), lax.axis_size("dp")
    factor = 3.0 / math.sqrt(HEAD * length * chips * 2)
    tokens, key_input, values, q_spikes, k_spikes, cotangent = (
        array.reshape(length, array.shape[2])
        for array in (tokens, key_input, values, q_spikes, k_spikes, cotangent)
    )
    special = chips == 4 and spread == 4

    def sibling(array):
        return lax.ppermute(array, "core", SWAP)

    def along(array, pairs):
        return lax.ppermute(array, "dp", pairs)

    def cross(array):
        return lax.ppermute(array, CTX, links(1)), lax.ppermute(array, CTX, links(2))

    def onward(array):
        return lax.ppermute(array, CTX, links(2))

    if special:
        chip, core, layer = (lax.axis_index(name) for name in ("chip", "core", "dp"))
        within = (layer == 1) | (layer == 2)
        ends = [(0, 1), (1, 0), (2, 3), (3, 2)]
        middle = [(1, 2), (2, 1)]
        outward = [(1, 0), (2, 3)]
        near = along(q_weight, ends)
        mid = along(q_weight, middle)
        first_0, second_0 = cross(q_weight)
        other_0 = sibling(q_weight)
        after = other_0
    else:
        arrived, places = gather_any(q_weight)
        after = q_weight
    keys, k_mask, own, sent = memory_call(key_input, k_spikes, values, after)
    high, low = scan_sum(own, sent, chips, False)
    masked, q_mask, masked_mark = masked_call(
        factor, cotangent, values, keys, q_spikes, high, low
    )

    if special:

        def numbers(sides, layers):
            return jnp.stack(
                [
                    ((chip ^ flip) * 2 + side) * spread + one
                    for one in layers
                    for side in sides
                    for flip in crossed(side)
                ]
            ).astype(jnp.int32)

        sides = (core, 1 - core)
        levels = [layer, layer ^ 1, jnp.where(layer < 2, 2, 1), jnp.where(layer < 2, 3, 0)]
        near, mid, first_0, second_0 = join([near, mid, first_0, second_0])
        third_0 = onward(first_0)
        first_1, second_1 = cross(near)
        far = along(near, middle)
        mid_out = along(mid, outward)
        third_0, first_1, second_1, far, mid_out = join(
            [third_0, first_1, second_1, far, mid_out]
        )
        third_1 = onward(first_1)
        next_layer = jnp.where(within, mid, mid_out)
        first_2, second_2 = cross(next_layer)
        far_out = along(far, outward)
        third_1, first_2, second_2, far_out = join(
            [third_1, first_2, second_2, far_out], [masked_mark]
        )
        third_2 = onward(first_2)
        last_layer = jnp.where(within, far, far_out)
        first_3, second_3 = cross(last_layer)

        def whole(*mine):
            return list(mine) + [sibling(one) for one in mine]

        early = [q_weight, first_0, second_0, third_0, other_0]
        early += [sibling(one) for one in early[1:4]]
        early += whole(near, first_1, second_1, third_1)
        *done, mark = products_call(numbers(sides, levels[:2]), tokens, early, masked, None)
        third_2, first_3, second_3 = join([third_2, first_3, second_3], [mark])
        third_3 = onward(first_3)
        middle_blocks = whole(next_layer, first_2, second_2, third_2)
        *done, mark = products_call(numbers(sides, levels[2:3]), tokens, middle_blocks, masked, done)
        third_3, = join([third_3], [mark])
        late = whole(last_layer, first_3, second_3, third_3)
        late_places = numbers(sides, levels[3:])
    else:
        half = places.shape[0] // 2
        *done, _ = products_call(places[:half], tokens, arrived[:1], masked, None)
        late, late_places = arrived[1:], places[half:]
    partial, grad_tokens = done
    queries, own, sent = query_call(late_places, tokens, late, partial, q_mask, cotangent)
    attended, attended_mark = attend_call(factor, queries, keys, values, high, low)
    key_part, value_part, inner_mark = inner_call(queries, keys, values, cotangent)
    adjoint = scan_sum(own, sent, chips, True, (attended_mark, inner_mark))
    grad_tokens = back_call(late_places, late, masked, grad_tokens)
    grad_keys, grad_values = outer_call(
        factor, key_part, value_part, keys, values, k_mask, *adjoint
    )
    return tuple(
        array.reshape(1, length, array.shape[1])
        for array in (attended, grad_tokens, grad_keys, grad_values)
    )


def solution(mesh):
    count, spread = mesh.shape["ctx"], mesh.shape["dp"]
    fine = Mesh(mesh.devices.reshape(count // 2, 2, spread), ("chip", "core", "dp"))
    block = P("dp", CTX, None)
    rows = P(("chip", "core", "dp"), None)
    in_specs = (block, block, block, rows, block, block, block)
    return jax.shard_map(
        per_device, mesh=fine, in_specs=in_specs, out_specs=(block,) * 4, check_vma=False
    )
```

```python
import functools
import math

import jax
import jax.numpy as jnp
from jax import lax
from jax.experimental import pallas as pl
from jax.experimental.pallas import tpu as pltpu
from jax.sharding import Mesh, PartitionSpec as P

HEAD = 128
PIECE = 128
WIDE = 512
CTX = ("chip", "core")
SWAP = [(0, 1), (1, 0)]
f32, bf16 = jnp.float32, jnp.bfloat16
VMEM_LIMIT = 26 * 1024 * 1024


def nn(a, b):
    return lax.dot_general(a, b, (((1,), (0,)), ((), ())), preferred_element_type=f32)


def nt(a, b):
    return lax.dot_general(a, b, (((1,), (1,)), ((), ())), preferred_element_type=f32)


def tn(a, b):
    return lax.dot_general(a, b, (((0,), (0,)), ((), ())), preferred_element_type=f32)


def params(flops, moved):
    return dict(
        compiler_params=pltpu.CompilerParams(vmem_limit_bytes=VMEM_LIMIT),
        cost_estimate=pl.CostEstimate(flops=flops, bytes_accessed=moved, transcendentals=0),
    )


MARK = jax.ShapeDtypeStruct((8, HEAD), f32)


def set_mark(mark_ref):
    mark_ref[...] = jnp.zeros_like(mark_ref)


def fast(array):
    return pltpu.with_memory_space_constraint(array, pltpu.VMEM)


def slow(array):
    return pltpu.with_memory_space_constraint(array, pltpu.HBM)


def specs(places):
    spaces = dict(V=pltpu.VMEM, H=pltpu.HBM, S=pltpu.SMEM, A=pl.ANY)
    return [pl.BlockSpec(memory_space=spaces[place]) for place in places]


def kernel_call(body, places, args, out_places, outs, name, cost, scratch=(), aliases=None):
    holds = dict(V=fast, H=slow)
    made = pl.pallas_call(
        body,
        in_specs=specs(places),
        out_specs=specs(out_places),
        out_shape=[
            pltpu.VMEM(shape, dtype) if place == "V" else jax.ShapeDtypeStruct(shape, dtype)
            for place, (shape, dtype) in zip(out_places, outs)
        ],
        scratch_shapes=list(scratch),
        input_output_aliases=aliases or {},
        name=name,
        **params(*cost),
    )
    return made(
        *[holds[place](one) if place in holds else one for place, one in zip(places, args)]
    )


class Copies:
    def __init__(self, sems):
        self.sems = sems
        self.used = 0

    def start(self, source, target):
        copy = pltpu.make_async_copy(source, target, self.sems.at[self.used])
        self.used += 1
        copy.start()
        return copy


def columns(at, wide=None):
    return (slice(None), pl.ds(at, wide or WIDE))


def groups(total, body):
    @pl.loop(0, total // WIDE)
    def _(group):
        body(group, pl.multiple_of(group * WIDE, WIDE))


def heads(at):
    return [pl.ds(pl.multiple_of(at + head, HEAD), HEAD) for head in range(0, WIDE, HEAD)]


def memory_kernel(
    key_ref, spike_ref, value_ref, keys_ref, mask_ref, values_ref, own_ref, sent_ref, mark_ref,
    key_in, spike_in, sems,
):
    set_mark(mark_ref)
    copies = Copies(sems)
    wide = range(0, keys_ref.shape[1], WIDE)
    pairs = ((key_ref, key_in), (spike_ref, spike_in), (value_ref, values_ref))
    parts = [
        [copies.start(here.at[columns(at)], there.at[columns(at)]) for here, there in pairs]
        for at in wide
    ]
    for at, part in zip(wide, parts):
        for copy in part:
            copy.wait()
        cols = slice(at, at + WIDE)
        mask = spike_in[:, cols].astype(f32).astype(bf16)
        keys = key_in[:, cols] * mask
        keys_ref[:, cols] = keys
        mask_ref[:, cols] = mask
        for head in range(0, WIDE, HEAD):
            here = slice(at + head, at + head + HEAD)
            own = tn(keys[:, head : head + HEAD], values_ref[:, here])
            own_ref[here, :] = own
            sent_ref[here, :] = own.astype(bf16)


def memory_call(key_input, k_spikes, values):
    length, total = values.shape
    block, state = (length, total), (total, HEAD)
    return kernel_call(
        memory_kernel,
        "HHH",
        (key_input, k_spikes, values),
        "VVVVVV",
        [(block, bf16)] * 3 + [(state, f32), (state, bf16), (MARK.shape, f32)],
        "own_memory",
        (2 * length * total * HEAD, 12 * length * total),
        [
            pltpu.VMEM(block, bf16),
            pltpu.VMEM(block, jnp.int32),
            pltpu.SemaphoreType.DMA((3 * total // WIDE,)),
        ],
    )


def join_kernel(*refs):
    del refs


def join(arrays, others=()):
    number = len(arrays)
    return kernel_call(
        join_kernel,
        ["H"] * number + ["A"] * len(others),
        (*arrays, *others),
        ["H"] * number,
        [(one.shape, one.dtype) for one in arrays],
        "join",
        (0, 0),
        aliases={at: at for at in range(number)},
    )


def keep_lower(square, flipped=False):
    row = lax.broadcasted_iota(jnp.int32, square.shape, 0)
    col = lax.broadcasted_iota(jnp.int32, square.shape, 1)
    return jnp.where((col >= row) if flipped else (col <= row), square, 0.0).astype(bf16)


def causal(a, b):
    length = a.shape[0]
    cut = length - HEAD
    top = keep_lower(nt(a[:cut], b[:cut]))
    whole = nt(a[cut:], b)
    bottom = jnp.concatenate([whole[:, :cut].astype(bf16), keep_lower(whole[:, cut:])], axis=1)
    return [(slice(0, cut), slice(0, cut), top), (slice(cut, length), slice(0, length), bottom)]


def causal_turned(a, b):
    length = a.shape[0]
    whole = nt(a[:HEAD], b)
    top = jnp.concatenate(
        [keep_lower(whole[:, :HEAD], True), whole[:, HEAD:].astype(bf16)], axis=1
    )
    bottom = keep_lower(nt(a[HEAD:], b[HEAD:]), True)
    return [
        (slice(0, HEAD), slice(0, length), top),
        (slice(HEAD, length), slice(HEAD, length), bottom),
    ]


def twice(array):
    return jnp.concatenate([array, array], axis=1)


def masked_kernel(
    factor, grad_ref, spike_ref, value_ref, keys_ref, high_ref, low_ref,
    out_ref, mask_ref, grads_ref, mark_ref, spike_in, sems,
):
    set_mark(mark_ref)
    total = out_ref.shape[1]

    def copies(group, at):
        return [
            pltpu.make_async_copy(grad_ref.at[columns(at)], grads_ref.at[columns(at)], sems.at[0, group]),
            pltpu.make_async_copy(spike_ref.at[columns(at)], spike_in.at[columns(at)], sems.at[1, group]),
        ]

    for group in range(total // WIDE):
        for copy in copies(group, group * WIDE):
            copy.start()

    def work(group, at):
        for copy in copies(group, at):
            copy.wait()
        for part in heads(at):
            mask = spike_in[:, part].astype(f32)
            mask_ref[:, part] = mask.astype(bf16)
            grad, value, keys = grads_ref[:, part], value_ref[:, part], keys_ref[:, part]
            state = jnp.concatenate([high_ref[part, :], low_ref[part, :]], axis=1)
            for rows, cols, scores in causal(grad, value):
                made = nn(scores, keys[cols]) + nt(twice(grad[rows]), state)
                out_ref[rows, part] = (factor * made * mask[rows]).astype(bf16)

    groups(total, work)


def masked_call(factor, cotangent, q_spikes, values, keys, high, low):
    length, total = values.shape
    block = (length, total)
    return kernel_call(
        functools.partial(masked_kernel, factor),
        "HHVVVV",
        (cotangent, q_spikes, values, keys, high, low),
        "VVVV",
        [(block, bf16)] * 3 + [(MARK.shape, f32)],
        "masked_grad",
        (8 * length * total * length, 12 * length * total),
        [pltpu.VMEM(block, jnp.int32), pltpu.SemaphoreType.DMA((2, total // WIDE))],
    )


def rows_of(blocks):
    return sum(block.shape[0] for block in blocks)


def spans(blocks):
    at = 0
    for block in blocks:
        yield block, at, block.shape[0]
        at += block.shape[0]


def load_rows(copies, blocks, w_ref):
    bring = []
    for block, at, rows in spans(blocks):
        copy = copies.start(block, w_ref.at[pl.ds(at, rows), :])
        bring += [copy] * (rows // PIECE)
    return bring


def load_tokens(copies, places_ref, tokens_ref, some_ref):
    bring = []
    for piece in range(some_ref.shape[1] // PIECE):
        place = pl.multiple_of(places_ref[piece] * PIECE, PIECE)
        bring.append(
            copies.start(
                tokens_ref.at[:, pl.ds(place, PIECE)], some_ref.at[:, pl.ds(piece * PIECE, PIECE)]
            )
        )
    return bring


def wait_once(copies, done):
    for copy in copies:
        if not any(copy is one for one in done):
            copy.wait()
            done.append(copy)


def back_part(copies, places_ref, masked, w_ref, bring, done, out_ref, round_ref):
    going = []
    for at in range(0, w_ref.shape[0], 2 * PIECE):
        wait_once(bring[at // PIECE : at // PIECE + 2], done)
        both = slice(at, at + 2 * PIECE)
        round_ref[:, both] = nt(masked[...], w_ref[both, :]).astype(bf16)
        for piece in (at // PIECE, at // PIECE + 1):
            place = pl.multiple_of(places_ref[piece] * PIECE, PIECE)
            going.append(
                copies.start(
                    round_ref.at[:, pl.ds(piece * PIECE, PIECE)],
                    out_ref.at[:, pl.ds(place, PIECE)],
                )
            )
    return going


def products_kernel(size, has_before, places_ref, tokens_ref, masked, *refs):
    blocks = refs[:size]
    refs = refs[size:]
    if has_before:
        before_ref, _, *refs = refs
    sum_ref, back_out, mark_ref, w_ref, some_ref, round_ref, sems = refs
    set_mark(mark_ref)
    copies = Copies(sems)
    bring = load_rows(copies, blocks, w_ref)
    token_copies = load_tokens(copies, places_ref, tokens_ref, some_ref)
    done = []
    going = back_part(copies, places_ref, masked, w_ref, bring, done, back_out, round_ref)
    wait_once(token_copies, done)
    for at in range(0, w_ref.shape[1], WIDE):
        part = slice(at, at + WIDE)
        made = nn(some_ref[...], w_ref[:, part])
        if has_before:
            made = made + before_ref[:, part]
        sum_ref[:, part] = made
    for copy in going:
        copy.wait()


def products_call(places, tokens, blocks, masked, before):
    length, width = tokens.shape
    total = masked.shape[1]
    depth = rows_of(blocks)
    number = depth // PIECE
    extra = [] if before is None else list(before)
    return kernel_call(
        functools.partial(products_kernel, len(blocks), before is not None),
        "SHV" + "H" * len(blocks) + "VH"[: len(extra)],
        (places, tokens, masked, *blocks, *extra),
        "VHV",
        [((length, total), f32), ((length, width), bf16), (MARK.shape, f32)],
        "products",
        (4 * length * depth * total, depth * total * 2 + 8 * length * total),
        [
            pltpu.VMEM((depth, total), bf16),
            pltpu.VMEM((length, depth), bf16),
            pltpu.VMEM((length, depth), bf16),
            pltpu.SemaphoreType.DMA((len(blocks) + 2 * number,)),
        ],
        {3 + len(blocks) + at: at for at in range(len(extra))},
    )


def back_kernel(size, places_ref, masked, *refs):
    blocks = refs[:size]
    _, back_out, w_ref, round_ref, sems = refs[size:]
    copies = Copies(sems)
    bring = load_rows(copies, blocks, w_ref)
    for copy in back_part(copies, places_ref, masked, w_ref, bring, [], back_out, round_ref):
        copy.wait()


def back_call(places, blocks, masked, before):
    length, total = masked.shape
    depth = rows_of(blocks)
    number = depth // PIECE
    return kernel_call(
        functools.partial(back_kernel, len(blocks)),
        "SV" + "H" * len(blocks) + "H",
        (places, masked, *blocks, before),
        "H",
        [(before.shape, bf16)],
        "grad_tokens",
        (2 * length * depth * total, depth * total * 2 + 4 * length * total),
        [
            pltpu.VMEM((depth, total), bf16),
            pltpu.VMEM((length, depth), bf16),
            pltpu.SemaphoreType.DMA((len(blocks) + number,)),
        ],
        {2 + len(blocks): 0},
    )[0]


def query_kernel(size, places_ref, tokens_ref, sum_ref, mask_ref, grad_ref, *refs):
    blocks = refs[:size]
    queries, own_ref, sent_ref, w_ref, some_ref, sems = refs[size:]
    copies = Copies(sems)
    bring = load_tokens(copies, places_ref, tokens_ref, some_ref)
    bring += load_rows(copies, blocks, w_ref)
    wait_once(bring, [])
    for at in range(0, w_ref.shape[1], WIDE):
        part = slice(at, at + WIDE)
        made = nn(some_ref[...], w_ref[:, part]) + sum_ref[:, part]
        made = (made * mask_ref[:, part].astype(f32)).astype(bf16)
        queries[:, part] = made
        for head in range(0, WIDE, HEAD):
            here = slice(at + head, at + head + HEAD)
            own = tn(made[:, head : head + HEAD], grad_ref[:, here])
            own_ref[here, :] = own
            sent_ref[here, :] = own.astype(bf16)


def query_call(places, tokens, blocks, before, q_mask, cotangent):
    length = tokens.shape[0]
    total = blocks[0].shape[1]
    depth = rows_of(blocks)
    number = depth // PIECE
    return kernel_call(
        functools.partial(query_kernel, len(blocks)),
        "SHVVV" + "H" * len(blocks),
        (places, tokens, before, q_mask, cotangent, *blocks),
        "VVV",
        [((length, total), bf16), ((total, HEAD), f32), ((total, HEAD), bf16)],
        "queries",
        (2 * length * depth * total, depth * total * 2 + 12 * length * total),
        [
            pltpu.VMEM((depth, total), bf16),
            pltpu.VMEM((length, depth), bf16),
            pltpu.SemaphoreType.DMA((len(blocks) + number,)),
        ],
    )


def out_copy(here, there, sems, group, at):
    return pltpu.make_async_copy(here.at[columns(at)], there.at[columns(at)], sems.at[group])


def attend_kernel(
    factor, query_ref, keys_ref, value_ref, high_ref, low_ref, out_ref, mark_ref, made_ref, sems
):
    set_mark(mark_ref)
    total = query_ref.shape[1]

    def work(group, at):
        for part in heads(at):
            query, keys, value = query_ref[:, part], keys_ref[:, part], value_ref[:, part]
            state = [high_ref[part, :], low_ref[part, :]]
            for rows, cols, scores in causal(query, keys):
                made = nn(
                    jnp.concatenate([scores, twice(query[rows])], axis=1),
                    jnp.concatenate([value[cols], *state], axis=0),
                )
                made_ref[rows, part] = (factor * made).astype(bf16)
        out_copy(made_ref, out_ref, sems, group, at).start()

    groups(total, work)
    for group in range(total // WIDE):
        out_copy(made_ref, out_ref, sems, group, group * WIDE).wait()


def attend_call(factor, queries, keys, values, high, low):
    length, total = values.shape
    return kernel_call(
        functools.partial(attend_kernel, factor),
        "VVVVV",
        (queries, keys, values, high, low),
        "HV",
        [((length, total), bf16), (MARK.shape, f32)],
        "attended",
        (8 * length * total * length, 8 * length * total),
        [pltpu.VMEM((length, total), bf16), pltpu.SemaphoreType.DMA((total // WIDE,))],
    )


def inner_kernel(query_ref, keys_ref, value_ref, grad_ref, key_ref, val_ref, mark_ref):
    set_mark(mark_ref)

    def work(group, at):
        for part in heads(at):
            query, keys = query_ref[:, part], keys_ref[:, part]
            value, grad = value_ref[:, part], grad_ref[:, part]
            for rows, cols, scores in causal_turned(keys, query):
                val_ref[rows, part] = nn(scores, grad[cols])
            for rows, cols, scores in causal_turned(value, grad):
                key_ref[rows, part] = nn(scores, query[cols])

    groups(query_ref.shape[1], work)


def inner_call(queries, keys, values, cotangent):
    length, total = values.shape
    block = (length, total)
    return kernel_call(
        inner_kernel,
        "VVVV",
        (queries, keys, values, cotangent),
        "VVV",
        [(block, f32), (block, f32), (MARK.shape, f32)],
        "inner",
        (12 * length * total * length, 16 * length * total),
    )


def outer_kernel(
    factor, key_ref, val_ref, keys_ref, value_ref, mask_ref, high_ref, low_ref,
    key_out, val_out, key_made, val_made, key_sems, val_sems,
):
    total = keys_ref.shape[1]

    def work(group, at):
        for part in heads(at):
            keys, value = keys_ref[:, part], value_ref[:, part]
            state = [high_ref[part, :], low_ref[part, :]]
            key_grad = key_ref[:, part] + nt(twice(value), jnp.concatenate(state, axis=1))
            key_made[:, part] = (factor * key_grad * mask_ref[:, part].astype(f32)).astype(bf16)
            value_grad = val_ref[:, part] + nn(twice(keys), jnp.concatenate(state, axis=0))
            val_made[:, part] = (factor * value_grad).astype(bf16)
        out_copy(key_made, key_out, key_sems, group, at).start()
        out_copy(val_made, val_out, val_sems, group, at).start()

    groups(total, work)
    for group in range(total // WIDE):
        out_copy(key_made, key_out, key_sems, group, group * WIDE).wait()
        out_copy(val_made, val_out, val_sems, group, group * WIDE).wait()


def outer_call(factor, key_part, value_part, keys, values, k_mask, high, low):
    length, total = values.shape
    block = (length, total)
    return kernel_call(
        functools.partial(outer_kernel, factor),
        "VVVVVVV",
        (key_part, value_part, keys, values, k_mask, high, low),
        "HH",
        [(block, bf16)] * 2,
        "outer",
        (8 * length * total * HEAD, 20 * length * total),
        [pltpu.VMEM(block, bf16)] * 2 + [pltpu.SemaphoreType.DMA((total // WIDE,))] * 2,
    )


def halves(state):
    high = state.astype(bf16)
    return high, (state - high.astype(f32)).astype(bf16)


def scan_any(own, sent, count, reverse):
    place = lax.axis_index(CTX)
    total = own
    state = jnp.zeros_like(own)
    bits = count.bit_length() - 1
    for bit in range(bits):
        step = 1 << bit
        last = bit == bits - 1
        pairs = []
        for source in range(count):
            high = bool(source & step)
            if not last or high == reverse:
                pairs.append((source, source ^ step))
        got = lax.ppermute(sent, CTX, pairs).astype(f32)
        if last:
            state = state + got
        else:
            mine = ((place // step) % 2) == (0 if reverse else 1)
            state = state + jnp.where(mine, got, 0.0)
            total = total + got
            sent = total.astype(bf16)
    return state


def links(first, keep=lambda source, target: True):
    pairs = []
    for chip in range(4):
        for core in range(2):
            other = chip ^ (first if core == 0 else 3 - first)
            if keep((chip, core), other):
                pairs.append((chip * 2 + core, other * 2 + core))
    return pairs


def scan_first(own, sent, reverse):
    chip, core = lax.axis_index("chip"), lax.axis_index("core")
    low_bit = 1 - chip % 2 if reverse else chip % 2
    half = own.shape[0] // 2
    sibling = lax.ppermute(sent, "core", SWAP)
    both = own + sibling.astype(f32)
    both = jnp.where(core == 0, both[:half], both[half:])
    got = lax.ppermute(both.astype(bf16), CTX, links(1, upward(reverse))).astype(f32)
    first = jnp.where((core == 1) | (low_bit == 1), got, 0.0)
    message = (got + jnp.where((core == 0) | (low_bit == 0), both, 0.0)).astype(bf16)
    return message, first, sibling


def upward(reverse):
    flip = 3 if reverse else 0

    def keep(source, target):
        at = source[0] ^ flip
        return source[0] ^ target == 1 or not at & 2

    return keep


def scan_second(message, first, sibling, reverse, others=()):
    core = lax.axis_index("core")
    more = lax.ppermute(message, CTX, links(2, upward(reverse))).astype(f32)
    state = first + more
    if others:
        state, = join([state], others)
    other = lax.ppermute(state, "core", SWAP)
    whole = jnp.concatenate(
        [jnp.where(core == 0, state, other), jnp.where(core == 0, other, state)], axis=0
    )
    return halves(whole + jnp.where(core == (0 if reverse else 1), sibling.astype(f32), 0.0))


def gather_any(q_weight):
    whole = lax.all_gather(q_weight, ("chip", "core", "dp"), axis=0, tiled=True)
    cut = whole.shape[0] // (2 * PIECE) * PIECE
    number = whole.shape[0] // PIECE
    return [whole[:cut], whole[cut:]], jnp.arange(number, dtype=jnp.int32)


def crossed(side):
    return (0, 1 + side, 2 - side, 3)


def per_device(tokens, key_input, values, q_weight, q_spikes, k_spikes, cotangent):
    batches, length, width = tokens.shape
    assert batches == 1
    total = q_weight.shape[1]
    chips, spread = lax.axis_size("chip"), lax.axis_size("dp")
    factor = 3.0 / math.sqrt(HEAD * length * chips * 2)
    tokens, key_input, values, q_spikes, k_spikes, cotangent = (
        array.reshape(length, array.shape[2])
        for array in (tokens, key_input, values, q_spikes, k_spikes, cotangent)
    )
    special = chips == 4 and spread == 4

    def sibling(array):
        return lax.ppermute(array, "core", SWAP)

    def along(array, pairs):
        return lax.ppermute(array, "dp", pairs)

    def cross(array):
        return lax.ppermute(array, CTX, links(1)), lax.ppermute(array, CTX, links(2))

    def onward(array):
        return lax.ppermute(array, CTX, links(2))

    keys, k_mask, values, own, sent, own_mark = memory_call(key_input, k_spikes, values)
    if special:
        chip, core, layer = (lax.axis_index(name) for name in ("chip", "core", "dp"))
        within = (layer == 1) | (layer == 2)
        ends = [(0, 1), (1, 0), (2, 3), (3, 2)]
        middle = [(1, 2), (2, 1)]
        outward = [(1, 0), (2, 3)]
        near = along(q_weight, ends)
        mid = along(q_weight, middle)
        first_0, second_0 = cross(q_weight)
        other_0 = sibling(q_weight)
        near, mid, first_0, second_0, sent = join([near, mid, first_0, second_0, sent])
        message, *rest = scan_first(own, sent, False)
    else:
        arrived, places = gather_any(q_weight)
        high, low = halves(scan_any(own, sent, chips * 2, False))

    if special:

        def numbers(sides, layers):
            return jnp.stack(
                [
                    ((chip ^ flip) * 2 + side) * spread + one
                    for one in layers
                    for side in sides
                    for flip in crossed(side)
                ]
            ).astype(jnp.int32)

        sides = (core, 1 - core)
        levels = [layer, layer ^ 1, jnp.where(layer < 2, 2, 1), jnp.where(layer < 2, 3, 0)]
        third_0 = onward(first_0)
        first_1, second_1 = cross(near)
        far = along(near, middle)
        mid_out = along(mid, outward)
        third_0, first_1, second_1, far, mid_out, message = join(
            [third_0, first_1, second_1, far, mid_out, message]
        )
        third_1 = onward(first_1)
        next_layer = jnp.where(within, mid, mid_out)
        first_2, second_2 = cross(next_layer)
        far_out = along(far, outward)
        high, low = scan_second(message, *rest, False)
        masked, q_mask, cotangent, mark = masked_call(
            factor, cotangent, q_spikes, values, keys, high, low
        )
        third_1, first_2, second_2, far_out = join(
            [third_1, first_2, second_2, far_out], [mark]
        )
        third_2 = onward(first_2)
        last_layer = jnp.where(within, far, far_out)
        first_3, second_3 = cross(last_layer)

        def whole(*mine):
            return list(mine) + [sibling(one) for one in mine]

        blocks = [q_weight, first_0, second_0, third_0, other_0]
        blocks += [sibling(one) for one in blocks[1:4]]
        *done, _ = products_call(numbers(sides, levels[:1]), tokens, blocks, masked, None)
        blocks = whole(near, first_1, second_1, third_1)
        *done, mark = products_call(numbers(sides, levels[1:2]), tokens, blocks, masked, done)
        third_2, first_3, second_3 = join([third_2, first_3, second_3], [mark])
        third_3 = onward(first_3)
        blocks = whole(next_layer, first_2, second_2, third_2)
        *done, mark = products_call(numbers(sides, levels[2:3]), tokens, blocks, masked, done)
        third_3, = join([third_3], [mark])
        late = whole(last_layer, first_3, second_3, third_3)
        late_places = numbers(sides, levels[3:])
    else:
        masked, q_mask, cotangent, _ = masked_call(
            factor, cotangent, q_spikes, values, keys, high, low
        )
        half = places.shape[0] // 2
        *done, _ = products_call(places[:half], tokens, arrived[:1], masked, None)
        late, late_places = arrived[1:], places[half:]
    partial, grad_tokens = done
    queries, own, sent = query_call(late_places, tokens, late, partial, q_mask, cotangent)
    attended, attended_mark = attend_call(factor, queries, keys, values, high, low)
    key_part, value_part, inner_mark = inner_call(queries, keys, values, cotangent)
    if special:
        message, *rest = scan_first(own, sent, True)
        message, = join([message], [attended_mark])
        adjoint = scan_second(message, *rest, True, [inner_mark])
    else:
        adjoint = halves(scan_any(own, sent, chips * 2, True))
    grad_tokens = back_call(late_places, late, masked, grad_tokens)
    grad_keys, grad_values = outer_call(
        factor, key_part, value_part, keys, values, k_mask, *adjoint
    )
    return tuple(
        array.reshape(1, length, array.shape[1])
        for array in (attended, grad_tokens, grad_keys, grad_values)
    )


def solution(mesh):
    count, spread = mesh.shape["ctx"], mesh.shape["dp"]
    fine = Mesh(mesh.devices.reshape(count // 2, 2, spread), ("chip", "core", "dp"))
    block = P("dp", CTX, None)
    rows = P(("chip", "core", "dp"), None)
    in_specs = (block, block, block, rows, block, block, block)
    return jax.shard_map(
        per_device, mesh=fine, in_specs=in_specs, out_specs=(block,) * 4, check_vma=False
    )
```

```python
import functools
import math

import jax
import jax.numpy as jnp
from jax import lax
from jax.experimental import pallas as pl
from jax.experimental.pallas import tpu as pltpu
from jax.sharding import Mesh, PartitionSpec as P

HEAD = 128
PIECE = 128
WIDE = 512
CTX = ("chip", "core")
SWAP = [(0, 1), (1, 0)]
f32, bf16 = jnp.float32, jnp.bfloat16
VMEM_LIMIT = 26 * 1024 * 1024


def nn(a, b):
    return lax.dot_general(a, b, (((1,), (0,)), ((), ())), preferred_element_type=f32)


def nt(a, b):
    return lax.dot_general(a, b, (((1,), (1,)), ((), ())), preferred_element_type=f32)


def tn(a, b):
    return lax.dot_general(a, b, (((0,), (0,)), ((), ())), preferred_element_type=f32)


def params(flops, moved):
    return dict(
        compiler_params=pltpu.CompilerParams(vmem_limit_bytes=VMEM_LIMIT),
        cost_estimate=pl.CostEstimate(flops=flops, bytes_accessed=moved, transcendentals=0),
    )


MARK = jax.ShapeDtypeStruct((8, HEAD), f32)


def set_mark(mark_ref):
    mark_ref[...] = jnp.zeros_like(mark_ref)


def fast(array):
    return pltpu.with_memory_space_constraint(array, pltpu.VMEM)


def slow(array):
    return pltpu.with_memory_space_constraint(array, pltpu.HBM)


def specs(places):
    spaces = dict(V=pltpu.VMEM, H=pltpu.HBM, S=pltpu.SMEM, A=pl.ANY)
    return [pl.BlockSpec(memory_space=spaces[place]) for place in places]


def kernel_call(body, places, args, out_places, outs, name, cost, scratch=(), aliases=None):
    holds = dict(V=fast, H=slow)
    made = pl.pallas_call(
        body,
        in_specs=specs(places),
        out_specs=specs(out_places),
        out_shape=[
            pltpu.VMEM(shape, dtype) if place == "V" else jax.ShapeDtypeStruct(shape, dtype)
            for place, (shape, dtype) in zip(out_places, outs)
        ],
        scratch_shapes=list(scratch),
        input_output_aliases=aliases or {},
        name=name,
        **params(*cost),
    )
    return made(
        *[holds[place](one) if place in holds else one for place, one in zip(places, args)]
    )


class Copies:
    def __init__(self, sems):
        self.sems = sems
        self.used = 0

    def start(self, source, target):
        copy = pltpu.make_async_copy(source, target, self.sems.at[self.used])
        self.used += 1
        copy.start()
        return copy


def columns(at, wide=None):
    return (slice(None), pl.ds(at, wide or WIDE))


def groups(total, body):
    @pl.loop(0, total // WIDE)
    def _(group):
        body(group, pl.multiple_of(group * WIDE, WIDE))


def heads(at):
    return [pl.ds(pl.multiple_of(at + head, HEAD), HEAD) for head in range(0, WIDE, HEAD)]


def memory_kernel(
    key_ref, spike_ref, value_ref, keys_ref, mask_ref, values_ref, own_ref, sent_ref, mark_ref,
    key_in, spike_in, sems,
):
    set_mark(mark_ref)
    copies = Copies(sems)
    wide = range(0, keys_ref.shape[1], WIDE)
    pairs = ((key_ref, key_in), (spike_ref, spike_in), (value_ref, values_ref))
    parts = [
        [copies.start(here.at[columns(at)], there.at[columns(at)]) for here, there in pairs]
        for at in wide
    ]
    for at, part in zip(wide, parts):
        for copy in part:
            copy.wait()
        cols = slice(at, at + WIDE)
        mask = spike_in[:, cols].astype(f32).astype(bf16)
        keys = key_in[:, cols] * mask
        keys_ref[:, cols] = keys
        mask_ref[:, cols] = mask
        for head in range(0, WIDE, HEAD):
            here = slice(at + head, at + head + HEAD)
            own = tn(keys[:, head : head + HEAD], values_ref[:, here])
            own_ref[here, :] = own
            sent_ref[here, :] = own.astype(bf16)


def memory_call(key_input, k_spikes, values):
    length, total = values.shape
    block, state = (length, total), (total, HEAD)
    return kernel_call(
        memory_kernel,
        "HHH",
        (key_input, k_spikes, values),
        "VVVVVV",
        [(block, bf16)] * 3 + [(state, f32), (state, bf16), (MARK.shape, f32)],
        "own_memory",
        (2 * length * total * HEAD, 12 * length * total),
        [
            pltpu.VMEM(block, bf16),
            pltpu.VMEM(block, jnp.int32),
            pltpu.SemaphoreType.DMA((3 * total // WIDE,)),
        ],
    )


def join_kernel(*refs):
    del refs


def join(arrays, others=()):
    number = len(arrays)
    return kernel_call(
        join_kernel,
        ["A"] * (number + len(others)),
        (*[fast(one) for one in arrays], *others),
        ["A"] * number,
        [(one.shape, one.dtype) for one in arrays],
        "join",
        (0, 0),
        aliases={at: at for at in range(number)},
    )


def keep_lower(square, flipped=False):
    row = lax.broadcasted_iota(jnp.int32, square.shape, 0)
    col = lax.broadcasted_iota(jnp.int32, square.shape, 1)
    return jnp.where((col >= row) if flipped else (col <= row), square, 0.0).astype(bf16)


def causal(a, b):
    length = a.shape[0]
    cut = length - HEAD
    top = keep_lower(nt(a[:cut], b[:cut]))
    whole = nt(a[cut:], b)
    bottom = jnp.concatenate([whole[:, :cut].astype(bf16), keep_lower(whole[:, cut:])], axis=1)
    return [(slice(0, cut), slice(0, cut), top), (slice(cut, length), slice(0, length), bottom)]


def causal_turned(a, b):
    length = a.shape[0]
    whole = nt(a[:HEAD], b)
    top = jnp.concatenate(
        [keep_lower(whole[:, :HEAD], True), whole[:, HEAD:].astype(bf16)], axis=1
    )
    bottom = keep_lower(nt(a[HEAD:], b[HEAD:]), True)
    return [
        (slice(0, HEAD), slice(0, length), top),
        (slice(HEAD, length), slice(HEAD, length), bottom),
    ]


def twice(array):
    return jnp.concatenate([array, array], axis=1)


def masked_kernel(
    factor, grad_ref, spike_ref, value_ref, keys_ref, high_ref, low_ref,
    out_ref, mask_ref, grads_ref, mark_ref, spike_in, sems,
):
    set_mark(mark_ref)
    total = out_ref.shape[1]

    def copies(group, at):
        return [
            pltpu.make_async_copy(grad_ref.at[columns(at)], grads_ref.at[columns(at)], sems.at[0, group]),
            pltpu.make_async_copy(spike_ref.at[columns(at)], spike_in.at[columns(at)], sems.at[1, group]),
        ]

    for group in range(total // WIDE):
        for copy in copies(group, group * WIDE):
            copy.start()

    def work(group, at):
        for copy in copies(group, at):
            copy.wait()
        for part in heads(at):
            mask = spike_in[:, part].astype(f32)
            mask_ref[:, part] = mask.astype(bf16)
            grad, value, keys = grads_ref[:, part], value_ref[:, part], keys_ref[:, part]
            state = jnp.concatenate([high_ref[part, :], low_ref[part, :]], axis=1)
            for rows, cols, scores in causal(grad, value):
                made = nn(scores, keys[cols]) + nt(twice(grad[rows]), state)
                out_ref[rows, part] = (factor * made * mask[rows]).astype(bf16)

    groups(total, work)


def masked_call(factor, cotangent, q_spikes, values, keys, high, low):
    length, total = values.shape
    block = (length, total)
    return kernel_call(
        functools.partial(masked_kernel, factor),
        "HHVVVV",
        (cotangent, q_spikes, values, keys, high, low),
        "VVVV",
        [(block, bf16)] * 3 + [(MARK.shape, f32)],
        "masked_grad",
        (8 * length * total * length, 12 * length * total),
        [pltpu.VMEM(block, jnp.int32), pltpu.SemaphoreType.DMA((2, total // WIDE))],
    )


def rows_of(blocks):
    return sum(block.shape[0] for block in blocks)


def back_blocks(blocks):
    at = 0
    for block in blocks:
        for row in range(0, block.shape[0], PIECE):
            yield at, block[row : row + PIECE, :]
            at += 1


def load_tokens(copies, places_ref, tokens_ref, some_ref):
    bring = []
    for piece in range(some_ref.shape[1] // PIECE):
        place = pl.multiple_of(places_ref[piece] * PIECE, PIECE)
        bring.append(
            copies.start(
                tokens_ref.at[:, pl.ds(place, PIECE)], some_ref.at[:, pl.ds(piece * PIECE, PIECE)]
            )
        )
    return bring


def back_part(copies, places_ref, masked, blocks, out_ref, round_ref):
    going = []
    pieces = list(back_blocks(blocks))
    for (first, upper), (second, lower) in zip(pieces[::2], pieces[1::2]):
        both = slice(first * PIECE, (second + 1) * PIECE)
        made = nt(masked[...], jnp.concatenate([upper, lower], axis=0))
        round_ref[:, both] = made.astype(bf16)
        for piece in (first, second):
            place = pl.multiple_of(places_ref[piece] * PIECE, PIECE)
            going.append(
                copies.start(
                    round_ref.at[:, pl.ds(piece * PIECE, PIECE)],
                    out_ref.at[:, pl.ds(place, PIECE)],
                )
            )
    return going


def products_kernel(size, project, back, has_sum, has_back, places_ref, *refs):
    blocks, refs = refs[:size], list(refs[size:])
    tokens_ref = refs.pop(0) if project else None
    before_ref = refs.pop(0) if has_sum else None
    masked = refs.pop(0) if back else None
    if has_back:
        refs.pop(0)
    sum_ref = refs.pop(0) if project else None
    back_out = refs.pop(0) if back else None
    mark_ref = refs.pop(0)
    sems = refs.pop()
    set_mark(mark_ref)
    copies = Copies(sems)
    going = []
    if project:
        some_ref = refs.pop(0)
        bring = load_tokens(copies, places_ref, tokens_ref, some_ref)
    if back:
        going = back_part(copies, places_ref, masked, blocks, back_out, refs.pop(0))
    if project:
        for copy in bring:
            copy.wait()
        for at in range(0, sum_ref.shape[1], WIDE):
            part = slice(at, at + WIDE)
            made = nn(some_ref[...], jnp.concatenate([block[:, part] for block in blocks], axis=0))
            if has_sum:
                made = made + before_ref[:, part]
            sum_ref[:, part] = made
    for copy in going:
        copy.wait()


def products_call(places, blocks, tokens, partial=None, masked=None, grad=None, project=True):
    length, width = tokens.shape
    total = blocks[0].shape[1]
    depth = rows_of(blocks)
    number = depth // PIECE
    back = masked is not None
    places_in, args = "S" + "V" * len(blocks), [places, *blocks]
    places_out, outs = "", []
    scratch, aliases = [], {}
    if project:
        places_in, args = places_in + "H", args + [tokens]
        if partial is not None:
            aliases[len(args)] = 0
            places_in, args = places_in + "V", args + [partial]
        places_out, outs = "V", [((length, total), f32)]
        scratch.append(pltpu.VMEM((length, depth), bf16))
    if back:
        places_in, args = places_in + "V", args + [masked]
        if grad is not None:
            aliases[len(args)] = len(outs)
            places_in, args = places_in + "H", args + [grad]
        places_out, outs = places_out + "H", outs + [((length, width), bf16)]
        scratch.append(pltpu.VMEM((length, depth), bf16))
    made = kernel_call(
        functools.partial(
            products_kernel, len(blocks), project, back, partial is not None, grad is not None
        ),
        places_in,
        args,
        places_out + "V",
        outs + [(MARK.shape, f32)],
        "products" if project and back else "project" if project else "grad_tokens",
        (2 * (project + back) * length * depth * total, 0),
        scratch + [pltpu.SemaphoreType.DMA((2 * number,))],
        aliases,
    )
    made = list(made)
    partial = made.pop(0) if project else partial
    grad = made.pop(0) if back else grad
    return partial, grad, made[0]


def query_kernel(size, places_ref, tokens_ref, sum_ref, mask_ref, grad_ref, *refs):
    blocks = refs[:size]
    queries, own_ref, sent_ref, some_ref, sems = refs[size:]
    copies = Copies(sems)
    bring = load_tokens(copies, places_ref, tokens_ref, some_ref)
    for copy in bring:
        copy.wait()
    for at in range(0, queries.shape[1], WIDE):
        part = slice(at, at + WIDE)
        made = nn(some_ref[...], jnp.concatenate([block[:, part] for block in blocks], axis=0))
        made = made + sum_ref[:, part]
        made = (made * mask_ref[:, part].astype(f32)).astype(bf16)
        queries[:, part] = made
        for head in range(0, WIDE, HEAD):
            here = slice(at + head, at + head + HEAD)
            own = tn(made[:, head : head + HEAD], grad_ref[:, here])
            own_ref[here, :] = own
            sent_ref[here, :] = own.astype(bf16)


def query_call(places, tokens, blocks, before, q_mask, cotangent):
    length = tokens.shape[0]
    total = blocks[0].shape[1]
    depth = rows_of(blocks)
    number = depth // PIECE
    return kernel_call(
        functools.partial(query_kernel, len(blocks)),
        "SHVVV" + "V" * len(blocks),
        (places, tokens, before, q_mask, cotangent, *blocks),
        "VVV",
        [((length, total), bf16), ((total, HEAD), f32), ((total, HEAD), bf16)],
        "queries",
        (2 * length * depth * total, 0),
        [pltpu.VMEM((length, depth), bf16), pltpu.SemaphoreType.DMA((number,))],
    )


def out_copy(here, there, sems, group, at):
    return pltpu.make_async_copy(here.at[columns(at)], there.at[columns(at)], sems.at[group])


def attend_kernel(
    factor, query_ref, keys_ref, value_ref, high_ref, low_ref, out_ref, mark_ref, made_ref, sems
):
    set_mark(mark_ref)
    total = query_ref.shape[1]

    def work(group, at):
        for part in heads(at):
            query, keys, value = query_ref[:, part], keys_ref[:, part], value_ref[:, part]
            state = [high_ref[part, :], low_ref[part, :]]
            for rows, cols, scores in causal(query, keys):
                made = nn(
                    jnp.concatenate([scores, twice(query[rows])], axis=1),
                    jnp.concatenate([value[cols], *state], axis=0),
                )
                made_ref[rows, part] = (factor * made).astype(bf16)
        out_copy(made_ref, out_ref, sems, group, at).start()

    groups(total, work)
    for group in range(total // WIDE):
        out_copy(made_ref, out_ref, sems, group, group * WIDE).wait()


def attend_call(factor, queries, keys, values, high, low):
    length, total = values.shape
    return kernel_call(
        functools.partial(attend_kernel, factor),
        "VVVVV",
        (queries, keys, values, high, low),
        "HV",
        [((length, total), bf16), (MARK.shape, f32)],
        "attended",
        (8 * length * total * length, 8 * length * total),
        [pltpu.VMEM((length, total), bf16), pltpu.SemaphoreType.DMA((total // WIDE,))],
    )


def inner_kernel(query_ref, keys_ref, value_ref, grad_ref, key_ref, val_ref, mark_ref):
    set_mark(mark_ref)

    def work(group, at):
        for part in heads(at):
            query, keys = query_ref[:, part], keys_ref[:, part]
            value, grad = value_ref[:, part], grad_ref[:, part]
            for rows, cols, scores in causal_turned(keys, query):
                val_ref[rows, part] = nn(scores, grad[cols])
            for rows, cols, scores in causal_turned(value, grad):
                key_ref[rows, part] = nn(scores, query[cols])

    groups(query_ref.shape[1], work)


def inner_call(queries, keys, values, cotangent):
    length, total = values.shape
    block = (length, total)
    return kernel_call(
        inner_kernel,
        "VVVV",
        (queries, keys, values, cotangent),
        "VVV",
        [(block, f32), (block, f32), (MARK.shape, f32)],
        "inner",
        (12 * length * total * length, 16 * length * total),
    )


def outer_kernel(
    factor, key_ref, val_ref, keys_ref, value_ref, mask_ref, high_ref, low_ref,
    key_out, val_out, key_made, val_made, key_sems, val_sems,
):
    total = keys_ref.shape[1]

    def work(group, at):
        for part in heads(at):
            keys, value = keys_ref[:, part], value_ref[:, part]
            state = [high_ref[part, :], low_ref[part, :]]
            key_grad = key_ref[:, part] + nt(twice(value), jnp.concatenate(state, axis=1))
            key_made[:, part] = (factor * key_grad * mask_ref[:, part].astype(f32)).astype(bf16)
            value_grad = val_ref[:, part] + nn(twice(keys), jnp.concatenate(state, axis=0))
            val_made[:, part] = (factor * value_grad).astype(bf16)
        out_copy(key_made, key_out, key_sems, group, at).start()
        out_copy(val_made, val_out, val_sems, group, at).start()

    groups(total, work)
    for group in range(total // WIDE):
        out_copy(key_made, key_out, key_sems, group, group * WIDE).wait()
        out_copy(val_made, val_out, val_sems, group, group * WIDE).wait()


def outer_call(factor, key_part, value_part, keys, values, k_mask, high, low):
    length, total = values.shape
    block = (length, total)
    return kernel_call(
        functools.partial(outer_kernel, factor),
        "VVVVVVV",
        (key_part, value_part, keys, values, k_mask, high, low),
        "HH",
        [(block, bf16)] * 2,
        "outer",
        (8 * length * total * HEAD, 20 * length * total),
        [pltpu.VMEM(block, bf16)] * 2 + [pltpu.SemaphoreType.DMA((total // WIDE,))] * 2,
    )


def halves(state):
    high = state.astype(bf16)
    return high, (state - high.astype(f32)).astype(bf16)


def scan_any(own, sent, count, reverse):
    place = lax.axis_index(CTX)
    total = own
    state = jnp.zeros_like(own)
    bits = count.bit_length() - 1
    for bit in range(bits):
        step = 1 << bit
        last = bit == bits - 1
        pairs = []
        for source in range(count):
            high = bool(source & step)
            if not last or high == reverse:
                pairs.append((source, source ^ step))
        got = lax.ppermute(sent, CTX, pairs).astype(f32)
        if last:
            state = state + got
        else:
            mine = ((place // step) % 2) == (0 if reverse else 1)
            state = state + jnp.where(mine, got, 0.0)
            total = total + got
            sent = total.astype(bf16)
    return state


def links(first, keep=lambda source, target: True):
    pairs = []
    for chip in range(4):
        for core in range(2):
            other = chip ^ (first if core == 0 else 3 - first)
            if keep((chip, core), other):
                pairs.append((chip * 2 + core, other * 2 + core))
    return pairs


def scan_first(own, sent, reverse):
    chip, core = lax.axis_index("chip"), lax.axis_index("core")
    low_bit = 1 - chip % 2 if reverse else chip % 2
    half = own.shape[0] // 2
    sibling = lax.ppermute(sent, "core", SWAP)
    both = own + sibling.astype(f32)
    both = jnp.where(core == 0, both[:half], both[half:])
    got = lax.ppermute(both.astype(bf16), CTX, links(1, upward(reverse))).astype(f32)
    first = jnp.where((core == 1) | (low_bit == 1), got, 0.0)
    message = (got + jnp.where((core == 0) | (low_bit == 0), both, 0.0)).astype(bf16)
    return message, first, sibling


def upward(reverse):
    flip = 3 if reverse else 0

    def keep(source, target):
        at = source[0] ^ flip
        return source[0] ^ target == 1 or not at & 2

    return keep


def scan_second(message, first, sibling, reverse, others=()):
    core = lax.axis_index("core")
    more = lax.ppermute(message, CTX, links(2, upward(reverse))).astype(f32)
    state = first + more
    if others:
        state, = join([state], others)
    other = lax.ppermute(state, "core", SWAP)
    whole = jnp.concatenate(
        [jnp.where(core == 0, state, other), jnp.where(core == 0, other, state)], axis=0
    )
    return halves(whole + jnp.where(core == (0 if reverse else 1), sibling.astype(f32), 0.0))


def gather_any(q_weight):
    whole = lax.all_gather(q_weight, ("chip", "core", "dp"), axis=0, tiled=True)
    cut = whole.shape[0] // (2 * PIECE) * PIECE
    number = whole.shape[0] // PIECE
    return [whole[:cut], whole[cut:]], jnp.arange(number, dtype=jnp.int32)


def crossed(side):
    return (0, 1 + side, 2 - side, 3)


def per_device(tokens, key_input, values, q_weight, q_spikes, k_spikes, cotangent):
    batches, length, width = tokens.shape
    assert batches == 1
    total = q_weight.shape[1]
    chips, spread = lax.axis_size("chip"), lax.axis_size("dp")
    factor = 3.0 / math.sqrt(HEAD * length * chips * 2)
    tokens, key_input, values, q_spikes, k_spikes, cotangent = (
        array.reshape(length, array.shape[2])
        for array in (tokens, key_input, values, q_spikes, k_spikes, cotangent)
    )
    special = chips == 4 and spread == 4

    def sibling(array):
        return lax.ppermute(array, "core", SWAP)

    def along(array, pairs):
        return lax.ppermute(array, "dp", pairs)

    def cross(array):
        return lax.ppermute(array, CTX, links(1)), lax.ppermute(array, CTX, links(2))

    def onward(array):
        return lax.ppermute(array, CTX, links(2))

    keys, k_mask, values, own, sent, own_mark = memory_call(key_input, k_spikes, values)
    if special:
        chip, core, layer = (lax.axis_index(name) for name in ("chip", "core", "dp"))
        within = (layer == 1) | (layer == 2)
        ends = [(0, 1), (1, 0), (2, 3), (3, 2)]
        middle = [(1, 2), (2, 1)]
        outward = [(1, 0), (2, 3)]
        near = along(q_weight, ends)
        mid = along(q_weight, middle)
        first_0, second_0 = cross(q_weight)
        other_0 = sibling(q_weight)
        near, mid, first_0, second_0, sent = join([near, mid, first_0, second_0, sent])
        message, *rest = scan_first(own, sent, False)
    else:
        arrived, places = gather_any(q_weight)
        high, low = halves(scan_any(own, sent, chips * 2, False))

    if special:

        def numbers(sides, layers):
            return jnp.stack(
                [
                    ((chip ^ flip) * 2 + side) * spread + one
                    for one in layers
                    for side in sides
                    for flip in crossed(side)
                ]
            ).astype(jnp.int32)

        sides = (core, 1 - core)
        levels = [layer, layer ^ 1, jnp.where(layer < 2, 2, 1), jnp.where(layer < 2, 3, 0)]
        third_0 = onward(first_0)
        first_1, second_1 = cross(near)
        far = along(near, middle)
        mid_out = along(mid, outward)
        third_0, first_1, second_1, far, mid_out = join(
            [third_0, first_1, second_1, far, mid_out]
        )
        third_1 = onward(first_1)
        next_layer = jnp.where(within, mid, mid_out)
        first_2, second_2 = cross(next_layer)
        far_out = along(far, outward)
        own_blocks = [q_weight, first_0, second_0, third_0, other_0]
        own_blocks += [sibling(one) for one in own_blocks[1:4]]
        own_places = numbers(sides, levels[:1])
        partial, _, own_mark = products_call(own_places, own_blocks, tokens)
        third_1, first_2, second_2, far_out = join(
            [third_1, first_2, second_2, far_out], [own_mark]
        )
        third_2 = onward(first_2)
        last_layer = jnp.where(within, far, far_out)
        first_3, second_3 = cross(last_layer)

        def whole(*mine):
            return list(mine) + [sibling(one) for one in mine]

        high, low = scan_second(message, *rest, False)
        masked, q_mask, cotangent, _ = masked_call(
            factor, cotangent, q_spikes, values, keys, high, low
        )
        _, grad, mark_0 = products_call(
            own_places, own_blocks, tokens, masked=masked, project=False
        )
        blocks = whole(near, first_1, second_1, third_1)
        partial, grad, mark_1 = products_call(
            numbers(sides, levels[1:2]), blocks, tokens, partial, masked, grad
        )
        third_2, first_3, second_3 = join([third_2, first_3, second_3], [mark_0, mark_1])
        third_3 = onward(first_3)
        blocks = whole(next_layer, first_2, second_2, third_2)
        partial, grad, mark = products_call(
            numbers(sides, levels[2:3]), blocks, tokens, partial, masked, grad
        )
        third_3, = join([third_3], [mark])
        late = whole(last_layer, first_3, second_3, third_3)
        late_places = numbers(sides, levels[3:])
    else:
        masked, q_mask, cotangent, _ = masked_call(
            factor, cotangent, q_spikes, values, keys, high, low
        )
        half = places.shape[0] // 2
        partial, grad, _ = products_call(places[:half], arrived[:1], tokens, masked=masked)
        late, late_places = arrived[1:], places[half:]
    queries, own, sent = query_call(late_places, tokens, late, partial, q_mask, cotangent)
    attended, attended_mark = attend_call(factor, queries, keys, values, high, low)
    key_part, value_part, inner_mark = inner_call(queries, keys, values, cotangent)
    if special:
        message, *rest = scan_first(own, sent, True)
        message, = join([message], [attended_mark])
        adjoint = scan_second(message, *rest, True, [inner_mark])
    else:
        adjoint = halves(scan_any(own, sent, chips * 2, True))
    _, grad_tokens, _ = products_call(
        late_places, late, tokens, masked=masked, grad=grad, project=False
    )
    grad_keys, grad_values = outer_call(
        factor, key_part, value_part, keys, values, k_mask, *adjoint
    )
    return tuple(
        array.reshape(1, length, array.shape[1])
        for array in (attended, grad_tokens, grad_keys, grad_values)
    )


def solution(mesh):
    count, spread = mesh.shape["ctx"], mesh.shape["dp"]
    fine = Mesh(mesh.devices.reshape(count // 2, 2, spread), ("chip", "core", "dp"))
    block = P("dp", CTX, None)
    rows = P(("chip", "core", "dp"), None)
    in_specs = (block, block, block, rows, block, block, block)
    return jax.shard_map(
        per_device, mesh=fine, in_specs=in_specs, out_specs=(block,) * 4, check_vma=False
    )
```

```python
import functools
import math

import jax
import jax.numpy as jnp
from jax import lax
from jax.experimental import pallas as pl
from jax.experimental.pallas import tpu as pltpu
from jax.sharding import Mesh, PartitionSpec as P

HEAD = 128
PIECE = 128
WIDE = 512
CTX = ("chip", "core")
SWAP = [(0, 1), (1, 0)]
f32, bf16 = jnp.float32, jnp.bfloat16
VMEM_LIMIT = 18 * 1024 * 1024


def nn(a, b):
    return lax.dot_general(a, b, (((1,), (0,)), ((), ())), preferred_element_type=f32)


def nt(a, b):
    return lax.dot_general(a, b, (((1,), (1,)), ((), ())), preferred_element_type=f32)


def tn(a, b):
    return lax.dot_general(a, b, (((0,), (0,)), ((), ())), preferred_element_type=f32)


def params(flops, moved):
    return dict(
        compiler_params=pltpu.CompilerParams(vmem_limit_bytes=VMEM_LIMIT),
        cost_estimate=pl.CostEstimate(flops=flops, bytes_accessed=moved, transcendentals=0),
    )


MARK = jax.ShapeDtypeStruct((8, HEAD), f32)


def set_mark(mark_ref):
    mark_ref[...] = jnp.zeros_like(mark_ref)


def fast(array):
    return pltpu.with_memory_space_constraint(array, pltpu.VMEM)


def slow(array):
    return pltpu.with_memory_space_constraint(array, pltpu.HBM)


def specs(places):
    spaces = dict(V=pltpu.VMEM, H=pltpu.HBM, S=pltpu.SMEM, A=pl.ANY)
    return [pl.BlockSpec(memory_space=spaces[place]) for place in places]


def kernel_call(body, places, args, out_places, outs, name, cost, scratch=(), aliases=None):
    holds = dict(V=fast, H=slow)
    made = pl.pallas_call(
        body,
        in_specs=specs(places),
        out_specs=specs(out_places),
        out_shape=[
            pltpu.VMEM(shape, dtype) if place == "V" else jax.ShapeDtypeStruct(shape, dtype)
            for place, (shape, dtype) in zip(out_places, outs)
        ],
        scratch_shapes=list(scratch),
        input_output_aliases=aliases or {},
        name=name,
        **params(*cost),
    )
    return made(
        *[holds[place](one) if place in holds else one for place, one in zip(places, args)]
    )


class Copies:
    def __init__(self, sems):
        self.sems = sems
        self.used = 0

    def start(self, source, target):
        copy = pltpu.make_async_copy(source, target, self.sems.at[self.used])
        self.used += 1
        copy.start()
        return copy


def crossed(side):
    return (0, 1 + side, 2 - side, 3)


def all_places(special, number):
    if not special:
        return list(range(number))
    chip, core, layer = (lax.axis_index(name) for name in ("chip", "core", "dp"))
    upper = layer < 2
    layers = [layer, layer ^ 1, jnp.where(upper, 2, 1), jnp.where(upper, 3, 0)]
    return [
        ((chip ^ flip) * 2 + side) * 4 + one
        for one in layers
        for side in (core, 1 - core)
        for flip in crossed(side)
    ]


def piece_columns(place):
    return (slice(None), pl.ds(pl.multiple_of(place * PIECE, PIECE), PIECE))


def columns(at, wide=None):
    return (slice(None), pl.ds(at, wide or WIDE))


def groups(total, body):
    @pl.loop(0, total // WIDE)
    def _(group):
        body(group, pl.multiple_of(group * WIDE, WIDE))


def heads(at):
    return [pl.ds(pl.multiple_of(at + head, HEAD), HEAD) for head in range(0, WIDE, HEAD)]


def memory_kernel(
    special, key_ref, spike_ref, value_ref, tokens_ref,
    keys_ref, mask_ref, values_ref, own_ref, sent_ref, some_ref,
    key_in, spike_in, sems,
):
    copies = Copies(sems)
    wide = range(0, keys_ref.shape[1], WIDE)
    pairs = ((key_ref, key_in), (spike_ref, spike_in), (value_ref, values_ref))
    parts = [
        [copies.start(here.at[columns(at)], there.at[columns(at)]) for here, there in pairs]
        for at in wide
    ]
    places = all_places(special, some_ref.shape[1] // PIECE)
    ordered = [
        copies.start(tokens_ref.at[piece_columns(place)], some_ref.at[piece_columns(piece)])
        for piece, place in enumerate(places)
    ]
    for at, part in zip(wide, parts):
        for copy in part:
            copy.wait()
        cols = slice(at, at + WIDE)
        mask = spike_in[:, cols].astype(f32).astype(bf16)
        keys = key_in[:, cols] * mask
        keys_ref[:, cols] = keys
        mask_ref[:, cols] = mask
        for head in range(0, WIDE, HEAD):
            here = slice(at + head, at + head + HEAD)
            own = tn(keys[:, head : head + HEAD], values_ref[:, here])
            own_ref[here, :] = own
            sent_ref[here, :] = own.astype(bf16)
    for copy in ordered:
        copy.wait()


def memory_call(special, key_input, k_spikes, values, tokens):
    length, total = values.shape
    block, state = (length, total), (total, HEAD)
    return kernel_call(
        functools.partial(memory_kernel, special),
        "HHHH",
        (key_input, k_spikes, values, tokens),
        "VVVVVV",
        [(block, bf16)] * 3 + [(state, f32), (state, bf16), (tokens.shape, bf16)],
        "own_memory",
        (2 * length * total * HEAD, 12 * length * total),
        [
            pltpu.VMEM(block, bf16),
            pltpu.VMEM(block, jnp.int32),
            pltpu.SemaphoreType.DMA((3 * total // WIDE + tokens.shape[1] // PIECE,)),
        ],
    )


def join_kernel(*refs):
    del refs


def join(arrays, others=()):
    number = len(arrays)
    return kernel_call(
        join_kernel,
        ["A"] * (number + len(others)),
        (*[fast(one) for one in arrays], *others),
        ["A"] * number,
        [(one.shape, one.dtype) for one in arrays],
        "join",
        (0, 0),
        aliases={at: at for at in range(number)},
    )


def keep_lower(square, flipped=False):
    row = lax.broadcasted_iota(jnp.int32, square.shape, 0)
    col = lax.broadcasted_iota(jnp.int32, square.shape, 1)
    return jnp.where((col >= row) if flipped else (col <= row), square, 0.0).astype(bf16)


def causal(a, b):
    length = a.shape[0]
    cut = length - HEAD
    top = keep_lower(nt(a[:cut], b[:cut]))
    whole = nt(a[cut:], b)
    bottom = jnp.concatenate([whole[:, :cut].astype(bf16), keep_lower(whole[:, cut:])], axis=1)
    return [(slice(0, cut), slice(0, cut), top), (slice(cut, length), slice(0, length), bottom)]


def causal_turned(a, b):
    length = a.shape[0]
    whole = nt(a[:HEAD], b)
    top = jnp.concatenate(
        [keep_lower(whole[:, :HEAD], True), whole[:, HEAD:].astype(bf16)], axis=1
    )
    bottom = keep_lower(nt(a[HEAD:], b[HEAD:]), True)
    return [
        (slice(0, HEAD), slice(0, length), top),
        (slice(HEAD, length), slice(HEAD, length), bottom),
    ]


def twice(array):
    return jnp.concatenate([array, array], axis=1)


def masked_kernel(
    factor, grad_ref, spike_ref, value_ref, keys_ref, high_ref, low_ref,
    out_ref, mask_ref, grads_ref, mark_ref, spike_in, sems,
):
    set_mark(mark_ref)
    total = out_ref.shape[1]

    def copies(group, at):
        return [
            pltpu.make_async_copy(grad_ref.at[columns(at)], grads_ref.at[columns(at)], sems.at[0, group]),
            pltpu.make_async_copy(spike_ref.at[columns(at)], spike_in.at[columns(at)], sems.at[1, group]),
        ]

    for group in range(total // WIDE):
        for copy in copies(group, group * WIDE):
            copy.start()

    def work(group, at):
        for copy in copies(group, at):
            copy.wait()
        for part in heads(at):
            mask = spike_in[:, part].astype(f32)
            mask_ref[:, part] = mask.astype(bf16)
            grad, value, keys = grads_ref[:, part], value_ref[:, part], keys_ref[:, part]
            state = jnp.concatenate([high_ref[part, :], low_ref[part, :]], axis=1)
            for rows, cols, scores in causal(grad, value):
                made = nn(scores, keys[cols]) + nt(twice(grad[rows]), state)
                out_ref[rows, part] = (factor * made * mask[rows]).astype(bf16)

    groups(total, work)


def masked_call(factor, cotangent, q_spikes, values, keys, high, low):
    length, total = values.shape
    block = (length, total)
    return kernel_call(
        functools.partial(masked_kernel, factor),
        "HHVVVV",
        (cotangent, q_spikes, values, keys, high, low),
        "VVVV",
        [(block, bf16)] * 3 + [(MARK.shape, f32)],
        "masked_grad",
        (8 * length * total * length, 12 * length * total),
        [pltpu.VMEM(block, jnp.int32), pltpu.SemaphoreType.DMA((2, total // WIDE))],
    )


def rows_of(blocks):
    return sum(block.shape[0] for block in blocks)


def back_blocks(blocks):
    at = 0
    for block in blocks:
        for row in range(0, block.shape[0], PIECE):
            yield at, block[row : row + PIECE, :]
            at += 1


def back_part(copies, places, masked, blocks, out_ref, round_ref):
    going = []
    pieces = list(back_blocks(blocks))
    for (first, upper), (second, lower) in zip(pieces[::2], pieces[1::2]):
        both = slice(first * PIECE, (second + 1) * PIECE)
        made = nt(masked[...], jnp.concatenate([upper, lower], axis=0))
        round_ref[:, both] = made.astype(bf16)
        for piece in (first, second):
            going.append(
                copies.start(
                    round_ref.at[piece_columns(piece)], out_ref.at[piece_columns(places[piece])]
                )
            )
    return going


def products_kernel(special, start, size, project, back, has_sum, has_back, *refs):
    blocks, refs = refs[:size], list(refs[size:])
    depth = rows_of(blocks)
    tokens_ref = refs.pop(0) if project else None
    before_ref = refs.pop(0) if has_sum else None
    masked = refs.pop(0) if back else None
    if has_back:
        refs.pop(0)
    sum_ref = refs.pop(0) if project else None
    back_out = refs.pop(0) if back else None
    mark_ref = refs.pop(0)
    set_mark(mark_ref)
    going = []
    if back:
        round_ref, sems = refs
        places = all_places(special, back_out.shape[1] // PIECE)[start:]
        going = back_part(Copies(sems), places, masked, blocks, back_out, round_ref)
    if project:
        cols = slice(start * PIECE, start * PIECE + depth)
        for at in range(0, sum_ref.shape[1], WIDE):
            part = slice(at, at + WIDE)
            made = nn(
                tokens_ref[:, cols],
                jnp.concatenate([block[:, part] for block in blocks], axis=0),
            )
            if has_sum:
                made = made + before_ref[:, part]
            sum_ref[:, part] = made
    for copy in going:
        copy.wait()


def products_call(
    special, start, blocks, tokens, partial=None, masked=None, grad=None, project=True
):
    length, width = tokens.shape
    total = blocks[0].shape[1]
    depth = rows_of(blocks)
    back = masked is not None
    places_in, args = "V" * len(blocks), list(blocks)
    places_out, outs = "", []
    scratch, aliases = [], {}
    if project:
        places_in, args = places_in + "V", args + [tokens]
        if partial is not None:
            aliases[len(args)] = 0
            places_in, args = places_in + "V", args + [partial]
        places_out, outs = "V", [((length, total), f32)]
    if back:
        places_in, args = places_in + "V", args + [masked]
        if grad is not None:
            aliases[len(args)] = len(outs)
            places_in, args = places_in + "H", args + [grad]
        places_out, outs = places_out + "H", outs + [((length, width), bf16)]
        scratch = [
            pltpu.VMEM((length, depth), bf16), pltpu.SemaphoreType.DMA((depth // PIECE,))
        ]
    made = kernel_call(
        functools.partial(
            products_kernel, special, start, len(blocks), project, back,
            partial is not None, grad is not None,
        ),
        places_in,
        args,
        places_out + "V",
        outs + [(MARK.shape, f32)],
        "products" if project and back else "project" if project else "grad_tokens",
        (2 * (project + back) * length * depth * total, 0),
        scratch,
        aliases,
    )
    made = list(made)
    partial = made.pop(0) if project else partial
    grad = made.pop(0) if back else grad
    return partial, grad, made[0]


def query_kernel(start, size, tokens_ref, sum_ref, mask_ref, grad_ref, *refs):
    blocks = refs[:size]
    queries, own_ref, sent_ref = refs[size:]
    cols = slice(start * PIECE, start * PIECE + rows_of(blocks))
    for at in range(0, queries.shape[1], WIDE):
        part = slice(at, at + WIDE)
        made = nn(
            tokens_ref[:, cols], jnp.concatenate([block[:, part] for block in blocks], axis=0)
        )
        made = made + sum_ref[:, part]
        made = (made * mask_ref[:, part].astype(f32)).astype(bf16)
        queries[:, part] = made
        for head in range(0, WIDE, HEAD):
            here = slice(at + head, at + head + HEAD)
            own = tn(made[:, head : head + HEAD], grad_ref[:, here])
            own_ref[here, :] = own
            sent_ref[here, :] = own.astype(bf16)


def query_call(start, tokens, blocks, before, q_mask, cotangent):
    length = tokens.shape[0]
    total = blocks[0].shape[1]
    depth = rows_of(blocks)
    return kernel_call(
        functools.partial(query_kernel, start, len(blocks)),
        "VVVV" + "V" * len(blocks),
        (tokens, before, q_mask, cotangent, *blocks),
        "VVV",
        [((length, total), bf16), ((total, HEAD), f32), ((total, HEAD), bf16)],
        "queries",
        (2 * length * depth * total, 0),
    )


def out_copy(here, there, sems, group, at):
    return pltpu.make_async_copy(here.at[columns(at)], there.at[columns(at)], sems.at[group])


def attend_kernel(
    factor, query_ref, keys_ref, value_ref, high_ref, low_ref, out_ref, mark_ref, made_ref, sems
):
    set_mark(mark_ref)
    total = query_ref.shape[1]

    def work(group, at):
        for part in heads(at):
            query, keys, value = query_ref[:, part], keys_ref[:, part], value_ref[:, part]
            state = [high_ref[part, :], low_ref[part, :]]
            for rows, cols, scores in causal(query, keys):
                made = nn(
                    jnp.concatenate([scores, twice(query[rows])], axis=1),
                    jnp.concatenate([value[cols], *state], axis=0),
                )
                made_ref[rows, part] = (factor * made).astype(bf16)
        out_copy(made_ref, out_ref, sems, group, at).start()

    groups(total, work)
    for group in range(total // WIDE):
        out_copy(made_ref, out_ref, sems, group, group * WIDE).wait()


def attend_call(factor, queries, keys, values, high, low):
    length, total = values.shape
    return kernel_call(
        functools.partial(attend_kernel, factor),
        "VVVVV",
        (queries, keys, values, high, low),
        "HV",
        [((length, total), bf16), (MARK.shape, f32)],
        "attended",
        (8 * length * total * length, 8 * length * total),
        [pltpu.VMEM((length, total), bf16), pltpu.SemaphoreType.DMA((total // WIDE,))],
    )


def inner_kernel(query_ref, keys_ref, value_ref, grad_ref, key_ref, val_ref, mark_ref):
    set_mark(mark_ref)

    def work(group, at):
        for part in heads(at):
            query, keys = query_ref[:, part], keys_ref[:, part]
            value, grad = value_ref[:, part], grad_ref[:, part]
            for rows, cols, scores in causal_turned(keys, query):
                val_ref[rows, part] = nn(scores, grad[cols])
            for rows, cols, scores in causal_turned(value, grad):
                key_ref[rows, part] = nn(scores, query[cols])

    groups(query_ref.shape[1], work)


def inner_call(queries, keys, values, cotangent):
    length, total = values.shape
    block = (length, total)
    return kernel_call(
        inner_kernel,
        "VVVV",
        (queries, keys, values, cotangent),
        "VVV",
        [(block, f32), (block, f32), (MARK.shape, f32)],
        "inner",
        (12 * length * total * length, 16 * length * total),
    )


def outer_kernel(
    factor, key_ref, val_ref, keys_ref, value_ref, mask_ref, high_ref, low_ref,
    key_out, val_out, key_made, val_made, key_sems, val_sems,
):
    total = keys_ref.shape[1]

    def work(group, at):
        for part in heads(at):
            keys, value = keys_ref[:, part], value_ref[:, part]
            state = [high_ref[part, :], low_ref[part, :]]
            key_grad = key_ref[:, part] + nt(twice(value), jnp.concatenate(state, axis=1))
            key_made[:, part] = (factor * key_grad * mask_ref[:, part].astype(f32)).astype(bf16)
            value_grad = val_ref[:, part] + nn(twice(keys), jnp.concatenate(state, axis=0))
            val_made[:, part] = (factor * value_grad).astype(bf16)
        out_copy(key_made, key_out, key_sems, group, at).start()
        out_copy(val_made, val_out, val_sems, group, at).start()

    groups(total, work)
    for group in range(total // WIDE):
        out_copy(key_made, key_out, key_sems, group, group * WIDE).wait()
        out_copy(val_made, val_out, val_sems, group, group * WIDE).wait()


def outer_call(factor, key_part, value_part, keys, values, k_mask, high, low):
    length, total = values.shape
    block = (length, total)
    return kernel_call(
        functools.partial(outer_kernel, factor),
        "VVVVVVV",
        (key_part, value_part, keys, values, k_mask, high, low),
        "HH",
        [(block, bf16)] * 2,
        "outer",
        (8 * length * total * HEAD, 20 * length * total),
        [pltpu.VMEM(block, bf16)] * 2 + [pltpu.SemaphoreType.DMA((total // WIDE,))] * 2,
    )


def halves(state):
    high = state.astype(bf16)
    return high, (state - high.astype(f32)).astype(bf16)


def scan_any(own, sent, count, reverse):
    place = lax.axis_index(CTX)
    total = own
    state = jnp.zeros_like(own)
    bits = count.bit_length() - 1
    for bit in range(bits):
        step = 1 << bit
        last = bit == bits - 1
        pairs = []
        for source in range(count):
            high = bool(source & step)
            if not last or high == reverse:
                pairs.append((source, source ^ step))
        got = lax.ppermute(sent, CTX, pairs).astype(f32)
        if last:
            state = state + got
        else:
            mine = ((place // step) % 2) == (0 if reverse else 1)
            state = state + jnp.where(mine, got, 0.0)
            total = total + got
            sent = total.astype(bf16)
    return state


def links(first, keep=lambda source, target: True):
    pairs = []
    for chip in range(4):
        for core in range(2):
            other = chip ^ (first if core == 0 else 3 - first)
            if keep((chip, core), other):
                pairs.append((chip * 2 + core, other * 2 + core))
    return pairs


def upward(reverse):
    flip = 3 if reverse else 0

    def keep(source, target):
        at = source[0] ^ flip
        return source[0] ^ target == 1 or not at & 2

    return keep


def half_rows(array_ref, core):
    half = array_ref.shape[0] // 2
    return array_ref[pl.ds(pl.multiple_of(core * half, half), half), :]


def both_kernel(own_ref, sibling_ref, both_ref, sent_ref):
    core = lax.axis_index("core")
    both = half_rows(own_ref, core) + half_rows(sibling_ref, core).astype(f32)
    both_ref[...] = both
    sent_ref[...] = both.astype(bf16)


def low_bit(reverse):
    chip = lax.axis_index("chip")
    return 1 - chip % 2 if reverse else chip % 2


def message_kernel(reverse, got_ref, both_ref, *refs):
    core = lax.axis_index("core")
    adds = jnp.where((core == 0) | (low_bit(reverse) == 0), 1.0, 0.0)
    refs[-1][...] = (got_ref[...].astype(f32) + adds * both_ref[...]).astype(bf16)


def state_kernel(reverse, got_ref, more_ref, *refs):
    core = lax.axis_index("core")
    adds = jnp.where((core == 1) | (low_bit(reverse) == 1), 1.0, 0.0)
    refs[-1][...] = adds * got_ref[...].astype(f32) + more_ref[...].astype(f32)


def whole_kernel(reverse, state_ref, other_ref, sibling_ref, high_ref, low_ref):
    core = lax.axis_index("core")
    adds = jnp.where(core == (0 if reverse else 1), 1.0, 0.0)
    half = state_ref.shape[0]
    for ref, side in ((state_ref, core), (other_ref, 1 - core)):
        rows = pl.ds(pl.multiple_of(side * half, half), half)
        whole = ref[...] + adds * sibling_ref[rows, :].astype(f32)
        high = whole.astype(bf16)
        high_ref[rows, :] = high
        low_ref[rows, :] = (whole - high.astype(f32)).astype(bf16)


def scan_first(own, sent, reverse, others=()):
    rows = own.shape[0]
    half = (rows // 2, HEAD)
    sibling = lax.ppermute(sent, "core", SWAP)
    both, sent = kernel_call(
        both_kernel, "VV", (own, sibling), "VV", [(half, f32), (half, bf16)], "both", (0, 0)
    )
    got = lax.ppermute(sent, CTX, links(1, upward(reverse)))
    (message,) = kernel_call(
        functools.partial(message_kernel, reverse),
        "VV" + "A" * len(others),
        (got, both, *others),
        "V",
        [(half, bf16)],
        "message",
        (0, 0),
    )
    return message, got, sibling


def scan_second(message, got, sibling, reverse, others=()):
    half, full = message.shape, sibling.shape
    more = lax.ppermute(message, CTX, links(2, upward(reverse)))
    (state,) = kernel_call(
        functools.partial(state_kernel, reverse),
        "VV" + "A" * len(others),
        (got, more, *others),
        "V",
        [(half, f32)],
        "state",
        (0, 0),
    )
    other = lax.ppermute(state, "core", SWAP)
    return kernel_call(
        functools.partial(whole_kernel, reverse),
        "VVV",
        (state, other, sibling),
        "VV",
        [(full, bf16)] * 2,
        "whole",
        (0, 0),
    )


def gather_any(q_weight):
    whole = lax.all_gather(q_weight, ("chip", "core", "dp"), axis=0, tiled=True)
    cut = whole.shape[0] // (2 * PIECE) * PIECE
    return [whole[:cut], whole[cut:]]


def choose_kernel(inner_ref, end_ref, out_ref, sem):
    del end_ref
    layer = lax.axis_index("dp")

    @pl.when((layer == 1) | (layer == 2))
    def _():
        copy = pltpu.make_async_copy(inner_ref, out_ref, sem)
        copy.start()
        copy.wait()


def choose(inner, end):
    return kernel_call(
        choose_kernel,
        "AA",
        (fast(inner), fast(end)),
        "A",
        [(inner.shape, inner.dtype)],
        "choose",
        (0, 0),
        [pltpu.SemaphoreType.DMA],
        {1: 0},
    )[0]


def per_device(tokens, key_input, values, q_weight, q_spikes, k_spikes, cotangent):
    batches, length, width = tokens.shape
    assert batches == 1
    total = q_weight.shape[1]
    chips, spread = lax.axis_size("chip"), lax.axis_size("dp")
    factor = 3.0 / math.sqrt(HEAD * length * chips * 2)
    tokens, key_input, values, q_spikes, k_spikes, cotangent = (
        array.reshape(length, array.shape[2])
        for array in (tokens, key_input, values, q_spikes, k_spikes, cotangent)
    )
    special = chips == 4 and spread == 4

    def sibling(array):
        return lax.ppermute(array, "core", SWAP)

    def along(array, pairs):
        return lax.ppermute(array, "dp", pairs)

    def cross(array):
        return lax.ppermute(array, CTX, links(1)), lax.ppermute(array, CTX, links(2))

    def onward(array):
        return lax.ppermute(array, CTX, links(2))

    keys, k_mask, values, own, sent, tokens = memory_call(
        special, key_input, k_spikes, values, tokens
    )
    if special:
        ends = [(0, 1), (1, 0), (2, 3), (3, 2)]
        middle = [(1, 2), (2, 1)]
        outward = [(1, 0), (2, 3)]
        near = along(q_weight, ends)
        mid = along(q_weight, middle)
        first_0, second_0 = cross(q_weight)
        other_0 = sibling(q_weight)
        near, mid, first_0, second_0, sent = join([near, mid, first_0, second_0, sent])
        message, *rest = scan_first(own, sent, False)
    else:
        arrived = gather_any(q_weight)
        high, low = halves(scan_any(own, sent, chips * 2, False))

    if special:
        third_0 = onward(first_0)
        first_1, second_1 = cross(near)
        far = along(near, middle)
        mid_out = along(mid, outward)
        third_0, first_1, second_1, far, mid_out = join(
            [third_0, first_1, second_1, far, mid_out]
        )
        third_1 = onward(first_1)
        next_layer = choose(mid, mid_out)
        first_2, second_2 = cross(next_layer)
        far_out = along(far, outward)
        own_blocks = [q_weight, first_0, second_0, third_0, other_0]
        own_blocks += [sibling(one) for one in own_blocks[1:4]]
        partial, _, own_mark = products_call(special, 0, own_blocks, tokens)
        third_1, first_2, second_2, far_out = join(
            [third_1, first_2, second_2, far_out], [own_mark]
        )
        third_2 = onward(first_2)
        last_layer = choose(far, far_out)
        first_3, second_3 = cross(last_layer)

        def whole(*mine):
            return list(mine) + [sibling(one) for one in mine]

        high, low = scan_second(message, *rest, False)
        masked, q_mask, cotangent, _ = masked_call(
            factor, cotangent, q_spikes, values, keys, high, low
        )
        _, grad, mark_0 = products_call(
            special, 0, own_blocks, tokens, masked=masked, project=False
        )
        blocks = whole(near, first_1, second_1, third_1)
        partial, grad, mark_1 = products_call(
            special, 8, blocks, tokens, partial, masked, grad
        )
        third_2, first_3, second_3 = join([third_2, first_3, second_3], [mark_0, mark_1])
        third_3 = onward(first_3)
        blocks = whole(next_layer, first_2, second_2, third_2)
        partial, grad, mark = products_call(
            special, 16, blocks, tokens, partial, masked, grad
        )
        third_3, = join([third_3], [mark])
        late = whole(last_layer, first_3, second_3, third_3)
        start = 24
    else:
        masked, q_mask, cotangent, _ = masked_call(
            factor, cotangent, q_spikes, values, keys, high, low
        )
        start = arrived[0].shape[0] // PIECE
        partial, grad, _ = products_call(special, 0, arrived[:1], tokens, masked=masked)
        late = arrived[1:]
    queries, own, sent = query_call(start, tokens, late, partial, q_mask, cotangent)
    attended, attended_mark = attend_call(factor, queries, keys, values, high, low)
    key_part, value_part, inner_mark = inner_call(queries, keys, values, cotangent)
    if special:
        message, *rest = scan_first(own, sent, True, [attended_mark])
        adjoint = scan_second(message, *rest, True, [inner_mark])
    else:
        adjoint = halves(scan_any(own, sent, chips * 2, True))
    _, grad_tokens, _ = products_call(
        special, start, late, tokens, masked=masked, grad=grad, project=False
    )
    grad_keys, grad_values = outer_call(
        factor, key_part, value_part, keys, values, k_mask, *adjoint
    )
    return tuple(
        array.reshape(1, length, array.shape[1])
        for array in (attended, grad_tokens, grad_keys, grad_values)
    )


def solution(mesh):
    count, spread = mesh.shape["ctx"], mesh.shape["dp"]
    fine = Mesh(mesh.devices.reshape(count // 2, 2, spread), ("chip", "core", "dp"))
    block = P("dp", CTX, None)
    rows = P(("chip", "core", "dp"), None)
    in_specs = (block, block, block, rows, block, block, block)
    return jax.shard_map(
        per_device, mesh=fine, in_specs=in_specs, out_specs=(block,) * 4, check_vma=False
    )
```

```python
import functools
import math

import jax
import jax.numpy as jnp
from jax import lax
from jax.experimental import pallas as pl
from jax.experimental.pallas import tpu as pltpu
from jax.sharding import Mesh, PartitionSpec as P

HEAD = 128
PIECE = 128
WIDE = 512
CTX = ("chip", "core")
SWAP = [(0, 1), (1, 0)]
f32, bf16 = jnp.float32, jnp.bfloat16
VMEM_LIMIT = 18 * 1024 * 1024


def nn(a, b):
    return lax.dot_general(a, b, (((1,), (0,)), ((), ())), preferred_element_type=f32)


def nt(a, b):
    return lax.dot_general(a, b, (((1,), (1,)), ((), ())), preferred_element_type=f32)


def tn(a, b):
    return lax.dot_general(a, b, (((0,), (0,)), ((), ())), preferred_element_type=f32)


def params(flops, moved):
    return dict(
        compiler_params=pltpu.CompilerParams(vmem_limit_bytes=VMEM_LIMIT),
        cost_estimate=pl.CostEstimate(flops=flops, bytes_accessed=moved, transcendentals=0),
    )


MARK = jax.ShapeDtypeStruct((8, HEAD), f32)


def set_mark(mark_ref):
    mark_ref[...] = jnp.zeros_like(mark_ref)


def fast(array):
    return pltpu.with_memory_space_constraint(array, pltpu.VMEM)


def slow(array):
    return pltpu.with_memory_space_constraint(array, pltpu.HBM)


def specs(places):
    spaces = dict(V=pltpu.VMEM, H=pltpu.HBM, S=pltpu.SMEM, A=pl.ANY)
    return [pl.BlockSpec(memory_space=spaces[place]) for place in places]


def kernel_call(body, places, args, out_places, outs, name, cost, scratch=(), aliases=None):
    holds = dict(V=fast, H=slow)
    made = pl.pallas_call(
        body,
        in_specs=specs(places),
        out_specs=specs(out_places),
        out_shape=[
            pltpu.VMEM(shape, dtype) if place == "V" else jax.ShapeDtypeStruct(shape, dtype)
            for place, (shape, dtype) in zip(out_places, outs)
        ],
        scratch_shapes=list(scratch),
        input_output_aliases=aliases or {},
        name=name,
        **params(*cost),
    )
    return made(
        *[holds[place](one) if place in holds else one for place, one in zip(places, args)]
    )


class Copies:
    def __init__(self, sems):
        self.sems = sems
        self.used = 0

    def start(self, source, target):
        copy = pltpu.make_async_copy(source, target, self.sems.at[self.used])
        self.used += 1
        copy.start()
        return copy


def crossed(side):
    return (0, 1 + side, 2 - side, 3)


def all_places(special, number):
    if not special:
        return list(range(number))
    chip, core, layer = (lax.axis_index(name) for name in ("chip", "core", "dp"))
    upper = layer < 2
    layers = [layer, layer ^ 1, jnp.where(upper, 2, 1), jnp.where(upper, 3, 0)]

    def some(one, flips):
        return [
            ((chip ^ crossed(side)[flip]) * 2 + side) * 4 + one
            for side in (core, 1 - core)
            for flip in flips
        ]

    first = [place for one in layers[:3] for place in some(one, range(4))]
    return first + some(layers[3], range(3)) + some(layers[3], [3])


def piece_columns(place):
    return (slice(None), pl.ds(pl.multiple_of(place * PIECE, PIECE), PIECE))


def columns(at, wide=None):
    return (slice(None), pl.ds(at, wide or WIDE))


def groups(total, body):
    @pl.loop(0, total // WIDE)
    def _(group):
        body(group, pl.multiple_of(group * WIDE, WIDE))


def heads(at):
    return [pl.ds(pl.multiple_of(at + head, HEAD), HEAD) for head in range(0, WIDE, HEAD)]


def memory_kernel(
    special, key_ref, spike_ref, value_ref, tokens_ref,
    keys_ref, mask_ref, values_ref, own_ref, sent_ref, some_ref,
    key_in, spike_in, sems,
):
    copies = Copies(sems)
    wide = range(0, keys_ref.shape[1], WIDE)
    pairs = ((key_ref, key_in), (spike_ref, spike_in), (value_ref, values_ref))
    parts = [
        [copies.start(here.at[columns(at)], there.at[columns(at)]) for here, there in pairs]
        for at in wide
    ]
    places = all_places(special, some_ref.shape[1] // PIECE)
    ordered = [
        copies.start(tokens_ref.at[piece_columns(place)], some_ref.at[piece_columns(piece)])
        for piece, place in enumerate(places)
    ]
    for at, part in zip(wide, parts):
        for copy in part:
            copy.wait()
        cols = slice(at, at + WIDE)
        mask = spike_in[:, cols].astype(f32).astype(bf16)
        keys = key_in[:, cols] * mask
        keys_ref[:, cols] = keys
        mask_ref[:, cols] = mask
        for head in range(0, WIDE, HEAD):
            here = slice(at + head, at + head + HEAD)
            own = tn(keys[:, head : head + HEAD], values_ref[:, here])
            own_ref[here, :] = own
            sent_ref[here, :] = own.astype(bf16)
    for copy in ordered:
        copy.wait()


def memory_call(special, key_input, k_spikes, values, tokens):
    length, total = values.shape
    block, state = (length, total), (total, HEAD)
    return kernel_call(
        functools.partial(memory_kernel, special),
        "HHHH",
        (key_input, k_spikes, values, tokens),
        "VVVVVV",
        [(block, bf16)] * 3 + [(state, f32), (state, bf16), (tokens.shape, bf16)],
        "own_memory",
        (2 * length * total * HEAD, 12 * length * total),
        [
            pltpu.VMEM(block, bf16),
            pltpu.VMEM(block, jnp.int32),
            pltpu.SemaphoreType.DMA((3 * total // WIDE + tokens.shape[1] // PIECE,)),
        ],
    )


def join_kernel(*refs):
    del refs


def join(arrays, others=()):
    number = len(arrays)
    return kernel_call(
        join_kernel,
        ["A"] * (number + len(others)),
        (*[fast(one) for one in arrays], *others),
        ["A"] * number,
        [(one.shape, one.dtype) for one in arrays],
        "join",
        (0, 0),
        aliases={at: at for at in range(number)},
    )


def keep_lower(square, flipped=False):
    row = lax.broadcasted_iota(jnp.int32, square.shape, 0)
    col = lax.broadcasted_iota(jnp.int32, square.shape, 1)
    return jnp.where((col >= row) if flipped else (col <= row), square, 0.0).astype(bf16)


def causal(a, b):
    length = a.shape[0]
    cut = length - HEAD
    top = keep_lower(nt(a[:cut], b[:cut]))
    whole = nt(a[cut:], b)
    bottom = jnp.concatenate([whole[:, :cut].astype(bf16), keep_lower(whole[:, cut:])], axis=1)
    return [(slice(0, cut), slice(0, cut), top), (slice(cut, length), slice(0, length), bottom)]


def causal_turned(a, b):
    length = a.shape[0]
    whole = nt(a[:HEAD], b)
    top = jnp.concatenate(
        [keep_lower(whole[:, :HEAD], True), whole[:, HEAD:].astype(bf16)], axis=1
    )
    bottom = keep_lower(nt(a[HEAD:], b[HEAD:]), True)
    return [
        (slice(0, HEAD), slice(0, length), top),
        (slice(HEAD, length), slice(HEAD, length), bottom),
    ]


def twice(array):
    return jnp.concatenate([array, array], axis=1)


def masked_kernel(
    factor, grad_ref, spike_ref, value_ref, keys_ref, high_ref, low_ref,
    out_ref, mask_ref, grads_ref, mark_ref, spike_in, sems,
):
    set_mark(mark_ref)
    total = out_ref.shape[1]

    def copies(group, at):
        return [
            pltpu.make_async_copy(grad_ref.at[columns(at)], grads_ref.at[columns(at)], sems.at[0, group]),
            pltpu.make_async_copy(spike_ref.at[columns(at)], spike_in.at[columns(at)], sems.at[1, group]),
        ]

    for group in range(total // WIDE):
        for copy in copies(group, group * WIDE):
            copy.start()

    def work(group, at):
        for copy in copies(group, at):
            copy.wait()
        for part in heads(at):
            mask = spike_in[:, part].astype(f32)
            mask_ref[:, part] = mask.astype(bf16)
            grad, value, keys = grads_ref[:, part], value_ref[:, part], keys_ref[:, part]
            state = jnp.concatenate([high_ref[part, :], low_ref[part, :]], axis=1)
            for rows, cols, scores in causal(grad, value):
                made = nn(scores, keys[cols]) + nt(twice(grad[rows]), state)
                out_ref[rows, part] = (factor * made * mask[rows]).astype(bf16)

    groups(total, work)


def masked_call(factor, cotangent, q_spikes, values, keys, high, low):
    length, total = values.shape
    block = (length, total)
    return kernel_call(
        functools.partial(masked_kernel, factor),
        "HHVVVV",
        (cotangent, q_spikes, values, keys, high, low),
        "VVVV",
        [(block, bf16)] * 3 + [(MARK.shape, f32)],
        "masked_grad",
        (8 * length * total * length, 12 * length * total),
        [pltpu.VMEM(block, jnp.int32), pltpu.SemaphoreType.DMA((2, total // WIDE))],
    )


def rows_of(blocks):
    return sum(block.shape[0] for block in blocks)


def back_blocks(blocks):
    at = 0
    for block in blocks:
        for row in range(0, block.shape[0], PIECE):
            yield at, block[row : row + PIECE, :]
            at += 1


def back_part(copies, places, masked, blocks, out_ref, round_ref):
    going = []
    pieces = list(back_blocks(blocks))
    for (first, upper), (second, lower) in zip(pieces[::2], pieces[1::2]):
        both = slice(first * PIECE, (second + 1) * PIECE)
        made = nt(masked[...], jnp.concatenate([upper, lower], axis=0))
        round_ref[:, both] = made.astype(bf16)
        for piece in (first, second):
            going.append(
                copies.start(
                    round_ref.at[piece_columns(piece)], out_ref.at[piece_columns(places[piece])]
                )
            )
    return going


def products_kernel(special, start, size, project, back, has_sum, has_back, *refs):
    blocks, refs = refs[:size], list(refs[size:])
    depth = rows_of(blocks)
    tokens_ref = refs.pop(0) if project else None
    before_ref = refs.pop(0) if has_sum else None
    masked = refs.pop(0) if back else None
    if has_back:
        refs.pop(0)
    sum_ref = refs.pop(0) if project else None
    back_out = refs.pop(0) if back else None
    mark_ref = refs.pop(0)
    set_mark(mark_ref)
    going = []
    if back:
        round_ref, sems = refs
        places = all_places(special, back_out.shape[1] // PIECE)[start:]
        going = back_part(Copies(sems), places, masked, blocks, back_out, round_ref)
    if project:
        cols = slice(start * PIECE, start * PIECE + depth)
        for at in range(0, sum_ref.shape[1], WIDE):
            part = slice(at, at + WIDE)
            made = nn(
                tokens_ref[:, cols],
                jnp.concatenate([block[:, part] for block in blocks], axis=0),
            )
            if has_sum:
                made = made + before_ref[:, part]
            sum_ref[:, part] = made
    for copy in going:
        copy.wait()


def products_call(
    special, start, blocks, tokens, partial=None, masked=None, grad=None, project=True
):
    length, width = tokens.shape
    total = blocks[0].shape[1]
    depth = rows_of(blocks)
    back = masked is not None
    places_in, args = "V" * len(blocks), list(blocks)
    places_out, outs = "", []
    scratch, aliases = [], {}
    if project:
        places_in, args = places_in + "V", args + [tokens]
        if partial is not None:
            aliases[len(args)] = 0
            places_in, args = places_in + "V", args + [partial]
        places_out, outs = "V", [((length, total), f32)]
    if back:
        places_in, args = places_in + "V", args + [masked]
        if grad is not None:
            aliases[len(args)] = len(outs)
            places_in, args = places_in + "H", args + [grad]
        places_out, outs = places_out + "H", outs + [((length, width), bf16)]
        scratch = [
            pltpu.VMEM((length, depth), bf16), pltpu.SemaphoreType.DMA((depth // PIECE,))
        ]
    made = kernel_call(
        functools.partial(
            products_kernel, special, start, len(blocks), project, back,
            partial is not None, grad is not None,
        ),
        places_in,
        args,
        places_out + "V",
        outs + [(MARK.shape, f32)],
        "products" if project and back else "project" if project else "grad_tokens",
        (2 * (project + back) * length * depth * total, 0),
        scratch,
        aliases,
    )
    made = list(made)
    partial = made.pop(0) if project else partial
    grad = made.pop(0) if back else grad
    return partial, grad, made[0]


def query_kernel(start, size, tokens_ref, sum_ref, mask_ref, grad_ref, *refs):
    blocks = refs[:size]
    queries, own_ref, sent_ref = refs[size:]
    cols = slice(start * PIECE, start * PIECE + rows_of(blocks))
    for at in range(0, queries.shape[1], WIDE):
        part = slice(at, at + WIDE)
        made = nn(
            tokens_ref[:, cols], jnp.concatenate([block[:, part] for block in blocks], axis=0)
        )
        made = made + sum_ref[:, part]
        made = (made * mask_ref[:, part].astype(f32)).astype(bf16)
        queries[:, part] = made
        for head in range(0, WIDE, HEAD):
            here = slice(at + head, at + head + HEAD)
            own = tn(made[:, head : head + HEAD], grad_ref[:, here])
            own_ref[here, :] = own
            sent_ref[here, :] = own.astype(bf16)


def query_call(start, tokens, blocks, before, q_mask, cotangent):
    length = tokens.shape[0]
    total = blocks[0].shape[1]
    depth = rows_of(blocks)
    return kernel_call(
        functools.partial(query_kernel, start, len(blocks)),
        "VVVV" + "V" * len(blocks),
        (tokens, before, q_mask, cotangent, *blocks),
        "VVV",
        [((length, total), bf16), ((total, HEAD), f32), ((total, HEAD), bf16)],
        "queries",
        (2 * length * depth * total, 0),
    )


def out_copy(here, there, sems, group, at):
    return pltpu.make_async_copy(here.at[columns(at)], there.at[columns(at)], sems.at[group])


def attend_kernel(
    factor, query_ref, keys_ref, value_ref, high_ref, low_ref, out_ref, mark_ref, made_ref, sems
):
    set_mark(mark_ref)
    total = query_ref.shape[1]

    def work(group, at):
        for part in heads(at):
            query, keys, value = query_ref[:, part], keys_ref[:, part], value_ref[:, part]
            state = [high_ref[part, :], low_ref[part, :]]
            for rows, cols, scores in causal(query, keys):
                made = nn(
                    jnp.concatenate([scores, twice(query[rows])], axis=1),
                    jnp.concatenate([value[cols], *state], axis=0),
                )
                made_ref[rows, part] = (factor * made).astype(bf16)
        out_copy(made_ref, out_ref, sems, group, at).start()

    groups(total, work)
    for group in range(total // WIDE):
        out_copy(made_ref, out_ref, sems, group, group * WIDE).wait()


def attend_call(factor, queries, keys, values, high, low):
    length, total = values.shape
    return kernel_call(
        functools.partial(attend_kernel, factor),
        "VVVVV",
        (queries, keys, values, high, low),
        "HV",
        [((length, total), bf16), (MARK.shape, f32)],
        "attended",
        (8 * length * total * length, 8 * length * total),
        [pltpu.VMEM((length, total), bf16), pltpu.SemaphoreType.DMA((total // WIDE,))],
    )


def inner_kernel(query_ref, keys_ref, value_ref, grad_ref, key_ref, val_ref, mark_ref):
    set_mark(mark_ref)

    def work(group, at):
        for part in heads(at):
            query, keys = query_ref[:, part], keys_ref[:, part]
            value, grad = value_ref[:, part], grad_ref[:, part]
            for rows, cols, scores in causal_turned(keys, query):
                val_ref[rows, part] = nn(scores, grad[cols])
            for rows, cols, scores in causal_turned(value, grad):
                key_ref[rows, part] = nn(scores, query[cols])

    groups(query_ref.shape[1], work)


def inner_call(queries, keys, values, cotangent):
    length, total = values.shape
    block = (length, total)
    return kernel_call(
        inner_kernel,
        "VVVV",
        (queries, keys, values, cotangent),
        "VVV",
        [(block, f32), (block, f32), (MARK.shape, f32)],
        "inner",
        (12 * length * total * length, 16 * length * total),
    )


def outer_kernel(
    factor, key_ref, val_ref, keys_ref, value_ref, mask_ref, high_ref, low_ref,
    key_out, val_out, key_made, val_made, key_sems, val_sems,
):
    total = keys_ref.shape[1]

    def work(group, at):
        for part in heads(at):
            keys, value = keys_ref[:, part], value_ref[:, part]
            state = [high_ref[part, :], low_ref[part, :]]
            key_grad = key_ref[:, part] + nt(twice(value), jnp.concatenate(state, axis=1))
            key_made[:, part] = (factor * key_grad * mask_ref[:, part].astype(f32)).astype(bf16)
            value_grad = val_ref[:, part] + nn(twice(keys), jnp.concatenate(state, axis=0))
            val_made[:, part] = (factor * value_grad).astype(bf16)
        out_copy(key_made, key_out, key_sems, group, at).start()
        out_copy(val_made, val_out, val_sems, group, at).start()

    groups(total, work)
    for group in range(total // WIDE):
        out_copy(key_made, key_out, key_sems, group, group * WIDE).wait()
        out_copy(val_made, val_out, val_sems, group, group * WIDE).wait()


def outer_call(factor, key_part, value_part, keys, values, k_mask, high, low):
    length, total = values.shape
    block = (length, total)
    return kernel_call(
        functools.partial(outer_kernel, factor),
        "VVVVVVV",
        (key_part, value_part, keys, values, k_mask, high, low),
        "HH",
        [(block, bf16)] * 2,
        "outer",
        (8 * length * total * HEAD, 20 * length * total),
        [pltpu.VMEM(block, bf16)] * 2 + [pltpu.SemaphoreType.DMA((total // WIDE,))] * 2,
    )


def halves(state):
    high = state.astype(bf16)
    return high, (state - high.astype(f32)).astype(bf16)


def scan_any(own, sent, count, reverse):
    place = lax.axis_index(CTX)
    total = own
    state = jnp.zeros_like(own)
    bits = count.bit_length() - 1
    for bit in range(bits):
        step = 1 << bit
        last = bit == bits - 1
        pairs = []
        for source in range(count):
            high = bool(source & step)
            if not last or high == reverse:
                pairs.append((source, source ^ step))
        got = lax.ppermute(sent, CTX, pairs).astype(f32)
        if last:
            state = state + got
        else:
            mine = ((place // step) % 2) == (0 if reverse else 1)
            state = state + jnp.where(mine, got, 0.0)
            total = total + got
            sent = total.astype(bf16)
    return state


def links(first, keep=lambda source, target: True):
    pairs = []
    for chip in range(4):
        for core in range(2):
            other = chip ^ (first if core == 0 else 3 - first)
            if keep((chip, core), other):
                pairs.append((chip * 2 + core, other * 2 + core))
    return pairs


def upward(reverse):
    flip = 3 if reverse else 0

    def keep(source, target):
        at = source[0] ^ flip
        return source[0] ^ target == 1 or not at & 2

    return keep


def low_bit(reverse):
    chip = lax.axis_index("chip")
    return 1 - chip % 2 if reverse else chip % 2


def between_kernel(reverse, got_ref, own_ref, *refs):
    core = lax.axis_index("core")
    adds = jnp.where((core == 0) | (low_bit(reverse) == 0), 1.0, 0.0)
    refs[-1][...] = (got_ref[...].astype(f32) + adds * own_ref[...]).astype(bf16)


def chips_kernel(reverse, got_ref, more_ref, own_ref, *refs):
    core = lax.axis_index("core")
    adds = jnp.where((core == 1) | (low_bit(reverse) == 1), 1.0, 0.0)
    mine = adds * got_ref[...].astype(f32) + more_ref[...].astype(f32)
    gives = jnp.where(core == (1 if reverse else 0), 1.0, 0.0)
    refs[-2][...] = mine
    refs[-1][...] = mine + gives * own_ref[...]


def add_kernel(mine_ref, other_ref, high_ref, low_ref):
    whole = mine_ref[...] + other_ref[...]
    high = whole.astype(bf16)
    high_ref[...] = high
    low_ref[...] = (whole - high.astype(f32)).astype(bf16)


def send_first(sent, reverse):
    return lax.ppermute(sent, CTX, links(1, upward(reverse)))


def send_second(got, own, reverse, others=()):
    (message,) = kernel_call(
        functools.partial(between_kernel, reverse),
        "VV" + "A" * len(others),
        (got, own, *others),
        "V",
        [(own.shape, bf16)],
        "message",
        (0, 0),
    )
    return lax.ppermute(message, CTX, links(2, upward(reverse)))


def add_cores(got, more, own, reverse, others=()):
    mine, gives = kernel_call(
        functools.partial(chips_kernel, reverse),
        "VVV" + "A" * len(others),
        (got, more, own, *others),
        "VV",
        [(own.shape, f32)] * 2,
        "chips",
        (0, 0),
    )
    other = lax.ppermute(gives, "core", SWAP)
    return kernel_call(
        add_kernel, "VV", (mine, other), "VV", [(own.shape, bf16)] * 2, "whole", (0, 0)
    )


def gather_any(q_weight):
    whole = lax.all_gather(q_weight, ("chip", "core", "dp"), axis=0, tiled=True)
    cut = whole.shape[0] // (2 * PIECE) * PIECE
    return [whole[:cut], whole[cut:]]


def pack_kernel(*refs):
    *arrays, out_ref, sems = refs
    copies = Copies(sems)
    rows = out_ref.shape[0] // len(arrays)
    going = [
        copies.start(array, out_ref.at[pl.ds(at * rows, rows), :])
        for at, array in enumerate(arrays)
    ]
    for copy in going:
        copy.wait()


def pack(*arrays):
    rows, total = arrays[0].shape
    number = len(arrays)
    (made,) = kernel_call(
        pack_kernel,
        "A" * number,
        arrays,
        "V",
        [((number * rows, total), arrays[0].dtype)],
        "pack",
        (0, 0),
        [pltpu.SemaphoreType.DMA((number,))],
    )
    return [made, lax.ppermute(made, "core", SWAP)]


def choose_kernel(inner_ref, end_ref, out_ref, sem):
    del end_ref
    layer = lax.axis_index("dp")

    @pl.when((layer == 1) | (layer == 2))
    def _():
        copy = pltpu.make_async_copy(inner_ref, out_ref, sem)
        copy.start()
        copy.wait()


def choose(inner, end):
    return kernel_call(
        choose_kernel,
        "AA",
        (fast(inner), fast(end)),
        "A",
        [(inner.shape, inner.dtype)],
        "choose",
        (0, 0),
        [pltpu.SemaphoreType.DMA],
        {1: 0},
    )[0]


def per_device(tokens, key_input, values, q_weight, q_spikes, k_spikes, cotangent):
    batches, length, width = tokens.shape
    assert batches == 1
    total = q_weight.shape[1]
    chips, spread = lax.axis_size("chip"), lax.axis_size("dp")
    factor = 3.0 / math.sqrt(HEAD * length * chips * 2)
    tokens, key_input, values, q_spikes, k_spikes, cotangent = (
        array.reshape(length, array.shape[2])
        for array in (tokens, key_input, values, q_spikes, k_spikes, cotangent)
    )
    special = chips == 4 and spread == 4

    def sibling(array):
        return lax.ppermute(array, "core", SWAP)

    def along(array, pairs):
        return lax.ppermute(array, "dp", pairs)

    def cross(array):
        return lax.ppermute(array, CTX, links(1)), lax.ppermute(array, CTX, links(2))

    def onward(array):
        return lax.ppermute(array, CTX, links(2))

    keys, k_mask, values, own, sent, tokens = memory_call(
        special, key_input, k_spikes, values, tokens
    )
    if special:
        ends = [(0, 1), (1, 0), (2, 3), (3, 2)]
        middle = [(1, 2), (2, 1)]
        outward = [(1, 0), (2, 3)]
        near = along(q_weight, ends)
        mid = along(q_weight, middle)
        first_0, second_0 = cross(q_weight)
        near, mid, first_0, second_0, sent = join([near, mid, first_0, second_0, sent])
    else:
        arrived = gather_any(q_weight)
        high, low = halves(scan_any(own, sent, chips * 2, False))

    if special:
        third_0 = onward(first_0)
        first_1, second_1 = cross(near)
        far = along(near, middle)
        mid_out = along(mid, outward)
        got = send_first(sent, False)
        third_0, first_1, second_1, far, mid_out, got = join(
            [third_0, first_1, second_1, far, mid_out, got]
        )
        third_1 = onward(first_1)
        next_layer = choose(mid, mid_out)
        first_2, second_2 = cross(next_layer)
        far_out = along(far, outward)
        more = send_second(got, own, False)
        own_blocks = pack(q_weight, first_0, second_0, third_0)
        partial, _, own_mark = products_call(special, 0, own_blocks, tokens)
        third_1, first_2, second_2, far_out, more = join(
            [third_1, first_2, second_2, far_out, more], [own_mark]
        )
        third_2 = onward(first_2)
        last_layer = choose(far, far_out)
        first_3, second_3 = cross(last_layer)

        high, low = add_cores(got, more, own, False)
        masked, q_mask, cotangent, _ = masked_call(
            factor, cotangent, q_spikes, values, keys, high, low
        )
        _, grad, mark_0 = products_call(
            special, 0, own_blocks, tokens, masked=masked, project=False
        )
        blocks = pack(near, first_1, second_1, third_1)
        partial, grad, mark_1 = products_call(
            special, 8, blocks, tokens, partial, masked, grad
        )
        third_2, first_3, second_3 = join([third_2, first_3, second_3], [mark_0, mark_1])
        third_3 = onward(first_3)
        blocks = pack(next_layer, first_2, second_2, third_2)
        partial, grad, mark = products_call(
            special, 16, blocks, tokens, partial, masked, grad
        )
        third_3, = join([third_3], [mark])
        blocks = pack(last_layer, first_3, second_3)
        partial, grad, _ = products_call(special, 24, blocks, tokens, partial, masked, grad)
        late = [third_3, sibling(third_3)]
        start = 30
    else:
        masked, q_mask, cotangent, _ = masked_call(
            factor, cotangent, q_spikes, values, keys, high, low
        )
        start = arrived[0].shape[0] // PIECE
        partial, grad, _ = products_call(special, 0, arrived[:1], tokens, masked=masked)
        late = arrived[1:]
    queries, own, sent = query_call(start, tokens, late, partial, q_mask, cotangent)
    attended, attended_mark = attend_call(factor, queries, keys, values, high, low)
    key_part, value_part, inner_mark = inner_call(queries, keys, values, cotangent)
    if special:
        got = send_first(sent, True)
        more = send_second(got, own, True, [attended_mark])
        adjoint = add_cores(got, more, own, True, [inner_mark])
    else:
        adjoint = halves(scan_any(own, sent, chips * 2, True))
    _, grad_tokens, _ = products_call(
        special, start, late, tokens, masked=masked, grad=grad, project=False
    )
    grad_keys, grad_values = outer_call(
        factor, key_part, value_part, keys, values, k_mask, *adjoint
    )
    return tuple(
        array.reshape(1, length, array.shape[1])
        for array in (attended, grad_tokens, grad_keys, grad_values)
    )


def solution(mesh):
    count, spread = mesh.shape["ctx"], mesh.shape["dp"]
    fine = Mesh(mesh.devices.reshape(count // 2, 2, spread), ("chip", "core", "dp"))
    block = P("dp", CTX, None)
    rows = P(("chip", "core", "dp"), None)
    in_specs = (block, block, block, rows, block, block, block)
    return jax.shard_map(
        per_device, mesh=fine, in_specs=in_specs, out_specs=(block,) * 4, check_vma=False
    )
```

```python
import functools
import math

import jax
import jax.numpy as jnp
from jax import lax
from jax.experimental import pallas as pl
from jax.experimental.pallas import tpu as pltpu
from jax.sharding import Mesh, PartitionSpec as P

HEAD = 128
PIECE = 128
WIDE = 512
CTX = ("chip", "core")
SWAP = [(0, 1), (1, 0)]
f32, bf16 = jnp.float32, jnp.bfloat16
VMEM_LIMIT = 18 * 1024 * 1024


def nn(a, b):
    return lax.dot_general(a, b, (((1,), (0,)), ((), ())), preferred_element_type=f32)


def nt(a, b):
    return lax.dot_general(a, b, (((1,), (1,)), ((), ())), preferred_element_type=f32)


def tn(a, b):
    return lax.dot_general(a, b, (((0,), (0,)), ((), ())), preferred_element_type=f32)


def params(flops, moved):
    return dict(
        compiler_params=pltpu.CompilerParams(vmem_limit_bytes=VMEM_LIMIT),
        cost_estimate=pl.CostEstimate(flops=flops, bytes_accessed=moved, transcendentals=0),
    )


MARK = jax.ShapeDtypeStruct((8, HEAD), f32)


def set_mark(mark_ref):
    mark_ref[...] = jnp.zeros_like(mark_ref)


def fast(array):
    return pltpu.with_memory_space_constraint(array, pltpu.VMEM)


def slow(array):
    return pltpu.with_memory_space_constraint(array, pltpu.HBM)


def specs(places):
    spaces = dict(V=pltpu.VMEM, H=pltpu.HBM, S=pltpu.SMEM, A=pl.ANY)
    return [pl.BlockSpec(memory_space=spaces[place]) for place in places]


def kernel_call(body, places, args, out_places, outs, name, cost, scratch=(), aliases=None):
    holds = dict(V=fast, H=slow)
    made = pl.pallas_call(
        body,
        in_specs=specs(places),
        out_specs=specs(out_places),
        out_shape=[
            pltpu.VMEM(shape, dtype) if place == "V" else jax.ShapeDtypeStruct(shape, dtype)
            for place, (shape, dtype) in zip(out_places, outs)
        ],
        scratch_shapes=list(scratch),
        input_output_aliases=aliases or {},
        name=name,
        **params(*cost),
    )
    return made(
        *[holds[place](one) if place in holds else one for place, one in zip(places, args)]
    )


class Copies:
    def __init__(self, sems):
        self.sems = sems
        self.used = 0

    def start(self, source, target):
        copy = pltpu.make_async_copy(source, target, self.sems.at[self.used])
        self.used += 1
        copy.start()
        return copy


def crossed(side):
    return (0, 1 + side, 2 - side, 3)


def all_places(special, number):
    if not special:
        return list(range(number))
    chip, core, layer = (lax.axis_index(name) for name in ("chip", "core", "dp"))
    upper = layer < 2
    layers = [layer, layer ^ 1, jnp.where(upper, 2, 1), jnp.where(upper, 3, 0)]

    def some(*arrivals):
        return [
            ((chip ^ crossed(side)[flip]) * 2 + side) * 4 + layers[one]
            for side in (core, 1 - core)
            for one, flips in arrivals
            for flip in flips
        ]

    three = (0, 1, 2)
    return (
        some((0, (0, 1, 2, 3)), (1, three))
        + some((2, three))
        + some((1, (3,)), (2, (3,)), (3, three))
        + some((3, (3,)))
    )


def piece_columns(place):
    return (slice(None), pl.ds(pl.multiple_of(place * PIECE, PIECE), PIECE))


def columns(at, wide=None):
    return (slice(None), pl.ds(at, wide or WIDE))


def groups(total, body):
    @pl.loop(0, total // WIDE)
    def _(group):
        body(group, pl.multiple_of(group * WIDE, WIDE))


def heads(at):
    return [pl.ds(pl.multiple_of(at + head, HEAD), HEAD) for head in range(0, WIDE, HEAD)]


def memory_kernel(
    special, key_ref, spike_ref, value_ref, tokens_ref,
    keys_ref, mask_ref, values_ref, own_ref, sent_ref, some_ref,
    key_in, spike_in, sems,
):
    copies = Copies(sems)
    wide = range(0, keys_ref.shape[1], WIDE)
    pairs = ((key_ref, key_in), (spike_ref, spike_in), (value_ref, values_ref))
    parts = [
        [copies.start(here.at[columns(at)], there.at[columns(at)]) for here, there in pairs]
        for at in wide
    ]
    places = all_places(special, some_ref.shape[1] // PIECE)
    ordered = [
        copies.start(tokens_ref.at[piece_columns(place)], some_ref.at[piece_columns(piece)])
        for piece, place in enumerate(places)
    ]
    for at, part in zip(wide, parts):
        for copy in part:
            copy.wait()
        cols = slice(at, at + WIDE)
        mask = spike_in[:, cols].astype(f32).astype(bf16)
        keys = key_in[:, cols] * mask
        keys_ref[:, cols] = keys
        mask_ref[:, cols] = mask
        for head in range(0, WIDE, HEAD):
            here = slice(at + head, at + head + HEAD)
            own = tn(keys[:, head : head + HEAD], values_ref[:, here])
            own_ref[here, :] = own
            sent_ref[here, :] = own.astype(bf16)
    for copy in ordered:
        copy.wait()


def memory_call(special, key_input, k_spikes, values, tokens):
    length, total = values.shape
    block, state = (length, total), (total, HEAD)
    return kernel_call(
        functools.partial(memory_kernel, special),
        "HHHH",
        (key_input, k_spikes, values, tokens),
        "VVVVVV",
        [(block, bf16)] * 3 + [(state, f32), (state, bf16), (tokens.shape, bf16)],
        "own_memory",
        (2 * length * total * HEAD, 12 * length * total),
        [
            pltpu.VMEM(block, bf16),
            pltpu.VMEM(block, jnp.int32),
            pltpu.SemaphoreType.DMA((3 * total // WIDE + tokens.shape[1] // PIECE,)),
        ],
    )


def join_kernel(*refs):
    del refs


def join(arrays, others=()):
    number = len(arrays)
    return kernel_call(
        join_kernel,
        ["A"] * (number + len(others)),
        (*[fast(one) for one in arrays], *others),
        ["A"] * number,
        [(one.shape, one.dtype) for one in arrays],
        "join",
        (0, 0),
        aliases={at: at for at in range(number)},
    )


def keep_lower(square, flipped=False):
    row = lax.broadcasted_iota(jnp.int32, square.shape, 0)
    col = lax.broadcasted_iota(jnp.int32, square.shape, 1)
    return jnp.where((col >= row) if flipped else (col <= row), square, 0.0).astype(bf16)


def causal(a, b):
    length = a.shape[0]
    cut = length - HEAD
    top = keep_lower(nt(a[:cut], b[:cut]))
    whole = nt(a[cut:], b)
    bottom = jnp.concatenate([whole[:, :cut].astype(bf16), keep_lower(whole[:, cut:])], axis=1)
    return [(slice(0, cut), slice(0, cut), top), (slice(cut, length), slice(0, length), bottom)]


def causal_turned(a, b):
    length = a.shape[0]
    whole = nt(a[:HEAD], b)
    top = jnp.concatenate(
        [keep_lower(whole[:, :HEAD], True), whole[:, HEAD:].astype(bf16)], axis=1
    )
    bottom = keep_lower(nt(a[HEAD:], b[HEAD:]), True)
    return [
        (slice(0, HEAD), slice(0, length), top),
        (slice(HEAD, length), slice(HEAD, length), bottom),
    ]


def twice(array):
    return jnp.concatenate([array, array], axis=1)


def masked_kernel(
    factor, grad_ref, spike_ref, value_ref, keys_ref, high_ref, low_ref,
    out_ref, mask_ref, grads_ref, mark_ref, spike_in, sems,
):
    set_mark(mark_ref)
    total = out_ref.shape[1]

    def copies(group, at):
        return [
            pltpu.make_async_copy(grad_ref.at[columns(at)], grads_ref.at[columns(at)], sems.at[0, group]),
            pltpu.make_async_copy(spike_ref.at[columns(at)], spike_in.at[columns(at)], sems.at[1, group]),
        ]

    for group in range(total // WIDE):
        for copy in copies(group, group * WIDE):
            copy.start()

    def work(group, at):
        for copy in copies(group, at):
            copy.wait()
        for part in heads(at):
            mask = spike_in[:, part].astype(f32)
            mask_ref[:, part] = mask.astype(bf16)
            grad, value, keys = grads_ref[:, part], value_ref[:, part], keys_ref[:, part]
            state = jnp.concatenate([high_ref[part, :], low_ref[part, :]], axis=1)
            for rows, cols, scores in causal(grad, value):
                made = nn(scores, keys[cols]) + nt(twice(grad[rows]), state)
                out_ref[rows, part] = (factor * made * mask[rows]).astype(bf16)

    groups(total, work)


def masked_call(factor, cotangent, q_spikes, values, keys, high, low):
    length, total = values.shape
    block = (length, total)
    return kernel_call(
        functools.partial(masked_kernel, factor),
        "HHVVVV",
        (cotangent, q_spikes, values, keys, high, low),
        "VVVV",
        [(block, bf16)] * 3 + [(MARK.shape, f32)],
        "masked_grad",
        (8 * length * total * length, 12 * length * total),
        [pltpu.VMEM(block, jnp.int32), pltpu.SemaphoreType.DMA((2, total // WIDE))],
    )


def rows_of(blocks):
    return sum(block.shape[0] for block in blocks)


def back_blocks(blocks):
    at = 0
    for block in blocks:
        for row in range(0, block.shape[0], PIECE):
            yield at, block[row : row + PIECE, :]
            at += 1


def back_part(copies, places, masked, blocks, out_ref, round_ref):
    going = []
    pieces = list(back_blocks(blocks))
    for (first, upper), (second, lower) in zip(pieces[::2], pieces[1::2]):
        both = slice(first * PIECE, (second + 1) * PIECE)
        made = nt(masked[...], jnp.concatenate([upper, lower], axis=0))
        round_ref[:, both] = made.astype(bf16)
        for piece in (first, second):
            going.append(
                copies.start(
                    round_ref.at[piece_columns(piece)], out_ref.at[piece_columns(places[piece])]
                )
            )
    return going


def products_kernel(special, start, size, project, back, has_sum, has_back, *refs):
    blocks, refs = refs[:size], list(refs[size:])
    depth = rows_of(blocks)
    tokens_ref = refs.pop(0) if project else None
    before_ref = refs.pop(0) if has_sum else None
    masked = refs.pop(0) if back else None
    if has_back:
        refs.pop(0)
    sum_ref = refs.pop(0) if project else None
    back_out = refs.pop(0) if back else None
    mark_ref = refs.pop(0)
    set_mark(mark_ref)
    going = []
    if back:
        round_ref, sems = refs
        places = all_places(special, back_out.shape[1] // PIECE)[start:]
        going = back_part(Copies(sems), places, masked, blocks, back_out, round_ref)
    if project:
        cols = slice(start * PIECE, start * PIECE + depth)
        for at in range(0, sum_ref.shape[1], WIDE):
            part = slice(at, at + WIDE)
            made = nn(
                tokens_ref[:, cols],
                jnp.concatenate([block[:, part] for block in blocks], axis=0),
            )
            if has_sum:
                made = made + before_ref[:, part]
            sum_ref[:, part] = made
    for copy in going:
        copy.wait()


def products_call(
    special, start, blocks, tokens, partial=None, masked=None, grad=None, project=True
):
    length, width = tokens.shape
    total = blocks[0].shape[1]
    depth = rows_of(blocks)
    back = masked is not None
    places_in, args = "V" * len(blocks), list(blocks)
    places_out, outs = "", []
    scratch, aliases = [], {}
    if project:
        places_in, args = places_in + "V", args + [tokens]
        if partial is not None:
            aliases[len(args)] = 0
            places_in, args = places_in + "V", args + [partial]
        places_out, outs = "V", [((length, total), f32)]
    if back:
        places_in, args = places_in + "V", args + [masked]
        if grad is not None:
            aliases[len(args)] = len(outs)
            places_in, args = places_in + "H", args + [grad]
        places_out, outs = places_out + "H", outs + [((length, width), bf16)]
        scratch = [
            pltpu.VMEM((length, depth), bf16), pltpu.SemaphoreType.DMA((depth // PIECE,))
        ]
    made = kernel_call(
        functools.partial(
            products_kernel, special, start, len(blocks), project, back,
            partial is not None, grad is not None,
        ),
        places_in,
        args,
        places_out + "V",
        outs + [(MARK.shape, f32)],
        "products" if project and back else "project" if project else "grad_tokens",
        (2 * (project + back) * length * depth * total, 0),
        scratch,
        aliases,
    )
    made = list(made)
    partial = made.pop(0) if project else partial
    grad = made.pop(0) if back else grad
    return partial, grad, made[0]


def query_kernel(start, size, tokens_ref, sum_ref, mask_ref, grad_ref, *refs):
    blocks = refs[:size]
    queries, own_ref, sent_ref = refs[size:]
    cols = slice(start * PIECE, start * PIECE + rows_of(blocks))
    for at in range(0, queries.shape[1], WIDE):
        part = slice(at, at + WIDE)
        made = nn(
            tokens_ref[:, cols], jnp.concatenate([block[:, part] for block in blocks], axis=0)
        )
        made = made + sum_ref[:, part]
        made = (made * mask_ref[:, part].astype(f32)).astype(bf16)
        queries[:, part] = made
        for head in range(0, WIDE, HEAD):
            here = slice(at + head, at + head + HEAD)
            own = tn(made[:, head : head + HEAD], grad_ref[:, here])
            own_ref[here, :] = own
            sent_ref[here, :] = own.astype(bf16)


def query_call(start, tokens, blocks, before, q_mask, cotangent):
    length = tokens.shape[0]
    total = blocks[0].shape[1]
    depth = rows_of(blocks)
    return kernel_call(
        functools.partial(query_kernel, start, len(blocks)),
        "VVVV" + "V" * len(blocks),
        (tokens, before, q_mask, cotangent, *blocks),
        "VVV",
        [((length, total), bf16), ((total, HEAD), f32), ((total, HEAD), bf16)],
        "queries",
        (2 * length * depth * total, 0),
    )


def out_copy(here, there, sems, group, at):
    return pltpu.make_async_copy(here.at[columns(at)], there.at[columns(at)], sems.at[group])


def attend_kernel(
    factor, query_ref, keys_ref, value_ref, high_ref, low_ref, out_ref, mark_ref, made_ref, sems
):
    set_mark(mark_ref)
    total = query_ref.shape[1]

    def work(group, at):
        for part in heads(at):
            query, keys, value = query_ref[:, part], keys_ref[:, part], value_ref[:, part]
            state = [high_ref[part, :], low_ref[part, :]]
            for rows, cols, scores in causal(query, keys):
                made = nn(
                    jnp.concatenate([scores, twice(query[rows])], axis=1),
                    jnp.concatenate([value[cols], *state], axis=0),
                )
                made_ref[rows, part] = (factor * made).astype(bf16)
        out_copy(made_ref, out_ref, sems, group, at).start()

    groups(total, work)
    for group in range(total // WIDE):
        out_copy(made_ref, out_ref, sems, group, group * WIDE).wait()


def attend_call(factor, queries, keys, values, high, low):
    length, total = values.shape
    return kernel_call(
        functools.partial(attend_kernel, factor),
        "VVVVV",
        (queries, keys, values, high, low),
        "HV",
        [((length, total), bf16), (MARK.shape, f32)],
        "attended",
        (8 * length * total * length, 8 * length * total),
        [pltpu.VMEM((length, total), bf16), pltpu.SemaphoreType.DMA((total // WIDE,))],
    )


def inner_kernel(query_ref, keys_ref, value_ref, grad_ref, key_ref, val_ref, mark_ref):
    set_mark(mark_ref)

    def work(group, at):
        for part in heads(at):
            query, keys = query_ref[:, part], keys_ref[:, part]
            value, grad = value_ref[:, part], grad_ref[:, part]
            for rows, cols, scores in causal_turned(keys, query):
                val_ref[rows, part] = nn(scores, grad[cols])
            for rows, cols, scores in causal_turned(value, grad):
                key_ref[rows, part] = nn(scores, query[cols])

    groups(query_ref.shape[1], work)


def inner_call(queries, keys, values, cotangent):
    length, total = values.shape
    block = (length, total)
    return kernel_call(
        inner_kernel,
        "VVVV",
        (queries, keys, values, cotangent),
        "VVV",
        [(block, f32), (block, f32), (MARK.shape, f32)],
        "inner",
        (12 * length * total * length, 16 * length * total),
    )


def outer_kernel(
    factor, key_ref, val_ref, keys_ref, value_ref, mask_ref, high_ref, low_ref,
    key_out, val_out, key_made, val_made, key_sems, val_sems,
):
    total = keys_ref.shape[1]

    def work(group, at):
        for part in heads(at):
            keys, value = keys_ref[:, part], value_ref[:, part]
            state = [high_ref[part, :], low_ref[part, :]]
            key_grad = key_ref[:, part] + nt(twice(value), jnp.concatenate(state, axis=1))
            key_made[:, part] = (factor * key_grad * mask_ref[:, part].astype(f32)).astype(bf16)
            value_grad = val_ref[:, part] + nn(twice(keys), jnp.concatenate(state, axis=0))
            val_made[:, part] = (factor * value_grad).astype(bf16)
        out_copy(key_made, key_out, key_sems, group, at).start()
        out_copy(val_made, val_out, val_sems, group, at).start()

    groups(total, work)
    for group in range(total // WIDE):
        out_copy(key_made, key_out, key_sems, group, group * WIDE).wait()
        out_copy(val_made, val_out, val_sems, group, group * WIDE).wait()


def outer_call(factor, key_part, value_part, keys, values, k_mask, high, low):
    length, total = values.shape
    block = (length, total)
    return kernel_call(
        functools.partial(outer_kernel, factor),
        "VVVVVVV",
        (key_part, value_part, keys, values, k_mask, high, low),
        "HH",
        [(block, bf16)] * 2,
        "outer",
        (8 * length * total * HEAD, 20 * length * total),
        [pltpu.VMEM(block, bf16)] * 2 + [pltpu.SemaphoreType.DMA((total // WIDE,))] * 2,
    )


def halves(state):
    high = state.astype(bf16)
    return high, (state - high.astype(f32)).astype(bf16)


def scan_any(own, sent, count, reverse):
    place = lax.axis_index(CTX)
    total = own
    state = jnp.zeros_like(own)
    bits = count.bit_length() - 1
    for bit in range(bits):
        step = 1 << bit
        last = bit == bits - 1
        pairs = []
        for source in range(count):
            high = bool(source & step)
            if not last or high == reverse:
                pairs.append((source, source ^ step))
        got = lax.ppermute(sent, CTX, pairs).astype(f32)
        if last:
            state = state + got
        else:
            mine = ((place // step) % 2) == (0 if reverse else 1)
            state = state + jnp.where(mine, got, 0.0)
            total = total + got
            sent = total.astype(bf16)
    return state


def links(first, keep=lambda source, target: True):
    pairs = []
    for chip in range(4):
        for core in range(2):
            other = chip ^ (first if core == 0 else 3 - first)
            if keep((chip, core), other):
                pairs.append((chip * 2 + core, other * 2 + core))
    return pairs


def upward(reverse):
    flip = 3 if reverse else 0

    def keep(source, target):
        at = source[0] ^ flip
        return source[0] ^ target == 1 or not at & 2

    return keep


def low_bit(reverse):
    chip = lax.axis_index("chip")
    return 1 - chip % 2 if reverse else chip % 2


def half_rows(array_ref, core):
    half = array_ref.shape[0] // 2
    return array_ref[pl.ds(pl.multiple_of(core * half, half), half), :]


def both_kernel(own_ref, sibling_ref, both_ref, sent_ref):
    core = lax.axis_index("core")
    both = half_rows(own_ref, core) + half_rows(sibling_ref, core).astype(f32)
    both_ref[...] = both
    sent_ref[...] = both.astype(bf16)


def message_kernel(reverse, got_ref, both_ref, *refs):
    core = lax.axis_index("core")
    adds = jnp.where((core == 0) | (low_bit(reverse) == 0), 1.0, 0.0)
    refs[-1][...] = (got_ref[...].astype(f32) + adds * both_ref[...]).astype(bf16)


def state_kernel(reverse, got_ref, more_ref, *refs):
    core = lax.axis_index("core")
    adds = jnp.where((core == 1) | (low_bit(reverse) == 1), 1.0, 0.0)
    refs[-1][...] = adds * got_ref[...].astype(f32) + more_ref[...].astype(f32)


def whole_kernel(reverse, state_ref, other_ref, sibling_ref, high_ref, low_ref):
    core = lax.axis_index("core")
    adds = jnp.where(core == (0 if reverse else 1), 1.0, 0.0)
    half = state_ref.shape[0]
    for ref, side in ((state_ref, core), (other_ref, 1 - core)):
        rows = pl.ds(pl.multiple_of(side * half, half), half)
        whole = ref[...] + adds * sibling_ref[rows, :].astype(f32)
        high = whole.astype(bf16)
        high_ref[rows, :] = high
        low_ref[rows, :] = (whole - high.astype(f32)).astype(bf16)


def send_first(own, sent, reverse):
    half = (own.shape[0] // 2, HEAD)
    sibling = lax.ppermute(sent, "core", SWAP)
    both, sent = kernel_call(
        both_kernel, "VV", (own, sibling), "VV", [(half, f32), (half, bf16)], "both", (0, 0)
    )
    return sibling, both, lax.ppermute(sent, CTX, links(1, upward(reverse)))


def send_second(got, both, reverse, others=()):
    (message,) = kernel_call(
        functools.partial(message_kernel, reverse),
        "VV" + "A" * len(others),
        (got, both, *others),
        "V",
        [(both.shape, bf16)],
        "message",
        (0, 0),
    )
    return lax.ppermute(message, CTX, links(2, upward(reverse)))


def add_up(got, more, sibling, reverse, others=()):
    (state,) = kernel_call(
        functools.partial(state_kernel, reverse),
        "VV" + "A" * len(others),
        (got, more, *others),
        "V",
        [(got.shape, f32)],
        "state",
        (0, 0),
    )
    other = lax.ppermute(state, "core", SWAP)
    return kernel_call(
        functools.partial(whole_kernel, reverse),
        "VVV",
        (state, other, sibling),
        "VV",
        [(sibling.shape, bf16)] * 2,
        "whole",
        (0, 0),
    )


def gather_any(q_weight):
    whole = lax.all_gather(q_weight, ("chip", "core", "dp"), axis=0, tiled=True)
    cut = whole.shape[0] // (2 * PIECE) * PIECE
    return [whole[:cut], whole[cut:]]


def pack_kernel(*refs):
    *arrays, out_ref, sems = refs
    copies = Copies(sems)
    rows = out_ref.shape[0] // len(arrays)
    going = [
        copies.start(array, out_ref.at[pl.ds(at * rows, rows), :])
        for at, array in enumerate(arrays)
    ]
    for copy in going:
        copy.wait()


def pack(*arrays):
    rows, total = arrays[0].shape
    number = len(arrays)
    (made,) = kernel_call(
        pack_kernel,
        "A" * number,
        arrays,
        "V",
        [((number * rows, total), arrays[0].dtype)],
        "pack",
        (0, 0),
        [pltpu.SemaphoreType.DMA((number,))],
    )
    return [made, lax.ppermute(made, "core", SWAP)]


def choose_kernel(inner_ref, end_ref, out_ref, sem):
    del end_ref
    layer = lax.axis_index("dp")

    @pl.when((layer == 1) | (layer == 2))
    def _():
        copy = pltpu.make_async_copy(inner_ref, out_ref, sem)
        copy.start()
        copy.wait()


def choose(inner, end):
    return kernel_call(
        choose_kernel,
        "AA",
        (fast(inner), fast(end)),
        "A",
        [(inner.shape, inner.dtype)],
        "choose",
        (0, 0),
        [pltpu.SemaphoreType.DMA],
        {1: 0},
    )[0]


def per_device(tokens, key_input, values, q_weight, q_spikes, k_spikes, cotangent):
    batches, length, width = tokens.shape
    assert batches == 1
    total = q_weight.shape[1]
    chips, spread = lax.axis_size("chip"), lax.axis_size("dp")
    factor = 3.0 / math.sqrt(HEAD * length * chips * 2)
    tokens, key_input, values, q_spikes, k_spikes, cotangent = (
        array.reshape(length, array.shape[2])
        for array in (tokens, key_input, values, q_spikes, k_spikes, cotangent)
    )
    special = chips == 4 and spread == 4

    def sibling(array):
        return lax.ppermute(array, "core", SWAP)

    def along(array, pairs):
        return lax.ppermute(array, "dp", pairs)

    def cross(array):
        return lax.ppermute(array, CTX, links(1)), lax.ppermute(array, CTX, links(2))

    def onward(array):
        return lax.ppermute(array, CTX, links(2))

    keys, k_mask, values, own, sent, tokens = memory_call(
        special, key_input, k_spikes, values, tokens
    )
    if special:
        ends = [(0, 1), (1, 0), (2, 3), (3, 2)]
        middle = [(1, 2), (2, 1)]
        outward = [(1, 0), (2, 3)]
        near = along(q_weight, ends)
        mid = along(q_weight, middle)
        first_0, second_0 = cross(q_weight)
        near, mid, first_0, second_0, sent = join([near, mid, first_0, second_0, sent])
    else:
        arrived = gather_any(q_weight)
        high, low = halves(scan_any(own, sent, chips * 2, False))

    if special:
        third_0 = onward(first_0)
        first_1, second_1 = cross(near)
        far = along(near, middle)
        mid_out = along(mid, outward)
        twin, both, got = send_first(own, sent, False)
        third_0, first_1, second_1, far, mid_out, got = join(
            [third_0, first_1, second_1, far, mid_out, got]
        )
        more = send_second(got, both, False)
        next_layer = choose(mid, mid_out)
        first_2, second_2 = cross(next_layer)
        far_out = along(far, outward)
        early = pack(q_weight, first_0, second_0, third_0, near, first_1, second_1)
        partial, _, mark = products_call(special, 0, early, tokens)
        third_0, first_2, second_2, far_out, more = join(
            [third_0, first_2, second_2, far_out, more], [mark]
        )
        third_1 = along(third_0, ends)
        third_2 = onward(first_2)
        last_layer = choose(far, far_out)
        first_3, second_3 = cross(last_layer)
        high, low = add_up(got, more, twin, False)
        masked, q_mask, cotangent, _ = masked_call(
            factor, cotangent, q_spikes, values, keys, high, low
        )
        _, grad, mark_0 = products_call(
            special, 0, early, tokens, masked=masked, project=False
        )
        blocks = pack(next_layer, first_2, second_2)
        partial, grad, mark_1 = products_call(special, 14, blocks, tokens, partial, masked, grad)
        third_1, third_2, first_3, second_3 = join(
            [third_1, third_2, first_3, second_3], [mark_0, mark_1]
        )
        third_3 = onward(first_3)
        blocks = pack(third_1, third_2, last_layer, first_3, second_3)
        partial, grad, mark = products_call(special, 20, blocks, tokens, partial, masked, grad)
        third_3, = join([third_3], [mark])
        late = [third_3, sibling(third_3)]
        start = 30
    else:
        masked, q_mask, cotangent, _ = masked_call(
            factor, cotangent, q_spikes, values, keys, high, low
        )
        start = arrived[0].shape[0] // PIECE
        partial, grad, _ = products_call(special, 0, arrived[:1], tokens, masked=masked)
        late = arrived[1:]
    queries, own, sent = query_call(start, tokens, late, partial, q_mask, cotangent)
    attended, attended_mark = attend_call(factor, queries, keys, values, high, low)
    key_part, value_part, inner_mark = inner_call(queries, keys, values, cotangent)
    if special:
        twin, both, got = send_first(own, sent, True)
        more = send_second(got, both, True, [attended_mark])
        adjoint = add_up(got, more, twin, True, [inner_mark])
    else:
        adjoint = halves(scan_any(own, sent, chips * 2, True))
    _, grad_tokens, _ = products_call(
        special, start, late, tokens, masked=masked, grad=grad, project=False
    )
    grad_keys, grad_values = outer_call(
        factor, key_part, value_part, keys, values, k_mask, *adjoint
    )
    return tuple(
        array.reshape(1, length, array.shape[1])
        for array in (attended, grad_tokens, grad_keys, grad_values)
    )


def solution(mesh):
    count, spread = mesh.shape["ctx"], mesh.shape["dp"]
    fine = Mesh(mesh.devices.reshape(count // 2, 2, spread), ("chip", "core", "dp"))
    block = P("dp", CTX, None)
    rows = P(("chip", "core", "dp"), None)
    in_specs = (block, block, block, rows, block, block, block)
    return jax.shard_map(
        per_device, mesh=fine, in_specs=in_specs, out_specs=(block,) * 4, check_vma=False
    )
```

```python
import functools
import math

import jax
import jax.numpy as jnp
from jax import lax
from jax.experimental import pallas as pl
from jax.experimental.pallas import tpu as pltpu
from jax.sharding import Mesh, PartitionSpec as P

HEAD = 128
PIECE = 128
WIDE = 512
CTX = ("chip", "core")
SWAP = [(0, 1), (1, 0)]
f32, bf16 = jnp.float32, jnp.bfloat16
VMEM_LIMIT = 18 * 1024 * 1024


def nn(a, b):
    return lax.dot_general(a, b, (((1,), (0,)), ((), ())), preferred_element_type=f32)


def nt(a, b):
    return lax.dot_general(a, b, (((1,), (1,)), ((), ())), preferred_element_type=f32)


def tn(a, b):
    return lax.dot_general(a, b, (((0,), (0,)), ((), ())), preferred_element_type=f32)


def params(flops, moved):
    return dict(
        compiler_params=pltpu.CompilerParams(vmem_limit_bytes=VMEM_LIMIT),
        cost_estimate=pl.CostEstimate(flops=flops, bytes_accessed=moved, transcendentals=0),
    )


MARK = jax.ShapeDtypeStruct((8, HEAD), f32)


def set_mark(mark_ref):
    mark_ref[...] = jnp.zeros_like(mark_ref)


def fast(array):
    return pltpu.with_memory_space_constraint(array, pltpu.VMEM)


def slow(array):
    return pltpu.with_memory_space_constraint(array, pltpu.HBM)


def specs(places):
    spaces = dict(V=pltpu.VMEM, H=pltpu.HBM, S=pltpu.SMEM, A=pl.ANY)
    return [pl.BlockSpec(memory_space=spaces[place]) for place in places]


def kernel_call(body, places, args, out_places, outs, name, cost, scratch=(), aliases=None):
    holds = dict(V=fast, H=slow)
    made = pl.pallas_call(
        body,
        in_specs=specs(places),
        out_specs=specs(out_places),
        out_shape=[
            pltpu.VMEM(shape, dtype) if place == "V" else jax.ShapeDtypeStruct(shape, dtype)
            for place, (shape, dtype) in zip(out_places, outs)
        ],
        scratch_shapes=list(scratch),
        input_output_aliases=aliases or {},
        name=name,
        **params(*cost),
    )
    return made(
        *[holds[place](one) if place in holds else one for place, one in zip(places, args)]
    )


class Copies:
    def __init__(self, sems):
        self.sems = sems
        self.used = 0

    def start(self, source, target):
        copy = pltpu.make_async_copy(source, target, self.sems.at[self.used])
        self.used += 1
        copy.start()
        return copy


def crossed(side):
    return (0, 1 + side, 2 - side, 3)


def all_places(special, number):
    if not special:
        return list(range(number))
    chip, core, layer = (lax.axis_index(name) for name in ("chip", "core", "dp"))
    upper = layer < 2
    layers = [layer, layer ^ 1, jnp.where(upper, 2, 1), jnp.where(upper, 3, 0)]

    def some(*arrivals):
        return [
            ((chip ^ crossed(side)[flip]) * 2 + side) * 4 + layers[one]
            for side in (core, 1 - core)
            for one, flips in arrivals
            for flip in flips
        ]

    three = (0, 1, 2)
    return (
        some((0, (0, 1, 2, 3)), (1, three))
        + some((2, three), (3, (0,)))
        + some((1, (3,)), (2, (3,)), (3, (1, 2)))
        + some((3, (3,)))
    )


def piece_columns(place):
    return (slice(None), pl.ds(pl.multiple_of(place * PIECE, PIECE), PIECE))


def columns(at, wide=None):
    return (slice(None), pl.ds(at, wide or WIDE))


def groups(total, body):
    @pl.loop(0, total // WIDE)
    def _(group):
        body(group, pl.multiple_of(group * WIDE, WIDE))


def heads(at):
    return [pl.ds(pl.multiple_of(at + head, HEAD), HEAD) for head in range(0, WIDE, HEAD)]


def memory_kernel(
    special, key_ref, spike_ref, value_ref, tokens_ref, grad_ref,
    keys_ref, mask_ref, values_ref, own_ref, sent_ref, some_ref, grads_ref,
    key_in, spike_in, sems,
):
    copies = Copies(sems)
    wide = range(0, keys_ref.shape[1], WIDE)
    pairs = ((key_ref, key_in), (spike_ref, spike_in), (value_ref, values_ref))
    parts = [
        [copies.start(here.at[columns(at)], there.at[columns(at)]) for here, there in pairs]
        for at in wide
    ]
    places = all_places(special, some_ref.shape[1] // PIECE)
    ordered = [
        copies.start(tokens_ref.at[piece_columns(place)], some_ref.at[piece_columns(piece)])
        for piece, place in enumerate(places)
    ]
    ordered.append(copies.start(grad_ref, grads_ref))
    for at, part in zip(wide, parts):
        for copy in part:
            copy.wait()
        cols = slice(at, at + WIDE)
        mask = spike_in[:, cols].astype(f32).astype(bf16)
        keys = key_in[:, cols] * mask
        keys_ref[:, cols] = keys
        mask_ref[:, cols] = mask
        for head in range(0, WIDE, HEAD):
            here = slice(at + head, at + head + HEAD)
            own = tn(keys[:, head : head + HEAD], values_ref[:, here])
            own_ref[here, :] = own
            sent_ref[here, :] = own.astype(bf16)
    for copy in ordered:
        copy.wait()


def memory_call(special, key_input, k_spikes, values, tokens, cotangent):
    length, total = values.shape
    block, state = (length, total), (total, HEAD)
    return kernel_call(
        functools.partial(memory_kernel, special),
        "HHHHH",
        (key_input, k_spikes, values, tokens, cotangent),
        "VVVVVVV",
        [(block, bf16)] * 3
        + [(state, f32), (state, bf16), (tokens.shape, bf16), (block, bf16)],
        "own_memory",
        (2 * length * total * HEAD, 12 * length * total),
        [
            pltpu.VMEM(block, bf16),
            pltpu.VMEM(block, jnp.int32),
            pltpu.SemaphoreType.DMA((3 * total // WIDE + tokens.shape[1] // PIECE + 1,)),
        ],
    )


def join_kernel(*refs):
    del refs


def join(arrays, others=()):
    number = len(arrays)
    return kernel_call(
        join_kernel,
        ["A"] * (number + len(others)),
        (*[fast(one) for one in arrays], *others),
        ["A"] * number,
        [(one.shape, one.dtype) for one in arrays],
        "join",
        (0, 0),
        aliases={at: at for at in range(number)},
    )


def keep_lower(square, flipped=False):
    row = lax.broadcasted_iota(jnp.int32, square.shape, 0)
    col = lax.broadcasted_iota(jnp.int32, square.shape, 1)
    return jnp.where((col >= row) if flipped else (col <= row), square, 0.0).astype(bf16)


def causal(a, b):
    length = a.shape[0]
    cut = length - HEAD
    top = keep_lower(nt(a[:cut], b[:cut]))
    whole = nt(a[cut:], b)
    bottom = jnp.concatenate([whole[:, :cut].astype(bf16), keep_lower(whole[:, cut:])], axis=1)
    return [(slice(0, cut), slice(0, cut), top), (slice(cut, length), slice(0, length), bottom)]


def causal_turned(a, b):
    length = a.shape[0]
    whole = nt(a[:HEAD], b)
    top = jnp.concatenate(
        [keep_lower(whole[:, :HEAD], True), whole[:, HEAD:].astype(bf16)], axis=1
    )
    bottom = keep_lower(nt(a[HEAD:], b[HEAD:]), True)
    return [
        (slice(0, HEAD), slice(0, length), top),
        (slice(HEAD, length), slice(HEAD, length), bottom),
    ]


def twice(array):
    return jnp.concatenate([array, array], axis=1)


def masked_kernel(
    factor, spike_ref, grad_ref, value_ref, keys_ref, high_ref, low_ref,
    out_ref, mask_ref, spike_in, sems,
):
    total = out_ref.shape[1]

    def bring(group, at):
        return pltpu.make_async_copy(
            spike_ref.at[columns(at)], spike_in.at[columns(at)], sems.at[group]
        )

    for group in range(total // WIDE):
        bring(group, group * WIDE).start()

    def work(group, at):
        bring(group, at).wait()
        for part in heads(at):
            mask = spike_in[:, part].astype(f32)
            mask_ref[:, part] = mask.astype(bf16)
            grad, value, keys = grad_ref[:, part], value_ref[:, part], keys_ref[:, part]
            state = jnp.concatenate([high_ref[part, :], low_ref[part, :]], axis=1)
            for rows, cols, scores in causal(grad, value):
                made = nn(scores, keys[cols]) + nt(twice(grad[rows]), state)
                out_ref[rows, part] = (factor * made * mask[rows]).astype(bf16)

    groups(total, work)


def masked_call(factor, q_spikes, cotangent, values, keys, high, low):
    length, total = values.shape
    block = (length, total)
    return kernel_call(
        functools.partial(masked_kernel, factor),
        "HVVVVV",
        (q_spikes, cotangent, values, keys, high, low),
        "VV",
        [(block, bf16)] * 2,
        "masked_grad",
        (8 * length * total * length, 12 * length * total),
        [pltpu.VMEM(block, jnp.int32), pltpu.SemaphoreType.DMA((total // WIDE,))],
    )


def turned_kernel(value_ref, grad_ref, after_ref, top_ref, bottom_ref, mark_ref):
    del after_ref
    set_mark(mark_ref)
    length, total = value_ref.shape
    rest = length - HEAD
    number = WIDE // HEAD

    def work(group, at):
        for head, part in enumerate(heads(at)):
            (_, _, top), (_, _, bottom) = causal_turned(value_ref[:, part], grad_ref[:, part])
            place = group * number + head
            top_ref[:, pl.ds(pl.multiple_of(place * length, HEAD), length)] = top
            bottom_ref[:, pl.ds(pl.multiple_of(place * rest, HEAD), rest)] = bottom

    groups(total, work)


def turned_call(values, cotangent, after):
    length, total = values.shape
    number, rest = total // HEAD, length - HEAD
    return kernel_call(
        turned_kernel,
        "VVA",
        (values, cotangent, after),
        "VVV",
        [((HEAD, number * length), bf16), ((rest, number * rest), bf16), (MARK.shape, f32)],
        "turned",
        (4 * length * total * length, 0),
    )


def rows_of(blocks):
    return sum(block.shape[0] for block in blocks)


def back_blocks(blocks):
    at = 0
    for block in blocks:
        for row in range(0, block.shape[0], PIECE):
            yield at, block[row : row + PIECE, :]
            at += 1


def back_part(copies, places, masked, blocks, out_ref, round_ref):
    going = []
    pieces = list(back_blocks(blocks))
    for (first, upper), (second, lower) in zip(pieces[::2], pieces[1::2]):
        both = slice(first * PIECE, (second + 1) * PIECE)
        made = nt(masked[...], jnp.concatenate([upper, lower], axis=0))
        round_ref[:, both] = made.astype(bf16)
        for piece in (first, second):
            going.append(
                copies.start(
                    round_ref.at[piece_columns(piece)], out_ref.at[piece_columns(places[piece])]
                )
            )
    return going


def products_kernel(special, start, size, project, back, has_sum, has_back, *refs):
    blocks, refs = refs[:size], list(refs[size:])
    depth = rows_of(blocks)
    tokens_ref = refs.pop(0) if project else None
    before_ref = refs.pop(0) if has_sum else None
    masked = refs.pop(0) if back else None
    if has_back:
        refs.pop(0)
    sum_ref = refs.pop(0) if project else None
    back_out = refs.pop(0) if back else None
    mark_ref = refs.pop(0)
    set_mark(mark_ref)
    going = []
    if back:
        round_ref, sems = refs
        places = all_places(special, back_out.shape[1] // PIECE)[start:]
        going = back_part(Copies(sems), places, masked, blocks, back_out, round_ref)
    if project:
        cols = slice(start * PIECE, start * PIECE + depth)
        for at in range(0, sum_ref.shape[1], WIDE):
            part = slice(at, at + WIDE)
            made = nn(
                tokens_ref[:, cols],
                jnp.concatenate([block[:, part] for block in blocks], axis=0),
            )
            if has_sum:
                made = made + before_ref[:, part]
            sum_ref[:, part] = made
    for copy in going:
        copy.wait()


def products_call(
    special, start, blocks, tokens, partial=None, masked=None, grad=None, project=True
):
    length, width = tokens.shape
    total = blocks[0].shape[1]
    depth = rows_of(blocks)
    back = masked is not None
    places_in, args = "V" * len(blocks), list(blocks)
    places_out, outs = "", []
    scratch, aliases = [], {}
    if project:
        places_in, args = places_in + "V", args + [tokens]
        if partial is not None:
            aliases[len(args)] = 0
            places_in, args = places_in + "V", args + [partial]
        places_out, outs = "V", [((length, total), f32)]
    if back:
        places_in, args = places_in + "V", args + [masked]
        if grad is not None:
            aliases[len(args)] = len(outs)
            places_in, args = places_in + "H", args + [grad]
        places_out, outs = places_out + "H", outs + [((length, width), bf16)]
        scratch = [
            pltpu.VMEM((length, depth), bf16), pltpu.SemaphoreType.DMA((depth // PIECE,))
        ]
    made = kernel_call(
        functools.partial(
            products_kernel, special, start, len(blocks), project, back,
            partial is not None, grad is not None,
        ),
        places_in,
        args,
        places_out + "V",
        outs + [(MARK.shape, f32)],
        "products" if project and back else "project" if project else "grad_tokens",
        (2 * (project + back) * length * depth * total, 0),
        scratch,
        aliases,
    )
    made = list(made)
    partial = made.pop(0) if project else partial
    grad = made.pop(0) if back else grad
    return partial, grad, made[0]


def query_kernel(start, size, tokens_ref, sum_ref, mask_ref, grad_ref, *refs):
    blocks = refs[:size]
    queries, own_ref, sent_ref = refs[-3:]
    cols = slice(start * PIECE, start * PIECE + rows_of(blocks))
    for at in range(0, queries.shape[1], WIDE):
        part = slice(at, at + WIDE)
        made = nn(
            tokens_ref[:, cols], jnp.concatenate([block[:, part] for block in blocks], axis=0)
        )
        made = made + sum_ref[:, part]
        made = (made * mask_ref[:, part].astype(f32)).astype(bf16)
        queries[:, part] = made
        for head in range(0, WIDE, HEAD):
            here = slice(at + head, at + head + HEAD)
            own = tn(made[:, head : head + HEAD], grad_ref[:, here])
            own_ref[here, :] = own
            sent_ref[here, :] = own.astype(bf16)


def query_call(start, tokens, blocks, before, q_mask, cotangent, others):
    length = tokens.shape[0]
    total = blocks[0].shape[1]
    depth = rows_of(blocks)
    return kernel_call(
        functools.partial(query_kernel, start, len(blocks)),
        "VVVV" + "V" * len(blocks) + "A" * len(others),
        (tokens, before, q_mask, cotangent, *blocks, *others),
        "VVV",
        [((length, total), bf16), ((total, HEAD), f32), ((total, HEAD), bf16)],
        "queries",
        (2 * length * depth * total, 0),
    )


def out_copy(here, there, sems, group, at):
    return pltpu.make_async_copy(here.at[columns(at)], there.at[columns(at)], sems.at[group])


def attend_kernel(
    factor, query_ref, keys_ref, value_ref, high_ref, low_ref, out_ref, mark_ref, made_ref, sems
):
    set_mark(mark_ref)
    total = query_ref.shape[1]

    def work(group, at):
        for part in heads(at):
            query, keys, value = query_ref[:, part], keys_ref[:, part], value_ref[:, part]
            state = [high_ref[part, :], low_ref[part, :]]
            for rows, cols, scores in causal(query, keys):
                made = nn(
                    jnp.concatenate([scores, twice(query[rows])], axis=1),
                    jnp.concatenate([value[cols], *state], axis=0),
                )
                made_ref[rows, part] = (factor * made).astype(bf16)
        out_copy(made_ref, out_ref, sems, group, at).start()

    groups(total, work)
    for group in range(total // WIDE):
        out_copy(made_ref, out_ref, sems, group, group * WIDE).wait()


def attend_call(factor, queries, keys, values, high, low):
    length, total = values.shape
    return kernel_call(
        functools.partial(attend_kernel, factor),
        "VVVVV",
        (queries, keys, values, high, low),
        "HV",
        [((length, total), bf16), (MARK.shape, f32)],
        "attended",
        (8 * length * total * length, 8 * length * total),
        [pltpu.VMEM((length, total), bf16), pltpu.SemaphoreType.DMA((total // WIDE,))],
    )


def value_kernel(query_ref, keys_ref, grad_ref, val_ref, mark_ref):
    set_mark(mark_ref)

    def work(group, at):
        for part in heads(at):
            query, keys, grad = query_ref[:, part], keys_ref[:, part], grad_ref[:, part]
            for rows, cols, scores in causal_turned(keys, query):
                val_ref[rows, part] = nn(scores, grad[cols])

    groups(query_ref.shape[1], work)


def value_call(queries, keys, cotangent):
    length, total = keys.shape
    return kernel_call(
        value_kernel,
        "VVV",
        (queries, keys, cotangent),
        "VV",
        [((length, total), f32), (MARK.shape, f32)],
        "value_part",
        (6 * length * total * length, 0),
    )


def key_kernel(query_ref, top_ref, bottom_ref, key_ref):
    length, total = query_ref.shape
    rest = length - HEAD
    number = WIDE // HEAD

    def work(group, at):
        for head, part in enumerate(heads(at)):
            query = query_ref[:, part]
            place = group * number + head
            top = top_ref[:, pl.ds(pl.multiple_of(place * length, HEAD), length)]
            bottom = bottom_ref[:, pl.ds(pl.multiple_of(place * rest, HEAD), rest)]
            key_ref[:HEAD, part] = nn(top, query)
            key_ref[HEAD:, part] = nn(bottom, query[HEAD:])

    groups(total, work)


def key_call(queries, top, bottom):
    length, total = queries.shape
    return kernel_call(
        key_kernel,
        "VVV",
        (queries, top, bottom),
        "V",
        [((length, total), f32)],
        "key_part",
        (4 * length * total * length, 0),
    )[0]


def outer_kernel(
    factor, key_ref, val_ref, keys_ref, value_ref, mask_ref, high_ref, low_ref,
    key_out, val_out, key_made, val_made, key_sems, val_sems,
):
    total = keys_ref.shape[1]

    def work(group, at):
        for part in heads(at):
            keys, value = keys_ref[:, part], value_ref[:, part]
            state = [high_ref[part, :], low_ref[part, :]]
            key_grad = key_ref[:, part] + nt(twice(value), jnp.concatenate(state, axis=1))
            key_made[:, part] = (factor * key_grad * mask_ref[:, part].astype(f32)).astype(bf16)
            value_grad = val_ref[:, part] + nn(twice(keys), jnp.concatenate(state, axis=0))
            val_made[:, part] = (factor * value_grad).astype(bf16)
        out_copy(key_made, key_out, key_sems, group, at).start()
        out_copy(val_made, val_out, val_sems, group, at).start()

    groups(total, work)
    for group in range(total // WIDE):
        out_copy(key_made, key_out, key_sems, group, group * WIDE).wait()
        out_copy(val_made, val_out, val_sems, group, group * WIDE).wait()


def outer_call(factor, key_part, value_part, keys, values, k_mask, high, low):
    length, total = values.shape
    block = (length, total)
    return kernel_call(
        functools.partial(outer_kernel, factor),
        "VVVVVVV",
        (key_part, value_part, keys, values, k_mask, high, low),
        "HH",
        [(block, bf16)] * 2,
        "outer",
        (8 * length * total * HEAD, 20 * length * total),
        [pltpu.VMEM(block, bf16)] * 2 + [pltpu.SemaphoreType.DMA((total // WIDE,))] * 2,
    )


def halves(state):
    high = state.astype(bf16)
    return high, (state - high.astype(f32)).astype(bf16)


def scan_any(own, sent, count, reverse):
    place = lax.axis_index(CTX)
    total = own
    state = jnp.zeros_like(own)
    bits = count.bit_length() - 1
    for bit in range(bits):
        step = 1 << bit
        last = bit == bits - 1
        pairs = []
        for source in range(count):
            high = bool(source & step)
            if not last or high == reverse:
                pairs.append((source, source ^ step))
        got = lax.ppermute(sent, CTX, pairs).astype(f32)
        if last:
            state = state + got
        else:
            mine = ((place // step) % 2) == (0 if reverse else 1)
            state = state + jnp.where(mine, got, 0.0)
            total = total + got
            sent = total.astype(bf16)
    return state


def links(first, keep=lambda source, target: True):
    pairs = []
    for chip in range(4):
        for core in range(2):
            other = chip ^ (first if core == 0 else 3 - first)
            if keep((chip, core), other):
                pairs.append((chip * 2 + core, other * 2 + core))
    return pairs


def upward(reverse):
    flip = 3 if reverse else 0

    def keep(source, target):
        at = source[0] ^ flip
        return source[0] ^ target == 1 or not at & 2

    return keep


def low_bit(reverse):
    chip = lax.axis_index("chip")
    return 1 - chip % 2 if reverse else chip % 2


def half_rows(array_ref, core):
    half = array_ref.shape[0] // 2
    return array_ref[pl.ds(pl.multiple_of(core * half, half), half), :]


def both_kernel(own_ref, sibling_ref, *refs):
    both_ref, sent_ref = refs[-2:]
    core = lax.axis_index("core")
    both = half_rows(own_ref, core) + half_rows(sibling_ref, core).astype(f32)
    both_ref[...] = both
    sent_ref[...] = both.astype(bf16)


def message_kernel(reverse, got_ref, both_ref, *refs):
    core = lax.axis_index("core")
    adds = jnp.where((core == 0) | (low_bit(reverse) == 0), 1.0, 0.0)
    refs[-1][...] = (got_ref[...].astype(f32) + adds * both_ref[...]).astype(bf16)


def state_kernel(reverse, got_ref, more_ref, *refs):
    core = lax.axis_index("core")
    adds = jnp.where((core == 1) | (low_bit(reverse) == 1), 1.0, 0.0)
    refs[-1][...] = adds * got_ref[...].astype(f32) + more_ref[...].astype(f32)


def whole_kernel(reverse, state_ref, other_ref, sibling_ref, high_ref, low_ref):
    core = lax.axis_index("core")
    adds = jnp.where(core == (0 if reverse else 1), 1.0, 0.0)
    half = state_ref.shape[0]
    for ref, side in ((state_ref, core), (other_ref, 1 - core)):
        rows = pl.ds(pl.multiple_of(side * half, half), half)
        whole = ref[...] + adds * sibling_ref[rows, :].astype(f32)
        high = whole.astype(bf16)
        high_ref[rows, :] = high
        low_ref[rows, :] = (whole - high.astype(f32)).astype(bf16)


def send_first(own, sent, reverse, others=()):
    half = (own.shape[0] // 2, HEAD)
    sibling = lax.ppermute(sent, "core", SWAP)
    both, sent = kernel_call(
        both_kernel,
        "VV" + "A" * len(others),
        (own, sibling, *others),
        "VV",
        [(half, f32), (half, bf16)],
        "both",
        (0, 0),
    )
    return sibling, both, lax.ppermute(sent, CTX, links(1, upward(reverse)))


def send_second(got, both, reverse, others=()):
    (message,) = kernel_call(
        functools.partial(message_kernel, reverse),
        "VV" + "A" * len(others),
        (got, both, *others),
        "V",
        [(both.shape, bf16)],
        "message",
        (0, 0),
    )
    return lax.ppermute(message, CTX, links(2, upward(reverse)))


def add_up(got, more, sibling, reverse, others=()):
    (state,) = kernel_call(
        functools.partial(state_kernel, reverse),
        "VV" + "A" * len(others),
        (got, more, *others),
        "V",
        [(got.shape, f32)],
        "state",
        (0, 0),
    )
    other = lax.ppermute(state, "core", SWAP)
    return kernel_call(
        functools.partial(whole_kernel, reverse),
        "VVV",
        (state, other, sibling),
        "VV",
        [(sibling.shape, bf16)] * 2,
        "whole",
        (0, 0),
    )


def gather_any(q_weight):
    whole = lax.all_gather(q_weight, ("chip", "core", "dp"), axis=0, tiled=True)
    cut = whole.shape[0] // (2 * PIECE) * PIECE
    return [whole[:cut], whole[cut:]]


def pack_kernel(*refs):
    *arrays, out_ref, sems = refs
    copies = Copies(sems)
    rows = out_ref.shape[0] // len(arrays)
    going = [
        copies.start(array, out_ref.at[pl.ds(at * rows, rows), :])
        for at, array in enumerate(arrays)
    ]
    for copy in going:
        copy.wait()


def pack(*arrays):
    rows, total = arrays[0].shape
    number = len(arrays)
    (made,) = kernel_call(
        pack_kernel,
        "A" * number,
        arrays,
        "V",
        [((number * rows, total), arrays[0].dtype)],
        "pack",
        (0, 0),
        [pltpu.SemaphoreType.DMA((number,))],
    )
    return [made, lax.ppermute(made, "core", SWAP)]


def choose_kernel(inner_ref, end_ref, out_ref, sem):
    del end_ref
    layer = lax.axis_index("dp")

    @pl.when((layer == 1) | (layer == 2))
    def _():
        copy = pltpu.make_async_copy(inner_ref, out_ref, sem)
        copy.start()
        copy.wait()


def choose(inner, end):
    return kernel_call(
        choose_kernel,
        "AA",
        (fast(inner), fast(end)),
        "A",
        [(inner.shape, inner.dtype)],
        "choose",
        (0, 0),
        [pltpu.SemaphoreType.DMA],
        {1: 0},
    )[0]


def per_device(tokens, key_input, values, q_weight, q_spikes, k_spikes, cotangent):
    batches, length, width = tokens.shape
    assert batches == 1
    total = q_weight.shape[1]
    chips, spread = lax.axis_size("chip"), lax.axis_size("dp")
    factor = 3.0 / math.sqrt(HEAD * length * chips * 2)
    tokens, key_input, values, q_spikes, k_spikes, cotangent = (
        array.reshape(length, array.shape[2])
        for array in (tokens, key_input, values, q_spikes, k_spikes, cotangent)
    )
    special = chips == 4 and spread == 4

    def sibling(array):
        return lax.ppermute(array, "core", SWAP)

    def along(array, pairs):
        return lax.ppermute(array, "dp", pairs)

    def cross(array):
        return lax.ppermute(array, CTX, links(1)), lax.ppermute(array, CTX, links(2))

    def onward(array):
        return lax.ppermute(array, CTX, links(2))

    keys, k_mask, values, own, sent, tokens, cotangent = memory_call(
        special, key_input, k_spikes, values, tokens, cotangent
    )
    if special:
        ends = [(0, 1), (1, 0), (2, 3), (3, 2)]
        middle = [(1, 2), (2, 1)]
        outward = [(1, 0), (2, 3)]
        near = along(q_weight, ends)
        mid = along(q_weight, middle)
        first_0, second_0 = cross(q_weight)
        near, mid, first_0, second_0, sent = join([near, mid, first_0, second_0, sent])
    else:
        arrived = gather_any(q_weight)
        high, low = halves(scan_any(own, sent, chips * 2, False))

    if special:
        third_0 = onward(first_0)
        first_1, second_1 = cross(near)
        far = along(near, middle)
        mid_out = along(mid, outward)
        twin, both, got = send_first(own, sent, False)
        third_0, first_1, second_1, far, mid_out, got = join(
            [third_0, first_1, second_1, far, mid_out, got]
        )
        more = send_second(got, both, False)
        next_layer = choose(mid, mid_out)
        first_2, second_2 = cross(next_layer)
        far_out = along(far, outward)
        early = pack(q_weight, first_0, second_0, third_0, near, first_1, second_1)
        partial, _, mark = products_call(special, 0, early, tokens)
        top, bottom, turned_mark = turned_call(values, cotangent, got)
        third_0, first_2, second_2, far_out, more = join(
            [third_0, first_2, second_2, far_out, more], [mark, turned_mark]
        )
        third_1 = along(third_0, ends)
        third_2 = onward(first_2)
        last_layer = choose(far, far_out)
        first_3, second_3 = cross(last_layer)
        high, low = add_up(got, more, twin, False)
        masked, q_mask = masked_call(factor, q_spikes, cotangent, values, keys, high, low)
        _, grad, mark_0 = products_call(
            special, 0, early, tokens, masked=masked, project=False
        )
        blocks = pack(next_layer, first_2, second_2, last_layer)
        partial, grad, mark_1 = products_call(special, 14, blocks, tokens, partial, masked, grad)
        third_1, third_2, first_3, second_3 = join(
            [third_1, third_2, first_3, second_3], [mark_0, mark_1]
        )
        third_3 = onward(first_3)
        blocks = pack(third_1, third_2, first_3, second_3)
        partial, _, mark = products_call(special, 22, blocks, tokens, partial)
        third_3, = join([third_3], [mark])
        _, grad, mark = products_call(
            special, 22, blocks, tokens, masked=masked, grad=grad, project=False
        )
        late = [third_3, sibling(third_3)]
        start = 30
    else:
        masked, q_mask = masked_call(factor, q_spikes, cotangent, values, keys, high, low)
        top, bottom, _ = turned_call(values, cotangent, own)
        start = arrived[0].shape[0] // PIECE
        partial, grad, mark = products_call(special, 0, arrived[:1], tokens, masked=masked)
        late = arrived[1:]
    queries, own, sent = query_call(start, tokens, late, partial, q_mask, cotangent, [mark])
    attended, attended_mark = attend_call(factor, queries, keys, values, high, low)
    value_part, value_mark = value_call(queries, keys, cotangent)
    key_part = key_call(queries, top, bottom)
    _, grad_tokens, back_mark = products_call(
        special, start, late, tokens, masked=masked, grad=grad, project=False
    )
    if special:
        twin, both, got = send_first(own, sent, True, [back_mark])
        more = send_second(got, both, True, [attended_mark])
        adjoint = add_up(got, more, twin, True, [value_mark])
    else:
        adjoint = halves(scan_any(own, sent, chips * 2, True))
    grad_keys, grad_values = outer_call(
        factor, key_part, value_part, keys, values, k_mask, *adjoint
    )
    return tuple(
        array.reshape(1, length, array.shape[1])
        for array in (attended, grad_tokens, grad_keys, grad_values)
    )


def solution(mesh):
    count, spread = mesh.shape["ctx"], mesh.shape["dp"]
    fine = Mesh(mesh.devices.reshape(count // 2, 2, spread), ("chip", "core", "dp"))
    block = P("dp", CTX, None)
    rows = P(("chip", "core", "dp"), None)
    in_specs = (block, block, block, rows, block, block, block)
    return jax.shard_map(
        per_device, mesh=fine, in_specs=in_specs, out_specs=(block,) * 4, check_vma=False
    )
```

```python
import functools
import math

import jax
import jax.numpy as jnp
from jax import lax
from jax.experimental import pallas as pl
from jax.experimental.pallas import tpu as pltpu
from jax.sharding import Mesh, PartitionSpec as P

HEAD = 128
PIECE = 128
WIDE = 512
CTX = ("chip", "core")
SWAP = [(0, 1), (1, 0)]
f32, bf16 = jnp.float32, jnp.bfloat16
VMEM_LIMIT = 18 * 1024 * 1024


def nn(a, b):
    return lax.dot_general(a, b, (((1,), (0,)), ((), ())), preferred_element_type=f32)


def nt(a, b):
    return lax.dot_general(a, b, (((1,), (1,)), ((), ())), preferred_element_type=f32)


def tn(a, b):
    return lax.dot_general(a, b, (((0,), (0,)), ((), ())), preferred_element_type=f32)


def params(flops, moved):
    return dict(
        compiler_params=pltpu.CompilerParams(vmem_limit_bytes=VMEM_LIMIT),
        cost_estimate=pl.CostEstimate(flops=flops, bytes_accessed=moved, transcendentals=0),
    )


MARK = jax.ShapeDtypeStruct((8, HEAD), f32)


def set_mark(mark_ref):
    mark_ref[...] = jnp.zeros_like(mark_ref)


def fast(array):
    return pltpu.with_memory_space_constraint(array, pltpu.VMEM)


def slow(array):
    return pltpu.with_memory_space_constraint(array, pltpu.HBM)


def specs(places):
    spaces = dict(V=pltpu.VMEM, H=pltpu.HBM, S=pltpu.SMEM, A=pl.ANY)
    return [pl.BlockSpec(memory_space=spaces[place]) for place in places]


def kernel_call(body, places, args, out_places, outs, name, cost, scratch=(), aliases=None):
    holds = dict(V=fast, H=slow)
    made = pl.pallas_call(
        body,
        in_specs=specs(places),
        out_specs=specs(out_places),
        out_shape=[
            pltpu.VMEM(shape, dtype) if place == "V" else jax.ShapeDtypeStruct(shape, dtype)
            for place, (shape, dtype) in zip(out_places, outs)
        ],
        scratch_shapes=list(scratch),
        input_output_aliases=aliases or {},
        name=name,
        **params(*cost),
    )
    return made(
        *[holds[place](one) if place in holds else one for place, one in zip(places, args)]
    )


class Copies:
    def __init__(self, sems):
        self.sems = sems
        self.used = 0

    def start(self, source, target):
        copy = pltpu.make_async_copy(source, target, self.sems.at[self.used])
        self.used += 1
        copy.start()
        return copy


def crossed(side):
    return (0, 1 + side, 2 - side, 3)


def all_places(special, number):
    if not special:
        return list(range(number))
    chip, core, layer = (lax.axis_index(name) for name in ("chip", "core", "dp"))
    upper = layer < 2
    layers = [layer, layer ^ 1, jnp.where(upper, 2, 1), jnp.where(upper, 3, 0)]

    def some(*arrivals):
        return [
            ((chip ^ crossed(side)[flip]) * 2 + side) * 4 + layers[one]
            for side in (core, 1 - core)
            for one, flips in arrivals
            for flip in flips
        ]

    three = (0, 1, 2)
    return (
        some((0, (0, 1, 2, 3)), (1, three))
        + some((2, three), (3, (0,)))
        + some((1, (3,)), (2, (3,)), (3, (1, 2)))
        + some((3, (3,)))
    )


def piece_columns(place):
    return (slice(None), pl.ds(pl.multiple_of(place * PIECE, PIECE), PIECE))


def columns(at, wide=None):
    return (slice(None), pl.ds(at, wide or WIDE))


def groups(total, body):
    @pl.loop(0, total // WIDE)
    def _(group):
        body(group, pl.multiple_of(group * WIDE, WIDE))


def heads(at):
    return [pl.ds(pl.multiple_of(at + head, HEAD), HEAD) for head in range(0, WIDE, HEAD)]


def memory_kernel(
    special, key_ref, spike_ref, value_ref, tokens_ref, grad_ref,
    keys_ref, mask_ref, values_ref, own_ref, sent_ref, some_ref, grads_ref,
    key_in, spike_in, sems,
):
    copies = Copies(sems)
    wide = range(0, keys_ref.shape[1], WIDE)
    pairs = ((key_ref, key_in), (spike_ref, spike_in), (value_ref, values_ref))
    parts = [
        [copies.start(here.at[columns(at)], there.at[columns(at)]) for here, there in pairs]
        for at in wide
    ]
    places = all_places(special, some_ref.shape[1] // PIECE)
    ordered = [
        copies.start(tokens_ref.at[piece_columns(place)], some_ref.at[piece_columns(piece)])
        for piece, place in enumerate(places)
    ]
    ordered.append(copies.start(grad_ref, grads_ref))
    for at, part in zip(wide, parts):
        for copy in part:
            copy.wait()
        cols = slice(at, at + WIDE)
        mask = spike_in[:, cols].astype(f32).astype(bf16)
        keys = key_in[:, cols] * mask
        keys_ref[:, cols] = keys
        mask_ref[:, cols] = mask
        for head in range(0, WIDE, HEAD):
            here = slice(at + head, at + head + HEAD)
            own = tn(keys[:, head : head + HEAD], values_ref[:, here])
            own_ref[here, :] = own
            sent_ref[here, :] = own.astype(bf16)
    for copy in ordered:
        copy.wait()


def memory_call(special, key_input, k_spikes, values, tokens, cotangent):
    length, total = values.shape
    block, state = (length, total), (total, HEAD)
    return kernel_call(
        functools.partial(memory_kernel, special),
        "HHHHH",
        (key_input, k_spikes, values, tokens, cotangent),
        "VVVVVVV",
        [(block, bf16)] * 3
        + [(state, f32), (state, bf16), (tokens.shape, bf16), (block, bf16)],
        "own_memory",
        (2 * length * total * HEAD, 12 * length * total),
        [
            pltpu.VMEM(block, bf16),
            pltpu.VMEM(block, jnp.int32),
            pltpu.SemaphoreType.DMA((3 * total // WIDE + tokens.shape[1] // PIECE + 1,)),
        ],
    )


def join_kernel(*refs):
    del refs


def join(arrays, others=()):
    number = len(arrays)
    return kernel_call(
        join_kernel,
        ["A"] * (number + len(others)),
        (*[fast(one) for one in arrays], *others),
        ["A"] * number,
        [(one.shape, one.dtype) for one in arrays],
        "join",
        (0, 0),
        aliases={at: at for at in range(number)},
    )


def keep_lower(square, flipped=False):
    row = lax.broadcasted_iota(jnp.int32, square.shape, 0)
    col = lax.broadcasted_iota(jnp.int32, square.shape, 1)
    return jnp.where((col >= row) if flipped else (col <= row), square, 0.0).astype(bf16)


def causal(a, b):
    length = a.shape[0]
    cut = length - HEAD
    top = keep_lower(nt(a[:cut], b[:cut]))
    whole = nt(a[cut:], b)
    bottom = jnp.concatenate([whole[:, :cut].astype(bf16), keep_lower(whole[:, cut:])], axis=1)
    return [(slice(0, cut), slice(0, cut), top), (slice(cut, length), slice(0, length), bottom)]


def causal_turned(a, b):
    length = a.shape[0]
    whole = nt(a[:HEAD], b)
    top = jnp.concatenate(
        [keep_lower(whole[:, :HEAD], True), whole[:, HEAD:].astype(bf16)], axis=1
    )
    bottom = keep_lower(nt(a[HEAD:], b[HEAD:]), True)
    return [
        (slice(0, HEAD), slice(0, length), top),
        (slice(HEAD, length), slice(HEAD, length), bottom),
    ]


def twice(array):
    return jnp.concatenate([array, array], axis=1)


def masked_kernel(
    factor, spike_ref, grad_ref, value_ref, keys_ref, high_ref, low_ref,
    out_ref, mask_ref, spike_in, sems,
):
    total = out_ref.shape[1]

    def bring(group, at):
        return pltpu.make_async_copy(
            spike_ref.at[columns(at)], spike_in.at[columns(at)], sems.at[group]
        )

    for group in range(total // WIDE):
        bring(group, group * WIDE).start()

    def work(group, at):
        bring(group, at).wait()
        for part in heads(at):
            mask = spike_in[:, part].astype(f32)
            mask_ref[:, part] = mask.astype(bf16)
            grad, value, keys = grad_ref[:, part], value_ref[:, part], keys_ref[:, part]
            state = jnp.concatenate([high_ref[part, :], low_ref[part, :]], axis=1)
            for rows, cols, scores in causal(grad, value):
                made = nn(scores, keys[cols]) + nt(twice(grad[rows]), state)
                out_ref[rows, part] = (factor * made * mask[rows]).astype(bf16)

    groups(total, work)


def masked_call(factor, q_spikes, cotangent, values, keys, high, low):
    length, total = values.shape
    block = (length, total)
    return kernel_call(
        functools.partial(masked_kernel, factor),
        "HVVVVV",
        (q_spikes, cotangent, values, keys, high, low),
        "VV",
        [(block, bf16)] * 2,
        "masked_grad",
        (8 * length * total * length, 12 * length * total),
        [pltpu.VMEM(block, jnp.int32), pltpu.SemaphoreType.DMA((total // WIDE,))],
    )


def turned_kernel(value_ref, grad_ref, after_ref, top_ref, bottom_ref, mark_ref):
    del after_ref
    set_mark(mark_ref)
    length, total = value_ref.shape
    rest = length - HEAD
    number = WIDE // HEAD

    def work(group, at):
        for head, part in enumerate(heads(at)):
            (_, _, top), (_, _, bottom) = causal_turned(value_ref[:, part], grad_ref[:, part])
            place = group * number + head
            top_ref[:, pl.ds(pl.multiple_of(place * length, HEAD), length)] = top
            bottom_ref[:, pl.ds(pl.multiple_of(place * rest, HEAD), rest)] = bottom

    groups(total, work)


def turned_call(values, cotangent, after):
    length, total = values.shape
    number, rest = total // HEAD, length - HEAD
    return kernel_call(
        turned_kernel,
        "VVA",
        (values, cotangent, after),
        "VVV",
        [((HEAD, number * length), bf16), ((rest, number * rest), bf16), (MARK.shape, f32)],
        "turned",
        (4 * length * total * length, 0),
    )


def rows_of(blocks):
    return sum(block.shape[0] for block in blocks)


def back_blocks(blocks):
    at = 0
    for block in blocks:
        for row in range(0, block.shape[0], PIECE):
            yield at, block[row : row + PIECE, :]
            at += 1


def back_part(copies, places, masked, blocks, out_ref, round_ref):
    going = []
    pieces = list(back_blocks(blocks))
    for (first, upper), (second, lower) in zip(pieces[::2], pieces[1::2]):
        both = slice(first * PIECE, (second + 1) * PIECE)
        made = nt(masked[...], jnp.concatenate([upper, lower], axis=0))
        round_ref[:, both] = made.astype(bf16)
        for piece in (first, second):
            going.append(
                copies.start(
                    round_ref.at[piece_columns(piece)], out_ref.at[piece_columns(places[piece])]
                )
            )
    return going


def products_kernel(special, start, size, project, back, has_sum, has_back, *refs):
    blocks, refs = refs[:size], list(refs[size:])
    depth = rows_of(blocks)
    tokens_ref = refs.pop(0) if project else None
    before_ref = refs.pop(0) if has_sum else None
    masked = refs.pop(0) if back else None
    if has_back:
        refs.pop(0)
    sum_ref = refs.pop(0) if project else None
    back_out = refs.pop(0) if back else None
    mark_ref = refs.pop(0)
    set_mark(mark_ref)
    going = []
    if back:
        round_ref, sems = refs
        places = all_places(special, back_out.shape[1] // PIECE)[start:]
        going = back_part(Copies(sems), places, masked, blocks, back_out, round_ref)
    if project:
        cols = slice(start * PIECE, start * PIECE + depth)
        for at in range(0, sum_ref.shape[1], WIDE):
            part = slice(at, at + WIDE)
            made = nn(
                tokens_ref[:, cols],
                jnp.concatenate([block[:, part] for block in blocks], axis=0),
            )
            if has_sum:
                made = made + before_ref[:, part]
            sum_ref[:, part] = made
    for copy in going:
        copy.wait()


def products_call(
    special, start, blocks, tokens, partial=None, masked=None, grad=None, project=True
):
    length, width = tokens.shape
    total = blocks[0].shape[1]
    depth = rows_of(blocks)
    back = masked is not None
    places_in, args = "V" * len(blocks), list(blocks)
    places_out, outs = "", []
    scratch, aliases = [], {}
    if project:
        places_in, args = places_in + "V", args + [tokens]
        if partial is not None:
            aliases[len(args)] = 0
            places_in, args = places_in + "V", args + [partial]
        places_out, outs = "V", [((length, total), f32)]
    if back:
        places_in, args = places_in + "V", args + [masked]
        if grad is not None:
            aliases[len(args)] = len(outs)
            places_in, args = places_in + "H", args + [grad]
        places_out, outs = places_out + "H", outs + [((length, width), bf16)]
        scratch = [
            pltpu.VMEM((length, depth), bf16), pltpu.SemaphoreType.DMA((depth // PIECE,))
        ]
    made = kernel_call(
        functools.partial(
            products_kernel, special, start, len(blocks), project, back,
            partial is not None, grad is not None,
        ),
        places_in,
        args,
        places_out + "V",
        outs + [(MARK.shape, f32)],
        "products" if project and back else "project" if project else "grad_tokens",
        (2 * (project + back) * length * depth * total, 0),
        scratch,
        aliases,
    )
    made = list(made)
    partial = made.pop(0) if project else partial
    grad = made.pop(0) if back else grad
    return partial, grad, made[0]


def query_kernel(start, size, tokens_ref, sum_ref, mask_ref, grad_ref, *refs):
    blocks = refs[:size]
    queries, own_ref, sent_ref = refs[-3:]
    cols = slice(start * PIECE, start * PIECE + rows_of(blocks))
    for at in range(0, queries.shape[1], WIDE):
        part = slice(at, at + WIDE)
        made = nn(
            tokens_ref[:, cols], jnp.concatenate([block[:, part] for block in blocks], axis=0)
        )
        made = made + sum_ref[:, part]
        made = (made * mask_ref[:, part].astype(f32)).astype(bf16)
        queries[:, part] = made
        for head in range(0, WIDE, HEAD):
            here = slice(at + head, at + head + HEAD)
            own = tn(made[:, head : head + HEAD], grad_ref[:, here])
            own_ref[here, :] = own
            sent_ref[here, :] = own.astype(bf16)


def query_call(start, tokens, blocks, before, q_mask, cotangent, others):
    length = tokens.shape[0]
    total = blocks[0].shape[1]
    depth = rows_of(blocks)
    return kernel_call(
        functools.partial(query_kernel, start, len(blocks)),
        "VVVV" + "V" * len(blocks) + "A" * len(others),
        (tokens, before, q_mask, cotangent, *blocks, *others),
        "VVV",
        [((length, total), bf16), ((total, HEAD), f32), ((total, HEAD), bf16)],
        "queries",
        (2 * length * depth * total, 0),
    )


def out_copy(here, there, sems, group, at):
    return pltpu.make_async_copy(here.at[columns(at)], there.at[columns(at)], sems.at[group])


def attend_kernel(
    factor, query_ref, keys_ref, value_ref, high_ref, low_ref, out_ref, mark_ref, made_ref, sems
):
    set_mark(mark_ref)
    total = query_ref.shape[1]

    def work(group, at):
        for part in heads(at):
            query, keys, value = query_ref[:, part], keys_ref[:, part], value_ref[:, part]
            state = [high_ref[part, :], low_ref[part, :]]
            for rows, cols, scores in causal(query, keys):
                made = nn(
                    jnp.concatenate([scores, twice(query[rows])], axis=1),
                    jnp.concatenate([value[cols], *state], axis=0),
                )
                made_ref[rows, part] = (factor * made).astype(bf16)
        out_copy(made_ref, out_ref, sems, group, at).start()

    groups(total, work)
    for group in range(total // WIDE):
        out_copy(made_ref, out_ref, sems, group, group * WIDE).wait()


def attend_call(factor, queries, keys, values, high, low):
    length, total = values.shape
    return kernel_call(
        functools.partial(attend_kernel, factor),
        "VVVVV",
        (queries, keys, values, high, low),
        "HV",
        [((length, total), bf16), (MARK.shape, f32)],
        "attended",
        (8 * length * total * length, 8 * length * total),
        [pltpu.VMEM((length, total), bf16), pltpu.SemaphoreType.DMA((total // WIDE,))],
    )


def value_kernel(query_ref, keys_ref, grad_ref, val_ref, mark_ref):
    set_mark(mark_ref)

    def work(group, at):
        for part in heads(at):
            query, keys, grad = query_ref[:, part], keys_ref[:, part], grad_ref[:, part]
            for rows, cols, scores in causal_turned(keys, query):
                val_ref[rows, part] = nn(scores, grad[cols])

    groups(query_ref.shape[1], work)


def value_call(queries, keys, cotangent):
    length, total = keys.shape
    return kernel_call(
        value_kernel,
        "VVV",
        (queries, keys, cotangent),
        "VV",
        [((length, total), f32), (MARK.shape, f32)],
        "value_part",
        (6 * length * total * length, 0),
    )


def key_kernel(query_ref, top_ref, bottom_ref, key_ref):
    length, total = query_ref.shape
    rest = length - HEAD
    number = WIDE // HEAD

    def work(group, at):
        for head, part in enumerate(heads(at)):
            query = query_ref[:, part]
            place = group * number + head
            top = top_ref[:, pl.ds(pl.multiple_of(place * length, HEAD), length)]
            bottom = bottom_ref[:, pl.ds(pl.multiple_of(place * rest, HEAD), rest)]
            key_ref[:HEAD, part] = nn(top, query)
            key_ref[HEAD:, part] = nn(bottom, query[HEAD:])

    groups(total, work)


def key_call(queries, top, bottom):
    length, total = queries.shape
    return kernel_call(
        key_kernel,
        "VVV",
        (queries, top, bottom),
        "V",
        [((length, total), f32)],
        "key_part",
        (4 * length * total * length, 0),
    )[0]


def outer_kernel(
    factor, key_ref, val_ref, keys_ref, value_ref, mask_ref, high_ref, low_ref,
    key_out, val_out, key_made, val_made, key_sems, val_sems,
):
    total = keys_ref.shape[1]

    def work(group, at):
        for part in heads(at):
            keys, value = keys_ref[:, part], value_ref[:, part]
            state = [high_ref[part, :], low_ref[part, :]]
            key_grad = key_ref[:, part] + nt(twice(value), jnp.concatenate(state, axis=1))
            key_made[:, part] = (factor * key_grad * mask_ref[:, part].astype(f32)).astype(bf16)
            value_grad = val_ref[:, part] + nn(twice(keys), jnp.concatenate(state, axis=0))
            val_made[:, part] = (factor * value_grad).astype(bf16)
        out_copy(key_made, key_out, key_sems, group, at).start()
        out_copy(val_made, val_out, val_sems, group, at).start()

    groups(total, work)
    for group in range(total // WIDE):
        out_copy(key_made, key_out, key_sems, group, group * WIDE).wait()
        out_copy(val_made, val_out, val_sems, group, group * WIDE).wait()


def outer_call(factor, key_part, value_part, keys, values, k_mask, high, low):
    length, total = values.shape
    block = (length, total)
    return kernel_call(
        functools.partial(outer_kernel, factor),
        "VVVVVVV",
        (key_part, value_part, keys, values, k_mask, high, low),
        "HH",
        [(block, bf16)] * 2,
        "outer",
        (8 * length * total * HEAD, 20 * length * total),
        [pltpu.VMEM(block, bf16)] * 2 + [pltpu.SemaphoreType.DMA((total // WIDE,))] * 2,
    )


def halves(state):
    high = state.astype(bf16)
    return high, (state - high.astype(f32)).astype(bf16)


def scan_any(own, sent, count, reverse):
    place = lax.axis_index(CTX)
    total = own
    state = jnp.zeros_like(own)
    bits = count.bit_length() - 1
    for bit in range(bits):
        step = 1 << bit
        last = bit == bits - 1
        pairs = []
        for source in range(count):
            high = bool(source & step)
            if not last or high == reverse:
                pairs.append((source, source ^ step))
        got = lax.ppermute(sent, CTX, pairs).astype(f32)
        if last:
            state = state + got
        else:
            mine = ((place // step) % 2) == (0 if reverse else 1)
            state = state + jnp.where(mine, got, 0.0)
            total = total + got
            sent = total.astype(bf16)
    return state


def links(first, keep=lambda source, target: True):
    pairs = []
    for chip in range(4):
        for core in range(2):
            other = chip ^ (first if core == 0 else 3 - first)
            if keep((chip, core), other):
                pairs.append((chip * 2 + core, other * 2 + core))
    return pairs


def upward(reverse):
    flip = 3 if reverse else 0

    def keep(source, target):
        at = source[0] ^ flip
        return source[0] ^ target == 1 or not at & 2

    return keep


def low_bit(reverse):
    chip = lax.axis_index("chip")
    return 1 - chip % 2 if reverse else chip % 2


def half_rows(array_ref, core):
    half = array_ref.shape[0] // 2
    return array_ref[pl.ds(pl.multiple_of(core * half, half), half), :]


def both_kernel(own_ref, sibling_ref, *refs):
    both_ref, sent_ref = refs[-2:]
    core = lax.axis_index("core")
    both = half_rows(own_ref, core) + half_rows(sibling_ref, core).astype(f32)
    both_ref[...] = both
    sent_ref[...] = both.astype(bf16)


def message_kernel(reverse, got_ref, both_ref, *refs):
    core = lax.axis_index("core")
    adds = jnp.where((core == 0) | (low_bit(reverse) == 0), 1.0, 0.0)
    refs[-1][...] = (got_ref[...].astype(f32) + adds * both_ref[...]).astype(bf16)


def state_kernel(reverse, got_ref, more_ref, *refs):
    core = lax.axis_index("core")
    adds = jnp.where((core == 1) | (low_bit(reverse) == 1), 1.0, 0.0)
    refs[-1][...] = adds * got_ref[...].astype(f32) + more_ref[...].astype(f32)


def whole_kernel(reverse, state_ref, other_ref, sibling_ref, high_ref, low_ref):
    core = lax.axis_index("core")
    adds = jnp.where(core == (0 if reverse else 1), 1.0, 0.0)
    half = state_ref.shape[0]
    for ref, side in ((state_ref, core), (other_ref, 1 - core)):
        rows = pl.ds(pl.multiple_of(side * half, half), half)
        whole = ref[...] + adds * sibling_ref[rows, :].astype(f32)
        high = whole.astype(bf16)
        high_ref[rows, :] = high
        low_ref[rows, :] = (whole - high.astype(f32)).astype(bf16)


def send_first(own, sent, reverse, others=()):
    half = (own.shape[0] // 2, HEAD)
    sibling = lax.ppermute(sent, "core", SWAP)
    both, sent = kernel_call(
        both_kernel,
        "VV" + "A" * len(others),
        (own, sibling, *others),
        "VV",
        [(half, f32), (half, bf16)],
        "both",
        (0, 0),
    )
    return sibling, both, lax.ppermute(sent, CTX, links(1, upward(reverse)))


def send_second(got, both, reverse, others=()):
    (message,) = kernel_call(
        functools.partial(message_kernel, reverse),
        "VV" + "A" * len(others),
        (got, both, *others),
        "V",
        [(both.shape, bf16)],
        "message",
        (0, 0),
    )
    return lax.ppermute(message, CTX, links(2, upward(reverse)))


def sum_kernel(*refs):
    total = refs[0][...].astype(f32) + refs[1][...].astype(f32)
    refs[-1][...] = total + refs[2][...].astype(f32)


def send_direct(own, sent, reverse, before, beside):
    half = (own.shape[0] // 2, HEAD)
    sibling = lax.ppermute(sent, "core", SWAP)
    _, sent = kernel_call(
        both_kernel,
        "VVA",
        (own, sibling, before),
        "VV",
        [(half, f32), (half, bf16)],
        "both",
        (0, 0),
    )
    got = []
    for flip in (3, 1, 2):
        pairs = [
            (chip * 2 + core, (chip ^ flip) * 2 + core)
            for chip in range(4)
            for core in range(2)
            if (chip ^ flip < chip) == reverse
        ]
        got.append(lax.ppermute(sent, CTX, pairs))
    (state,) = kernel_call(
        sum_kernel, "VVV" + "A" * len(beside), (*got, *beside), "V", [(half, f32)], "state", (0, 0)
    )
    return add_siblings(state, sibling, reverse)


def add_up(got, more, sibling, reverse, others=()):
    (state,) = kernel_call(
        functools.partial(state_kernel, reverse),
        "VV" + "A" * len(others),
        (got, more, *others),
        "V",
        [(got.shape, f32)],
        "state",
        (0, 0),
    )
    return add_siblings(state, sibling, reverse)


def add_siblings(state, sibling, reverse):
    other = lax.ppermute(state, "core", SWAP)
    return kernel_call(
        functools.partial(whole_kernel, reverse),
        "VVV",
        (state, other, sibling),
        "VV",
        [(sibling.shape, bf16)] * 2,
        "whole",
        (0, 0),
    )


def gather_any(q_weight):
    whole = lax.all_gather(q_weight, ("chip", "core", "dp"), axis=0, tiled=True)
    cut = whole.shape[0] // (2 * PIECE) * PIECE
    return [whole[:cut], whole[cut:]]


def pack_kernel(*refs):
    *arrays, out_ref, sems = refs
    copies = Copies(sems)
    rows = out_ref.shape[0] // len(arrays)
    going = [
        copies.start(array, out_ref.at[pl.ds(at * rows, rows), :])
        for at, array in enumerate(arrays)
    ]
    for copy in going:
        copy.wait()


def pack(*arrays):
    rows, total = arrays[0].shape
    number = len(arrays)
    (made,) = kernel_call(
        pack_kernel,
        "A" * number,
        arrays,
        "V",
        [((number * rows, total), arrays[0].dtype)],
        "pack",
        (0, 0),
        [pltpu.SemaphoreType.DMA((number,))],
    )
    return [made, lax.ppermute(made, "core", SWAP)]


def choose_kernel(inner_ref, end_ref, out_ref, sem):
    del end_ref
    layer = lax.axis_index("dp")

    @pl.when((layer == 1) | (layer == 2))
    def _():
        copy = pltpu.make_async_copy(inner_ref, out_ref, sem)
        copy.start()
        copy.wait()


def choose(inner, end):
    return kernel_call(
        choose_kernel,
        "AA",
        (fast(inner), fast(end)),
        "A",
        [(inner.shape, inner.dtype)],
        "choose",
        (0, 0),
        [pltpu.SemaphoreType.DMA],
        {1: 0},
    )[0]


def per_device(tokens, key_input, values, q_weight, q_spikes, k_spikes, cotangent):
    batches, length, width = tokens.shape
    assert batches == 1
    total = q_weight.shape[1]
    chips, spread = lax.axis_size("chip"), lax.axis_size("dp")
    factor = 3.0 / math.sqrt(HEAD * length * chips * 2)
    tokens, key_input, values, q_spikes, k_spikes, cotangent = (
        array.reshape(length, array.shape[2])
        for array in (tokens, key_input, values, q_spikes, k_spikes, cotangent)
    )
    special = chips == 4 and spread == 4

    def sibling(array):
        return lax.ppermute(array, "core", SWAP)

    def along(array, pairs):
        return lax.ppermute(array, "dp", pairs)

    def cross(array):
        return lax.ppermute(array, CTX, links(1)), lax.ppermute(array, CTX, links(2))

    def onward(array):
        return lax.ppermute(array, CTX, links(2))

    keys, k_mask, values, own, sent, tokens, cotangent = memory_call(
        special, key_input, k_spikes, values, tokens, cotangent
    )
    if special:
        ends = [(0, 1), (1, 0), (2, 3), (3, 2)]
        middle = [(1, 2), (2, 1)]
        outward = [(1, 0), (2, 3)]
        near = along(q_weight, ends)
        mid = along(q_weight, middle)
        first_0, second_0 = cross(q_weight)
        near, mid, first_0, second_0, sent = join([near, mid, first_0, second_0, sent])
    else:
        arrived = gather_any(q_weight)
        high, low = halves(scan_any(own, sent, chips * 2, False))

    if special:
        third_0 = onward(first_0)
        first_1, second_1 = cross(near)
        far = along(near, middle)
        mid_out = along(mid, outward)
        twin, both, got = send_first(own, sent, False)
        third_0, first_1, second_1, far, mid_out, got = join(
            [third_0, first_1, second_1, far, mid_out, got]
        )
        more = send_second(got, both, False)
        next_layer = choose(mid, mid_out)
        first_2, second_2 = cross(next_layer)
        far_out = along(far, outward)
        early = pack(q_weight, first_0, second_0, third_0, near, first_1, second_1)
        partial, _, mark = products_call(special, 0, early, tokens)
        top, bottom, turned_mark = turned_call(values, cotangent, got)
        third_0, first_2, second_2, far_out, more = join(
            [third_0, first_2, second_2, far_out, more], [mark, turned_mark]
        )
        third_1 = along(third_0, ends)
        third_2 = onward(first_2)
        last_layer = choose(far, far_out)
        first_3, second_3 = cross(last_layer)
        high, low = add_up(got, more, twin, False)
        masked, q_mask = masked_call(factor, q_spikes, cotangent, values, keys, high, low)
        _, grad, mark_0 = products_call(
            special, 0, early, tokens, masked=masked, project=False
        )
        blocks = pack(next_layer, first_2, second_2, last_layer)
        partial, grad, mark_1 = products_call(special, 14, blocks, tokens, partial, masked, grad)
        third_1, third_2, first_3, second_3 = join(
            [third_1, third_2, first_3, second_3], [mark_0, mark_1]
        )
        third_3 = onward(first_3)
        blocks = pack(third_1, third_2, first_3, second_3)
        partial, _, mark = products_call(special, 22, blocks, tokens, partial)
        third_3, = join([third_3], [mark])
        _, grad, mark = products_call(
            special, 22, blocks, tokens, masked=masked, grad=grad, project=False
        )
        late = [third_3, sibling(third_3)]
        start = 30
    else:
        masked, q_mask = masked_call(factor, q_spikes, cotangent, values, keys, high, low)
        top, bottom, _ = turned_call(values, cotangent, own)
        start = arrived[0].shape[0] // PIECE
        partial, grad, mark = products_call(special, 0, arrived[:1], tokens, masked=masked)
        late = arrived[1:]
    queries, own, sent = query_call(start, tokens, late, partial, q_mask, cotangent, [mark])
    attended, attended_mark = attend_call(factor, queries, keys, values, high, low)
    value_part, value_mark = value_call(queries, keys, cotangent)
    key_part = key_call(queries, top, bottom)
    _, grad_tokens, back_mark = products_call(
        special, start, late, tokens, masked=masked, grad=grad, project=False
    )
    if special:
        adjoint = send_direct(own, sent, True, back_mark, (attended_mark, value_mark))
    else:
        adjoint = halves(scan_any(own, sent, chips * 2, True))
    grad_keys, grad_values = outer_call(
        factor, key_part, value_part, keys, values, k_mask, *adjoint
    )
    return tuple(
        array.reshape(1, length, array.shape[1])
        for array in (attended, grad_tokens, grad_keys, grad_values)
    )


def solution(mesh):
    count, spread = mesh.shape["ctx"], mesh.shape["dp"]
    fine = Mesh(mesh.devices.reshape(count // 2, 2, spread), ("chip", "core", "dp"))
    block = P("dp", CTX, None)
    rows = P(("chip", "core", "dp"), None)
    in_specs = (block, block, block, rows, block, block, block)
    return jax.shard_map(
        per_device, mesh=fine, in_specs=in_specs, out_specs=(block,) * 4, check_vma=False
    )
```

```python
import functools
import math

import jax
import jax.numpy as jnp
from jax import lax
from jax.experimental import pallas as pl
from jax.experimental.pallas import tpu as pltpu
from jax.sharding import Mesh, PartitionSpec as P

HEAD = 128
PIECE = 128
WIDE = 512
CTX = ("chip", "core")
SWAP = [(0, 1), (1, 0)]
f32, bf16 = jnp.float32, jnp.bfloat16
VMEM_LIMIT = 18 * 1024 * 1024


def nn(a, b):
    return lax.dot_general(a, b, (((1,), (0,)), ((), ())), preferred_element_type=f32)


def nt(a, b):
    return lax.dot_general(a, b, (((1,), (1,)), ((), ())), preferred_element_type=f32)


def tn(a, b):
    return lax.dot_general(a, b, (((0,), (0,)), ((), ())), preferred_element_type=f32)


def params(flops, moved):
    return dict(
        compiler_params=pltpu.CompilerParams(vmem_limit_bytes=VMEM_LIMIT),
        cost_estimate=pl.CostEstimate(flops=flops, bytes_accessed=moved, transcendentals=0),
    )


MARK = jax.ShapeDtypeStruct((8, HEAD), f32)


def set_mark(mark_ref):
    mark_ref[...] = jnp.zeros_like(mark_ref)


def fast(array):
    return pltpu.with_memory_space_constraint(array, pltpu.VMEM)


def slow(array):
    return pltpu.with_memory_space_constraint(array, pltpu.HBM)


def specs(places):
    spaces = dict(V=pltpu.VMEM, H=pltpu.HBM, S=pltpu.SMEM, A=pl.ANY)
    return [pl.BlockSpec(memory_space=spaces[place]) for place in places]


def kernel_call(body, places, args, out_places, outs, name, cost, scratch=(), aliases=None):
    holds = dict(V=fast, H=slow)
    made = pl.pallas_call(
        body,
        in_specs=specs(places),
        out_specs=specs(out_places),
        out_shape=[
            pltpu.VMEM(shape, dtype) if place == "V" else jax.ShapeDtypeStruct(shape, dtype)
            for place, (shape, dtype) in zip(out_places, outs)
        ],
        scratch_shapes=list(scratch),
        input_output_aliases=aliases or {},
        name=name,
        **params(*cost),
    )
    return made(
        *[holds[place](one) if place in holds else one for place, one in zip(places, args)]
    )


class Copies:
    def __init__(self, sems):
        self.sems = sems
        self.used = 0

    def start(self, source, target):
        copy = pltpu.make_async_copy(source, target, self.sems.at[self.used])
        self.used += 1
        copy.start()
        return copy


def crossed(side):
    return (0, 1 + side, 2 - side, 3)


def all_places(special, number):
    if not special:
        return list(range(number))
    chip, core, layer = (lax.axis_index(name) for name in ("chip", "core", "dp"))
    upper = layer < 2
    layers = [layer, layer ^ 1, jnp.where(upper, 2, 1), jnp.where(upper, 3, 0)]

    def some(*arrivals):
        return [
            ((chip ^ crossed(side)[flip]) * 2 + side) * 4 + layers[one]
            for side in (core, 1 - core)
            for one, flips in arrivals
            for flip in flips
        ]

    three = (0, 1, 2)
    return (
        some((0, (0, 1, 2, 3)), (1, three))
        + some((2, three), (3, (0,)))
        + some((1, (3,)), (2, (3,)), (3, (1, 2)))
        + some((3, (3,)))
    )


def piece_columns(place):
    return (slice(None), pl.ds(pl.multiple_of(place * PIECE, PIECE), PIECE))


def columns(at, wide=None):
    return (slice(None), pl.ds(at, wide or WIDE))


def groups(total, body):
    @pl.loop(0, total // WIDE)
    def _(group):
        body(group, pl.multiple_of(group * WIDE, WIDE))


def heads(at):
    return [pl.ds(pl.multiple_of(at + head, HEAD), HEAD) for head in range(0, WIDE, HEAD)]


def memory_kernel(
    special, key_ref, spike_ref, value_ref, tokens_ref, grad_ref,
    keys_ref, mask_ref, values_ref, own_ref, sent_ref, some_ref, grads_ref,
    key_in, spike_in, sems,
):
    copies = Copies(sems)
    wide = range(0, keys_ref.shape[1], WIDE)
    pairs = ((key_ref, key_in), (spike_ref, spike_in), (value_ref, values_ref))
    parts = [
        [copies.start(here.at[columns(at)], there.at[columns(at)]) for here, there in pairs]
        for at in wide
    ]
    places = all_places(special, some_ref.shape[1] // PIECE)
    ordered = [
        copies.start(tokens_ref.at[piece_columns(place)], some_ref.at[piece_columns(piece)])
        for piece, place in enumerate(places)
    ]
    ordered.append(copies.start(grad_ref, grads_ref))
    for at, part in zip(wide, parts):
        for copy in part:
            copy.wait()
        cols = slice(at, at + WIDE)
        mask = spike_in[:, cols].astype(f32).astype(bf16)
        keys = key_in[:, cols] * mask
        keys_ref[:, cols] = keys
        mask_ref[:, cols] = mask
        for head in range(0, WIDE, HEAD):
            here = slice(at + head, at + head + HEAD)
            own = tn(keys[:, head : head + HEAD], values_ref[:, here])
            own_ref[here, :] = own
            sent_ref[here, :] = own.astype(bf16)
    for copy in ordered:
        copy.wait()


def memory_call(special, key_input, k_spikes, values, tokens, cotangent):
    length, total = values.shape
    block, state = (length, total), (total, HEAD)
    return kernel_call(
        functools.partial(memory_kernel, special),
        "HHHHH",
        (key_input, k_spikes, values, tokens, cotangent),
        "VVVVVVV",
        [(block, bf16)] * 3
        + [(state, f32), (state, bf16), (tokens.shape, bf16), (block, bf16)],
        "own_memory",
        (2 * length * total * HEAD, 12 * length * total),
        [
            pltpu.VMEM(block, bf16),
            pltpu.VMEM(block, jnp.int32),
            pltpu.SemaphoreType.DMA((3 * total // WIDE + tokens.shape[1] // PIECE + 1,)),
        ],
    )


def join_kernel(*refs):
    del refs


def join(arrays, others=()):
    number = len(arrays)
    return kernel_call(
        join_kernel,
        ["A"] * (number + len(others)),
        (*[fast(one) for one in arrays], *others),
        ["A"] * number,
        [(one.shape, one.dtype) for one in arrays],
        "join",
        (0, 0),
        aliases={at: at for at in range(number)},
    )


def keep_lower(square, flipped=False):
    row = lax.broadcasted_iota(jnp.int32, square.shape, 0)
    col = lax.broadcasted_iota(jnp.int32, square.shape, 1)
    return jnp.where((col >= row) if flipped else (col <= row), square, 0.0).astype(bf16)


def causal(a, b):
    length = a.shape[0]
    cut = length - HEAD
    top = keep_lower(nt(a[:cut], b[:cut]))
    whole = nt(a[cut:], b)
    bottom = jnp.concatenate([whole[:, :cut].astype(bf16), keep_lower(whole[:, cut:])], axis=1)
    return [(slice(0, cut), slice(0, cut), top), (slice(cut, length), slice(0, length), bottom)]


def causal_turned(a, b):
    length = a.shape[0]
    whole = nt(a[:HEAD], b)
    top = jnp.concatenate(
        [keep_lower(whole[:, :HEAD], True), whole[:, HEAD:].astype(bf16)], axis=1
    )
    bottom = keep_lower(nt(a[HEAD:], b[HEAD:]), True)
    return [
        (slice(0, HEAD), slice(0, length), top),
        (slice(HEAD, length), slice(HEAD, length), bottom),
    ]


def twice(array):
    return jnp.concatenate([array, array], axis=1)


def masked_kernel(
    factor, spike_ref, grad_ref, value_ref, keys_ref, high_ref, low_ref,
    out_ref, mask_ref, spike_in, sems,
):
    total = out_ref.shape[1]

    def bring(group, at):
        return pltpu.make_async_copy(
            spike_ref.at[columns(at)], spike_in.at[columns(at)], sems.at[group]
        )

    for group in range(total // WIDE):
        bring(group, group * WIDE).start()

    def work(group, at):
        bring(group, at).wait()
        for part in heads(at):
            mask = spike_in[:, part].astype(f32)
            mask_ref[:, part] = mask.astype(bf16)
            grad, value, keys = grad_ref[:, part], value_ref[:, part], keys_ref[:, part]
            state = jnp.concatenate([high_ref[part, :], low_ref[part, :]], axis=1)
            for rows, cols, scores in causal(grad, value):
                made = nn(scores, keys[cols]) + nt(twice(grad[rows]), state)
                out_ref[rows, part] = (factor * made * mask[rows]).astype(bf16)

    groups(total, work)


def masked_call(factor, q_spikes, cotangent, values, keys, high, low):
    length, total = values.shape
    block = (length, total)
    return kernel_call(
        functools.partial(masked_kernel, factor),
        "HVVVVV",
        (q_spikes, cotangent, values, keys, high, low),
        "VV",
        [(block, bf16)] * 2,
        "masked_grad",
        (8 * length * total * length, 12 * length * total),
        [pltpu.VMEM(block, jnp.int32), pltpu.SemaphoreType.DMA((total // WIDE,))],
    )


def turned_kernel(value_ref, grad_ref, after_ref, top_ref, bottom_ref, mark_ref):
    del after_ref
    set_mark(mark_ref)
    length, total = value_ref.shape
    rest = length - HEAD
    number = WIDE // HEAD

    def work(group, at):
        for head, part in enumerate(heads(at)):
            (_, _, top), (_, _, bottom) = causal_turned(value_ref[:, part], grad_ref[:, part])
            place = group * number + head
            top_ref[:, pl.ds(pl.multiple_of(place * length, HEAD), length)] = top
            bottom_ref[:, pl.ds(pl.multiple_of(place * rest, HEAD), rest)] = bottom

    groups(total, work)


def turned_call(values, cotangent, after):
    length, total = values.shape
    number, rest = total // HEAD, length - HEAD
    return kernel_call(
        turned_kernel,
        "VVA",
        (values, cotangent, after),
        "VVV",
        [((HEAD, number * length), bf16), ((rest, number * rest), bf16), (MARK.shape, f32)],
        "turned",
        (4 * length * total * length, 0),
    )


def rows_of(blocks):
    return sum(block.shape[0] for block in blocks)


def back_blocks(blocks):
    at = 0
    for block in blocks:
        for row in range(0, block.shape[0], PIECE):
            yield at, block[row : row + PIECE, :]
            at += 1


def back_part(copies, places, masked, blocks, out_ref, round_ref):
    going = []
    pieces = list(back_blocks(blocks))
    for (first, upper), (second, lower) in zip(pieces[::2], pieces[1::2]):
        both = slice(first * PIECE, (second + 1) * PIECE)
        made = nt(masked[...], jnp.concatenate([upper, lower], axis=0))
        round_ref[:, both] = made.astype(bf16)
        for piece in (first, second):
            going.append(
                copies.start(
                    round_ref.at[piece_columns(piece)], out_ref.at[piece_columns(places[piece])]
                )
            )
    return going


def products_kernel(special, start, size, project, back, has_sum, has_back, *refs):
    blocks, refs = refs[:size], list(refs[size:])
    depth = rows_of(blocks)
    tokens_ref = refs.pop(0) if project else None
    before_ref = refs.pop(0) if has_sum else None
    masked = refs.pop(0) if back else None
    if has_back:
        refs.pop(0)
    sum_ref = refs.pop(0) if project else None
    back_out = refs.pop(0) if back else None
    mark_ref = refs.pop(0)
    set_mark(mark_ref)
    going = []
    if back:
        round_ref, sems = refs
        places = all_places(special, back_out.shape[1] // PIECE)[start:]
        going = back_part(Copies(sems), places, masked, blocks, back_out, round_ref)
    if project:
        cols = slice(start * PIECE, start * PIECE + depth)
        for at in range(0, sum_ref.shape[1], WIDE):
            part = slice(at, at + WIDE)
            made = nn(
                tokens_ref[:, cols],
                jnp.concatenate([block[:, part] for block in blocks], axis=0),
            )
            if has_sum:
                made = made + before_ref[:, part]
            sum_ref[:, part] = made
    for copy in going:
        copy.wait()


def products_call(
    special, start, blocks, tokens, partial=None, masked=None, grad=None, project=True
):
    length, width = tokens.shape
    total = blocks[0].shape[1]
    depth = rows_of(blocks)
    back = masked is not None
    places_in, args = "V" * len(blocks), list(blocks)
    places_out, outs = "", []
    scratch, aliases = [], {}
    if project:
        places_in, args = places_in + "V", args + [tokens]
        if partial is not None:
            aliases[len(args)] = 0
            places_in, args = places_in + "V", args + [partial]
        places_out, outs = "V", [((length, total), f32)]
    if back:
        places_in, args = places_in + "V", args + [masked]
        if grad is not None:
            aliases[len(args)] = len(outs)
            places_in, args = places_in + "H", args + [grad]
        places_out, outs = places_out + "H", outs + [((length, width), bf16)]
        scratch = [
            pltpu.VMEM((length, depth), bf16), pltpu.SemaphoreType.DMA((depth // PIECE,))
        ]
    made = kernel_call(
        functools.partial(
            products_kernel, special, start, len(blocks), project, back,
            partial is not None, grad is not None,
        ),
        places_in,
        args,
        places_out + "V",
        outs + [(MARK.shape, f32)],
        "products" if project and back else "project" if project else "grad_tokens",
        (2 * (project + back) * length * depth * total, 0),
        scratch,
        aliases,
    )
    made = list(made)
    partial = made.pop(0) if project else partial
    grad = made.pop(0) if back else grad
    return partial, grad, made[0]


def query_kernel(start, size, tokens_ref, sum_ref, mask_ref, grad_ref, *refs):
    blocks = refs[:size]
    queries, own_ref, sent_ref = refs[-3:]
    cols = slice(start * PIECE, start * PIECE + rows_of(blocks))
    for at in range(0, queries.shape[1], WIDE):
        part = slice(at, at + WIDE)
        made = nn(
            tokens_ref[:, cols], jnp.concatenate([block[:, part] for block in blocks], axis=0)
        )
        made = made + sum_ref[:, part]
        made = (made * mask_ref[:, part].astype(f32)).astype(bf16)
        queries[:, part] = made
        for head in range(0, WIDE, HEAD):
            here = slice(at + head, at + head + HEAD)
            own = tn(made[:, head : head + HEAD], grad_ref[:, here])
            own_ref[here, :] = own
            sent_ref[here, :] = own.astype(bf16)


def query_call(start, tokens, blocks, before, q_mask, cotangent, others):
    length = tokens.shape[0]
    total = blocks[0].shape[1]
    depth = rows_of(blocks)
    return kernel_call(
        functools.partial(query_kernel, start, len(blocks)),
        "VVVV" + "V" * len(blocks) + "A" * len(others),
        (tokens, before, q_mask, cotangent, *blocks, *others),
        "VVV",
        [((length, total), bf16), ((total, HEAD), f32), ((total, HEAD), bf16)],
        "queries",
        (2 * length * depth * total, 0),
    )


def out_copy(here, there, sems, group, at):
    return pltpu.make_async_copy(here.at[columns(at)], there.at[columns(at)], sems.at[group])


def attend_kernel(
    factor, query_ref, keys_ref, value_ref, high_ref, low_ref, out_ref, mark_ref, made_ref, sems
):
    set_mark(mark_ref)
    total = query_ref.shape[1]

    def work(group, at):
        for part in heads(at):
            query, keys, value = query_ref[:, part], keys_ref[:, part], value_ref[:, part]
            state = [high_ref[part, :], low_ref[part, :]]
            for rows, cols, scores in causal(query, keys):
                made = nn(
                    jnp.concatenate([scores, twice(query[rows])], axis=1),
                    jnp.concatenate([value[cols], *state], axis=0),
                )
                made_ref[rows, part] = (factor * made).astype(bf16)
        out_copy(made_ref, out_ref, sems, group, at).start()

    groups(total, work)
    for group in range(total // WIDE):
        out_copy(made_ref, out_ref, sems, group, group * WIDE).wait()


def attend_call(factor, queries, keys, values, high, low):
    length, total = values.shape
    return kernel_call(
        functools.partial(attend_kernel, factor),
        "VVVVV",
        (queries, keys, values, high, low),
        "HV",
        [((length, total), bf16), (MARK.shape, f32)],
        "attended",
        (8 * length * total * length, 8 * length * total),
        [pltpu.VMEM((length, total), bf16), pltpu.SemaphoreType.DMA((total // WIDE,))],
    )


def value_kernel(query_ref, keys_ref, grad_ref, val_ref, mark_ref):
    set_mark(mark_ref)

    def work(group, at):
        for part in heads(at):
            query, keys, grad = query_ref[:, part], keys_ref[:, part], grad_ref[:, part]
            for rows, cols, scores in causal_turned(keys, query):
                val_ref[rows, part] = nn(scores, grad[cols])

    groups(query_ref.shape[1], work)


def value_call(queries, keys, cotangent):
    length, total = keys.shape
    return kernel_call(
        value_kernel,
        "VVV",
        (queries, keys, cotangent),
        "VV",
        [((length, total), f32), (MARK.shape, f32)],
        "value_part",
        (6 * length * total * length, 0),
    )


def key_kernel(query_ref, top_ref, bottom_ref, key_ref):
    length, total = query_ref.shape
    rest = length - HEAD
    number = WIDE // HEAD

    def work(group, at):
        for head, part in enumerate(heads(at)):
            query = query_ref[:, part]
            place = group * number + head
            top = top_ref[:, pl.ds(pl.multiple_of(place * length, HEAD), length)]
            bottom = bottom_ref[:, pl.ds(pl.multiple_of(place * rest, HEAD), rest)]
            key_ref[:HEAD, part] = nn(top, query)
            key_ref[HEAD:, part] = nn(bottom, query[HEAD:])

    groups(total, work)


def key_call(queries, top, bottom):
    length, total = queries.shape
    return kernel_call(
        key_kernel,
        "VVV",
        (queries, top, bottom),
        "V",
        [((length, total), f32)],
        "key_part",
        (4 * length * total * length, 0),
    )[0]


def outer_kernel(
    factor, key_ref, val_ref, keys_ref, value_ref, mask_ref, high_ref, low_ref,
    key_out, val_out, key_made, val_made, key_sems, val_sems,
):
    total = keys_ref.shape[1]

    def work(group, at):
        for part in heads(at):
            keys, value = keys_ref[:, part], value_ref[:, part]
            state = [high_ref[part, :], low_ref[part, :]]
            key_grad = key_ref[:, part] + nt(twice(value), jnp.concatenate(state, axis=1))
            key_made[:, part] = (factor * key_grad * mask_ref[:, part].astype(f32)).astype(bf16)
            value_grad = val_ref[:, part] + nn(twice(keys), jnp.concatenate(state, axis=0))
            val_made[:, part] = (factor * value_grad).astype(bf16)
        out_copy(key_made, key_out, key_sems, group, at).start()
        out_copy(val_made, val_out, val_sems, group, at).start()

    groups(total, work)
    for group in range(total // WIDE):
        out_copy(key_made, key_out, key_sems, group, group * WIDE).wait()
        out_copy(val_made, val_out, val_sems, group, group * WIDE).wait()


def outer_call(factor, key_part, value_part, keys, values, k_mask, high, low):
    length, total = values.shape
    block = (length, total)
    return kernel_call(
        functools.partial(outer_kernel, factor),
        "VVVVVVV",
        (key_part, value_part, keys, values, k_mask, high, low),
        "HH",
        [(block, bf16)] * 2,
        "outer",
        (8 * length * total * HEAD, 20 * length * total),
        [pltpu.VMEM(block, bf16)] * 2 + [pltpu.SemaphoreType.DMA((total // WIDE,))] * 2,
    )


def halves(state):
    high = state.astype(bf16)
    return high, (state - high.astype(f32)).astype(bf16)


def scan_any(own, sent, count, reverse):
    place = lax.axis_index(CTX)
    total = own
    state = jnp.zeros_like(own)
    bits = count.bit_length() - 1
    for bit in range(bits):
        step = 1 << bit
        last = bit == bits - 1
        pairs = []
        for source in range(count):
            high = bool(source & step)
            if not last or high == reverse:
                pairs.append((source, source ^ step))
        got = lax.ppermute(sent, CTX, pairs).astype(f32)
        if last:
            state = state + got
        else:
            mine = ((place // step) % 2) == (0 if reverse else 1)
            state = state + jnp.where(mine, got, 0.0)
            total = total + got
            sent = total.astype(bf16)
    return state


def links(first, keep=lambda source, target: True):
    pairs = []
    for chip in range(4):
        for core in range(2):
            other = chip ^ (first if core == 0 else 3 - first)
            if keep((chip, core), other):
                pairs.append((chip * 2 + core, other * 2 + core))
    return pairs


def upward(reverse):
    flip = 3 if reverse else 0

    def keep(source, target):
        at = source[0] ^ flip
        return source[0] ^ target == 1 or not at & 2

    return keep


def low_bit(reverse):
    chip = lax.axis_index("chip")
    return 1 - chip % 2 if reverse else chip % 2


def half_rows(array_ref, core):
    half = array_ref.shape[0] // 2
    return array_ref[pl.ds(pl.multiple_of(core * half, half), half), :]


def both_kernel(own_ref, sibling_ref, *refs):
    both_ref, sent_ref = refs[-2:]
    core = lax.axis_index("core")
    both = half_rows(own_ref, core) + half_rows(sibling_ref, core).astype(f32)
    both_ref[...] = both
    sent_ref[...] = both.astype(bf16)


def message_kernel(reverse, got_ref, both_ref, *refs):
    core = lax.axis_index("core")
    adds = jnp.where((core == 0) | (low_bit(reverse) == 0), 1.0, 0.0)
    refs[-1][...] = (got_ref[...].astype(f32) + adds * both_ref[...]).astype(bf16)


def state_kernel(reverse, got_ref, more_ref, *refs):
    core = lax.axis_index("core")
    adds = jnp.where((core == 1) | (low_bit(reverse) == 1), 1.0, 0.0)
    refs[-1][...] = adds * got_ref[...].astype(f32) + more_ref[...].astype(f32)


def whole_kernel(reverse, state_ref, other_ref, sibling_ref, high_ref, low_ref):
    core = lax.axis_index("core")
    adds = jnp.where(core == (0 if reverse else 1), 1.0, 0.0)
    half = state_ref.shape[0]
    for ref, side in ((state_ref, core), (other_ref, 1 - core)):
        rows = pl.ds(pl.multiple_of(side * half, half), half)
        whole = ref[...] + adds * sibling_ref[rows, :].astype(f32)
        high = whole.astype(bf16)
        high_ref[rows, :] = high
        low_ref[rows, :] = (whole - high.astype(f32)).astype(bf16)


def send_first(own, sent, reverse, others=()):
    half = (own.shape[0] // 2, HEAD)
    sibling = lax.ppermute(sent, "core", SWAP)
    both, sent = kernel_call(
        both_kernel,
        "VV" + "A" * len(others),
        (own, sibling, *others),
        "VV",
        [(half, f32), (half, bf16)],
        "both",
        (0, 0),
    )
    return sibling, both, lax.ppermute(sent, CTX, links(1, upward(reverse)))


def send_second(got, both, reverse, others=()):
    (message,) = kernel_call(
        functools.partial(message_kernel, reverse),
        "VV" + "A" * len(others),
        (got, both, *others),
        "V",
        [(both.shape, bf16)],
        "message",
        (0, 0),
    )
    return lax.ppermute(message, CTX, links(2, upward(reverse)))


def add_up(got, more, sibling, reverse, others=()):
    (state,) = kernel_call(
        functools.partial(state_kernel, reverse),
        "VV" + "A" * len(others),
        (got, more, *others),
        "V",
        [(got.shape, f32)],
        "state",
        (0, 0),
    )
    other = lax.ppermute(state, "core", SWAP)
    return kernel_call(
        functools.partial(whole_kernel, reverse),
        "VVV",
        (state, other, sibling),
        "VV",
        [(sibling.shape, bf16)] * 2,
        "whole",
        (0, 0),
    )


def gather_any(q_weight):
    whole = lax.all_gather(q_weight, ("chip", "core", "dp"), axis=0, tiled=True)
    cut = whole.shape[0] // (2 * PIECE) * PIECE
    return [whole[:cut], whole[cut:]]


def pack_kernel(*refs):
    *arrays, out_ref, sems = refs
    copies = Copies(sems)
    rows = out_ref.shape[0] // len(arrays)
    going = [
        copies.start(array, out_ref.at[pl.ds(at * rows, rows), :])
        for at, array in enumerate(arrays)
    ]
    for copy in going:
        copy.wait()


def pack(*arrays):
    rows, total = arrays[0].shape
    number = len(arrays)
    (made,) = kernel_call(
        pack_kernel,
        "A" * number,
        arrays,
        "V",
        [((number * rows, total), arrays[0].dtype)],
        "pack",
        (0, 0),
        [pltpu.SemaphoreType.DMA((number,))],
    )
    return [made, lax.ppermute(made, "core", SWAP)]


def choose_kernel(inner_ref, end_ref, out_ref, sem):
    del end_ref
    layer = lax.axis_index("dp")

    @pl.when((layer == 1) | (layer == 2))
    def _():
        copy = pltpu.make_async_copy(inner_ref, out_ref, sem)
        copy.start()
        copy.wait()


def choose(inner, end):
    return kernel_call(
        choose_kernel,
        "AA",
        (fast(inner), fast(end)),
        "A",
        [(inner.shape, inner.dtype)],
        "choose",
        (0, 0),
        [pltpu.SemaphoreType.DMA],
        {1: 0},
    )[0]


def per_device(tokens, key_input, values, q_weight, q_spikes, k_spikes, cotangent):
    batches, length, width = tokens.shape
    assert batches == 1
    total = q_weight.shape[1]
    chips, spread = lax.axis_size("chip"), lax.axis_size("dp")
    factor = 3.0 / math.sqrt(HEAD * length * chips * 2)
    tokens, key_input, values, q_spikes, k_spikes, cotangent = (
        array.reshape(length, array.shape[2])
        for array in (tokens, key_input, values, q_spikes, k_spikes, cotangent)
    )
    special = chips == 4 and spread == 4

    def sibling(array):
        return lax.ppermute(array, "core", SWAP)

    def along(array, pairs):
        return lax.ppermute(array, "dp", pairs)

    def cross(array):
        return lax.ppermute(array, CTX, links(1)), lax.ppermute(array, CTX, links(2))

    def onward(array):
        return lax.ppermute(array, CTX, links(2))

    keys, k_mask, values, own, sent, tokens, cotangent = memory_call(
        special, key_input, k_spikes, values, tokens, cotangent
    )
    if special:
        ends = [(0, 1), (1, 0), (2, 3), (3, 2)]
        middle = [(1, 2), (2, 1)]
        outward = [(1, 0), (2, 3)]
        near = along(q_weight, ends)
        mid = along(q_weight, middle)
        first_0, second_0 = cross(q_weight)
        first_0, second_0, near, mid, sent = join([first_0, second_0, near, mid, sent])
    else:
        arrived = gather_any(q_weight)
        high, low = halves(scan_any(own, sent, chips * 2, False))

    if special:
        third_0 = onward(first_0)
        first_1, second_1 = cross(near)
        far = along(near, middle)
        mid_out = along(mid, outward)
        twin, both, got = send_first(own, sent, False)
        third_0, first_1, second_1, far, mid_out, got = join(
            [third_0, first_1, second_1, far, mid_out, got]
        )
        more = send_second(got, both, False)
        next_layer = choose(mid, mid_out)
        first_2, second_2 = cross(next_layer)
        far_out = along(far, outward)
        early = pack(q_weight, first_0, second_0, third_0, near, first_1, second_1)
        partial, _, mark = products_call(special, 0, early, tokens)
        top, bottom, turned_mark = turned_call(values, cotangent, got)
        far_out, first_2, second_2, more, third_0 = join(
            [far_out, first_2, second_2, more, third_0], [mark, turned_mark]
        )
        third_1 = along(third_0, ends)
        third_2 = onward(first_2)
        last_layer = choose(far, far_out)
        first_3, second_3 = cross(last_layer)
        high, low = add_up(got, more, twin, False)
        masked, q_mask = masked_call(factor, q_spikes, cotangent, values, keys, high, low)
        _, grad, mark_0 = products_call(
            special, 0, early, tokens, masked=masked, project=False
        )
        blocks = pack(next_layer, first_2, second_2, last_layer)
        partial, grad, mark_1 = products_call(special, 14, blocks, tokens, partial, masked, grad)
        third_1, third_2, first_3, second_3 = join(
            [third_1, third_2, first_3, second_3], [mark_0, mark_1]
        )
        third_3 = onward(first_3)
        blocks = pack(third_1, third_2, first_3, second_3)
        partial, _, mark = products_call(special, 22, blocks, tokens, partial)
        third_3, = join([third_3], [mark])
        _, grad, mark = products_call(
            special, 22, blocks, tokens, masked=masked, grad=grad, project=False
        )
        late = [third_3, sibling(third_3)]
        start = 30
    else:
        masked, q_mask = masked_call(factor, q_spikes, cotangent, values, keys, high, low)
        top, bottom, _ = turned_call(values, cotangent, own)
        start = arrived[0].shape[0] // PIECE
        partial, grad, mark = products_call(special, 0, arrived[:1], tokens, masked=masked)
        late = arrived[1:]
    queries, own, sent = query_call(start, tokens, late, partial, q_mask, cotangent, [mark])
    attended, attended_mark = attend_call(factor, queries, keys, values, high, low)
    value_part, value_mark = value_call(queries, keys, cotangent)
    key_part = key_call(queries, top, bottom)
    _, grad_tokens, back_mark = products_call(
        special, start, late, tokens, masked=masked, grad=grad, project=False
    )
    if special:
        twin, both, got = send_first(own, sent, True, [back_mark])
        more = send_second(got, both, True, [attended_mark])
        adjoint = add_up(got, more, twin, True, [value_mark])
    else:
        adjoint = halves(scan_any(own, sent, chips * 2, True))
    grad_keys, grad_values = outer_call(
        factor, key_part, value_part, keys, values, k_mask, *adjoint
    )
    return tuple(
        array.reshape(1, length, array.shape[1])
        for array in (attended, grad_tokens, grad_keys, grad_values)
    )


def solution(mesh):
    count, spread = mesh.shape["ctx"], mesh.shape["dp"]
    fine = Mesh(mesh.devices.reshape(count // 2, 2, spread), ("chip", "core", "dp"))
    block = P("dp", CTX, None)
    rows = P(("chip", "core", "dp"), None)
    in_specs = (block, block, block, rows, block, block, block)
    return jax.shard_map(
        per_device, mesh=fine, in_specs=in_specs, out_specs=(block,) * 4, check_vma=False
    )
```

```python
import functools
import math

import jax
import jax.numpy as jnp
from jax import lax
from jax.experimental import pallas as pl
from jax.experimental.pallas import tpu as pltpu
from jax.sharding import Mesh, PartitionSpec as P

HEAD = 128
PIECE = 128
WIDE = 512
CTX = ("chip", "core")
SWAP = [(0, 1), (1, 0)]
f32, bf16 = jnp.float32, jnp.bfloat16
VMEM_LIMIT = 18 * 1024 * 1024


def nn(a, b):
    return lax.dot_general(a, b, (((1,), (0,)), ((), ())), preferred_element_type=f32)


def nt(a, b):
    return lax.dot_general(a, b, (((1,), (1,)), ((), ())), preferred_element_type=f32)


def tn(a, b):
    return lax.dot_general(a, b, (((0,), (0,)), ((), ())), preferred_element_type=f32)


def params(flops, moved):
    return dict(
        compiler_params=pltpu.CompilerParams(vmem_limit_bytes=VMEM_LIMIT),
        cost_estimate=pl.CostEstimate(flops=flops, bytes_accessed=moved, transcendentals=0),
    )


MARK = jax.ShapeDtypeStruct((8, HEAD), f32)


def set_mark(mark_ref):
    mark_ref[...] = jnp.zeros_like(mark_ref)


def fast(array):
    return pltpu.with_memory_space_constraint(array, pltpu.VMEM)


def slow(array):
    return pltpu.with_memory_space_constraint(array, pltpu.HBM)


def specs(places):
    spaces = dict(V=pltpu.VMEM, H=pltpu.HBM, S=pltpu.SMEM, A=pl.ANY)
    return [pl.BlockSpec(memory_space=spaces[place]) for place in places]


def kernel_call(body, places, args, out_places, outs, name, cost, scratch=(), aliases=None):
    holds = dict(V=fast, H=slow)
    made = pl.pallas_call(
        body,
        in_specs=specs(places),
        out_specs=specs(out_places),
        out_shape=[
            pltpu.VMEM(shape, dtype) if place == "V" else jax.ShapeDtypeStruct(shape, dtype)
            for place, (shape, dtype) in zip(out_places, outs)
        ],
        scratch_shapes=list(scratch),
        input_output_aliases=aliases or {},
        name=name,
        **params(*cost),
    )
    return made(
        *[holds[place](one) if place in holds else one for place, one in zip(places, args)]
    )


class Copies:
    def __init__(self, sems):
        self.sems = sems
        self.used = 0

    def start(self, source, target):
        copy = pltpu.make_async_copy(source, target, self.sems.at[self.used])
        self.used += 1
        copy.start()
        return copy


def crossed(side):
    return (0, 1 + side, 2 - side, 3)


def all_places(special, number):
    if not special:
        return list(range(number))
    chip, core, layer = (lax.axis_index(name) for name in ("chip", "core", "dp"))
    upper = layer < 2
    layers = [layer, layer ^ 1, jnp.where(upper, 2, 1), jnp.where(upper, 3, 0)]

    def some(*arrivals):
        return [
            ((chip ^ crossed(side)[flip]) * 2 + side) * 4 + layers[one]
            for side in (core, 1 - core)
            for one, flips in arrivals
            for flip in flips
        ]

    three = (0, 1, 2)
    return (
        some((0, (0, 1, 2, 3)), (1, three))
        + some((2, three), (3, (0,)))
        + some((1, (3,)), (2, (3,)), (3, (1, 2)))
        + some((3, (3,)))
    )


def piece_columns(place):
    return (slice(None), pl.ds(pl.multiple_of(place * PIECE, PIECE), PIECE))


def columns(at, wide=None):
    return (slice(None), pl.ds(at, wide or WIDE))


def groups(total, body):
    @pl.loop(0, total // WIDE)
    def _(group):
        body(group, pl.multiple_of(group * WIDE, WIDE))


def heads(at):
    return [pl.ds(pl.multiple_of(at + head, HEAD), HEAD) for head in range(0, WIDE, HEAD)]


def memory_kernel(
    special, key_ref, spike_ref, value_ref, tokens_ref, grad_ref,
    keys_ref, mask_ref, values_ref, own_ref, sent_ref, some_ref, grads_ref,
    key_in, spike_in, sems,
):
    copies = Copies(sems)
    wide = range(0, keys_ref.shape[1], WIDE)
    pairs = ((key_ref, key_in), (spike_ref, spike_in), (value_ref, values_ref))
    parts = [
        [copies.start(here.at[columns(at)], there.at[columns(at)]) for here, there in pairs]
        for at in wide
    ]
    places = all_places(special, some_ref.shape[1] // PIECE)
    ordered = [
        copies.start(tokens_ref.at[piece_columns(place)], some_ref.at[piece_columns(piece)])
        for piece, place in enumerate(places)
    ]
    ordered.append(copies.start(grad_ref, grads_ref))
    for at, part in zip(wide, parts):
        for copy in part:
            copy.wait()
        cols = slice(at, at + WIDE)
        mask = spike_in[:, cols].astype(f32).astype(bf16)
        keys = key_in[:, cols] * mask
        keys_ref[:, cols] = keys
        mask_ref[:, cols] = mask
        for head in range(0, WIDE, HEAD):
            here = slice(at + head, at + head + HEAD)
            own = tn(keys[:, head : head + HEAD], values_ref[:, here])
            own_ref[here, :] = own
            sent_ref[here, :] = own.astype(bf16)
    for copy in ordered:
        copy.wait()


def memory_call(special, key_input, k_spikes, values, tokens, cotangent):
    length, total = values.shape
    block, state = (length, total), (total, HEAD)
    return kernel_call(
        functools.partial(memory_kernel, special),
        "HHHHH",
        (key_input, k_spikes, values, tokens, cotangent),
        "VVVVVVV",
        [(block, bf16)] * 3
        + [(state, f32), (state, bf16), (tokens.shape, bf16), (block, bf16)],
        "own_memory",
        (2 * length * total * HEAD, 12 * length * total),
        [
            pltpu.VMEM(block, bf16),
            pltpu.VMEM(block, jnp.int32),
            pltpu.SemaphoreType.DMA((3 * total // WIDE + tokens.shape[1] // PIECE + 1,)),
        ],
    )


def join_kernel(*refs):
    del refs


def join(arrays, others=()):
    number = len(arrays)
    return kernel_call(
        join_kernel,
        ["A"] * (number + len(others)),
        (*[fast(one) for one in arrays], *others),
        ["A"] * number,
        [(one.shape, one.dtype) for one in arrays],
        "join",
        (0, 0),
        aliases={at: at for at in range(number)},
    )


def keep_lower(square, flipped=False):
    row = lax.broadcasted_iota(jnp.int32, square.shape, 0)
    col = lax.broadcasted_iota(jnp.int32, square.shape, 1)
    return jnp.where((col >= row) if flipped else (col <= row), square, 0.0).astype(bf16)


def causal(a, b):
    length = a.shape[0]
    cut = length - HEAD
    top = keep_lower(nt(a[:cut], b[:cut]))
    whole = nt(a[cut:], b)
    bottom = jnp.concatenate([whole[:, :cut].astype(bf16), keep_lower(whole[:, cut:])], axis=1)
    return [(slice(0, cut), slice(0, cut), top), (slice(cut, length), slice(0, length), bottom)]


def causal_turned(a, b):
    length = a.shape[0]
    whole = nt(a[:HEAD], b)
    top = jnp.concatenate(
        [keep_lower(whole[:, :HEAD], True), whole[:, HEAD:].astype(bf16)], axis=1
    )
    bottom = keep_lower(nt(a[HEAD:], b[HEAD:]), True)
    return [
        (slice(0, HEAD), slice(0, length), top),
        (slice(HEAD, length), slice(HEAD, length), bottom),
    ]


def twice(array):
    return jnp.concatenate([array, array], axis=1)


def masked_kernel(
    factor, spike_ref, grad_ref, value_ref, keys_ref, high_ref, low_ref,
    out_ref, mask_ref, spike_in, sems,
):
    total = out_ref.shape[1]

    def bring(group, at):
        return pltpu.make_async_copy(
            spike_ref.at[columns(at)], spike_in.at[columns(at)], sems.at[group]
        )

    for group in range(total // WIDE):
        bring(group, group * WIDE).start()

    def work(group, at):
        bring(group, at).wait()
        for part in heads(at):
            mask = spike_in[:, part].astype(f32)
            mask_ref[:, part] = mask.astype(bf16)
            grad, value, keys = grad_ref[:, part], value_ref[:, part], keys_ref[:, part]
            state = jnp.concatenate([high_ref[part, :], low_ref[part, :]], axis=1)
            for rows, cols, scores in causal(grad, value):
                made = nn(scores, keys[cols]) + nt(twice(grad[rows]), state)
                out_ref[rows, part] = (factor * made * mask[rows]).astype(bf16)

    groups(total, work)


def masked_call(factor, q_spikes, cotangent, values, keys, high, low):
    length, total = values.shape
    block = (length, total)
    return kernel_call(
        functools.partial(masked_kernel, factor),
        "HVVVVV",
        (q_spikes, cotangent, values, keys, high, low),
        "VV",
        [(block, bf16)] * 2,
        "masked_grad",
        (8 * length * total * length, 12 * length * total),
        [pltpu.VMEM(block, jnp.int32), pltpu.SemaphoreType.DMA((total // WIDE,))],
    )


def turned_kernel(value_ref, grad_ref, after_ref, top_ref, bottom_ref, mark_ref):
    del after_ref
    set_mark(mark_ref)
    length, total = value_ref.shape
    rest = length - HEAD
    number = WIDE // HEAD

    def work(group, at):
        for head, part in enumerate(heads(at)):
            (_, _, top), (_, _, bottom) = causal_turned(value_ref[:, part], grad_ref[:, part])
            place = group * number + head
            top_ref[:, pl.ds(pl.multiple_of(place * length, HEAD), length)] = top
            bottom_ref[:, pl.ds(pl.multiple_of(place * rest, HEAD), rest)] = bottom

    groups(total, work)


def turned_call(values, cotangent, after):
    length, total = values.shape
    number, rest = total // HEAD, length - HEAD
    return kernel_call(
        turned_kernel,
        "VVA",
        (values, cotangent, after),
        "VVV",
        [((HEAD, number * length), bf16), ((rest, number * rest), bf16), (MARK.shape, f32)],
        "turned",
        (4 * length * total * length, 0),
    )


def rows_of(blocks):
    return sum(block.shape[0] for block in blocks)


def back_blocks(blocks):
    at = 0
    for block in blocks:
        for row in range(0, block.shape[0], PIECE):
            yield at, block[row : row + PIECE, :]
            at += 1


def back_part(copies, places, masked, blocks, out_ref, round_ref):
    going = []
    pieces = list(back_blocks(blocks))
    for (first, upper), (second, lower) in zip(pieces[::2], pieces[1::2]):
        both = slice(first * PIECE, (second + 1) * PIECE)
        made = nt(masked[...], jnp.concatenate([upper, lower], axis=0))
        round_ref[:, both] = made.astype(bf16)
        for piece in (first, second):
            going.append(
                copies.start(
                    round_ref.at[piece_columns(piece)], out_ref.at[piece_columns(places[piece])]
                )
            )
    return going


def products_kernel(special, start, size, project, back, has_sum, has_back, *refs):
    blocks, refs = refs[:size], list(refs[size:])
    depth = rows_of(blocks)
    tokens_ref = refs.pop(0) if project else None
    before_ref = refs.pop(0) if has_sum else None
    masked = refs.pop(0) if back else None
    if has_back:
        refs.pop(0)
    sum_ref = refs.pop(0) if project else None
    back_out = refs.pop(0) if back else None
    mark_ref = refs.pop(0)
    set_mark(mark_ref)
    going = []
    if back:
        round_ref, sems = refs
        places = all_places(special, back_out.shape[1] // PIECE)[start:]
        going = back_part(Copies(sems), places, masked, blocks, back_out, round_ref)
    if project:
        cols = slice(start * PIECE, start * PIECE + depth)
        for at in range(0, sum_ref.shape[1], WIDE):
            part = slice(at, at + WIDE)
            made = nn(
                tokens_ref[:, cols],
                jnp.concatenate([block[:, part] for block in blocks], axis=0),
            )
            if has_sum:
                made = made + before_ref[:, part]
            sum_ref[:, part] = made
    for copy in going:
        copy.wait()


def products_call(
    special, start, blocks, tokens, partial=None, masked=None, grad=None, project=True
):
    length, width = tokens.shape
    total = blocks[0].shape[1]
    depth = rows_of(blocks)
    back = masked is not None
    places_in, args = "V" * len(blocks), list(blocks)
    places_out, outs = "", []
    scratch, aliases = [], {}
    if project:
        places_in, args = places_in + "V", args + [tokens]
        if partial is not None:
            aliases[len(args)] = 0
            places_in, args = places_in + "V", args + [partial]
        places_out, outs = "V", [((length, total), f32)]
    if back:
        places_in, args = places_in + "V", args + [masked]
        if grad is not None:
            aliases[len(args)] = len(outs)
            places_in, args = places_in + "H", args + [grad]
        places_out, outs = places_out + "H", outs + [((length, width), bf16)]
        scratch = [
            pltpu.VMEM((length, depth), bf16), pltpu.SemaphoreType.DMA((depth // PIECE,))
        ]
    made = kernel_call(
        functools.partial(
            products_kernel, special, start, len(blocks), project, back,
            partial is not None, grad is not None,
        ),
        places_in,
        args,
        places_out + "V",
        outs + [(MARK.shape, f32)],
        "products" if project and back else "project" if project else "grad_tokens",
        (2 * (project + back) * length * depth * total, 0),
        scratch,
        aliases,
    )
    made = list(made)
    partial = made.pop(0) if project else partial
    grad = made.pop(0) if back else grad
    return partial, grad, made[0]


def query_kernel(start, size, tokens_ref, sum_ref, mask_ref, grad_ref, *refs):
    blocks = refs[:size]
    queries, own_ref, sent_ref = refs[-3:]
    cols = slice(start * PIECE, start * PIECE + rows_of(blocks))
    for at in range(0, queries.shape[1], WIDE):
        part = slice(at, at + WIDE)
        made = nn(
            tokens_ref[:, cols], jnp.concatenate([block[:, part] for block in blocks], axis=0)
        )
        made = made + sum_ref[:, part]
        made = (made * mask_ref[:, part].astype(f32)).astype(bf16)
        queries[:, part] = made
        for head in range(0, WIDE, HEAD):
            here = slice(at + head, at + head + HEAD)
            own = tn(made[:, head : head + HEAD], grad_ref[:, here])
            own_ref[here, :] = own
            sent_ref[here, :] = own.astype(bf16)


def query_call(start, tokens, blocks, before, q_mask, cotangent, others):
    length = tokens.shape[0]
    total = blocks[0].shape[1]
    depth = rows_of(blocks)
    return kernel_call(
        functools.partial(query_kernel, start, len(blocks)),
        "VVVV" + "V" * len(blocks) + "A" * len(others),
        (tokens, before, q_mask, cotangent, *blocks, *others),
        "VVV",
        [((length, total), bf16), ((total, HEAD), f32), ((total, HEAD), bf16)],
        "queries",
        (2 * length * depth * total, 0),
    )


def out_copy(here, there, sems, group, at):
    return pltpu.make_async_copy(here.at[columns(at)], there.at[columns(at)], sems.at[group])


def attend_kernel(
    factor, query_ref, keys_ref, value_ref, high_ref, low_ref, out_ref, mark_ref, made_ref, sems
):
    set_mark(mark_ref)
    total = query_ref.shape[1]

    def work(group, at):
        for part in heads(at):
            query, keys, value = query_ref[:, part], keys_ref[:, part], value_ref[:, part]
            state = [high_ref[part, :], low_ref[part, :]]
            for rows, cols, scores in causal(query, keys):
                made = nn(
                    jnp.concatenate([scores, twice(query[rows])], axis=1),
                    jnp.concatenate([value[cols], *state], axis=0),
                )
                made_ref[rows, part] = (factor * made).astype(bf16)
        out_copy(made_ref, out_ref, sems, group, at).start()

    groups(total, work)
    for group in range(total // WIDE):
        out_copy(made_ref, out_ref, sems, group, group * WIDE).wait()


def attend_call(factor, queries, keys, values, high, low):
    length, total = values.shape
    return kernel_call(
        functools.partial(attend_kernel, factor),
        "VVVVV",
        (queries, keys, values, high, low),
        "HV",
        [((length, total), bf16), (MARK.shape, f32)],
        "attended",
        (8 * length * total * length, 8 * length * total),
        [pltpu.VMEM((length, total), bf16), pltpu.SemaphoreType.DMA((total // WIDE,))],
    )


def value_kernel(query_ref, keys_ref, grad_ref, val_ref, mark_ref):
    set_mark(mark_ref)

    def work(group, at):
        for part in heads(at):
            query, keys, grad = query_ref[:, part], keys_ref[:, part], grad_ref[:, part]
            for rows, cols, scores in causal_turned(keys, query):
                val_ref[rows, part] = nn(scores, grad[cols])

    groups(query_ref.shape[1], work)


def value_call(queries, keys, cotangent):
    length, total = keys.shape
    return kernel_call(
        value_kernel,
        "VVV",
        (queries, keys, cotangent),
        "VV",
        [((length, total), f32), (MARK.shape, f32)],
        "value_part",
        (6 * length * total * length, 0),
    )


def key_kernel(query_ref, top_ref, bottom_ref, key_ref):
    length, total = query_ref.shape
    rest = length - HEAD
    number = WIDE // HEAD

    def work(group, at):
        for head, part in enumerate(heads(at)):
            query = query_ref[:, part]
            place = group * number + head
            top = top_ref[:, pl.ds(pl.multiple_of(place * length, HEAD), length)]
            bottom = bottom_ref[:, pl.ds(pl.multiple_of(place * rest, HEAD), rest)]
            key_ref[:HEAD, part] = nn(top, query)
            key_ref[HEAD:, part] = nn(bottom, query[HEAD:])

    groups(total, work)


def key_call(queries, top, bottom):
    length, total = queries.shape
    return kernel_call(
        key_kernel,
        "VVV",
        (queries, top, bottom),
        "V",
        [((length, total), f32)],
        "key_part",
        (4 * length * total * length, 0),
    )[0]


def outer_kernel(
    factor, key_ref, val_ref, keys_ref, value_ref, mask_ref, high_ref, low_ref,
    key_out, val_out, key_made, val_made, key_sems, val_sems,
):
    total = keys_ref.shape[1]

    def work(group, at):
        for part in heads(at):
            keys, value = keys_ref[:, part], value_ref[:, part]
            state = [high_ref[part, :], low_ref[part, :]]
            key_grad = key_ref[:, part] + nt(twice(value), jnp.concatenate(state, axis=1))
            key_made[:, part] = (factor * key_grad * mask_ref[:, part].astype(f32)).astype(bf16)
            value_grad = val_ref[:, part] + nn(twice(keys), jnp.concatenate(state, axis=0))
            val_made[:, part] = (factor * value_grad).astype(bf16)
        out_copy(key_made, key_out, key_sems, group, at).start()
        out_copy(val_made, val_out, val_sems, group, at).start()

    groups(total, work)
    for group in range(total // WIDE):
        out_copy(key_made, key_out, key_sems, group, group * WIDE).wait()
        out_copy(val_made, val_out, val_sems, group, group * WIDE).wait()


def outer_call(factor, key_part, value_part, keys, values, k_mask, high, low):
    length, total = values.shape
    block = (length, total)
    return kernel_call(
        functools.partial(outer_kernel, factor),
        "VVVVVVV",
        (key_part, value_part, keys, values, k_mask, high, low),
        "HH",
        [(block, bf16)] * 2,
        "outer",
        (8 * length * total * HEAD, 20 * length * total),
        [pltpu.VMEM(block, bf16)] * 2 + [pltpu.SemaphoreType.DMA((total // WIDE,))] * 2,
    )


def halves(state):
    high = state.astype(bf16)
    return high, (state - high.astype(f32)).astype(bf16)


def scan_any(own, sent, count, reverse):
    place = lax.axis_index(CTX)
    total = own
    state = jnp.zeros_like(own)
    bits = count.bit_length() - 1
    for bit in range(bits):
        step = 1 << bit
        last = bit == bits - 1
        pairs = []
        for source in range(count):
            high = bool(source & step)
            if not last or high == reverse:
                pairs.append((source, source ^ step))
        got = lax.ppermute(sent, CTX, pairs).astype(f32)
        if last:
            state = state + got
        else:
            mine = ((place // step) % 2) == (0 if reverse else 1)
            state = state + jnp.where(mine, got, 0.0)
            total = total + got
            sent = total.astype(bf16)
    return state


def links(first, keep=lambda source, target: True):
    pairs = []
    for chip in range(4):
        for core in range(2):
            other = chip ^ (first if core == 0 else 3 - first)
            if keep((chip, core), other):
                pairs.append((chip * 2 + core, other * 2 + core))
    return pairs


def upward(reverse):
    flip = 3 if reverse else 0

    def keep(source, target):
        at = source[0] ^ flip
        return source[0] ^ target == 1 or not at & 2

    return keep


def low_bit(reverse):
    chip = lax.axis_index("chip")
    return 1 - chip % 2 if reverse else chip % 2


def half_rows(array_ref, core):
    half = array_ref.shape[0] // 2
    return array_ref[pl.ds(pl.multiple_of(core * half, half), half), :]


def both_kernel(own_ref, sibling_ref, *refs):
    both_ref, sent_ref = refs[-2:]
    core = lax.axis_index("core")
    both = half_rows(own_ref, core) + half_rows(sibling_ref, core).astype(f32)
    both_ref[...] = both
    sent_ref[...] = both.astype(bf16)


def message_kernel(reverse, got_ref, both_ref, *refs):
    core = lax.axis_index("core")
    adds = jnp.where((core == 0) | (low_bit(reverse) == 0), 1.0, 0.0)
    refs[-1][...] = (got_ref[...].astype(f32) + adds * both_ref[...]).astype(bf16)


def state_kernel(reverse, got_ref, more_ref, *refs):
    core = lax.axis_index("core")
    adds = jnp.where((core == 1) | (low_bit(reverse) == 1), 1.0, 0.0)
    refs[-1][...] = adds * got_ref[...].astype(f32) + more_ref[...].astype(f32)


def whole_kernel(reverse, state_ref, other_ref, sibling_ref, high_ref, low_ref):
    core = lax.axis_index("core")
    adds = jnp.where(core == (0 if reverse else 1), 1.0, 0.0)
    half = state_ref.shape[0]
    for ref, side in ((state_ref, core), (other_ref, 1 - core)):
        rows = pl.ds(pl.multiple_of(side * half, half), half)
        whole = ref[...] + adds * sibling_ref[rows, :].astype(f32)
        high = whole.astype(bf16)
        high_ref[rows, :] = high
        low_ref[rows, :] = (whole - high.astype(f32)).astype(bf16)


def send_first(own, sent, reverse, others=()):
    half = (own.shape[0] // 2, HEAD)
    sibling = lax.ppermute(sent, "core", SWAP)
    both, sent = kernel_call(
        both_kernel,
        "VV" + "A" * len(others),
        (own, sibling, *others),
        "VV",
        [(half, f32), (half, bf16)],
        "both",
        (0, 0),
    )
    return sibling, both, lax.ppermute(sent, CTX, links(1, upward(reverse)))


def send_second(got, both, reverse, others=()):
    (message,) = kernel_call(
        functools.partial(message_kernel, reverse),
        "VV" + "A" * len(others),
        (got, both, *others),
        "V",
        [(both.shape, bf16)],
        "message",
        (0, 0),
    )
    return lax.ppermute(message, CTX, links(2, upward(reverse)))


def add_up(got, more, sibling, reverse, others=()):
    (state,) = kernel_call(
        functools.partial(state_kernel, reverse),
        "VV" + "A" * len(others),
        (got, more, *others),
        "V",
        [(got.shape, f32)],
        "state",
        (0, 0),
    )
    other = lax.ppermute(state, "core", SWAP)
    return kernel_call(
        functools.partial(whole_kernel, reverse),
        "VVV",
        (state, other, sibling),
        "VV",
        [(sibling.shape, bf16)] * 2,
        "whole",
        (0, 0),
    )


def gather_any(q_weight):
    whole = lax.all_gather(q_weight, ("chip", "core", "dp"), axis=0, tiled=True)
    cut = whole.shape[0] // (2 * PIECE) * PIECE
    return [whole[:cut], whole[cut:]]


def pack_kernel(number, *refs):
    arrays, (out_ref, sems) = refs[:number], refs[-2:]
    copies = Copies(sems)
    rows = out_ref.shape[0] // len(arrays)
    going = [
        copies.start(array, out_ref.at[pl.ds(at * rows, rows), :])
        for at, array in enumerate(arrays)
    ]
    for copy in going:
        copy.wait()


def pack(*arrays, others=()):
    rows, total = arrays[0].shape
    number = len(arrays)
    (made,) = kernel_call(
        functools.partial(pack_kernel, number),
        "A" * (number + len(others)),
        (*arrays, *others),
        "V",
        [((number * rows, total), arrays[0].dtype)],
        "pack",
        (0, 0),
        [pltpu.SemaphoreType.DMA((number,))],
    )
    return [made, lax.ppermute(made, "core", SWAP)]


def choose_kernel(inner_ref, end_ref, out_ref, sem):
    del end_ref
    layer = lax.axis_index("dp")

    @pl.when((layer == 1) | (layer == 2))
    def _():
        copy = pltpu.make_async_copy(inner_ref, out_ref, sem)
        copy.start()
        copy.wait()


def choose(inner, end):
    return kernel_call(
        choose_kernel,
        "AA",
        (fast(inner), fast(end)),
        "A",
        [(inner.shape, inner.dtype)],
        "choose",
        (0, 0),
        [pltpu.SemaphoreType.DMA],
        {1: 0},
    )[0]


def per_device(tokens, key_input, values, q_weight, q_spikes, k_spikes, cotangent):
    batches, length, width = tokens.shape
    assert batches == 1
    total = q_weight.shape[1]
    chips, spread = lax.axis_size("chip"), lax.axis_size("dp")
    factor = 3.0 / math.sqrt(HEAD * length * chips * 2)
    tokens, key_input, values, q_spikes, k_spikes, cotangent = (
        array.reshape(length, array.shape[2])
        for array in (tokens, key_input, values, q_spikes, k_spikes, cotangent)
    )
    special = chips == 4 and spread == 4

    def sibling(array):
        return lax.ppermute(array, "core", SWAP)

    def along(array, pairs):
        return lax.ppermute(array, "dp", pairs)

    def cross(array):
        return lax.ppermute(array, CTX, links(1)), lax.ppermute(array, CTX, links(2))

    def onward(array):
        return lax.ppermute(array, CTX, links(2))

    keys, k_mask, values, own, sent, tokens, cotangent = memory_call(
        special, key_input, k_spikes, values, tokens, cotangent
    )
    if special:
        ends = [(0, 1), (1, 0), (2, 3), (3, 2)]
        middle = [(1, 2), (2, 1)]
        outward = [(1, 0), (2, 3)]
        near = along(q_weight, ends)
        mid = along(q_weight, middle)
        first_0, second_0 = cross(q_weight)
        first_0, second_0, near, mid, sent = join([first_0, second_0, near, mid, sent])
    else:
        arrived = gather_any(q_weight)
        high, low = halves(scan_any(own, sent, chips * 2, False))

    if special:
        third_0 = onward(first_0)
        first_1, second_1 = cross(near)
        far = along(near, middle)
        mid_out = along(mid, outward)
        twin, both, got = send_first(own, sent, False)
        third_0, first_1, second_1, far, mid_out, got = join(
            [third_0, first_1, second_1, far, mid_out, got]
        )
        more = send_second(got, both, False)
        next_layer = choose(mid, mid_out)
        first_2, second_2 = cross(next_layer)
        far_out = along(far, outward)
        early = pack(q_weight, first_0, second_0, third_0, near, first_1, second_1)
        partial, _, mark = products_call(special, 0, early, tokens)
        top, bottom, turned_mark = turned_call(values, cotangent, got)
        far_out, first_2, second_2, more, third_0 = join(
            [far_out, first_2, second_2, more, third_0], [mark, turned_mark]
        )
        third_1 = along(third_0, ends)
        third_2 = onward(first_2)
        last_layer = choose(far, far_out)
        first_3, second_3 = cross(last_layer)
        high, low = add_up(got, more, twin, False)
        masked, q_mask = masked_call(factor, q_spikes, cotangent, values, keys, high, low)
        middle = pack(next_layer, first_2, second_2, last_layer)
        _, grad, mark = products_call(special, 0, early, tokens, masked=masked, project=False)
        third_2, first_3, second_3, third_1, middle[1] = join(
            [third_2, first_3, second_3, third_1, middle[1]], [mark]
        )
        third_3 = onward(first_3)
        late = pack(third_1, third_2, first_3, second_3)
        partial, grad, mark_0 = products_call(
            special, 14, middle, tokens, partial, masked, grad
        )
        partial, _, mark_1 = products_call(special, 22, late, tokens, partial)
        third_3, = join([third_3], [mark_0, mark_1])
        _, grad, mark = products_call(
            special, 22, late, tokens, masked=masked, grad=grad, project=False
        )
        late = [third_3, sibling(third_3)]
        start = 30
    else:
        masked, q_mask = masked_call(factor, q_spikes, cotangent, values, keys, high, low)
        top, bottom, _ = turned_call(values, cotangent, own)
        start = arrived[0].shape[0] // PIECE
        partial, grad, mark = products_call(special, 0, arrived[:1], tokens, masked=masked)
        late = arrived[1:]
    queries, own, sent = query_call(start, tokens, late, partial, q_mask, cotangent, [mark])
    attended, attended_mark = attend_call(factor, queries, keys, values, high, low)
    value_part, value_mark = value_call(queries, keys, cotangent)
    key_part = key_call(queries, top, bottom)
    _, grad_tokens, back_mark = products_call(
        special, start, late, tokens, masked=masked, grad=grad, project=False
    )
    if special:
        twin, both, got = send_first(own, sent, True, [back_mark])
        more = send_second(got, both, True, [attended_mark])
        adjoint = add_up(got, more, twin, True, [value_mark])
    else:
        adjoint = halves(scan_any(own, sent, chips * 2, True))
    grad_keys, grad_values = outer_call(
        factor, key_part, value_part, keys, values, k_mask, *adjoint
    )
    return tuple(
        array.reshape(1, length, array.shape[1])
        for array in (attended, grad_tokens, grad_keys, grad_values)
    )


def solution(mesh):
    count, spread = mesh.shape["ctx"], mesh.shape["dp"]
    fine = Mesh(mesh.devices.reshape(count // 2, 2, spread), ("chip", "core", "dp"))
    block = P("dp", CTX, None)
    rows = P(("chip", "core", "dp"), None)
    in_specs = (block, block, block, rows, block, block, block)
    return jax.shard_map(
        per_device, mesh=fine, in_specs=in_specs, out_specs=(block,) * 4, check_vma=False
    )
```

```python
import functools
import math

import jax
import jax.numpy as jnp
from jax import lax
from jax.experimental import pallas as pl
from jax.experimental.pallas import tpu as pltpu
from jax.sharding import Mesh, PartitionSpec as P

HEAD = 128
PIECE = 128
WIDE = 512
CTX = ("chip", "core")
SWAP = [(0, 1), (1, 0)]
f32, bf16 = jnp.float32, jnp.bfloat16
VMEM_LIMIT = 18 * 1024 * 1024


def nn(a, b):
    return lax.dot_general(a, b, (((1,), (0,)), ((), ())), preferred_element_type=f32)


def nt(a, b):
    return lax.dot_general(a, b, (((1,), (1,)), ((), ())), preferred_element_type=f32)


def tn(a, b):
    return lax.dot_general(a, b, (((0,), (0,)), ((), ())), preferred_element_type=f32)


def params(flops, moved):
    return dict(
        compiler_params=pltpu.CompilerParams(vmem_limit_bytes=VMEM_LIMIT),
        cost_estimate=pl.CostEstimate(flops=flops, bytes_accessed=moved, transcendentals=0),
    )


MARK = jax.ShapeDtypeStruct((8, HEAD), f32)


def set_mark(mark_ref):
    mark_ref[...] = jnp.zeros_like(mark_ref)


def fast(array):
    return pltpu.with_memory_space_constraint(array, pltpu.VMEM)


def slow(array):
    return pltpu.with_memory_space_constraint(array, pltpu.HBM)


def specs(places):
    spaces = dict(V=pltpu.VMEM, H=pltpu.HBM, S=pltpu.SMEM, A=pl.ANY)
    return [pl.BlockSpec(memory_space=spaces[place]) for place in places]


def kernel_call(body, places, args, out_places, outs, name, cost, scratch=(), aliases=None):
    holds = dict(V=fast, H=slow)
    made = pl.pallas_call(
        body,
        in_specs=specs(places),
        out_specs=specs(out_places),
        out_shape=[
            pltpu.VMEM(shape, dtype) if place == "V" else jax.ShapeDtypeStruct(shape, dtype)
            for place, (shape, dtype) in zip(out_places, outs)
        ],
        scratch_shapes=list(scratch),
        input_output_aliases=aliases or {},
        name=name,
        **params(*cost),
    )
    return made(
        *[holds[place](one) if place in holds else one for place, one in zip(places, args)]
    )


class Copies:
    def __init__(self, sems):
        self.sems = sems
        self.used = 0

    def start(self, source, target):
        copy = pltpu.make_async_copy(source, target, self.sems.at[self.used])
        self.used += 1
        copy.start()
        return copy


def crossed(side):
    return (0, 1 + side, 2 - side, 3)


def all_places(special, number):
    if not special:
        return list(range(number))
    chip, core, layer = (lax.axis_index(name) for name in ("chip", "core", "dp"))
    upper = layer < 2
    layers = [layer, layer ^ 1, jnp.where(upper, 2, 1), jnp.where(upper, 3, 0)]

    def some(*arrivals):
        return [
            ((chip ^ crossed(side)[flip]) * 2 + side) * 4 + layers[one]
            for side in (core, 1 - core)
            for one, flips in arrivals
            for flip in flips
        ]

    three = (0, 1, 2)
    return (
        some((0, (0, 1, 2, 3)), (1, three))
        + some((2, three), (3, (0,)))
        + some((1, (3,)), (2, (3,)), (3, (1, 2)))
        + some((3, (3,)))
    )


def piece_columns(place):
    return (slice(None), pl.ds(pl.multiple_of(place * PIECE, PIECE), PIECE))


def columns(at, wide=None):
    return (slice(None), pl.ds(at, wide or WIDE))


def groups(total, body):
    @pl.loop(0, total // WIDE)
    def _(group):
        body(group, pl.multiple_of(group * WIDE, WIDE))


def heads(at):
    return [pl.ds(pl.multiple_of(at + head, HEAD), HEAD) for head in range(0, WIDE, HEAD)]


def memory_kernel(
    special, key_ref, spike_ref, value_ref, tokens_ref, grad_ref,
    keys_ref, mask_ref, values_ref, own_ref, sent_ref, some_ref, grads_ref,
    key_in, spike_in, sems,
):
    copies = Copies(sems)
    wide = range(0, keys_ref.shape[1], WIDE)
    pairs = ((key_ref, key_in), (spike_ref, spike_in), (value_ref, values_ref))
    parts = [
        [copies.start(here.at[columns(at)], there.at[columns(at)]) for here, there in pairs]
        for at in wide
    ]
    places = all_places(special, some_ref.shape[1] // PIECE)
    ordered = [
        copies.start(tokens_ref.at[piece_columns(place)], some_ref.at[piece_columns(piece)])
        for piece, place in enumerate(places)
    ]
    ordered.append(copies.start(grad_ref, grads_ref))
    for at, part in zip(wide, parts):
        for copy in part:
            copy.wait()
        cols = slice(at, at + WIDE)
        mask = spike_in[:, cols].astype(f32).astype(bf16)
        keys = key_in[:, cols] * mask
        keys_ref[:, cols] = keys
        mask_ref[:, cols] = mask
        for head in range(0, WIDE, HEAD):
            here = slice(at + head, at + head + HEAD)
            own = tn(keys[:, head : head + HEAD], values_ref[:, here])
            own_ref[here, :] = own
            sent_ref[here, :] = own.astype(bf16)
    for copy in ordered:
        copy.wait()


def memory_call(special, key_input, k_spikes, values, tokens, cotangent):
    length, total = values.shape
    block, state = (length, total), (total, HEAD)
    return kernel_call(
        functools.partial(memory_kernel, special),
        "HHHHH",
        (key_input, k_spikes, values, tokens, cotangent),
        "VVVVVVV",
        [(block, bf16)] * 3
        + [(state, f32), (state, bf16), (tokens.shape, bf16), (block, bf16)],
        "own_memory",
        (2 * length * total * HEAD, 12 * length * total),
        [
            pltpu.VMEM(block, bf16),
            pltpu.VMEM(block, jnp.int32),
            pltpu.SemaphoreType.DMA((3 * total // WIDE + tokens.shape[1] // PIECE + 1,)),
        ],
    )


def join_kernel(*refs):
    del refs


def join(arrays, others=()):
    number = len(arrays)
    return kernel_call(
        join_kernel,
        ["A"] * (number + len(others)),
        (*[fast(one) for one in arrays], *others),
        ["A"] * number,
        [(one.shape, one.dtype) for one in arrays],
        "join",
        (0, 0),
        aliases={at: at for at in range(number)},
    )


def keep_lower(square, flipped=False):
    row = lax.broadcasted_iota(jnp.int32, square.shape, 0)
    col = lax.broadcasted_iota(jnp.int32, square.shape, 1)
    return jnp.where((col >= row) if flipped else (col <= row), square, 0.0).astype(bf16)


def causal(a, b):
    length = a.shape[0]
    cut = length - HEAD
    top = keep_lower(nt(a[:cut], b[:cut]))
    whole = nt(a[cut:], b)
    bottom = jnp.concatenate([whole[:, :cut].astype(bf16), keep_lower(whole[:, cut:])], axis=1)
    return [(slice(0, cut), slice(0, cut), top), (slice(cut, length), slice(0, length), bottom)]


def causal_turned(a, b):
    length = a.shape[0]
    whole = nt(a[:HEAD], b)
    top = jnp.concatenate(
        [keep_lower(whole[:, :HEAD], True), whole[:, HEAD:].astype(bf16)], axis=1
    )
    bottom = keep_lower(nt(a[HEAD:], b[HEAD:]), True)
    return [
        (slice(0, HEAD), slice(0, length), top),
        (slice(HEAD, length), slice(HEAD, length), bottom),
    ]


def twice(array):
    return jnp.concatenate([array, array], axis=1)


def masked_kernel(
    factor, spike_ref, grad_ref, value_ref, keys_ref, high_ref, low_ref,
    out_ref, mask_ref, spike_in, sems,
):
    total = out_ref.shape[1]

    def bring(group, at):
        return pltpu.make_async_copy(
            spike_ref.at[columns(at)], spike_in.at[columns(at)], sems.at[group]
        )

    for group in range(total // WIDE):
        bring(group, group * WIDE).start()

    def work(group, at):
        bring(group, at).wait()
        for part in heads(at):
            mask = spike_in[:, part].astype(f32)
            mask_ref[:, part] = mask.astype(bf16)
            grad, value, keys = grad_ref[:, part], value_ref[:, part], keys_ref[:, part]
            state = jnp.concatenate([high_ref[part, :], low_ref[part, :]], axis=1)
            for rows, cols, scores in causal(grad, value):
                made = nn(scores, keys[cols]) + nt(twice(grad[rows]), state)
                out_ref[rows, part] = (factor * made * mask[rows]).astype(bf16)

    groups(total, work)


def masked_call(factor, q_spikes, cotangent, values, keys, high, low):
    length, total = values.shape
    block = (length, total)
    return kernel_call(
        functools.partial(masked_kernel, factor),
        "HVVVVV",
        (q_spikes, cotangent, values, keys, high, low),
        "VV",
        [(block, bf16)] * 2,
        "masked_grad",
        (8 * length * total * length, 12 * length * total),
        [pltpu.VMEM(block, jnp.int32), pltpu.SemaphoreType.DMA((total // WIDE,))],
    )


def turned_kernel(value_ref, grad_ref, after_ref, top_ref, bottom_ref, mark_ref):
    del after_ref
    set_mark(mark_ref)
    length, total = value_ref.shape
    rest = length - HEAD
    number = WIDE // HEAD

    def work(group, at):
        for head, part in enumerate(heads(at)):
            (_, _, top), (_, _, bottom) = causal_turned(value_ref[:, part], grad_ref[:, part])
            place = group * number + head
            top_ref[:, pl.ds(pl.multiple_of(place * length, HEAD), length)] = top
            bottom_ref[:, pl.ds(pl.multiple_of(place * rest, HEAD), rest)] = bottom

    groups(total, work)


def turned_call(values, cotangent, after):
    length, total = values.shape
    number, rest = total // HEAD, length - HEAD
    return kernel_call(
        turned_kernel,
        "VVA",
        (values, cotangent, after),
        "VVV",
        [((HEAD, number * length), bf16), ((rest, number * rest), bf16), (MARK.shape, f32)],
        "turned",
        (4 * length * total * length, 0),
    )


def rows_of(blocks):
    return sum(block.shape[0] for block in blocks)


def back_blocks(blocks):
    at = 0
    for block in blocks:
        for row in range(0, block.shape[0], PIECE):
            yield at, block[row : row + PIECE, :]
            at += 1


def back_part(copies, places, masked, blocks, out_ref, round_ref):
    going = []
    pieces = list(back_blocks(blocks))
    for (first, upper), (second, lower) in zip(pieces[::2], pieces[1::2]):
        both = slice(first * PIECE, (second + 1) * PIECE)
        made = nt(masked[...], jnp.concatenate([upper, lower], axis=0))
        round_ref[:, both] = made.astype(bf16)
        for piece in (first, second):
            going.append(
                copies.start(
                    round_ref.at[piece_columns(piece)], out_ref.at[piece_columns(places[piece])]
                )
            )
    return going


def products_kernel(special, start, size, project, back, has_sum, has_back, *refs):
    blocks, refs = refs[:size], list(refs[size:])
    depth = rows_of(blocks)
    tokens_ref = refs.pop(0) if project else None
    before_ref = refs.pop(0) if has_sum else None
    masked = refs.pop(0) if back else None
    if has_back:
        refs.pop(0)
    sum_ref = refs.pop(0) if project else None
    back_out = refs.pop(0) if back else None
    mark_ref = refs.pop(0)
    set_mark(mark_ref)
    going = []
    if back:
        round_ref, sems = refs
        places = all_places(special, back_out.shape[1] // PIECE)[start:]
        going = back_part(Copies(sems), places, masked, blocks, back_out, round_ref)
    if project:
        cols = slice(start * PIECE, start * PIECE + depth)
        for at in range(0, sum_ref.shape[1], WIDE):
            part = slice(at, at + WIDE)
            made = nn(
                tokens_ref[:, cols],
                jnp.concatenate([block[:, part] for block in blocks], axis=0),
            )
            if has_sum:
                made = made + before_ref[:, part]
            sum_ref[:, part] = made
    for copy in going:
        copy.wait()


def products_call(
    special, start, blocks, tokens, partial=None, masked=None, grad=None, project=True
):
    length, width = tokens.shape
    total = blocks[0].shape[1]
    depth = rows_of(blocks)
    back = masked is not None
    places_in, args = "V" * len(blocks), list(blocks)
    places_out, outs = "", []
    scratch, aliases = [], {}
    if project:
        places_in, args = places_in + "V", args + [tokens]
        if partial is not None:
            aliases[len(args)] = 0
            places_in, args = places_in + "V", args + [partial]
        places_out, outs = "V", [((length, total), f32)]
    if back:
        places_in, args = places_in + "V", args + [masked]
        if grad is not None:
            aliases[len(args)] = len(outs)
            places_in, args = places_in + "H", args + [grad]
        places_out, outs = places_out + "H", outs + [((length, width), bf16)]
        scratch = [
            pltpu.VMEM((length, depth), bf16), pltpu.SemaphoreType.DMA((depth // PIECE,))
        ]
    made = kernel_call(
        functools.partial(
            products_kernel, special, start, len(blocks), project, back,
            partial is not None, grad is not None,
        ),
        places_in,
        args,
        places_out + "V",
        outs + [(MARK.shape, f32)],
        "products" if project and back else "project" if project else "grad_tokens",
        (2 * (project + back) * length * depth * total, 0),
        scratch,
        aliases,
    )
    made = list(made)
    partial = made.pop(0) if project else partial
    grad = made.pop(0) if back else grad
    return partial, grad, made[0]


def query_kernel(start, size, tokens_ref, sum_ref, mask_ref, grad_ref, *refs):
    blocks = refs[:size]
    queries, own_ref, sent_ref = refs[-3:]
    cols = slice(start * PIECE, start * PIECE + rows_of(blocks))
    for at in range(0, queries.shape[1], WIDE):
        part = slice(at, at + WIDE)
        made = nn(
            tokens_ref[:, cols], jnp.concatenate([block[:, part] for block in blocks], axis=0)
        )
        made = made + sum_ref[:, part]
        made = (made * mask_ref[:, part].astype(f32)).astype(bf16)
        queries[:, part] = made
        for head in range(0, WIDE, HEAD):
            here = slice(at + head, at + head + HEAD)
            own = tn(made[:, head : head + HEAD], grad_ref[:, here])
            own_ref[here, :] = own
            sent_ref[here, :] = own.astype(bf16)


def query_call(start, tokens, blocks, before, q_mask, cotangent, others):
    length = tokens.shape[0]
    total = blocks[0].shape[1]
    depth = rows_of(blocks)
    return kernel_call(
        functools.partial(query_kernel, start, len(blocks)),
        "VVVV" + "V" * len(blocks) + "A" * len(others),
        (tokens, before, q_mask, cotangent, *blocks, *others),
        "VVV",
        [((length, total), bf16), ((total, HEAD), f32), ((total, HEAD), bf16)],
        "queries",
        (2 * length * depth * total, 0),
    )


def out_copy(here, there, sems, group, at):
    return pltpu.make_async_copy(here.at[columns(at)], there.at[columns(at)], sems.at[group])


def attend_kernel(
    factor, query_ref, keys_ref, value_ref, high_ref, low_ref, out_ref, mark_ref, made_ref, sems
):
    set_mark(mark_ref)
    total = query_ref.shape[1]

    def work(group, at):
        for part in heads(at):
            query, keys, value = query_ref[:, part], keys_ref[:, part], value_ref[:, part]
            state = [high_ref[part, :], low_ref[part, :]]
            for rows, cols, scores in causal(query, keys):
                made = nn(
                    jnp.concatenate([scores, twice(query[rows])], axis=1),
                    jnp.concatenate([value[cols], *state], axis=0),
                )
                made_ref[rows, part] = (factor * made).astype(bf16)
        out_copy(made_ref, out_ref, sems, group, at).start()

    groups(total, work)
    for group in range(total // WIDE):
        out_copy(made_ref, out_ref, sems, group, group * WIDE).wait()


def attend_call(factor, queries, keys, values, high, low):
    length, total = values.shape
    return kernel_call(
        functools.partial(attend_kernel, factor),
        "VVVVV",
        (queries, keys, values, high, low),
        "HV",
        [((length, total), bf16), (MARK.shape, f32)],
        "attended",
        (8 * length * total * length, 8 * length * total),
        [pltpu.VMEM((length, total), bf16), pltpu.SemaphoreType.DMA((total // WIDE,))],
    )


def value_kernel(query_ref, keys_ref, grad_ref, val_ref, mark_ref):
    set_mark(mark_ref)

    def work(group, at):
        for part in heads(at):
            query, keys, grad = query_ref[:, part], keys_ref[:, part], grad_ref[:, part]
            for rows, cols, scores in causal_turned(keys, query):
                val_ref[rows, part] = nn(scores, grad[cols])

    groups(query_ref.shape[1], work)


def value_call(queries, keys, cotangent):
    length, total = keys.shape
    return kernel_call(
        value_kernel,
        "VVV",
        (queries, keys, cotangent),
        "VV",
        [((length, total), f32), (MARK.shape, f32)],
        "value_part",
        (6 * length * total * length, 0),
    )


def key_kernel(query_ref, top_ref, bottom_ref, key_ref, mark_ref):
    set_mark(mark_ref)
    length, total = query_ref.shape
    rest = length - HEAD
    number = WIDE // HEAD

    def work(group, at):
        for head, part in enumerate(heads(at)):
            query = query_ref[:, part]
            place = group * number + head
            top = top_ref[:, pl.ds(pl.multiple_of(place * length, HEAD), length)]
            bottom = bottom_ref[:, pl.ds(pl.multiple_of(place * rest, HEAD), rest)]
            key_ref[:HEAD, part] = nn(top, query)
            key_ref[HEAD:, part] = nn(bottom, query[HEAD:])

    groups(total, work)


def key_call(queries, top, bottom):
    length, total = queries.shape
    return kernel_call(
        key_kernel,
        "VVV",
        (queries, top, bottom),
        "VV",
        [((length, total), f32), (MARK.shape, f32)],
        "key_part",
        (4 * length * total * length, 0),
    )


def outer_kernel(
    factor, key_ref, val_ref, keys_ref, value_ref, mask_ref, high_ref, low_ref,
    key_out, val_out, key_made, val_made, key_sems, val_sems,
):
    total = keys_ref.shape[1]

    def work(group, at):
        for part in heads(at):
            keys, value = keys_ref[:, part], value_ref[:, part]
            state = [high_ref[part, :], low_ref[part, :]]
            key_grad = key_ref[:, part] + nt(twice(value), jnp.concatenate(state, axis=1))
            key_made[:, part] = (factor * key_grad * mask_ref[:, part].astype(f32)).astype(bf16)
            value_grad = val_ref[:, part] + nn(twice(keys), jnp.concatenate(state, axis=0))
            val_made[:, part] = (factor * value_grad).astype(bf16)
        out_copy(key_made, key_out, key_sems, group, at).start()
        out_copy(val_made, val_out, val_sems, group, at).start()

    groups(total, work)
    for group in range(total // WIDE):
        out_copy(key_made, key_out, key_sems, group, group * WIDE).wait()
        out_copy(val_made, val_out, val_sems, group, group * WIDE).wait()


def outer_call(factor, key_part, value_part, keys, values, k_mask, high, low):
    length, total = values.shape
    block = (length, total)
    return kernel_call(
        functools.partial(outer_kernel, factor),
        "VVVVVVV",
        (key_part, value_part, keys, values, k_mask, high, low),
        "HH",
        [(block, bf16)] * 2,
        "outer",
        (8 * length * total * HEAD, 20 * length * total),
        [pltpu.VMEM(block, bf16)] * 2 + [pltpu.SemaphoreType.DMA((total // WIDE,))] * 2,
    )


def half_kernel(
    factor, mine, has_before,
    state_ref, sibling_ref, key_ref, val_ref, keys_ref, value_ref, mask_ref, *refs,
):
    key_out, val_out, key_made, val_made, key_sems, val_sems = refs[2 if has_before else 0 :]
    core = lax.axis_index("core")
    half = state_ref.shape[0]
    base = (core if mine else 1 - core) * half
    adds = jnp.where(core == 0, 1.0, 0.0)

    def out_copies(group, at):
        there = columns(pl.multiple_of(base + at, WIDE))
        return [
            pltpu.make_async_copy(made.at[columns(at)], out.at[there], sems.at[group])
            for made, out, sems in (
                (key_made, key_out, key_sems), (val_made, val_out, val_sems)
            )
        ]

    def work(group, at):
        for here in heads(at):
            part = pl.ds(pl.multiple_of(base + here.start, HEAD), HEAD)
            whole = state_ref[here, :] + adds * sibling_ref[part, :].astype(f32)
            high = whole.astype(bf16)
            state = [high, (whole - high.astype(f32)).astype(bf16)]
            keys, value = keys_ref[:, part], value_ref[:, part]
            key_grad = key_ref[:, part] + nt(twice(value), jnp.concatenate(state, axis=1))
            key_made[:, here] = (factor * key_grad * mask_ref[:, part].astype(f32)).astype(bf16)
            value_grad = val_ref[:, part] + nn(twice(keys), jnp.concatenate(state, axis=0))
            val_made[:, here] = (factor * value_grad).astype(bf16)
        for copy in out_copies(group, at):
            copy.start()

    groups(half, work)
    for group in range(half // WIDE):
        for copy in out_copies(group, group * WIDE):
            copy.wait()


def half_call(factor, state, sibling, key_part, value_part, keys, values, k_mask, before=()):
    length, total = values.shape
    half = state.shape[0]
    return kernel_call(
        functools.partial(half_kernel, factor, not before, bool(before)),
        "VVVVVVV" + "H" * len(before),
        (state, sibling, key_part, value_part, keys, values, k_mask, *before),
        "HH",
        [((length, total), bf16)] * 2,
        "outer",
        (4 * length * total * HEAD, 10 * length * total),
        [pltpu.VMEM((length, half), bf16)] * 2
        + [pltpu.SemaphoreType.DMA((half // WIDE,))] * 2,
        {7 + at: at for at in range(len(before))},
    )


def halves(state):
    high = state.astype(bf16)
    return high, (state - high.astype(f32)).astype(bf16)


def scan_any(own, sent, count, reverse):
    place = lax.axis_index(CTX)
    total = own
    state = jnp.zeros_like(own)
    bits = count.bit_length() - 1
    for bit in range(bits):
        step = 1 << bit
        last = bit == bits - 1
        pairs = []
        for source in range(count):
            high = bool(source & step)
            if not last or high == reverse:
                pairs.append((source, source ^ step))
        got = lax.ppermute(sent, CTX, pairs).astype(f32)
        if last:
            state = state + got
        else:
            mine = ((place // step) % 2) == (0 if reverse else 1)
            state = state + jnp.where(mine, got, 0.0)
            total = total + got
            sent = total.astype(bf16)
    return state


def links(first, keep=lambda source, target: True):
    pairs = []
    for chip in range(4):
        for core in range(2):
            other = chip ^ (first if core == 0 else 3 - first)
            if keep((chip, core), other):
                pairs.append((chip * 2 + core, other * 2 + core))
    return pairs


def upward(reverse):
    flip = 3 if reverse else 0

    def keep(source, target):
        at = source[0] ^ flip
        return source[0] ^ target == 1 or not at & 2

    return keep


def low_bit(reverse):
    chip = lax.axis_index("chip")
    return 1 - chip % 2 if reverse else chip % 2


def half_rows(array_ref, core):
    half = array_ref.shape[0] // 2
    return array_ref[pl.ds(pl.multiple_of(core * half, half), half), :]


def both_kernel(own_ref, sibling_ref, *refs):
    both_ref, sent_ref = refs[-2:]
    core = lax.axis_index("core")
    both = half_rows(own_ref, core) + half_rows(sibling_ref, core).astype(f32)
    both_ref[...] = both
    sent_ref[...] = both.astype(bf16)


def message_kernel(reverse, got_ref, both_ref, *refs):
    core = lax.axis_index("core")
    adds = jnp.where((core == 0) | (low_bit(reverse) == 0), 1.0, 0.0)
    refs[-1][...] = (got_ref[...].astype(f32) + adds * both_ref[...]).astype(bf16)


def state_kernel(reverse, got_ref, more_ref, *refs):
    core = lax.axis_index("core")
    adds = jnp.where((core == 1) | (low_bit(reverse) == 1), 1.0, 0.0)
    refs[-1][...] = adds * got_ref[...].astype(f32) + more_ref[...].astype(f32)


def whole_kernel(reverse, state_ref, other_ref, sibling_ref, high_ref, low_ref):
    core = lax.axis_index("core")
    adds = jnp.where(core == (0 if reverse else 1), 1.0, 0.0)
    half = state_ref.shape[0]
    for ref, side in ((state_ref, core), (other_ref, 1 - core)):
        rows = pl.ds(pl.multiple_of(side * half, half), half)
        whole = ref[...] + adds * sibling_ref[rows, :].astype(f32)
        high = whole.astype(bf16)
        high_ref[rows, :] = high
        low_ref[rows, :] = (whole - high.astype(f32)).astype(bf16)


def send_first(own, sent, reverse, others=()):
    half = (own.shape[0] // 2, HEAD)
    sibling = lax.ppermute(sent, "core", SWAP)
    both, sent = kernel_call(
        both_kernel,
        "VV" + "A" * len(others),
        (own, sibling, *others),
        "VV",
        [(half, f32), (half, bf16)],
        "both",
        (0, 0),
    )
    return sibling, both, lax.ppermute(sent, CTX, links(1, upward(reverse)))


def send_second(got, both, reverse, others=()):
    (message,) = kernel_call(
        functools.partial(message_kernel, reverse),
        "VV" + "A" * len(others),
        (got, both, *others),
        "V",
        [(both.shape, bf16)],
        "message",
        (0, 0),
    )
    return lax.ppermute(message, CTX, links(2, upward(reverse)))


def add_halves(got, more, reverse, others=()):
    (state,) = kernel_call(
        functools.partial(state_kernel, reverse),
        "VV" + "A" * len(others),
        (got, more, *others),
        "V",
        [(got.shape, f32)],
        "state",
        (0, 0),
    )
    return state, lax.ppermute(state, "core", SWAP)


def add_up(got, more, sibling, reverse):
    state, other = add_halves(got, more, reverse)
    return kernel_call(
        functools.partial(whole_kernel, reverse),
        "VVV",
        (state, other, sibling),
        "VV",
        [(sibling.shape, bf16)] * 2,
        "whole",
        (0, 0),
    )


def gather_any(q_weight):
    whole = lax.all_gather(q_weight, ("chip", "core", "dp"), axis=0, tiled=True)
    cut = whole.shape[0] // (2 * PIECE) * PIECE
    return [whole[:cut], whole[cut:]]


def pack_kernel(number, *refs):
    arrays, (out_ref, sems) = refs[:number], refs[-2:]
    copies = Copies(sems)
    rows = out_ref.shape[0] // len(arrays)
    going = [
        copies.start(array, out_ref.at[pl.ds(at * rows, rows), :])
        for at, array in enumerate(arrays)
    ]
    for copy in going:
        copy.wait()


def pack(*arrays, others=()):
    rows, total = arrays[0].shape
    number = len(arrays)
    (made,) = kernel_call(
        functools.partial(pack_kernel, number),
        "A" * (number + len(others)),
        (*arrays, *others),
        "V",
        [((number * rows, total), arrays[0].dtype)],
        "pack",
        (0, 0),
        [pltpu.SemaphoreType.DMA((number,))],
    )
    return [made, lax.ppermute(made, "core", SWAP)]


def choose_kernel(inner_ref, end_ref, out_ref, sem):
    del end_ref
    layer = lax.axis_index("dp")

    @pl.when((layer == 1) | (layer == 2))
    def _():
        copy = pltpu.make_async_copy(inner_ref, out_ref, sem)
        copy.start()
        copy.wait()


def choose(inner, end):
    return kernel_call(
        choose_kernel,
        "AA",
        (fast(inner), fast(end)),
        "A",
        [(inner.shape, inner.dtype)],
        "choose",
        (0, 0),
        [pltpu.SemaphoreType.DMA],
        {1: 0},
    )[0]


def per_device(tokens, key_input, values, q_weight, q_spikes, k_spikes, cotangent):
    batches, length, width = tokens.shape
    assert batches == 1
    total = q_weight.shape[1]
    chips, spread = lax.axis_size("chip"), lax.axis_size("dp")
    factor = 3.0 / math.sqrt(HEAD * length * chips * 2)
    tokens, key_input, values, q_spikes, k_spikes, cotangent = (
        array.reshape(length, array.shape[2])
        for array in (tokens, key_input, values, q_spikes, k_spikes, cotangent)
    )
    special = chips == 4 and spread == 4

    def sibling(array):
        return lax.ppermute(array, "core", SWAP)

    def along(array, pairs):
        return lax.ppermute(array, "dp", pairs)

    def cross(array):
        return lax.ppermute(array, CTX, links(1)), lax.ppermute(array, CTX, links(2))

    def onward(array):
        return lax.ppermute(array, CTX, links(2))

    keys, k_mask, values, own, sent, tokens, cotangent = memory_call(
        special, key_input, k_spikes, values, tokens, cotangent
    )
    if special:
        ends = [(0, 1), (1, 0), (2, 3), (3, 2)]
        middle = [(1, 2), (2, 1)]
        outward = [(1, 0), (2, 3)]
        near = along(q_weight, ends)
        mid = along(q_weight, middle)
        first_0, second_0 = cross(q_weight)
        first_0, second_0, near, mid, sent = join([first_0, second_0, near, mid, sent])
    else:
        arrived = gather_any(q_weight)
        high, low = halves(scan_any(own, sent, chips * 2, False))

    if special:
        third_0 = onward(first_0)
        first_1, second_1 = cross(near)
        far = along(near, middle)
        mid_out = along(mid, outward)
        twin, both, got = send_first(own, sent, False)
        third_0, first_1, second_1, far, mid_out, got = join(
            [third_0, first_1, second_1, far, mid_out, got]
        )
        more = send_second(got, both, False)
        next_layer = choose(mid, mid_out)
        first_2, second_2 = cross(next_layer)
        far_out = along(far, outward)
        early = pack(q_weight, first_0, second_0, third_0, near, first_1, second_1)
        partial, _, mark = products_call(special, 0, early, tokens)
        top, bottom, turned_mark = turned_call(values, cotangent, got)
        far_out, first_2, second_2, more, third_0 = join(
            [far_out, first_2, second_2, more, third_0], [mark, turned_mark]
        )
        third_1 = along(third_0, ends)
        third_2 = onward(first_2)
        last_layer = choose(far, far_out)
        first_3, second_3 = cross(last_layer)
        high, low = add_up(got, more, twin, False)
        masked, q_mask = masked_call(factor, q_spikes, cotangent, values, keys, high, low)
        middle = pack(next_layer, first_2, second_2, last_layer)
        _, grad, mark = products_call(special, 0, early, tokens, masked=masked, project=False)
        third_2, first_3, second_3, third_1, middle[1] = join(
            [third_2, first_3, second_3, third_1, middle[1]], [mark]
        )
        third_3 = onward(first_3)
        late = pack(third_1, third_2, first_3, second_3)
        partial, grad, mark_0 = products_call(
            special, 14, middle, tokens, partial, masked, grad
        )
        partial, _, mark_1 = products_call(special, 22, late, tokens, partial)
        third_3, = join([third_3], [mark_0, mark_1])
        _, grad, mark = products_call(
            special, 22, late, tokens, masked=masked, grad=grad, project=False
        )
        late = [third_3, sibling(third_3)]
        start = 30
    else:
        masked, q_mask = masked_call(factor, q_spikes, cotangent, values, keys, high, low)
        top, bottom, _ = turned_call(values, cotangent, own)
        start = arrived[0].shape[0] // PIECE
        partial, grad, mark = products_call(special, 0, arrived[:1], tokens, masked=masked)
        late = arrived[1:]
    queries, own, sent = query_call(start, tokens, late, partial, q_mask, cotangent, [mark])
    attended, attended_mark = attend_call(factor, queries, keys, values, high, low)
    value_part, value_mark = value_call(queries, keys, cotangent)
    key_part, key_mark = key_call(queries, top, bottom)
    _, grad_tokens, back_mark = products_call(
        special, start, late, tokens, masked=masked, grad=grad, project=False
    )
    if special:
        twin, both, got = send_first(own, sent, True, [back_mark])
        more = send_second(got, both, True, [attended_mark])
        state, other = add_halves(got, more, True, [value_mark, key_mark])
        rest = (twin, key_part, value_part, keys, values, k_mask)
        made = half_call(factor, state, *rest)
        grad_keys, grad_values = half_call(factor, other, *rest, made)
    else:
        adjoint = halves(scan_any(own, sent, chips * 2, True))
        grad_keys, grad_values = outer_call(
            factor, key_part, value_part, keys, values, k_mask, *adjoint
        )
    return tuple(
        array.reshape(1, length, array.shape[1])
        for array in (attended, grad_tokens, grad_keys, grad_values)
    )


def solution(mesh):
    count, spread = mesh.shape["ctx"], mesh.shape["dp"]
    fine = Mesh(mesh.devices.reshape(count // 2, 2, spread), ("chip", "core", "dp"))
    block = P("dp", CTX, None)
    rows = P(("chip", "core", "dp"), None)
    in_specs = (block, block, block, rows, block, block, block)
    return jax.shard_map(
        per_device, mesh=fine, in_specs=in_specs, out_specs=(block,) * 4, check_vma=False
    )
```

```python
import functools
import math

import jax
import jax.numpy as jnp
from jax import lax
from jax.experimental import pallas as pl
from jax.experimental.pallas import tpu as pltpu
from jax.sharding import Mesh, PartitionSpec as P

HEAD = 128
PIECE = 128
WIDE = 512
CTX = ("chip", "core")
SWAP = [(0, 1), (1, 0)]
f32, bf16 = jnp.float32, jnp.bfloat16
VMEM_LIMIT = 18 * 1024 * 1024


def nn(a, b):
    return lax.dot_general(a, b, (((1,), (0,)), ((), ())), preferred_element_type=f32)


def nt(a, b):
    return lax.dot_general(a, b, (((1,), (1,)), ((), ())), preferred_element_type=f32)


def tn(a, b):
    return lax.dot_general(a, b, (((0,), (0,)), ((), ())), preferred_element_type=f32)


def params(flops, moved):
    return dict(
        compiler_params=pltpu.CompilerParams(vmem_limit_bytes=VMEM_LIMIT),
        cost_estimate=pl.CostEstimate(flops=flops, bytes_accessed=moved, transcendentals=0),
    )


MARK = jax.ShapeDtypeStruct((8, HEAD), f32)


def set_mark(mark_ref):
    mark_ref[...] = jnp.zeros_like(mark_ref)


def fast(array):
    return pltpu.with_memory_space_constraint(array, pltpu.VMEM)


def slow(array):
    return pltpu.with_memory_space_constraint(array, pltpu.HBM)


def specs(places):
    spaces = dict(V=pltpu.VMEM, H=pltpu.HBM, S=pltpu.SMEM, A=pl.ANY)
    return [pl.BlockSpec(memory_space=spaces[place]) for place in places]


def kernel_call(body, places, args, out_places, outs, name, cost, scratch=(), aliases=None):
    holds = dict(V=fast, H=slow)
    made = pl.pallas_call(
        body,
        in_specs=specs(places),
        out_specs=specs(out_places),
        out_shape=[
            pltpu.VMEM(shape, dtype) if place == "V" else jax.ShapeDtypeStruct(shape, dtype)
            for place, (shape, dtype) in zip(out_places, outs)
        ],
        scratch_shapes=list(scratch),
        input_output_aliases=aliases or {},
        name=name,
        **params(*cost),
    )
    return made(
        *[holds[place](one) if place in holds else one for place, one in zip(places, args)]
    )


class Copies:
    def __init__(self, sems):
        self.sems = sems
        self.used = 0

    def start(self, source, target):
        copy = pltpu.make_async_copy(source, target, self.sems.at[self.used])
        self.used += 1
        copy.start()
        return copy


def crossed(side):
    return (0, 1 + side, 2 - side, 3)


def all_places(special, number):
    if not special:
        return list(range(number))
    chip, core, layer = (lax.axis_index(name) for name in ("chip", "core", "dp"))
    upper = layer < 2
    layers = [layer, layer ^ 1, jnp.where(upper, 2, 1), jnp.where(upper, 3, 0)]

    def some(*arrivals):
        return [
            ((chip ^ crossed(side)[flip]) * 2 + side) * 4 + layers[one]
            for side in (core, 1 - core)
            for one, flips in arrivals
            for flip in flips
        ]

    three = (0, 1, 2)
    return (
        some((0, (0, 1, 2, 3)), (1, three))
        + some((2, three), (3, (0,)))
        + some((1, (3,)), (2, (3,)), (3, (1, 2)))
        + some((3, (3,)))
    )


def piece_columns(place):
    return (slice(None), pl.ds(pl.multiple_of(place * PIECE, PIECE), PIECE))


def columns(at, wide=None):
    return (slice(None), pl.ds(at, wide or WIDE))


def groups(total, body):
    @pl.loop(0, total // WIDE)
    def _(group):
        body(group, pl.multiple_of(group * WIDE, WIDE))


def heads(at):
    return [pl.ds(pl.multiple_of(at + head, HEAD), HEAD) for head in range(0, WIDE, HEAD)]


def memory_kernel(
    special, key_ref, spike_ref, value_ref, tokens_ref, grad_ref,
    keys_ref, mask_ref, values_ref, own_ref, sent_ref, some_ref, grads_ref,
    key_in, spike_in, sems,
):
    copies = Copies(sems)
    wide = range(0, keys_ref.shape[1], WIDE)
    pairs = ((key_ref, key_in), (spike_ref, spike_in), (value_ref, values_ref))
    parts = [
        [copies.start(here.at[columns(at)], there.at[columns(at)]) for here, there in pairs]
        for at in wide
    ]
    places = all_places(special, some_ref.shape[1] // PIECE)
    ordered = [
        copies.start(tokens_ref.at[piece_columns(place)], some_ref.at[piece_columns(piece)])
        for piece, place in enumerate(places)
    ]
    ordered.append(copies.start(grad_ref, grads_ref))
    for at, part in zip(wide, parts):
        for copy in part:
            copy.wait()
        cols = slice(at, at + WIDE)
        mask = spike_in[:, cols].astype(f32).astype(bf16)
        keys = key_in[:, cols] * mask
        keys_ref[:, cols] = keys
        mask_ref[:, cols] = mask
        for head in range(0, WIDE, HEAD):
            here = slice(at + head, at + head + HEAD)
            own = tn(keys[:, head : head + HEAD], values_ref[:, here])
            own_ref[here, :] = own
            sent_ref[here, :] = own.astype(bf16)
    for copy in ordered:
        copy.wait()


def memory_call(special, key_input, k_spikes, values, tokens, cotangent):
    length, total = values.shape
    block, state = (length, total), (total, HEAD)
    return kernel_call(
        functools.partial(memory_kernel, special),
        "HHHHH",
        (key_input, k_spikes, values, tokens, cotangent),
        "VVVVVVV",
        [(block, bf16)] * 3
        + [(state, f32), (state, bf16), (tokens.shape, bf16), (block, bf16)],
        "own_memory",
        (2 * length * total * HEAD, 12 * length * total),
        [
            pltpu.VMEM(block, bf16),
            pltpu.VMEM(block, jnp.int32),
            pltpu.SemaphoreType.DMA((3 * total // WIDE + tokens.shape[1] // PIECE + 1,)),
        ],
    )


def join_kernel(*refs):
    del refs


def join(arrays, others=()):
    number = len(arrays)
    return kernel_call(
        join_kernel,
        ["A"] * (number + len(others)),
        (*[fast(one) for one in arrays], *others),
        ["A"] * number,
        [(one.shape, one.dtype) for one in arrays],
        "join",
        (0, 0),
        aliases={at: at for at in range(number)},
    )


def keep_lower(square, flipped=False):
    row = lax.broadcasted_iota(jnp.int32, square.shape, 0)
    col = lax.broadcasted_iota(jnp.int32, square.shape, 1)
    return jnp.where((col >= row) if flipped else (col <= row), square, 0.0).astype(bf16)


def causal(a, b):
    length = a.shape[0]
    cut = length - HEAD
    top = keep_lower(nt(a[:cut], b[:cut]))
    whole = nt(a[cut:], b)
    bottom = jnp.concatenate([whole[:, :cut].astype(bf16), keep_lower(whole[:, cut:])], axis=1)
    return [(slice(0, cut), slice(0, cut), top), (slice(cut, length), slice(0, length), bottom)]


def causal_turned(a, b):
    length = a.shape[0]
    whole = nt(a[:HEAD], b)
    top = jnp.concatenate(
        [keep_lower(whole[:, :HEAD], True), whole[:, HEAD:].astype(bf16)], axis=1
    )
    bottom = keep_lower(nt(a[HEAD:], b[HEAD:]), True)
    return [
        (slice(0, HEAD), slice(0, length), top),
        (slice(HEAD, length), slice(HEAD, length), bottom),
    ]


def twice(array):
    return jnp.concatenate([array, array], axis=1)


def masked_kernel(
    factor, spike_ref, grad_ref, value_ref, keys_ref, high_ref, low_ref,
    out_ref, mask_ref, spike_in, sems,
):
    total = out_ref.shape[1]

    def bring(group, at):
        return pltpu.make_async_copy(
            spike_ref.at[columns(at)], spike_in.at[columns(at)], sems.at[group]
        )

    for group in range(total // WIDE):
        bring(group, group * WIDE).start()

    def work(group, at):
        bring(group, at).wait()
        for part in heads(at):
            mask = spike_in[:, part].astype(f32)
            mask_ref[:, part] = mask.astype(bf16)
            grad, value, keys = grad_ref[:, part], value_ref[:, part], keys_ref[:, part]
            state = jnp.concatenate([high_ref[part, :], low_ref[part, :]], axis=1)
            for rows, cols, scores in causal(grad, value):
                made = nn(scores, keys[cols]) + nt(twice(grad[rows]), state)
                out_ref[rows, part] = (factor * made * mask[rows]).astype(bf16)

    groups(total, work)


def masked_call(factor, q_spikes, cotangent, values, keys, high, low):
    length, total = values.shape
    block = (length, total)
    return kernel_call(
        functools.partial(masked_kernel, factor),
        "HVVVVV",
        (q_spikes, cotangent, values, keys, high, low),
        "VV",
        [(block, bf16)] * 2,
        "masked_grad",
        (8 * length * total * length, 12 * length * total),
        [pltpu.VMEM(block, jnp.int32), pltpu.SemaphoreType.DMA((total // WIDE,))],
    )


def turned_kernel(value_ref, grad_ref, after_ref, top_ref, bottom_ref, mark_ref):
    del after_ref
    set_mark(mark_ref)
    length, total = value_ref.shape
    rest = length - HEAD
    number = WIDE // HEAD

    def work(group, at):
        for head, part in enumerate(heads(at)):
            (_, _, top), (_, _, bottom) = causal_turned(value_ref[:, part], grad_ref[:, part])
            place = group * number + head
            top_ref[:, pl.ds(pl.multiple_of(place * length, HEAD), length)] = top
            bottom_ref[:, pl.ds(pl.multiple_of(place * rest, HEAD), rest)] = bottom

    groups(total, work)


def turned_call(values, cotangent, after):
    length, total = values.shape
    number, rest = total // HEAD, length - HEAD
    return kernel_call(
        turned_kernel,
        "VVA",
        (values, cotangent, after),
        "VVV",
        [((HEAD, number * length), bf16), ((rest, number * rest), bf16), (MARK.shape, f32)],
        "turned",
        (4 * length * total * length, 0),
    )


def rows_of(blocks):
    return sum(block.shape[0] for block in blocks)


def back_blocks(blocks):
    at = 0
    for block in blocks:
        for row in range(0, block.shape[0], PIECE):
            yield at, block[row : row + PIECE, :]
            at += 1


def back_part(copies, places, masked, blocks, out_ref, round_ref):
    going = []
    pieces = list(back_blocks(blocks))
    for (first, upper), (second, lower) in zip(pieces[::2], pieces[1::2]):
        both = slice(first * PIECE, (second + 1) * PIECE)
        made = nt(masked[...], jnp.concatenate([upper, lower], axis=0))
        round_ref[:, both] = made.astype(bf16)
        for piece in (first, second):
            going.append(
                copies.start(
                    round_ref.at[piece_columns(piece)], out_ref.at[piece_columns(places[piece])]
                )
            )
    return going


def products_kernel(special, start, size, project, back, has_sum, has_back, *refs):
    blocks, refs = refs[:size], list(refs[size:])
    depth = rows_of(blocks)
    tokens_ref = refs.pop(0) if project else None
    before_ref = refs.pop(0) if has_sum else None
    masked = refs.pop(0) if back else None
    if has_back:
        refs.pop(0)
    sum_ref = refs.pop(0) if project else None
    back_out = refs.pop(0) if back else None
    mark_ref = refs.pop(0)
    set_mark(mark_ref)
    going = []
    if back:
        round_ref, sems = refs
        places = all_places(special, back_out.shape[1] // PIECE)[start:]
        going = back_part(Copies(sems), places, masked, blocks, back_out, round_ref)
    if project:
        cols = slice(start * PIECE, start * PIECE + depth)
        for at in range(0, sum_ref.shape[1], WIDE):
            part = slice(at, at + WIDE)
            made = nn(
                tokens_ref[:, cols],
                jnp.concatenate([block[:, part] for block in blocks], axis=0),
            )
            if has_sum:
                made = made + before_ref[:, part]
            sum_ref[:, part] = made
    for copy in going:
        copy.wait()


def products_call(
    special, start, blocks, tokens, partial=None, masked=None, grad=None, project=True
):
    length, width = tokens.shape
    total = blocks[0].shape[1]
    depth = rows_of(blocks)
    back = masked is not None
    places_in, args = "V" * len(blocks), list(blocks)
    places_out, outs = "", []
    scratch, aliases = [], {}
    if project:
        places_in, args = places_in + "V", args + [tokens]
        if partial is not None:
            aliases[len(args)] = 0
            places_in, args = places_in + "V", args + [partial]
        places_out, outs = "V", [((length, total), f32)]
    if back:
        places_in, args = places_in + "V", args + [masked]
        if grad is not None:
            aliases[len(args)] = len(outs)
            places_in, args = places_in + "H", args + [grad]
        places_out, outs = places_out + "H", outs + [((length, width), bf16)]
        scratch = [
            pltpu.VMEM((length, depth), bf16), pltpu.SemaphoreType.DMA((depth // PIECE,))
        ]
    made = kernel_call(
        functools.partial(
            products_kernel, special, start, len(blocks), project, back,
            partial is not None, grad is not None,
        ),
        places_in,
        args,
        places_out + "V",
        outs + [(MARK.shape, f32)],
        "products" if project and back else "project" if project else "grad_tokens",
        (2 * (project + back) * length * depth * total, 0),
        scratch,
        aliases,
    )
    made = list(made)
    partial = made.pop(0) if project else partial
    grad = made.pop(0) if back else grad
    return partial, grad, made[0]


def query_kernel(start, size, tokens_ref, sum_ref, mask_ref, grad_ref, *refs):
    blocks = refs[:size]
    queries, own_ref, sent_ref = refs[-3:]
    cols = slice(start * PIECE, start * PIECE + rows_of(blocks))
    for at in range(0, queries.shape[1], WIDE):
        part = slice(at, at + WIDE)
        made = nn(
            tokens_ref[:, cols], jnp.concatenate([block[:, part] for block in blocks], axis=0)
        )
        made = made + sum_ref[:, part]
        made = (made * mask_ref[:, part].astype(f32)).astype(bf16)
        queries[:, part] = made
        for head in range(0, WIDE, HEAD):
            here = slice(at + head, at + head + HEAD)
            own = tn(made[:, head : head + HEAD], grad_ref[:, here])
            own_ref[here, :] = own
            sent_ref[here, :] = own.astype(bf16)


def query_call(start, tokens, blocks, before, q_mask, cotangent, others):
    length = tokens.shape[0]
    total = blocks[0].shape[1]
    depth = rows_of(blocks)
    return kernel_call(
        functools.partial(query_kernel, start, len(blocks)),
        "VVVV" + "V" * len(blocks) + "A" * len(others),
        (tokens, before, q_mask, cotangent, *blocks, *others),
        "VVV",
        [((length, total), bf16), ((total, HEAD), f32), ((total, HEAD), bf16)],
        "queries",
        (2 * length * depth * total, 0),
    )


def out_copy(here, there, sems, group, at):
    return pltpu.make_async_copy(here.at[columns(at)], there.at[columns(at)], sems.at[group])


def attend_kernel(
    factor, query_ref, keys_ref, value_ref, high_ref, low_ref, out_ref, mark_ref, made_ref, sems
):
    set_mark(mark_ref)
    total = query_ref.shape[1]

    def work(group, at):
        for part in heads(at):
            query, keys, value = query_ref[:, part], keys_ref[:, part], value_ref[:, part]
            state = [high_ref[part, :], low_ref[part, :]]
            for rows, cols, scores in causal(query, keys):
                made = nn(
                    jnp.concatenate([scores, twice(query[rows])], axis=1),
                    jnp.concatenate([value[cols], *state], axis=0),
                )
                made_ref[rows, part] = (factor * made).astype(bf16)
        out_copy(made_ref, out_ref, sems, group, at).start()

    groups(total, work)
    for group in range(total // WIDE):
        out_copy(made_ref, out_ref, sems, group, group * WIDE).wait()


def attend_call(factor, queries, keys, values, high, low):
    length, total = values.shape
    return kernel_call(
        functools.partial(attend_kernel, factor),
        "VVVVV",
        (queries, keys, values, high, low),
        "HV",
        [((length, total), bf16), (MARK.shape, f32)],
        "attended",
        (8 * length * total * length, 8 * length * total),
        [pltpu.VMEM((length, total), bf16), pltpu.SemaphoreType.DMA((total // WIDE,))],
    )


def value_kernel(query_ref, keys_ref, grad_ref, val_ref, mark_ref):
    set_mark(mark_ref)

    def work(group, at):
        for part in heads(at):
            query, keys, grad = query_ref[:, part], keys_ref[:, part], grad_ref[:, part]
            for rows, cols, scores in causal_turned(keys, query):
                val_ref[rows, part] = nn(scores, grad[cols])

    groups(query_ref.shape[1], work)


def value_call(queries, keys, cotangent):
    length, total = keys.shape
    return kernel_call(
        value_kernel,
        "VVV",
        (queries, keys, cotangent),
        "VV",
        [((length, total), f32), (MARK.shape, f32)],
        "value_part",
        (6 * length * total * length, 0),
    )


def key_kernel(query_ref, top_ref, bottom_ref, key_ref, mark_ref):
    set_mark(mark_ref)
    length, total = query_ref.shape
    rest = length - HEAD
    number = WIDE // HEAD

    def work(group, at):
        for head, part in enumerate(heads(at)):
            query = query_ref[:, part]
            place = group * number + head
            top = top_ref[:, pl.ds(pl.multiple_of(place * length, HEAD), length)]
            bottom = bottom_ref[:, pl.ds(pl.multiple_of(place * rest, HEAD), rest)]
            key_ref[:HEAD, part] = nn(top, query)
            key_ref[HEAD:, part] = nn(bottom, query[HEAD:])

    groups(total, work)


def key_call(queries, top, bottom):
    length, total = queries.shape
    return kernel_call(
        key_kernel,
        "VVV",
        (queries, top, bottom),
        "VV",
        [((length, total), f32), (MARK.shape, f32)],
        "key_part",
        (4 * length * total * length, 0),
    )


def outer_kernel(
    factor, key_ref, val_ref, keys_ref, value_ref, mask_ref, high_ref, low_ref,
    key_out, val_out, key_made, val_made, key_sems, val_sems,
):
    total = keys_ref.shape[1]

    def work(group, at):
        for part in heads(at):
            keys, value = keys_ref[:, part], value_ref[:, part]
            state = [high_ref[part, :], low_ref[part, :]]
            key_grad = key_ref[:, part] + nt(twice(value), jnp.concatenate(state, axis=1))
            key_made[:, part] = (factor * key_grad * mask_ref[:, part].astype(f32)).astype(bf16)
            value_grad = val_ref[:, part] + nn(twice(keys), jnp.concatenate(state, axis=0))
            val_made[:, part] = (factor * value_grad).astype(bf16)
        out_copy(key_made, key_out, key_sems, group, at).start()
        out_copy(val_made, val_out, val_sems, group, at).start()

    groups(total, work)
    for group in range(total // WIDE):
        out_copy(key_made, key_out, key_sems, group, group * WIDE).wait()
        out_copy(val_made, val_out, val_sems, group, group * WIDE).wait()


def outer_call(factor, key_part, value_part, keys, values, k_mask, high, low):
    length, total = values.shape
    block = (length, total)
    return kernel_call(
        functools.partial(outer_kernel, factor),
        "VVVVVVV",
        (key_part, value_part, keys, values, k_mask, high, low),
        "HH",
        [(block, bf16)] * 2,
        "outer",
        (8 * length * total * HEAD, 20 * length * total),
        [pltpu.VMEM(block, bf16)] * 2 + [pltpu.SemaphoreType.DMA((total // WIDE,))] * 2,
    )


def half_kernel(
    factor, mine, has_before,
    state_ref, sibling_ref, key_ref, val_ref, keys_ref, value_ref, mask_ref, *refs,
):
    key_out, val_out, key_made, val_made, key_sems, val_sems = refs[2 if has_before else 0 :]
    core = lax.axis_index("core")
    half = state_ref.shape[0]
    base = (core if mine else 1 - core) * half
    adds = jnp.where(core == 0, 1.0, 0.0)

    def out_copies(group, at):
        there = columns(pl.multiple_of(base + at, WIDE))
        return [
            pltpu.make_async_copy(made.at[columns(at)], out.at[there], sems.at[group])
            for made, out, sems in (
                (key_made, key_out, key_sems), (val_made, val_out, val_sems)
            )
        ]

    def work(group, at):
        for here in heads(at):
            part = pl.ds(pl.multiple_of(base + here.start, HEAD), HEAD)
            whole = state_ref[here, :] + adds * sibling_ref[part, :].astype(f32)
            high = whole.astype(bf16)
            state = [high, (whole - high.astype(f32)).astype(bf16)]
            keys, value = keys_ref[:, part], value_ref[:, part]
            key_grad = key_ref[:, part] + nt(twice(value), jnp.concatenate(state, axis=1))
            key_made[:, here] = (factor * key_grad * mask_ref[:, part].astype(f32)).astype(bf16)
            value_grad = val_ref[:, part] + nn(twice(keys), jnp.concatenate(state, axis=0))
            val_made[:, here] = (factor * value_grad).astype(bf16)
        for copy in out_copies(group, at):
            copy.start()

    groups(half, work)
    for group in range(half // WIDE):
        for copy in out_copies(group, group * WIDE):
            copy.wait()


def half_call(factor, state, sibling, key_part, value_part, keys, values, k_mask, before=()):
    length, total = values.shape
    half = state.shape[0]
    return kernel_call(
        functools.partial(half_kernel, factor, not before, bool(before)),
        "VVVVVVV" + "H" * len(before),
        (state, sibling, key_part, value_part, keys, values, k_mask, *before),
        "HH",
        [((length, total), bf16)] * 2,
        "outer",
        (4 * length * total * HEAD, 10 * length * total),
        [pltpu.VMEM((length, half), bf16)] * 2
        + [pltpu.SemaphoreType.DMA((half // WIDE,))] * 2,
        {7 + at: at for at in range(len(before))},
    )


def halves(state):
    high = state.astype(bf16)
    return high, (state - high.astype(f32)).astype(bf16)


def scan_any(own, sent, count, reverse):
    place = lax.axis_index(CTX)
    total = own
    state = jnp.zeros_like(own)
    bits = count.bit_length() - 1
    for bit in range(bits):
        step = 1 << bit
        last = bit == bits - 1
        pairs = []
        for source in range(count):
            high = bool(source & step)
            if not last or high == reverse:
                pairs.append((source, source ^ step))
        got = lax.ppermute(sent, CTX, pairs).astype(f32)
        if last:
            state = state + got
        else:
            mine = ((place // step) % 2) == (0 if reverse else 1)
            state = state + jnp.where(mine, got, 0.0)
            total = total + got
            sent = total.astype(bf16)
    return state


def links(first, keep=lambda source, target: True):
    pairs = []
    for chip in range(4):
        for core in range(2):
            other = chip ^ (first if core == 0 else 3 - first)
            if keep((chip, core), other):
                pairs.append((chip * 2 + core, other * 2 + core))
    return pairs


def upward(reverse):
    flip = 3 if reverse else 0

    def keep(source, target):
        at = source[0] ^ flip
        return source[0] ^ target == 1 or not at & 2

    return keep


def low_bit(reverse):
    chip = lax.axis_index("chip")
    return 1 - chip % 2 if reverse else chip % 2


def half_rows(array_ref, core):
    half = array_ref.shape[0] // 2
    return array_ref[pl.ds(pl.multiple_of(core * half, half), half), :]


def both_kernel(own_ref, sibling_ref, *refs):
    both_ref, sent_ref = refs[-2:]
    core = lax.axis_index("core")
    both = half_rows(own_ref, core) + half_rows(sibling_ref, core).astype(f32)
    both_ref[...] = both
    sent_ref[...] = both.astype(bf16)


def message_kernel(reverse, got_ref, both_ref, *refs):
    core = lax.axis_index("core")
    adds = jnp.where((core == 0) | (low_bit(reverse) == 0), 1.0, 0.0)
    refs[-1][...] = (got_ref[...].astype(f32) + adds * both_ref[...]).astype(bf16)


def state_kernel(reverse, got_ref, more_ref, *refs):
    core = lax.axis_index("core")
    adds = jnp.where((core == 1) | (low_bit(reverse) == 1), 1.0, 0.0)
    refs[-1][...] = adds * got_ref[...].astype(f32) + more_ref[...].astype(f32)


def whole_kernel(reverse, state_ref, other_ref, sibling_ref, high_ref, low_ref):
    core = lax.axis_index("core")
    adds = jnp.where(core == (0 if reverse else 1), 1.0, 0.0)
    half = state_ref.shape[0]
    for ref, side in ((state_ref, core), (other_ref, 1 - core)):
        rows = pl.ds(pl.multiple_of(side * half, half), half)
        whole = ref[...] + adds * sibling_ref[rows, :].astype(f32)
        high = whole.astype(bf16)
        high_ref[rows, :] = high
        low_ref[rows, :] = (whole - high.astype(f32)).astype(bf16)


def send_first(own, sent, reverse, others=()):
    half = (own.shape[0] // 2, HEAD)
    sibling = lax.ppermute(sent, "core", SWAP)
    both, sent = kernel_call(
        both_kernel,
        "VV" + "A" * len(others),
        (own, sibling, *others),
        "VV",
        [(half, f32), (half, bf16)],
        "both",
        (0, 0),
    )
    return sibling, both, lax.ppermute(sent, CTX, links(1, upward(reverse)))


def send_second(got, both, reverse, others=()):
    (message,) = kernel_call(
        functools.partial(message_kernel, reverse),
        "VV" + "A" * len(others),
        (got, both, *others),
        "V",
        [(both.shape, bf16)],
        "message",
        (0, 0),
    )
    return lax.ppermute(message, CTX, links(2, upward(reverse)))


def add_halves(got, more, reverse, others=()):
    (state,) = kernel_call(
        functools.partial(state_kernel, reverse),
        "VV" + "A" * len(others),
        (got, more, *others),
        "V",
        [(got.shape, f32)],
        "state",
        (0, 0),
    )
    return state, lax.ppermute(state, "core", SWAP)


def add_up(got, more, sibling, reverse):
    state, other = add_halves(got, more, reverse)
    return kernel_call(
        functools.partial(whole_kernel, reverse),
        "VVV",
        (state, other, sibling),
        "VV",
        [(sibling.shape, bf16)] * 2,
        "whole",
        (0, 0),
    )


def gather_any(q_weight):
    whole = lax.all_gather(q_weight, ("chip", "core", "dp"), axis=0, tiled=True)
    cut = whole.shape[0] // (2 * PIECE) * PIECE
    return [whole[:cut], whole[cut:]]


def pack_kernel(number, *refs):
    arrays, (out_ref, sems) = refs[:number], refs[-2:]
    copies = Copies(sems)
    rows = out_ref.shape[0] // len(arrays)
    going = [
        copies.start(array, out_ref.at[pl.ds(at * rows, rows), :])
        for at, array in enumerate(arrays)
    ]
    for copy in going:
        copy.wait()


def pack(*arrays, others=()):
    rows, total = arrays[0].shape
    number = len(arrays)
    (made,) = kernel_call(
        functools.partial(pack_kernel, number),
        "A" * (number + len(others)),
        (*arrays, *others),
        "V",
        [((number * rows, total), arrays[0].dtype)],
        "pack",
        (0, 0),
        [pltpu.SemaphoreType.DMA((number,))],
    )
    return [made, lax.ppermute(made, "core", SWAP)]


def choose_kernel(inner_ref, end_ref, out_ref, sem):
    del end_ref
    layer = lax.axis_index("dp")

    @pl.when((layer == 1) | (layer == 2))
    def _():
        copy = pltpu.make_async_copy(inner_ref, out_ref, sem)
        copy.start()
        copy.wait()


def choose(inner, end):
    return kernel_call(
        choose_kernel,
        "AA",
        (fast(inner), fast(end)),
        "A",
        [(inner.shape, inner.dtype)],
        "choose",
        (0, 0),
        [pltpu.SemaphoreType.DMA],
        {1: 0},
    )[0]


def per_device(tokens, key_input, values, q_weight, q_spikes, k_spikes, cotangent):
    batches, length, width = tokens.shape
    assert batches == 1
    total = q_weight.shape[1]
    chips, spread = lax.axis_size("chip"), lax.axis_size("dp")
    factor = 3.0 / math.sqrt(HEAD * length * chips * 2)
    tokens, key_input, values, q_spikes, k_spikes, cotangent = (
        array.reshape(length, array.shape[2])
        for array in (tokens, key_input, values, q_spikes, k_spikes, cotangent)
    )
    special = chips == 4 and spread == 4

    def sibling(array):
        return lax.ppermute(array, "core", SWAP)

    def along(array, pairs):
        return lax.ppermute(array, "dp", pairs)

    def cross(array):
        return lax.ppermute(array, CTX, links(1)), lax.ppermute(array, CTX, links(2))

    def onward(array):
        return lax.ppermute(array, CTX, links(2))

    keys, k_mask, values, own, sent, tokens, cotangent = memory_call(
        special, key_input, k_spikes, values, tokens, cotangent
    )
    if special:
        ends = [(0, 1), (1, 0), (2, 3), (3, 2)]
        middle = [(1, 2), (2, 1)]
        outward = [(1, 0), (2, 3)]
        near = along(q_weight, ends)
        mid = along(q_weight, middle)
        first_0, second_0 = cross(q_weight)
        first_0, second_0, near, mid, sent = join([first_0, second_0, near, mid, sent])
    else:
        arrived = gather_any(q_weight)
        high, low = halves(scan_any(own, sent, chips * 2, False))

    if special:
        third_0 = onward(first_0)
        first_1, second_1 = cross(near)
        far = along(near, middle)
        mid_out = along(mid, outward)
        twin, both, got = send_first(own, sent, False)
        mid_out, third_0, first_1, second_1, far, got = join(
            [mid_out, third_0, first_1, second_1, far, got]
        )
        more = send_second(got, both, False)
        next_layer = choose(mid, mid_out)
        first_2, second_2 = cross(next_layer)
        far_out = along(far, outward)
        early = pack(q_weight, first_0, second_0, third_0, near, first_1, second_1)
        partial, _, mark = products_call(special, 0, early, tokens)
        top, bottom, turned_mark = turned_call(values, cotangent, got)
        far_out, first_2, second_2, more, third_0 = join(
            [far_out, first_2, second_2, more, third_0], [mark, turned_mark]
        )
        third_1 = along(third_0, ends)
        third_2 = onward(first_2)
        last_layer = choose(far, far_out)
        first_3, second_3 = cross(last_layer)
        high, low = add_up(got, more, twin, False)
        masked, q_mask = masked_call(factor, q_spikes, cotangent, values, keys, high, low)
        middle = pack(next_layer, first_2, second_2, last_layer)
        _, grad, mark = products_call(special, 0, early, tokens, masked=masked, project=False)
        third_2, first_3, second_3, third_1, middle[1] = join(
            [third_2, first_3, second_3, third_1, middle[1]], [mark]
        )
        third_3 = onward(first_3)
        late = pack(third_1, third_2, first_3, second_3)
        partial, grad, mark_0 = products_call(
            special, 14, middle, tokens, partial, masked, grad
        )
        partial, _, mark_1 = products_call(special, 22, late, tokens, partial)
        third_3, = join([third_3], [mark_0, mark_1])
        _, grad, mark = products_call(
            special, 22, late, tokens, masked=masked, grad=grad, project=False
        )
        late = [third_3, sibling(third_3)]
        start = 30
    else:
        masked, q_mask = masked_call(factor, q_spikes, cotangent, values, keys, high, low)
        top, bottom, _ = turned_call(values, cotangent, own)
        start = arrived[0].shape[0] // PIECE
        partial, grad, mark = products_call(special, 0, arrived[:1], tokens, masked=masked)
        late = arrived[1:]
    queries, own, sent = query_call(start, tokens, late, partial, q_mask, cotangent, [mark])
    attended, attended_mark = attend_call(factor, queries, keys, values, high, low)
    value_part, value_mark = value_call(queries, keys, cotangent)
    key_part, key_mark = key_call(queries, top, bottom)
    _, grad_tokens, back_mark = products_call(
        special, start, late, tokens, masked=masked, grad=grad, project=False
    )
    if special:
        twin, both, got = send_first(own, sent, True, [back_mark])
        more = send_second(got, both, True, [attended_mark])
        state, other = add_halves(got, more, True, [value_mark, key_mark])
        rest = (twin, key_part, value_part, keys, values, k_mask)
        made = half_call(factor, state, *rest)
        grad_keys, grad_values = half_call(factor, other, *rest, made)
    else:
        adjoint = halves(scan_any(own, sent, chips * 2, True))
        grad_keys, grad_values = outer_call(
            factor, key_part, value_part, keys, values, k_mask, *adjoint
        )
    return tuple(
        array.reshape(1, length, array.shape[1])
        for array in (attended, grad_tokens, grad_keys, grad_values)
    )


def solution(mesh):
    count, spread = mesh.shape["ctx"], mesh.shape["dp"]
    fine = Mesh(mesh.devices.reshape(count // 2, 2, spread), ("chip", "core", "dp"))
    block = P("dp", CTX, None)
    rows = P(("chip", "core", "dp"), None)
    in_specs = (block, block, block, rows, block, block, block)
    return jax.shard_map(
        per_device, mesh=fine, in_specs=in_specs, out_specs=(block,) * 4, check_vma=False
    )
```

```python
import functools
import math

import jax
import jax.numpy as jnp
from jax import lax
from jax.experimental import pallas as pl
from jax.experimental.pallas import tpu as pltpu
from jax.sharding import Mesh, PartitionSpec as P

HEAD = 128
PIECE = 128
WIDE = 512
CTX = ("chip", "core")
SWAP = [(0, 1), (1, 0)]
f32, bf16 = jnp.float32, jnp.bfloat16
VMEM_LIMIT = 18 * 1024 * 1024


def nn(a, b):
    return lax.dot_general(a, b, (((1,), (0,)), ((), ())), preferred_element_type=f32)


def nt(a, b):
    return lax.dot_general(a, b, (((1,), (1,)), ((), ())), preferred_element_type=f32)


def tn(a, b):
    return lax.dot_general(a, b, (((0,), (0,)), ((), ())), preferred_element_type=f32)


def params(flops, moved):
    return dict(
        compiler_params=pltpu.CompilerParams(vmem_limit_bytes=VMEM_LIMIT),
        cost_estimate=pl.CostEstimate(flops=flops, bytes_accessed=moved, transcendentals=0),
    )


MARK = jax.ShapeDtypeStruct((8, HEAD), f32)


def set_mark(mark_ref):
    mark_ref[...] = jnp.zeros_like(mark_ref)


def fast(array):
    return pltpu.with_memory_space_constraint(array, pltpu.VMEM)


def slow(array):
    return pltpu.with_memory_space_constraint(array, pltpu.HBM)


def specs(places):
    spaces = dict(V=pltpu.VMEM, H=pltpu.HBM, S=pltpu.SMEM, A=pl.ANY)
    return [pl.BlockSpec(memory_space=spaces[place]) for place in places]


def kernel_call(body, places, args, out_places, outs, name, cost, scratch=(), aliases=None):
    holds = dict(V=fast, H=slow)
    made = pl.pallas_call(
        body,
        in_specs=specs(places),
        out_specs=specs(out_places),
        out_shape=[
            pltpu.VMEM(shape, dtype) if place == "V" else jax.ShapeDtypeStruct(shape, dtype)
            for place, (shape, dtype) in zip(out_places, outs)
        ],
        scratch_shapes=list(scratch),
        input_output_aliases=aliases or {},
        name=name,
        **params(*cost),
    )
    return made(
        *[holds[place](one) if place in holds else one for place, one in zip(places, args)]
    )


class Copies:
    def __init__(self, sems):
        self.sems = sems
        self.used = 0

    def start(self, source, target):
        copy = pltpu.make_async_copy(source, target, self.sems.at[self.used])
        self.used += 1
        copy.start()
        return copy


def crossed(side):
    return (0, 1 + side, 2 - side, 3)


def all_places(special, number):
    if not special:
        return list(range(number))
    chip, core, layer = (lax.axis_index(name) for name in ("chip", "core", "dp"))
    upper = layer < 2
    layers = [layer, layer ^ 1, jnp.where(upper, 2, 1), jnp.where(upper, 3, 0)]

    def some(*arrivals):
        return [
            ((chip ^ crossed(side)[flip]) * 2 + side) * 4 + layers[one]
            for side in (core, 1 - core)
            for one, flips in arrivals
            for flip in flips
        ]

    three = (0, 1, 2)
    return (
        some((0, three), (1, three))
        + some((0, (3,)), (2, three), (3, (0,)))
        + some((1, (3,)), (2, (3,)), (3, (1, 2)))
        + some((3, (3,)))
    )


def piece_columns(place):
    return (slice(None), pl.ds(pl.multiple_of(place * PIECE, PIECE), PIECE))


def columns(at, wide=None):
    return (slice(None), pl.ds(at, wide or WIDE))


def groups(total, body):
    @pl.loop(0, total // WIDE)
    def _(group):
        body(group, pl.multiple_of(group * WIDE, WIDE))


def heads(at):
    return [pl.ds(pl.multiple_of(at + head, HEAD), HEAD) for head in range(0, WIDE, HEAD)]


def memory_kernel(
    special, key_ref, spike_ref, value_ref, tokens_ref, grad_ref,
    keys_ref, mask_ref, values_ref, own_ref, sent_ref, some_ref, grads_ref,
    key_in, spike_in, sems,
):
    copies = Copies(sems)
    wide = range(0, keys_ref.shape[1], WIDE)
    pairs = ((key_ref, key_in), (spike_ref, spike_in), (value_ref, values_ref))
    parts = [
        [copies.start(here.at[columns(at)], there.at[columns(at)]) for here, there in pairs]
        for at in wide
    ]
    places = all_places(special, some_ref.shape[1] // PIECE)
    ordered = [
        copies.start(tokens_ref.at[piece_columns(place)], some_ref.at[piece_columns(piece)])
        for piece, place in enumerate(places)
    ]
    ordered.append(copies.start(grad_ref, grads_ref))
    for at, part in zip(wide, parts):
        for copy in part:
            copy.wait()
        cols = slice(at, at + WIDE)
        mask = spike_in[:, cols].astype(f32).astype(bf16)
        keys = key_in[:, cols] * mask
        keys_ref[:, cols] = keys
        mask_ref[:, cols] = mask
        for head in range(0, WIDE, HEAD):
            here = slice(at + head, at + head + HEAD)
            own = tn(keys[:, head : head + HEAD], values_ref[:, here])
            own_ref[here, :] = own
            sent_ref[here, :] = own.astype(bf16)
    for copy in ordered:
        copy.wait()


def memory_call(special, key_input, k_spikes, values, tokens, cotangent):
    length, total = values.shape
    block, state = (length, total), (total, HEAD)
    return kernel_call(
        functools.partial(memory_kernel, special),
        "HHHHH",
        (key_input, k_spikes, values, tokens, cotangent),
        "VVVVVVV",
        [(block, bf16)] * 3
        + [(state, f32), (state, bf16), (tokens.shape, bf16), (block, bf16)],
        "own_memory",
        (2 * length * total * HEAD, 12 * length * total),
        [
            pltpu.VMEM(block, bf16),
            pltpu.VMEM(block, jnp.int32),
            pltpu.SemaphoreType.DMA((3 * total // WIDE + tokens.shape[1] // PIECE + 1,)),
        ],
    )


def join_kernel(*refs):
    del refs


def join(arrays, others=()):
    number = len(arrays)
    return kernel_call(
        join_kernel,
        ["A"] * (number + len(others)),
        (*[fast(one) for one in arrays], *others),
        ["A"] * number,
        [(one.shape, one.dtype) for one in arrays],
        "join",
        (0, 0),
        aliases={at: at for at in range(number)},
    )


def keep_lower(square, flipped=False):
    row = lax.broadcasted_iota(jnp.int32, square.shape, 0)
    col = lax.broadcasted_iota(jnp.int32, square.shape, 1)
    return jnp.where((col >= row) if flipped else (col <= row), square, 0.0).astype(bf16)


def causal(a, b):
    length = a.shape[0]
    cut = length - HEAD
    top = keep_lower(nt(a[:cut], b[:cut]))
    whole = nt(a[cut:], b)
    bottom = jnp.concatenate([whole[:, :cut].astype(bf16), keep_lower(whole[:, cut:])], axis=1)
    return [(slice(0, cut), slice(0, cut), top), (slice(cut, length), slice(0, length), bottom)]


def causal_turned(a, b):
    length = a.shape[0]
    whole = nt(a[:HEAD], b)
    top = jnp.concatenate(
        [keep_lower(whole[:, :HEAD], True), whole[:, HEAD:].astype(bf16)], axis=1
    )
    bottom = keep_lower(nt(a[HEAD:], b[HEAD:]), True)
    return [
        (slice(0, HEAD), slice(0, length), top),
        (slice(HEAD, length), slice(HEAD, length), bottom),
    ]


def twice(array):
    return jnp.concatenate([array, array], axis=1)


def masked_kernel(
    factor, spike_ref, grad_ref, value_ref, keys_ref, high_ref, low_ref,
    out_ref, mask_ref, spike_in, sems,
):
    total = out_ref.shape[1]

    def bring(group, at):
        return pltpu.make_async_copy(
            spike_ref.at[columns(at)], spike_in.at[columns(at)], sems.at[group]
        )

    for group in range(total // WIDE):
        bring(group, group * WIDE).start()

    def work(group, at):
        bring(group, at).wait()
        for part in heads(at):
            mask = spike_in[:, part].astype(f32)
            mask_ref[:, part] = mask.astype(bf16)
            grad, value, keys = grad_ref[:, part], value_ref[:, part], keys_ref[:, part]
            state = jnp.concatenate([high_ref[part, :], low_ref[part, :]], axis=1)
            for rows, cols, scores in causal(grad, value):
                made = nn(scores, keys[cols]) + nt(twice(grad[rows]), state)
                out_ref[rows, part] = (factor * made * mask[rows]).astype(bf16)

    groups(total, work)


def masked_call(factor, q_spikes, cotangent, values, keys, high, low):
    length, total = values.shape
    block = (length, total)
    return kernel_call(
        functools.partial(masked_kernel, factor),
        "HVVVVV",
        (q_spikes, cotangent, values, keys, high, low),
        "VV",
        [(block, bf16)] * 2,
        "masked_grad",
        (8 * length * total * length, 12 * length * total),
        [pltpu.VMEM(block, jnp.int32), pltpu.SemaphoreType.DMA((total // WIDE,))],
    )


def turned_kernel(value_ref, grad_ref, after_ref, top_ref, bottom_ref, mark_ref):
    del after_ref
    set_mark(mark_ref)
    length, total = value_ref.shape
    rest = length - HEAD
    number = WIDE // HEAD

    def work(group, at):
        for head, part in enumerate(heads(at)):
            (_, _, top), (_, _, bottom) = causal_turned(value_ref[:, part], grad_ref[:, part])
            place = group * number + head
            top_ref[:, pl.ds(pl.multiple_of(place * length, HEAD), length)] = top
            bottom_ref[:, pl.ds(pl.multiple_of(place * rest, HEAD), rest)] = bottom

    groups(total, work)


def turned_call(values, cotangent, after):
    length, total = values.shape
    number, rest = total // HEAD, length - HEAD
    return kernel_call(
        turned_kernel,
        "VVA",
        (values, cotangent, after),
        "VVV",
        [((HEAD, number * length), bf16), ((rest, number * rest), bf16), (MARK.shape, f32)],
        "turned",
        (4 * length * total * length, 0),
    )


def rows_of(blocks):
    return sum(block.shape[0] for block in blocks)


def back_blocks(blocks):
    at = 0
    for block in blocks:
        for row in range(0, block.shape[0], PIECE):
            yield at, block[row : row + PIECE, :]
            at += 1


def back_part(copies, places, masked, blocks, out_ref, round_ref):
    going = []
    pieces = list(back_blocks(blocks))
    for (first, upper), (second, lower) in zip(pieces[::2], pieces[1::2]):
        both = slice(first * PIECE, (second + 1) * PIECE)
        made = nt(masked[...], jnp.concatenate([upper, lower], axis=0))
        round_ref[:, both] = made.astype(bf16)
        for piece in (first, second):
            going.append(
                copies.start(
                    round_ref.at[piece_columns(piece)], out_ref.at[piece_columns(places[piece])]
                )
            )
    return going


def products_kernel(special, start, size, project, back, has_sum, has_back, *refs):
    blocks, refs = refs[:size], list(refs[size:])
    depth = rows_of(blocks)
    tokens_ref = refs.pop(0) if project else None
    before_ref = refs.pop(0) if has_sum else None
    masked = refs.pop(0) if back else None
    if has_back:
        refs.pop(0)
    sum_ref = refs.pop(0) if project else None
    back_out = refs.pop(0) if back else None
    mark_ref = refs.pop(0)
    set_mark(mark_ref)
    going = []
    if back:
        round_ref, sems = refs
        places = all_places(special, back_out.shape[1] // PIECE)[start:]
        going = back_part(Copies(sems), places, masked, blocks, back_out, round_ref)
    if project:
        cols = slice(start * PIECE, start * PIECE + depth)
        for at in range(0, sum_ref.shape[1], WIDE):
            part = slice(at, at + WIDE)
            made = nn(
                tokens_ref[:, cols],
                jnp.concatenate([block[:, part] for block in blocks], axis=0),
            )
            if has_sum:
                made = made + before_ref[:, part]
            sum_ref[:, part] = made
    for copy in going:
        copy.wait()


def products_call(
    special, start, blocks, tokens, partial=None, masked=None, grad=None, project=True
):
    length, width = tokens.shape
    total = blocks[0].shape[1]
    depth = rows_of(blocks)
    back = masked is not None
    places_in, args = "V" * len(blocks), list(blocks)
    places_out, outs = "", []
    scratch, aliases = [], {}
    if project:
        places_in, args = places_in + "V", args + [tokens]
        if partial is not None:
            aliases[len(args)] = 0
            places_in, args = places_in + "V", args + [partial]
        places_out, outs = "V", [((length, total), f32)]
    if back:
        places_in, args = places_in + "V", args + [masked]
        if grad is not None:
            aliases[len(args)] = len(outs)
            places_in, args = places_in + "H", args + [grad]
        places_out, outs = places_out + "H", outs + [((length, width), bf16)]
        scratch = [
            pltpu.VMEM((length, depth), bf16), pltpu.SemaphoreType.DMA((depth // PIECE,))
        ]
    made = kernel_call(
        functools.partial(
            products_kernel, special, start, len(blocks), project, back,
            partial is not None, grad is not None,
        ),
        places_in,
        args,
        places_out + "V",
        outs + [(MARK.shape, f32)],
        "products" if project and back else "project" if project else "grad_tokens",
        (2 * (project + back) * length * depth * total, 0),
        scratch,
        aliases,
    )
    made = list(made)
    partial = made.pop(0) if project else partial
    grad = made.pop(0) if back else grad
    return partial, grad, made[0]


def query_kernel(start, size, tokens_ref, sum_ref, mask_ref, grad_ref, *refs):
    blocks = refs[:size]
    queries, own_ref, sent_ref = refs[-3:]
    cols = slice(start * PIECE, start * PIECE + rows_of(blocks))
    for at in range(0, queries.shape[1], WIDE):
        part = slice(at, at + WIDE)
        made = nn(
            tokens_ref[:, cols], jnp.concatenate([block[:, part] for block in blocks], axis=0)
        )
        made = made + sum_ref[:, part]
        made = (made * mask_ref[:, part].astype(f32)).astype(bf16)
        queries[:, part] = made
        for head in range(0, WIDE, HEAD):
            here = slice(at + head, at + head + HEAD)
            own = tn(made[:, head : head + HEAD], grad_ref[:, here])
            own_ref[here, :] = own
            sent_ref[here, :] = own.astype(bf16)


def query_call(start, tokens, blocks, before, q_mask, cotangent, others):
    length = tokens.shape[0]
    total = blocks[0].shape[1]
    depth = rows_of(blocks)
    return kernel_call(
        functools.partial(query_kernel, start, len(blocks)),
        "VVVV" + "V" * len(blocks) + "A" * len(others),
        (tokens, before, q_mask, cotangent, *blocks, *others),
        "VVV",
        [((length, total), bf16), ((total, HEAD), f32), ((total, HEAD), bf16)],
        "queries",
        (2 * length * depth * total, 0),
    )


def out_copy(here, there, sems, group, at):
    return pltpu.make_async_copy(here.at[columns(at)], there.at[columns(at)], sems.at[group])


def attend_kernel(
    factor, query_ref, keys_ref, value_ref, high_ref, low_ref, out_ref, mark_ref, made_ref, sems
):
    set_mark(mark_ref)
    total = query_ref.shape[1]

    def work(group, at):
        for part in heads(at):
            query, keys, value = query_ref[:, part], keys_ref[:, part], value_ref[:, part]
            state = [high_ref[part, :], low_ref[part, :]]
            for rows, cols, scores in causal(query, keys):
                made = nn(
                    jnp.concatenate([scores, twice(query[rows])], axis=1),
                    jnp.concatenate([value[cols], *state], axis=0),
                )
                made_ref[rows, part] = (factor * made).astype(bf16)
        out_copy(made_ref, out_ref, sems, group, at).start()

    groups(total, work)
    for group in range(total // WIDE):
        out_copy(made_ref, out_ref, sems, group, group * WIDE).wait()


def attend_call(factor, queries, keys, values, high, low):
    length, total = values.shape
    return kernel_call(
        functools.partial(attend_kernel, factor),
        "VVVVV",
        (queries, keys, values, high, low),
        "HV",
        [((length, total), bf16), (MARK.shape, f32)],
        "attended",
        (8 * length * total * length, 8 * length * total),
        [pltpu.VMEM((length, total), bf16), pltpu.SemaphoreType.DMA((total // WIDE,))],
    )


def value_kernel(query_ref, keys_ref, grad_ref, val_ref, mark_ref):
    set_mark(mark_ref)

    def work(group, at):
        for part in heads(at):
            query, keys, grad = query_ref[:, part], keys_ref[:, part], grad_ref[:, part]
            for rows, cols, scores in causal_turned(keys, query):
                val_ref[rows, part] = nn(scores, grad[cols])

    groups(query_ref.shape[1], work)


def value_call(queries, keys, cotangent):
    length, total = keys.shape
    return kernel_call(
        value_kernel,
        "VVV",
        (queries, keys, cotangent),
        "VV",
        [((length, total), f32), (MARK.shape, f32)],
        "value_part",
        (6 * length * total * length, 0),
    )


def key_kernel(query_ref, top_ref, bottom_ref, key_ref, mark_ref):
    set_mark(mark_ref)
    length, total = query_ref.shape
    rest = length - HEAD
    number = WIDE // HEAD

    def work(group, at):
        for head, part in enumerate(heads(at)):
            query = query_ref[:, part]
            place = group * number + head
            top = top_ref[:, pl.ds(pl.multiple_of(place * length, HEAD), length)]
            bottom = bottom_ref[:, pl.ds(pl.multiple_of(place * rest, HEAD), rest)]
            key_ref[:HEAD, part] = nn(top, query)
            key_ref[HEAD:, part] = nn(bottom, query[HEAD:])

    groups(total, work)


def key_call(queries, top, bottom):
    length, total = queries.shape
    return kernel_call(
        key_kernel,
        "VVV",
        (queries, top, bottom),
        "VV",
        [((length, total), f32), (MARK.shape, f32)],
        "key_part",
        (4 * length * total * length, 0),
    )


def outer_kernel(
    factor, key_ref, val_ref, keys_ref, value_ref, mask_ref, high_ref, low_ref,
    key_out, val_out, key_made, val_made, key_sems, val_sems,
):
    total = keys_ref.shape[1]

    def work(group, at):
        for part in heads(at):
            keys, value = keys_ref[:, part], value_ref[:, part]
            state = [high_ref[part, :], low_ref[part, :]]
            key_grad = key_ref[:, part] + nt(twice(value), jnp.concatenate(state, axis=1))
            key_made[:, part] = (factor * key_grad * mask_ref[:, part].astype(f32)).astype(bf16)
            value_grad = val_ref[:, part] + nn(twice(keys), jnp.concatenate(state, axis=0))
            val_made[:, part] = (factor * value_grad).astype(bf16)
        out_copy(key_made, key_out, key_sems, group, at).start()
        out_copy(val_made, val_out, val_sems, group, at).start()

    groups(total, work)
    for group in range(total // WIDE):
        out_copy(key_made, key_out, key_sems, group, group * WIDE).wait()
        out_copy(val_made, val_out, val_sems, group, group * WIDE).wait()


def outer_call(factor, key_part, value_part, keys, values, k_mask, high, low):
    length, total = values.shape
    block = (length, total)
    return kernel_call(
        functools.partial(outer_kernel, factor),
        "VVVVVVV",
        (key_part, value_part, keys, values, k_mask, high, low),
        "HH",
        [(block, bf16)] * 2,
        "outer",
        (8 * length * total * HEAD, 20 * length * total),
        [pltpu.VMEM(block, bf16)] * 2 + [pltpu.SemaphoreType.DMA((total // WIDE,))] * 2,
    )


def half_kernel(
    factor, mine, has_before,
    state_ref, sibling_ref, key_ref, val_ref, keys_ref, value_ref, mask_ref, *refs,
):
    key_out, val_out, key_made, val_made, key_sems, val_sems = refs[2 if has_before else 0 :]
    core = lax.axis_index("core")
    half = state_ref.shape[0]
    base = (core if mine else 1 - core) * half
    adds = jnp.where(core == 0, 1.0, 0.0)

    def out_copies(group, at):
        there = columns(pl.multiple_of(base + at, WIDE))
        return [
            pltpu.make_async_copy(made.at[columns(at)], out.at[there], sems.at[group])
            for made, out, sems in (
                (key_made, key_out, key_sems), (val_made, val_out, val_sems)
            )
        ]

    def work(group, at):
        for here in heads(at):
            part = pl.ds(pl.multiple_of(base + here.start, HEAD), HEAD)
            whole = state_ref[here, :] + adds * sibling_ref[part, :].astype(f32)
            high = whole.astype(bf16)
            state = [high, (whole - high.astype(f32)).astype(bf16)]
            keys, value = keys_ref[:, part], value_ref[:, part]
            key_grad = key_ref[:, part] + nt(twice(value), jnp.concatenate(state, axis=1))
            key_made[:, here] = (factor * key_grad * mask_ref[:, part].astype(f32)).astype(bf16)
            value_grad = val_ref[:, part] + nn(twice(keys), jnp.concatenate(state, axis=0))
            val_made[:, here] = (factor * value_grad).astype(bf16)
        for copy in out_copies(group, at):
            copy.start()

    groups(half, work)
    for group in range(half // WIDE):
        for copy in out_copies(group, group * WIDE):
            copy.wait()


def half_call(factor, state, sibling, key_part, value_part, keys, values, k_mask, before=()):
    length, total = values.shape
    half = state.shape[0]
    return kernel_call(
        functools.partial(half_kernel, factor, not before, bool(before)),
        "VVVVVVV" + "H" * len(before),
        (state, sibling, key_part, value_part, keys, values, k_mask, *before),
        "HH",
        [((length, total), bf16)] * 2,
        "outer",
        (4 * length * total * HEAD, 10 * length * total),
        [pltpu.VMEM((length, half), bf16)] * 2
        + [pltpu.SemaphoreType.DMA((half // WIDE,))] * 2,
        {7 + at: at for at in range(len(before))},
    )


def halves(state):
    high = state.astype(bf16)
    return high, (state - high.astype(f32)).astype(bf16)


def scan_any(own, sent, count, reverse):
    place = lax.axis_index(CTX)
    total = own
    state = jnp.zeros_like(own)
    bits = count.bit_length() - 1
    for bit in range(bits):
        step = 1 << bit
        last = bit == bits - 1
        pairs = []
        for source in range(count):
            high = bool(source & step)
            if not last or high == reverse:
                pairs.append((source, source ^ step))
        got = lax.ppermute(sent, CTX, pairs).astype(f32)
        if last:
            state = state + got
        else:
            mine = ((place // step) % 2) == (0 if reverse else 1)
            state = state + jnp.where(mine, got, 0.0)
            total = total + got
            sent = total.astype(bf16)
    return state


def links(first, keep=lambda source, target: True):
    pairs = []
    for chip in range(4):
        for core in range(2):
            other = chip ^ (first if core == 0 else 3 - first)
            if keep((chip, core), other):
                pairs.append((chip * 2 + core, other * 2 + core))
    return pairs


def upward(reverse):
    flip = 3 if reverse else 0

    def keep(source, target):
        at = source[0] ^ flip
        return source[0] ^ target == 1 or not at & 2

    return keep


def low_bit(reverse):
    chip = lax.axis_index("chip")
    return 1 - chip % 2 if reverse else chip % 2


def half_rows(array_ref, core):
    half = array_ref.shape[0] // 2
    return array_ref[pl.ds(pl.multiple_of(core * half, half), half), :]


def both_kernel(own_ref, sibling_ref, *refs):
    both_ref, sent_ref = refs[-2:]
    core = lax.axis_index("core")
    both = half_rows(own_ref, core) + half_rows(sibling_ref, core).astype(f32)
    both_ref[...] = both
    sent_ref[...] = both.astype(bf16)


def message_kernel(reverse, got_ref, both_ref, *refs):
    core = lax.axis_index("core")
    adds = jnp.where((core == 0) | (low_bit(reverse) == 0), 1.0, 0.0)
    refs[-1][...] = (got_ref[...].astype(f32) + adds * both_ref[...]).astype(bf16)


def state_kernel(reverse, got_ref, more_ref, *refs):
    core = lax.axis_index("core")
    adds = jnp.where((core == 1) | (low_bit(reverse) == 1), 1.0, 0.0)
    refs[-1][...] = adds * got_ref[...].astype(f32) + more_ref[...].astype(f32)


def whole_kernel(reverse, state_ref, other_ref, sibling_ref, high_ref, low_ref):
    core = lax.axis_index("core")
    adds = jnp.where(core == (0 if reverse else 1), 1.0, 0.0)
    half = state_ref.shape[0]
    for ref, side in ((state_ref, core), (other_ref, 1 - core)):
        rows = pl.ds(pl.multiple_of(side * half, half), half)
        whole = ref[...] + adds * sibling_ref[rows, :].astype(f32)
        high = whole.astype(bf16)
        high_ref[rows, :] = high
        low_ref[rows, :] = (whole - high.astype(f32)).astype(bf16)


def send_first(own, sent, reverse, others=()):
    half = (own.shape[0] // 2, HEAD)
    sibling = lax.ppermute(sent, "core", SWAP)
    both, sent = kernel_call(
        both_kernel,
        "VV" + "A" * len(others),
        (own, sibling, *others),
        "VV",
        [(half, f32), (half, bf16)],
        "both",
        (0, 0),
    )
    return sibling, both, lax.ppermute(sent, CTX, links(1, upward(reverse)))


def send_second(got, both, reverse, others=()):
    (message,) = kernel_call(
        functools.partial(message_kernel, reverse),
        "VV" + "A" * len(others),
        (got, both, *others),
        "V",
        [(both.shape, bf16)],
        "message",
        (0, 0),
    )
    return lax.ppermute(message, CTX, links(2, upward(reverse)))


def add_halves(got, more, reverse, others=()):
    (state,) = kernel_call(
        functools.partial(state_kernel, reverse),
        "VV" + "A" * len(others),
        (got, more, *others),
        "V",
        [(got.shape, f32)],
        "state",
        (0, 0),
    )
    return state, lax.ppermute(state, "core", SWAP)


def add_up(got, more, sibling, reverse):
    state, other = add_halves(got, more, reverse)
    return kernel_call(
        functools.partial(whole_kernel, reverse),
        "VVV",
        (state, other, sibling),
        "VV",
        [(sibling.shape, bf16)] * 2,
        "whole",
        (0, 0),
    )


def gather_any(q_weight):
    whole = lax.all_gather(q_weight, ("chip", "core", "dp"), axis=0, tiled=True)
    cut = whole.shape[0] // (2 * PIECE) * PIECE
    return [whole[:cut], whole[cut:]]


def pack_kernel(number, *refs):
    arrays, (out_ref, sems) = refs[:number], refs[-2:]
    copies = Copies(sems)
    rows = out_ref.shape[0] // len(arrays)
    going = [
        copies.start(array, out_ref.at[pl.ds(at * rows, rows), :])
        for at, array in enumerate(arrays)
    ]
    for copy in going:
        copy.wait()


def pack(*arrays, others=()):
    rows, total = arrays[0].shape
    number = len(arrays)
    (made,) = kernel_call(
        functools.partial(pack_kernel, number),
        "A" * (number + len(others)),
        (*arrays, *others),
        "V",
        [((number * rows, total), arrays[0].dtype)],
        "pack",
        (0, 0),
        [pltpu.SemaphoreType.DMA((number,))],
    )
    return [made, lax.ppermute(made, "core", SWAP)]


def choose_kernel(inner_ref, end_ref, out_ref, sem):
    del end_ref
    layer = lax.axis_index("dp")

    @pl.when((layer == 1) | (layer == 2))
    def _():
        copy = pltpu.make_async_copy(inner_ref, out_ref, sem)
        copy.start()
        copy.wait()


def choose(inner, end):
    return kernel_call(
        choose_kernel,
        "AA",
        (fast(inner), fast(end)),
        "A",
        [(inner.shape, inner.dtype)],
        "choose",
        (0, 0),
        [pltpu.SemaphoreType.DMA],
        {1: 0},
    )[0]


def per_device(tokens, key_input, values, q_weight, q_spikes, k_spikes, cotangent):
    batches, length, width = tokens.shape
    assert batches == 1
    total = q_weight.shape[1]
    chips, spread = lax.axis_size("chip"), lax.axis_size("dp")
    factor = 3.0 / math.sqrt(HEAD * length * chips * 2)
    tokens, key_input, values, q_spikes, k_spikes, cotangent = (
        array.reshape(length, array.shape[2])
        for array in (tokens, key_input, values, q_spikes, k_spikes, cotangent)
    )
    special = chips == 4 and spread == 4

    def sibling(array):
        return lax.ppermute(array, "core", SWAP)

    def along(array, pairs):
        return lax.ppermute(array, "dp", pairs)

    def cross(array):
        return lax.ppermute(array, CTX, links(1)), lax.ppermute(array, CTX, links(2))

    def onward(array):
        return lax.ppermute(array, CTX, links(2))

    keys, k_mask, values, own, sent, tokens, cotangent = memory_call(
        special, key_input, k_spikes, values, tokens, cotangent
    )
    if special:
        ends = [(0, 1), (1, 0), (2, 3), (3, 2)]
        middle = [(1, 2), (2, 1)]
        outward = [(1, 0), (2, 3)]
        near = along(q_weight, ends)
        mid = along(q_weight, middle)
        first_0, second_0 = cross(q_weight)
        first_0, second_0, near, mid, sent = join([first_0, second_0, near, mid, sent])
    else:
        arrived = gather_any(q_weight)
        high, low = halves(scan_any(own, sent, chips * 2, False))

    if special:
        first_1, second_1 = cross(near)
        far = along(near, middle)
        mid_out = along(mid, outward)
        twin, both, got = send_first(own, sent, False)
        mid_out, first_1, second_1, far, got, first_0 = join(
            [mid_out, first_1, second_1, far, got, first_0]
        )
        third_0 = onward(first_0)
        more = send_second(got, both, False)
        next_layer = choose(mid, mid_out)
        first_2, second_2 = cross(next_layer)
        far_out = along(far, outward)
        early = pack(q_weight, first_0, second_0, near, first_1, second_1)
        partial, _, mark = products_call(special, 0, early, tokens)
        top, bottom, turned_mark = turned_call(values, cotangent, got)
        far_out, first_2, second_2, more, third_0 = join(
            [far_out, first_2, second_2, more, third_0], [mark, turned_mark]
        )
        third_1 = along(third_0, ends)
        third_2 = onward(first_2)
        last_layer = choose(far, far_out)
        first_3, second_3 = cross(last_layer)
        high, low = add_up(got, more, twin, False)
        masked, q_mask = masked_call(factor, q_spikes, cotangent, values, keys, high, low)
        middle = pack(third_0, next_layer, first_2, second_2, last_layer)
        _, grad, mark = products_call(special, 0, early, tokens, masked=masked, project=False)
        third_2, first_3, second_3, third_1, middle[1] = join(
            [third_2, first_3, second_3, third_1, middle[1]], [mark]
        )
        third_3 = onward(first_3)
        late = pack(third_1, third_2, first_3, second_3)
        partial, grad, mark_0 = products_call(
            special, 12, middle, tokens, partial, masked, grad
        )
        partial, _, mark_1 = products_call(special, 22, late, tokens, partial)
        third_3, = join([third_3], [mark_0, mark_1])
        _, grad, mark = products_call(
            special, 22, late, tokens, masked=masked, grad=grad, project=False
        )
        late = [third_3, sibling(third_3)]
        start = 30
    else:
        masked, q_mask = masked_call(factor, q_spikes, cotangent, values, keys, high, low)
        top, bottom, _ = turned_call(values, cotangent, own)
        start = arrived[0].shape[0] // PIECE
        partial, grad, mark = products_call(special, 0, arrived[:1], tokens, masked=masked)
        late = arrived[1:]
    queries, own, sent = query_call(start, tokens, late, partial, q_mask, cotangent, [mark])
    attended, attended_mark = attend_call(factor, queries, keys, values, high, low)
    value_part, value_mark = value_call(queries, keys, cotangent)
    key_part, key_mark = key_call(queries, top, bottom)
    _, grad_tokens, back_mark = products_call(
        special, start, late, tokens, masked=masked, grad=grad, project=False
    )
    if special:
        twin, both, got = send_first(own, sent, True, [back_mark])
        more = send_second(got, both, True, [attended_mark])
        state, other = add_halves(got, more, True, [value_mark, key_mark])
        rest = (twin, key_part, value_part, keys, values, k_mask)
        made = half_call(factor, state, *rest)
        grad_keys, grad_values = half_call(factor, other, *rest, made)
    else:
        adjoint = halves(scan_any(own, sent, chips * 2, True))
        grad_keys, grad_values = outer_call(
            factor, key_part, value_part, keys, values, k_mask, *adjoint
        )
    return tuple(
        array.reshape(1, length, array.shape[1])
        for array in (attended, grad_tokens, grad_keys, grad_values)
    )


def solution(mesh):
    count, spread = mesh.shape["ctx"], mesh.shape["dp"]
    fine = Mesh(mesh.devices.reshape(count // 2, 2, spread), ("chip", "core", "dp"))
    block = P("dp", CTX, None)
    rows = P(("chip", "core", "dp"), None)
    in_specs = (block, block, block, rows, block, block, block)
    return jax.shard_map(
        per_device, mesh=fine, in_specs=in_specs, out_specs=(block,) * 4, check_vma=False
    )
```
